32 devices in a mesh: dp: 8 (over y, x, core), fsdp: 4 (over z).
Axes of the slice: x: 2, y: 2, z: 4, core: 2. Of those that a mesh axis runs over, the one named last changes fastest.
Arguments:
- tokens: bfloat16 [8192, 1536], P(('dp', 'fsdp')), may hold values from -6 to 6
- gain_attn: bfloat16 [2, 1536], P(None, ('dp', 'fsdp')), may hold values from 0.099609375 to 1.8984375
- w_query: bfloat16 [2, 1536, 1536], P(None, ('dp', 'fsdp')), may hold values from -0.15625 to 0.15625
- w_key: bfloat16 [2, 1536, 768], P(None, ('dp', 'fsdp')), may hold values from -0.15625 to 0.15625
- w_value: bfloat16 [2, 1536, 768], P(None, ('dp', 'fsdp')), may hold values from -0.15625 to 0.15625
- w_out: bfloat16 [2, 1536, 1536], P(None, ('dp', 'fsdp')), may hold values from -1.25 to 1.25
- gain_ffn: bfloat16 [2, 1536], P(None, ('dp', 'fsdp')), may hold values from 0.099609375 to 1.8984375
- w_gate: bfloat16 [2, 1536, 4096], P(None, ('dp', 'fsdp')), may hold values from -0.15625 to 0.15625
- w_up: bfloat16 [2, 1536, 4096], P(None, ('dp', 'fsdp')), may hold values from -0.15625 to 0.15625
- w_down: bfloat16 [2, 4096, 1536], P(None, ('dp', 'fsdp')), may hold values from -0.09375 to 0.09375
- lengths: int32 [8, 4], P('dp'), may hold values from 1 to 128, 384 in all within a row
- cotangent: bfloat16 [8192, 1536], P(('dp', 'fsdp')), may hold values from -6 to 6
Outputs:
- layer_outputs: bfloat16 [2, 8192, 1536], P(None, ('dp', 'fsdp'))
- input_grad: float32 [8192, 1536], P(('dp', 'fsdp'))
- grad_gain_attn: float32 [2, 1536], P(None, ('dp', 'fsdp'))
- grad_w_query: float32 [2, 1536, 1536], P(None, ('dp', 'fsdp'))
- grad_w_key: float32 [2, 1536, 768], P(None, ('dp', 'fsdp'))
- grad_w_value: float32 [2, 1536, 768], P(None, ('dp', 'fsdp'))
- grad_w_out: float32 [2, 1536, 1536], P(None, ('dp', 'fsdp'))
- grad_gain_ffn: float32 [2, 1536], P(None, ('dp', 'fsdp'))
- grad_w_gate: float32 [2, 1536, 4096], P(None, ('dp', 'fsdp'))
- grad_w_up: float32 [2, 1536, 4096], P(None, ('dp', 'fsdp'))
- grad_w_down: float32 [2, 4096, 1536], P(None, ('dp', 'fsdp'))
The draws below stay inside these ranges and needn't reach their ends.
Inputs may be any that keep to these rules, and one draw needn't show every extreme that they name: Each group's 4 continuation lengths sum to 384 and one of them is 128.
All inputs are finite; a program needn't handle non-finite values.
Results may differ from the reference program's by a relative error of at most 0.029.
Values may be sent and summed in bfloat16 or wider, within the bound.
A program may use at most 448 MiB of HBM per device.

```python
import math
import jax
import jax.numpy as jnp
import numpy as np
from jax import lax

D = 1536
HEADS = 16
KV_HEADS = 8
HEAD_DIM = 96
FF = 4096
CONT_MOST = 128
LAYERS = 2
CONTS = 4
CONT_TOTAL = 384
GROUP_TOK = 1024
GROUPS = 8
TOKENS = 8192
KV = 768


def block_scale(own_key, extent, cuts, smallest, top_value):
    def one(dim, blocks):
        draws = jax.random.uniform(jax.random.fold_in(jax.random.fold_in(own_key, 6), dim), (blocks,), jnp.float32, smallest / len(cuts), top_value / len(cuts))
        return jnp.repeat(jnp.exp(draws), extent[dim] // blocks).reshape((-1,) + (1,) * (len(extent) - dim - 1))

    gain = one(*cuts[0])
    for cut in cuts[1:]:
        gain = gain * one(*cut)
    return gain


def split_up(number_of, total, limit, skew):
    weights = [(1 << 20) // math.isqrt(rank ** skew) + 1 for rank in range(2, number_of + 1)]
    spare, given = total - limit - (number_of - 1), [1] * (number_of - 1)
    while spare > 0:
        candidates = [i for i in range(number_of - 1) if given[i] < limit]
        mass, budget = sum([weights[i] for i in candidates]), spare
        for i in candidates:
            more = min(limit - given[i], max(1, budget * weights[i] // mass), spare)
            given[i] = given[i] + more
            spare = spare - more
    return np.array([limit] + given)


def ragged_sizes(own_key, count, total, bound, skew):
    if count == 2:
        one = jax.random.randint(own_key, (), max(1, total - bound), min(bound, total - 1) + 1)
        return jnp.stack([one, total - one])
    sizes = jnp.asarray(split_up(count, total, bound, skew), jnp.int32)
    couples = (count - 1) // 2
    giver, receiver = sizes[1:1 + 2 * couples:2], sizes[2:2 + 2 * couples:2]
    margin = jnp.minimum(giver - 1, bound - receiver)
    shifted = jax.random.randint(jax.random.fold_in(own_key, 1), (couples,), 0, 1 << 20) % (margin + 1)
    sizes = sizes.at[1:1 + 2 * couples:2].set(giver - shifted).at[2:2 + 2 * couples:2].set(receiver + shifted)
    return sizes[jax.random.permutation(jax.random.fold_in(own_key, 2), count)]


def bell_draw(key, shape, scale, reach, split=(), kind=jnp.bfloat16):
    factor_of = block_scale(key, shape, split, -0.22, 0.18) if split else 1.0
    array = jax.random.normal(key, shape, jnp.float32) * scale * factor_of
    return jnp.minimum(jnp.maximum(array, -reach), reach).astype(kind)


def setup_inputs(seed: int = 0) -> dict:
    arg_keys = jax.random.split(jax.random.key(seed), 13)
    return {
        "tokens": bell_draw(arg_keys[0], (TOKENS, D), 1.0, 6.0, ((0, 32),)),
        "gain_attn": jnp.clip(1.0 + 0.18 * jax.random.normal(arg_keys[1], (LAYERS, D), jnp.float32), 0.099609375, 1.8984375).astype(jnp.bfloat16),
        "w_query": bell_draw(arg_keys[2], (LAYERS, D, D), D ** -0.5, 0.15625, ((1, 32),)),
        "w_key": bell_draw(arg_keys[3], (LAYERS, D, KV), D ** -0.5, 0.15625, ((1, 32),)),
        "w_value": bell_draw(arg_keys[4], (LAYERS, D, KV), D ** -0.5, 0.15625, ((1, 32),)),
        "w_out": bell_draw(arg_keys[5], (LAYERS, D, D), (D // 64) ** -0.5, 1.25, ((1, 32),)),
        "gain_ffn": jnp.clip(1.0 + 0.18 * jax.random.normal(arg_keys[6], (LAYERS, D), jnp.float32), 0.099609375, 1.8984375).astype(jnp.bfloat16),
        "w_gate": bell_draw(arg_keys[7], (LAYERS, D, FF), D ** -0.5, 0.15625, ((1, 32),)),
        "w_up": bell_draw(arg_keys[8], (LAYERS, D, FF), D ** -0.5, 0.15625, ((1, 32),)),
        "w_down": bell_draw(arg_keys[9], (LAYERS, FF, D), FF ** -0.5, 0.09375, ((1, 32),)),
        "lengths": jax.vmap(lambda own: ragged_sizes(own, CONTS, CONT_TOTAL, CONT_MOST, 1))(jax.random.split(arg_keys[10], GROUPS)).reshape((GROUPS, CONTS)).astype(jnp.int32),
        "cotangent": bell_draw(arg_keys[11], (TOKENS, D), 1.0, 6.0, ((0, 32),)),
    }


@jax.custom_vjp
def low(v):
    return lax.optimization_barrier(v.astype(jnp.bfloat16)).astype(jnp.float32)

@jax.custom_vjp
def low_back(v):
    return v

def low_keep(v):
    return (low(v), None)

def low_pass(kept, grad):
    return (grad,)

def back_keep(v):
    return (v, None)

def back_low(kept, grad):
    return (low(grad),)
low.defvjp(low_keep, low_pass)
low_back.defvjp(back_keep, back_low)
EPSILON = 1e-05
ROPE_BASE = 100000.0
NEGATIVE = -1e+30
HIGHEST = lax.Precision.HIGHEST

def layout(lengths_row):
    places = jnp.arange(GROUP_TOK, dtype=jnp.int32)
    prompt_len = GROUP_TOK - jnp.sum(lengths_row)
    starts = prompt_len + jnp.cumsum(lengths_row) - lengths_row
    inside = places[:, None] >= starts[None, :]
    segment = lax.optimization_barrier(jnp.sum(inside.astype(jnp.int32), axis=1))
    begins = lax.optimization_barrier(jnp.max(jnp.where(inside, starts[None, :], 0), axis=1))
    position = jnp.where(segment > 0, places - begins + prompt_len, places)
    return (segment, position)

def rotate(values, position, direction):
    row_count = values.shape[0]
    shaped = values.reshape(row_count, -1, HEAD_DIM)
    halfway = HEAD_DIM // 2
    frequency = ROPE_BASE ** (-jnp.arange(halfway, dtype=jnp.float32) * 2.0 / HEAD_DIM)
    angles = position.astype(jnp.float32)[:, None] * frequency[None, :]
    cosine = jnp.cos(angles)[:, None, :]
    sine_part = direction * jnp.sin(angles)[:, None, :]
    first_half = shaped[..., :halfway]
    second_half = shaped[..., halfway:]
    turned = jnp.concatenate([first_half * cosine - second_half * sine_part, second_half * cosine + first_half * sine_part], axis=-1)
    return turned.reshape(values.shape)

def norm_apply(values, gain_vec):
    inv_rms = lax.rsqrt(lax.optimization_barrier(jnp.mean(values * values, axis=-1, keepdims=True)) + EPSILON)
    return values * inv_rms * gain_vec

def matmul(left, right):
    return jnp.dot(left, right, precision=HIGHEST, preferred_element_type=jnp.float32)

def group_attention(pieces):
    queries, key_rows, value_rows, segment = pieces
    block_rows = min(512, GROUP_TOK)
    block_count = GROUP_TOK // block_rows
    places = jnp.arange(GROUP_TOK, dtype=jnp.int32)
    factor = 1.0 / math.sqrt(HEAD_DIM)
    sharing = HEADS // KV_HEADS

    def one_block(block_parts):
        query_block, seg_block, place_block = block_parts
        grouped = query_block.reshape(block_rows, KV_HEADS, sharing, HEAD_DIM)
        scores = low_back(jnp.einsum('bngd,knd->ngbk', grouped, key_rows, precision=HIGHEST) * factor)
        visible = (seg_block[:, None] == segment[None, :]) & (places[None, :] <= place_block[:, None]) | (segment[None, :] == 0) & (seg_block[:, None] > 0)
        masked = jnp.where(visible, scores, NEGATIVE)
        peak_score = lax.optimization_barrier(jnp.max(masked, axis=-1, keepdims=True))
        exponent = jnp.where(visible, jnp.exp(masked - peak_score), 0.0)
        probability = low(exponent / lax.optimization_barrier(jnp.sum(exponent, axis=-1, keepdims=True)))
        mixed_heads = jnp.einsum('ngbk,knd->bngd', probability, value_rows, precision=HIGHEST)
        return mixed_heads.reshape(block_rows, HEADS * HEAD_DIM)
    attended = lax.map(jax.checkpoint(one_block), (queries.reshape(block_count, block_rows, HEADS, HEAD_DIM), segment.reshape(block_count, block_rows), places.reshape(block_count, block_rows)))
    return attended.reshape(GROUP_TOK, HEADS * HEAD_DIM)

def apply_layer(hidden, weight_set, segment, position):
    gain_attn, w_query, w_key, w_value, w_out, gain_ffn, w_gate, w_up, w_down = weight_set
    normed = low(norm_apply(hidden, gain_attn))
    queries = low(rotate(low_back(matmul(normed, w_query)), position, 1.0))
    key_rows = low(rotate(low_back(matmul(normed, w_key)), position, 1.0))
    value_rows = low(low_back(matmul(normed, w_value)))
    attended = lax.map(jax.checkpoint(group_attention), (queries.reshape(GROUPS, GROUP_TOK, HEADS, HEAD_DIM), key_rows.reshape(GROUPS, GROUP_TOK, KV_HEADS, HEAD_DIM), value_rows.reshape(GROUPS, GROUP_TOK, KV_HEADS, HEAD_DIM), segment))
    mixed_heads = low(low_back(attended.reshape(TOKENS, D)))
    middle = hidden + low_back(matmul(mixed_heads, w_out))
    normed_ffn = low(norm_apply(middle, gain_ffn))
    gating = low_back(matmul(normed_ffn, w_gate))
    upward = low_back(matmul(normed_ffn, w_up))
    activated = low(jax.nn.silu(gating) * upward)
    return middle + low_back(matmul(activated, w_down))

def reference(tokens, gain_attn, w_query, w_key, w_value, w_out, gain_ffn, w_gate, w_up, w_down, lengths, cotangent):
    segment, position = jax.vmap(layout)(lengths)
    position = position.reshape(TOKENS)
    weights = tuple((weight_item.astype(jnp.float32) for weight_item in (gain_attn, w_query, w_key, w_value, w_out, gain_ffn, w_gate, w_up, w_down)))

    def forward(start, weight_set):
        first_out = apply_layer(start, tuple((weight_item[0] for weight_item in weight_set)), segment, position)
        second_out = apply_layer(first_out, tuple((weight_item[1] for weight_item in weight_set)), segment, position)
        return (first_out, second_out)
    (first_out, second_out), pullback = jax.vjp(forward, tokens.astype(jnp.float32), weights)
    input_grad, grads = pullback((jnp.zeros_like(first_out), cotangent.astype(jnp.float32)))
    layer_outputs = jnp.stack([first_out, second_out]).astype(jnp.bfloat16)
    return (layer_outputs, input_grad, grads[0], grads[1], grads[2], grads[3], grads[4], grads[5], grads[6], grads[7], grads[8])
```

```python
import functools
import math

import jax
import jax.numpy as jnp
from jax import lax
from jax.experimental import pallas as pl
from jax.experimental.pallas import tpu as pltpu
from jax.sharding import PartitionSpec as P

HEAD_DIM = 96


EPSILON = 1e-05
ROPE_BASE = 100000.0
NEGATIVE = -1e30


def layout(lengths_row, group_tok):
    places = jnp.arange(group_tok, dtype=jnp.int32)
    prompt_len = group_tok - jnp.sum(lengths_row)
    starts = prompt_len + jnp.cumsum(lengths_row) - lengths_row
    inside = places[:, None] >= starts[None, :]
    segment = jnp.sum(inside.astype(jnp.int32), axis=1)
    begins = jnp.max(jnp.where(inside, starts[None, :], 0), axis=1)
    position = jnp.where(segment > 0, places - begins + prompt_len, places)
    return (segment, position)


def rotate(values, position, direction):
    row_count = values.shape[0]
    shaped = values.reshape(row_count, -1, HEAD_DIM)
    halfway = HEAD_DIM // 2
    frequency = ROPE_BASE ** (-jnp.arange(halfway, dtype=jnp.float32) * 2.0 / HEAD_DIM)
    angles = position.astype(jnp.float32)[:, None] * frequency[None, :]
    cosine = jnp.cos(angles)[:, None, :]
    sine_part = direction * jnp.sin(angles)[:, None, :]
    first_half = shaped[..., :halfway]
    second_half = shaped[..., halfway:]
    turned = jnp.concatenate(
        [
            first_half * cosine - second_half * sine_part,
            second_half * cosine + first_half * sine_part,
        ],
        axis=-1,
    )
    return turned.reshape(values.shape)


def norm_apply(values, gain_vec):
    inv_rms = lax.rsqrt(jnp.mean(values * values, axis=-1, keepdims=True) + EPSILON)
    return values * inv_rms * gain_vec


def norm_back(values, gain_vec, incoming):
    inv_rms = lax.rsqrt(jnp.mean(values * values, axis=-1, keepdims=True) + EPSILON)
    weighted = incoming * gain_vec
    inner_sum = jnp.mean(weighted * values, axis=-1, keepdims=True)
    grad_values = inv_rms * weighted - values * inv_rms * inv_rms * inv_rms * inner_sum
    grad_gain = jnp.sum(incoming * values * inv_rms, axis=0)
    return (grad_values, grad_gain)


def matmul(left, right):
    return jnp.dot(left, right, preferred_element_type=jnp.float32)


def visibility(seg_rows, row_places, segment, places):
    same_seq = (seg_rows[:, None] == segment[None, :]) & (places[None, :] <= row_places[:, None])
    prompt_seen = (segment[None, :] == 0) & (seg_rows[:, None] > 0)
    return same_seq | prompt_seen


def head_slices(query_b, keys_all, head_index):
    row_count = query_b.shape[0]
    kv_width = keys_all.shape[1] // 2
    sharing = query_b.shape[1] // kv_width
    query_part = lax.dynamic_slice_in_dim(
        query_b, head_index * sharing * HEAD_DIM, sharing * HEAD_DIM, 1
    ).reshape(row_count, sharing, HEAD_DIM)
    key_part = lax.dynamic_slice_in_dim(keys_all, head_index * HEAD_DIM, HEAD_DIM, 1)
    value_part = lax.dynamic_slice_in_dim(keys_all, kv_width + head_index * HEAD_DIM, HEAD_DIM, 1)
    return (query_part, key_part, value_part)


def attend_forward(query_b, keys_all, visible):
    row_count = query_b.shape[0]
    kv_heads = keys_all.shape[1] // 2 // HEAD_DIM
    factor = 1.0 / math.sqrt(HEAD_DIM)

    def per_head(head_index):
        query_part, key_part, value_part = head_slices(query_b, keys_all, head_index)
        scores = (
            jnp.einsum("tgd,kd->gtk", query_part, key_part, preferred_element_type=jnp.float32)
            * factor
        )
        masked = jnp.where(visible[None], scores, NEGATIVE)
        peak_score = jnp.max(masked, axis=-1)
        exponent = jnp.where(visible[None], jnp.exp(masked - peak_score[..., None]), 0.0)
        totals = jnp.sum(exponent, axis=-1)
        probability = (exponent / totals[..., None]).astype(jnp.bfloat16)
        mixed_heads = jnp.einsum(
            "gtk,kd->tgd", probability, value_part, preferred_element_type=jnp.float32
        )
        return (mixed_heads.reshape(row_count, -1), peak_score, totals)

    mixed_heads, peak_score, totals = lax.map(per_head, jnp.arange(kv_heads, dtype=jnp.int32))
    return (jnp.transpose(mixed_heads, (1, 0, 2)).reshape(row_count, -1), peak_score, totals)


def attend_backward(query_b, keys_all, visible, peak_score, totals, grad_mixed):
    row_count = query_b.shape[0]
    kv_width = keys_all.shape[1] // 2
    kv_heads = kv_width // HEAD_DIM
    sharing = query_b.shape[1] // kv_width
    factor = 1.0 / math.sqrt(HEAD_DIM)

    def per_head(pieces):
        head_index, peak_head, total_head = pieces
        query_part, key_part, value_part = head_slices(query_b, keys_all, head_index)
        grad_part = lax.dynamic_slice_in_dim(
            grad_mixed, head_index * sharing * HEAD_DIM, sharing * HEAD_DIM, 1
        ).reshape(row_count, sharing, HEAD_DIM)
        scores = (
            jnp.einsum("tgd,kd->gtk", query_part, key_part, preferred_element_type=jnp.float32)
            * factor
        )
        masked = jnp.where(visible[None], scores, NEGATIVE)
        exponent = jnp.where(visible[None], jnp.exp(masked - peak_head[..., None]), 0.0)
        probability = exponent / total_head[..., None]
        prob_low = probability.astype(jnp.bfloat16)
        grad_probs = jnp.einsum(
            "tgd,kd->gtk", grad_part, value_part, preferred_element_type=jnp.float32
        )
        inner_sum = jnp.sum(probability * grad_probs, axis=-1, keepdims=True)
        grad_scores = (probability * (grad_probs - inner_sum)).astype(jnp.bfloat16)
        grad_query = (
            jnp.einsum("gtk,kd->tgd", grad_scores, key_part, preferred_element_type=jnp.float32)
            * factor
        )
        grad_key = (
            jnp.einsum("gtk,tgd->kd", grad_scores, query_part, preferred_element_type=jnp.float32)
            * factor
        )
        grad_value = jnp.einsum(
            "gtk,tgd->kd", prob_low, grad_part, preferred_element_type=jnp.float32
        )
        return (grad_query.reshape(row_count, -1), grad_key, grad_value)

    grad_query, grad_key, grad_value = lax.map(
        per_head, (jnp.arange(kv_heads, dtype=jnp.int32), peak_score, totals)
    )
    group_rows = keys_all.shape[0]
    key_terms = jnp.concatenate(
        [
            jnp.transpose(grad_key, (1, 0, 2)).reshape(group_rows, -1),
            jnp.transpose(grad_value, (1, 0, 2)).reshape(group_rows, -1),
        ],
        axis=1,
    )
    return (jnp.transpose(grad_query, (1, 0, 2)).reshape(row_count, -1), key_terms)


def fetch_attention(layer_index, gain_attn, w_query, w_key, w_value, w_out):
    return (
        lax.all_gather(gain_attn[layer_index], ("dp", "fsdp"), axis=0, tiled=True),
        lax.all_gather(w_query[layer_index], ("dp", "fsdp"), axis=0, tiled=True),
        lax.all_gather(w_key[layer_index], ("dp", "fsdp"), axis=0, tiled=True),
        lax.all_gather(w_value[layer_index], ("dp", "fsdp"), axis=0, tiled=True),
        lax.all_gather(w_out[layer_index], ("dp", "fsdp"), axis=0, tiled=True),
    )


def fetch_ffn(layer_index, gain_ffn, w_gate, w_up, w_down):
    return (
        lax.all_gather(gain_ffn[layer_index], ("dp", "fsdp"), axis=0, tiled=True),
        lax.all_gather(w_gate[layer_index], ("dp", "fsdp"), axis=0, tiled=True),
        lax.all_gather(w_up[layer_index], ("dp", "fsdp"), axis=0, tiled=True),
        lax.all_gather(w_down[layer_index], ("dp", "fsdp"), axis=0, tiled=True),
    )


def share_keys(stacked):
    return lax.all_gather(stacked, "fsdp", axis=0, tiled=True)


def layer_forward(hidden, attn_weights, ffn_weights, pos_rows, visible):
    gain_a, query_w, key_w, value_w, out_w = attn_weights
    gain_f, gate_w, upper_w, down_w = ffn_weights
    normed = norm_apply(hidden, gain_a.astype(jnp.float32)).astype(jnp.bfloat16)
    query_b = rotate(matmul(normed, query_w), pos_rows, 1.0).astype(jnp.bfloat16)
    key_b = rotate(matmul(normed, key_w), pos_rows, 1.0).astype(jnp.bfloat16)
    value_b = matmul(normed, value_w).astype(jnp.bfloat16)
    stacked = jnp.concatenate([key_b, value_b], axis=1)
    keys_all = share_keys(stacked)
    mixed_heads, peak_score, totals = attend_forward(query_b, keys_all, visible)
    mixed_b = mixed_heads.astype(jnp.bfloat16)
    middle = hidden + matmul(mixed_b, out_w)
    normed_ffn = norm_apply(middle, gain_f.astype(jnp.float32)).astype(jnp.bfloat16)
    gating = matmul(normed_ffn, gate_w)
    upward = matmul(normed_ffn, upper_w)
    activated = (jax.nn.silu(gating) * upward).astype(jnp.bfloat16)
    result = middle + matmul(activated, down_w)
    saved = (
        hidden,
        normed,
        query_b,
        stacked,
        keys_all,
        peak_score,
        totals,
        mixed_b,
        middle,
        normed_ffn,
        gating,
        upward,
        activated,
    )
    return (result, saved)


def layer_backward(upstream, saved, attn_weights, ffn_weights, keys_all, pos_rows, visible):
    (
        hidden,
        normed,
        query_b,
        stacked,
        unused_keys,
        peak_score,
        totals,
        mixed_b,
        middle,
        normed_ffn,
        gating,
        upward,
        activated,
    ) = saved
    gain_a, query_w, key_w, value_w, out_w = attn_weights
    gain_f, gate_w, upper_w, down_w = ffn_weights
    grad_branch = upstream.astype(jnp.bfloat16)
    grad_down_w = matmul(activated.T, grad_branch)
    grad_act = matmul(grad_branch, down_w.T)
    sigmoid_g = jax.nn.sigmoid(gating)
    grad_gate = (grad_act * upward * sigmoid_g * (1.0 + gating * (1.0 - sigmoid_g))).astype(
        jnp.bfloat16
    )
    grad_up = (grad_act * gating * sigmoid_g).astype(jnp.bfloat16)
    grad_gate_w = matmul(normed_ffn.T, grad_gate)
    grad_up_w = matmul(normed_ffn.T, grad_up)
    grad_normed_ffn = matmul(grad_gate, gate_w.T) + matmul(grad_up, upper_w.T)
    grad_middle_part, grad_gain_f = norm_back(middle, gain_f.astype(jnp.float32), grad_normed_ffn)
    ffn_blocks = (
        lax.psum_scatter(
            grad_gain_f.astype(jnp.bfloat16), "dp", scatter_dimension=0, tiled=True
        ).astype(jnp.float32),
        lax.psum_scatter(
            grad_gate_w.astype(jnp.bfloat16), "dp", scatter_dimension=0, tiled=True
        ).astype(jnp.float32),
        lax.psum_scatter(
            grad_up_w.astype(jnp.bfloat16), "dp", scatter_dimension=0, tiled=True
        ).astype(jnp.float32),
        lax.psum_scatter(
            grad_down_w.astype(jnp.bfloat16), "dp", scatter_dimension=0, tiled=True
        ).astype(jnp.float32),
    )
    ffn_grads = (
        lax.psum_scatter(
            ffn_blocks[0].astype(jnp.bfloat16), "fsdp", scatter_dimension=0, tiled=True
        ).astype(jnp.float32),
        lax.psum_scatter(
            ffn_blocks[1].astype(jnp.bfloat16), "fsdp", scatter_dimension=0, tiled=True
        ).astype(jnp.float32),
        lax.psum_scatter(
            ffn_blocks[2].astype(jnp.bfloat16), "fsdp", scatter_dimension=0, tiled=True
        ).astype(jnp.float32),
        lax.psum_scatter(
            ffn_blocks[3].astype(jnp.bfloat16), "fsdp", scatter_dimension=0, tiled=True
        ).astype(jnp.float32),
    )
    grad_middle = upstream + grad_middle_part
    grad_proj = grad_middle.astype(jnp.bfloat16)
    grad_out_w = matmul(mixed_b.T, grad_proj)
    grad_mixed = matmul(grad_proj, out_w.T).astype(jnp.bfloat16)
    grad_query_rot, key_terms = attend_backward(
        query_b, keys_all, visible, peak_score, totals, grad_mixed
    )
    key_grads = lax.psum_scatter(
        key_terms.astype(jnp.bfloat16), "fsdp", scatter_dimension=0, tiled=True
    ).astype(jnp.float32)
    kv_width = key_terms.shape[1] // 2
    grad_query = rotate(grad_query_rot, pos_rows, -1.0).astype(jnp.bfloat16)
    grad_key = rotate(key_grads[:, :kv_width], pos_rows, -1.0).astype(jnp.bfloat16)
    grad_value = key_grads[:, kv_width:].astype(jnp.bfloat16)
    grad_normed = (
        matmul(grad_query, query_w.T) + matmul(grad_key, key_w.T) + matmul(grad_value, value_w.T)
    )
    grad_query_w = matmul(normed.T, grad_query)
    grad_key_w = matmul(normed.T, grad_key)
    grad_value_w = matmul(normed.T, grad_value)
    grad_hidden_part, grad_gain_a = norm_back(hidden, gain_a.astype(jnp.float32), grad_normed)
    attn_blocks = (
        lax.psum_scatter(
            grad_gain_a.astype(jnp.bfloat16), "dp", scatter_dimension=0, tiled=True
        ).astype(jnp.float32),
        lax.psum_scatter(
            grad_query_w.astype(jnp.bfloat16), "dp", scatter_dimension=0, tiled=True
        ).astype(jnp.float32),
        lax.psum_scatter(
            grad_key_w.astype(jnp.bfloat16), "dp", scatter_dimension=0, tiled=True
        ).astype(jnp.float32),
        lax.psum_scatter(
            grad_value_w.astype(jnp.bfloat16), "dp", scatter_dimension=0, tiled=True
        ).astype(jnp.float32),
        lax.psum_scatter(
            grad_out_w.astype(jnp.bfloat16), "dp", scatter_dimension=0, tiled=True
        ).astype(jnp.float32),
    )
    attn_grads = (
        lax.psum_scatter(
            attn_blocks[0].astype(jnp.bfloat16), "fsdp", scatter_dimension=0, tiled=True
        ).astype(jnp.float32),
        lax.psum_scatter(
            attn_blocks[1].astype(jnp.bfloat16), "fsdp", scatter_dimension=0, tiled=True
        ).astype(jnp.float32),
        lax.psum_scatter(
            attn_blocks[2].astype(jnp.bfloat16), "fsdp", scatter_dimension=0, tiled=True
        ).astype(jnp.float32),
        lax.psum_scatter(
            attn_blocks[3].astype(jnp.bfloat16), "fsdp", scatter_dimension=0, tiled=True
        ).astype(jnp.float32),
        lax.psum_scatter(
            attn_blocks[4].astype(jnp.bfloat16), "fsdp", scatter_dimension=0, tiled=True
        ).astype(jnp.float32),
    )
    return (grad_middle + grad_hidden_part, attn_grads, ffn_grads)


def general_device(
    tokens,
    gain_attn,
    w_query,
    w_key,
    w_value,
    w_out,
    gain_ffn,
    w_gate,
    w_up,
    w_down,
    lengths,
    cotangent,
):
    tok_rows = tokens.shape[0]
    group_tok = tok_rows * lax.axis_size("fsdp")
    segment, position = layout(lengths[0], group_tok)
    first_row = lax.axis_index("fsdp") * tok_rows
    row_places = first_row + jnp.arange(tok_rows, dtype=jnp.int32)
    seg_rows = lax.dynamic_slice_in_dim(segment, first_row, tok_rows)
    pos_rows = lax.dynamic_slice_in_dim(position, first_row, tok_rows)
    visible = visibility(seg_rows, row_places, segment, jnp.arange(group_tok, dtype=jnp.int32))
    hidden = tokens.astype(jnp.float32)
    layer_store = []
    results = []
    for layer_index in range(2):
        attn_weights = fetch_attention(layer_index, gain_attn, w_query, w_key, w_value, w_out)
        ffn_weights = fetch_ffn(layer_index, gain_ffn, w_gate, w_up, w_down)
        hidden, saved = layer_forward(hidden, attn_weights, ffn_weights, pos_rows, visible)
        layer_store.append(saved)
        results.append(hidden.astype(jnp.bfloat16))
    upstream = cotangent.astype(jnp.float32)
    attn_list = []
    ffn_list = []
    for layer_index in (1, 0):
        attn_weights = fetch_attention(layer_index, gain_attn, w_query, w_key, w_value, w_out)
        ffn_weights = fetch_ffn(layer_index, gain_ffn, w_gate, w_up, w_down)
        saved = layer_store[layer_index]
        keys_all = share_keys(saved[3])
        upstream, attn_grads, ffn_grads = layer_backward(
            upstream, saved, attn_weights, ffn_weights, keys_all, pos_rows, visible
        )
        attn_list.append(attn_grads)
        ffn_list.append(ffn_grads)
    layer_outputs = jnp.stack(results)
    grad_gain_attn = jnp.stack([attn_list[1][0], attn_list[0][0]])
    grad_w_query = jnp.stack([attn_list[1][1], attn_list[0][1]])
    grad_w_key = jnp.stack([attn_list[1][2], attn_list[0][2]])
    grad_w_value = jnp.stack([attn_list[1][3], attn_list[0][3]])
    grad_w_out = jnp.stack([attn_list[1][4], attn_list[0][4]])
    grad_gain_ffn = jnp.stack([ffn_list[1][0], ffn_list[0][0]])
    grad_w_gate = jnp.stack([ffn_list[1][1], ffn_list[0][1]])
    grad_w_up = jnp.stack([ffn_list[1][2], ffn_list[0][2]])
    grad_w_down = jnp.stack([ffn_list[1][3], ffn_list[0][3]])
    return (
        layer_outputs,
        upstream,
        grad_gain_attn,
        grad_w_query,
        grad_w_key,
        grad_w_value,
        grad_w_out,
        grad_gain_ffn,
        grad_w_gate,
        grad_w_up,
        grad_w_down,
    )


TP = 4


def halves_swapped(value):
    return (value % 2) * 2 + value // 2


def flip_dp(dp_size, bits):
    return [(i, i ^ bits) for i in range(dp_size)]


def flip_z(z_size, bits):
    return [(i, i ^ bits) for i in range(z_size)]


def regroup_pairs(dp_size, z_size):
    pairs = []
    for high in range(dp_size // TP):
        for rank in range(TP):
            for z in range(z_size):
                new_dp = high * TP + halves_swapped(z)
                pairs.append(((high * TP + rank) * z_size + z, new_dp * z_size + halves_swapped(rank)))
    return pairs


def head_partner(values, halfway):
    width = values.shape[1]
    lane = lax.broadcasted_iota(jnp.int32, values.shape, 1)
    ahead = pltpu.roll(values, width - halfway, 1)
    behind = pltpu.roll(values, halfway, 1)
    return jnp.where(lane % HEAD_DIM < halfway, ahead, behind)


def qkv_kernel(rows_ref, weight_ref, cos_ref, sin_ref, out_ref):
    raw = jnp.dot(rows_ref[...], weight_ref[...], preferred_element_type=jnp.float32)
    turned = raw * cos_ref[...] + head_partner(raw, HEAD_DIM // 2) * sin_ref[...]
    out_ref[...] = turned.astype(jnp.bfloat16)


def project_qkv(rows, weight, cosine, sine):
    total, depth = rows.shape
    width = weight.shape[1]
    block = total // TP
    return pl.pallas_call(
        qkv_kernel,
        grid=(TP,),
        out_shape=jax.ShapeDtypeStruct((total, width), jnp.bfloat16),
        in_specs=[
            pl.BlockSpec((block, depth), lambda i: (i, 0)),
            pl.BlockSpec((depth, width), lambda i: (0, 0)),
            pl.BlockSpec((block, width), lambda i: (i, 0)),
            pl.BlockSpec((block, width), lambda i: (i, 0)),
        ],
        out_specs=pl.BlockSpec((block, width), lambda i: (i, 0)),
        compiler_params=pltpu.CompilerParams(vmem_limit_bytes=48 * 2**20),
        cost_estimate=pl.CostEstimate(
            flops=2 * total * depth * width,
            bytes_accessed=2 * total * depth + 2 * depth * width + 10 * total * width,
            transcendentals=0,
        ),
    )(rows, weight, cosine, sine)


def block_mask(row_seg, col_seg, same_block, block):
    visible = (row_seg == col_seg) | (col_seg == 0)
    if same_block:
        rows = lax.broadcasted_iota(jnp.int32, (block, block), 0)
        cols = lax.broadcasted_iota(jnp.int32, (block, block), 1)
        visible = visible & (cols <= rows)
    return visible


def attend_fwd_kernel(slot_ref, qkv_ref, row_seg_ref, col_seg_ref, mixed_ref, lse_ref):
    total, width = qkv_ref.shape
    block = total // TP
    q_heads = width // (2 * HEAD_DIM)
    kv_heads = q_heads // 2
    factor = 1.0 / math.sqrt(HEAD_DIM)
    key_at = q_heads * HEAD_DIM
    value_at = key_at + kv_heads * HEAD_DIM
    places = [pl.ds(pl.multiple_of(slot_ref[b] * block, block), block) for b in range(TP)]
    nt = (((1,), (1,)), ((), ()))
    for i in range(TP):
        row_seg = row_seg_ref[i]
        masks = [block_mask(row_seg, col_seg_ref[j], i == j, block) for j in range(i + 1)]
        lse_cols = []
        for h in range(q_heads):
            kv = h // 2
            query = qkv_ref[places[i], h * HEAD_DIM : (h + 1) * HEAD_DIM]
            scores = []
            for j in range(i + 1):
                key = qkv_ref[places[j], key_at + kv * HEAD_DIM : key_at + (kv + 1) * HEAD_DIM]
                s = lax.dot_general(query, key, nt, preferred_element_type=jnp.float32) * factor
                scores.append(jnp.where(masks[j], s, NEGATIVE))
            peak = scores[0].max(axis=1, keepdims=True)
            for s in scores[1:]:
                peak = jnp.maximum(peak, s.max(axis=1, keepdims=True))
            total_e = jnp.zeros((block, 1), jnp.float32)
            mixed = jnp.zeros((block, HEAD_DIM), jnp.float32)
            for j in range(i + 1):
                e = jnp.exp(scores[j] - peak)
                total_e = total_e + e.sum(axis=1, keepdims=True)
                value = qkv_ref[places[j], value_at + kv * HEAD_DIM : value_at + (kv + 1) * HEAD_DIM]
                mixed = mixed + jnp.dot(
                    e.astype(jnp.bfloat16), value, preferred_element_type=jnp.float32
                )
            mixed_ref[places[i], h * HEAD_DIM : (h + 1) * HEAD_DIM] = (mixed / total_e).astype(
                jnp.bfloat16
            )
            lse_ref[i, :, h : h + 1] = peak + jnp.log(total_e)


def attend_fwd(slots, qkv, row_seg, col_seg):
    total, width = qkv.shape
    block = total // TP
    q_heads = width // (2 * HEAD_DIM)
    whole = lambda shape: pl.BlockSpec(shape, lambda i, s: (0,) * len(shape))
    return pl.pallas_call(
        attend_fwd_kernel,
        out_shape=[
            jax.ShapeDtypeStruct((total, width // 2), jnp.bfloat16),
            jax.ShapeDtypeStruct((TP, block, q_heads), jnp.float32),
        ],
        grid_spec=pltpu.PrefetchScalarGridSpec(
            num_scalar_prefetch=1,
            grid=(1,),
            in_specs=[whole(qkv.shape), whole(row_seg.shape), whole(col_seg.shape)],
            out_specs=[whole((total, width // 2)), whole((TP, block, q_heads))],
        ),
        compiler_params=pltpu.CompilerParams(vmem_limit_bytes=48 * 2**20),
        cost_estimate=pl.CostEstimate(
            flops=4 * total * total * q_heads * HEAD_DIM,
            bytes_accessed=3 * total * width,
            transcendentals=total * total * q_heads // 2,
        ),
    )(slots, qkv, row_seg, col_seg)


def attend_bwd_kernel(
    slot_ref, qkv_ref, grad_ref, mixed_ref, lse_ref, row_seg_ref, col_seg_ref, cos_ref, sin_ref, out_ref, acc_ref
):
    total, width = qkv_ref.shape
    block = total // TP
    q_heads = width // (2 * HEAD_DIM)
    kv_heads = q_heads // 2
    factor = 1.0 / math.sqrt(HEAD_DIM)
    key_at = q_heads * HEAD_DIM
    value_at = key_at + kv_heads * HEAD_DIM
    places = [pl.ds(pl.multiple_of(slot_ref[b] * block, block), block) for b in range(TP)]
    nt = (((1,), (1,)), ((), ()))
    tn = (((0,), (0,)), ((), ()))
    acc_ref[:, key_at:] = jnp.zeros((total, width - key_at), jnp.float32)
    for i in range(TP):
        row_seg = row_seg_ref[i]
        masks = [block_mask(row_seg, col_seg_ref[j], i == j, block) for j in range(i + 1)]
        for h in range(q_heads):
            kv = h // 2
            lanes = slice(h * HEAD_DIM, (h + 1) * HEAD_DIM)
            query = qkv_ref[places[i], lanes]
            grad = grad_ref[places[i], lanes]
            lse = lse_ref[i, :, h : h + 1]
            inner = jnp.sum(
                grad.astype(jnp.float32) * mixed_ref[places[i], lanes].astype(jnp.float32),
                axis=1,
                keepdims=True,
            )
            grad_query = jnp.zeros((block, HEAD_DIM), jnp.float32)
            key_lanes = slice(key_at + kv * HEAD_DIM, key_at + (kv + 1) * HEAD_DIM)
            value_lanes = slice(value_at + kv * HEAD_DIM, value_at + (kv + 1) * HEAD_DIM)
            for j in range(i + 1):
                key = qkv_ref[places[j], key_lanes]
                value = qkv_ref[places[j], value_lanes]
                s = lax.dot_general(query, key, nt, preferred_element_type=jnp.float32) * factor
                prob = jnp.where(masks[j], jnp.exp(s - lse), 0.0)
                grad_prob = lax.dot_general(grad, value, nt, preferred_element_type=jnp.float32)
                grad_score = (prob * (grad_prob - inner)).astype(jnp.bfloat16)
                grad_query = grad_query + jnp.dot(
                    grad_score, key, preferred_element_type=jnp.float32
                )
                acc_ref[places[j], key_lanes] += (
                    lax.dot_general(grad_score, query, tn, preferred_element_type=jnp.float32)
                    * factor
                )
                acc_ref[places[j], value_lanes] += lax.dot_general(
                    prob.astype(jnp.bfloat16), grad, tn, preferred_element_type=jnp.float32
                )
            acc_ref[places[i], lanes] = grad_query * factor
    for b in range(TP):
        rows = slice(b * block, (b + 1) * block)
        acc = acc_ref[rows, :]
        turned = acc * cos_ref[rows, :] - head_partner(acc, HEAD_DIM // 2) * sin_ref[rows, :]
        out_ref[rows, :] = turned.astype(jnp.bfloat16)


def attend_bwd(slots, qkv, grad, mixed, lse, row_seg, col_seg, cosine, sine):
    total, width = qkv.shape
    q_heads = width // (2 * HEAD_DIM)
    operands = (qkv, grad, mixed, lse, row_seg, col_seg, cosine, sine)
    whole = lambda shape: pl.BlockSpec(shape, lambda i, s: (0,) * len(shape))
    return pl.pallas_call(
        attend_bwd_kernel,
        out_shape=jax.ShapeDtypeStruct((total, width), jnp.bfloat16),
        grid_spec=pltpu.PrefetchScalarGridSpec(
            num_scalar_prefetch=1,
            grid=(1,),
            in_specs=[whole(v.shape) for v in operands],
            out_specs=whole((total, width)),
            scratch_shapes=[pltpu.VMEM((total, width), jnp.float32)],
        ),
        compiler_params=pltpu.CompilerParams(vmem_limit_bytes=56 * 2**20),
        cost_estimate=pl.CostEstimate(
            flops=10 * total * total * q_heads * HEAD_DIM,
            bytes_accessed=12 * total * width,
            transcendentals=total * total * q_heads // 2,
        ),
    )(slots, *operands)


def place_attn_kernel(order_ref, chunk_ref, qkv_ref, out_ref):
    rows, half = qkv_ref.shape[0], out_ref.shape[1] // 2
    orows = out_ref.shape[0]
    qkv_ref[...] = chunk_ref[0, :rows]
    out_ref[:, :half] = chunk_ref[0, rows : rows + orows]
    out_ref[:, half:] = chunk_ref[0, rows + orows :]


def place_attn(order, chunks, depth):
    rows, width = chunks[0].shape
    col_rows = depth // 8
    orows = (rows - col_rows) // 2
    stacked = jnp.stack(chunks)
    return pl.pallas_call(
        place_attn_kernel,
        out_shape=[
            jax.ShapeDtypeStruct((depth, width), jnp.bfloat16),
            jax.ShapeDtypeStruct((orows * 8, width * 2), jnp.bfloat16),
        ],
        grid_spec=pltpu.PrefetchScalarGridSpec(
            num_scalar_prefetch=1,
            grid=(8,),
            in_specs=[pl.BlockSpec((1, rows, width), lambda r, o: (o[r], 0, 0))],
            out_specs=[
                pl.BlockSpec((col_rows, width), lambda r, o: (r, 0)),
                pl.BlockSpec((orows, width * 2), lambda r, o: (r, 0)),
            ],
        ),
        cost_estimate=pl.CostEstimate(flops=0, bytes_accessed=32 * rows * width, transcendentals=0),
    )(order, stacked)


def place_ffn_kernel(order_ref, chunk_ref, gate_ref, up_ref, down_ref):
    rows, units = gate_ref.shape
    drows = down_ref.shape[0]
    hd, qd = drows // 2, drows // 4
    gate_ref[...] = chunk_ref[0, :rows, :units]
    up_ref[...] = chunk_ref[0, :rows, units:]
    for s in range(2):
        down_ref[s * hd : (s + 1) * hd, :units] = chunk_ref[
            0, rows : rows + hd, s * units : (s + 1) * units
        ]
    for s in range(4):
        down_ref[s * qd : (s + 1) * qd, units:] = chunk_ref[
            0, rows + hd :, s * units // 2 : (s + 1) * units // 2
        ]


def place_ffn(order, chunks, depth):
    rows, width = chunks[0].shape
    col_rows = depth // 8
    units = width // 2
    drows = (rows - col_rows) * 4 // 3
    stacked = jnp.stack(chunks)
    return pl.pallas_call(
        place_ffn_kernel,
        out_shape=[
            jax.ShapeDtypeStruct((depth, units), jnp.bfloat16),
            jax.ShapeDtypeStruct((depth, units), jnp.bfloat16),
            jax.ShapeDtypeStruct((drows * 8, units * 3 // 2), jnp.bfloat16),
        ],
        grid_spec=pltpu.PrefetchScalarGridSpec(
            num_scalar_prefetch=1,
            grid=(8,),
            in_specs=[pl.BlockSpec((1, rows, width), lambda r, o: (o[r], 0, 0))],
            out_specs=[
                pl.BlockSpec((col_rows, units), lambda r, o: (r, 0)),
                pl.BlockSpec((col_rows, units), lambda r, o: (r, 0)),
                pl.BlockSpec((drows, units * 3 // 2), lambda r, o: (r, 0)),
            ],
        ),
        cost_estimate=pl.CostEstimate(flops=0, bytes_accessed=32 * rows * width, transcendentals=0),
    )(order, stacked)


class Fabric:
    def __init__(self):
        self.dp_size = lax.axis_size("dp")
        self.z_size = lax.axis_size("fsdp")
        dp = lax.axis_index("dp")
        self.z = lax.axis_index("fsdp")
        self.q = dp % TP
        self.y = dp // TP

    def rank(self, values, bits):
        return lax.ppermute(values, "dp", flip_dp(self.dp_size, bits))

    def core(self, values):
        return self.rank(values, 1)

    def across(self, values):
        return self.rank(values, 2)

    def over_y(self, values):
        return self.rank(values, TP)

    def over_z(self, values, bits):
        return lax.ppermute(values, "fsdp", flip_z(self.z_size, bits))

    def regroup(self, values):
        return lax.ppermute(values, ("dp", "fsdp"), regroup_pairs(self.dp_size, self.z_size))

    def natural(self, pieces):
        low, high = (self.q % 2) == 1, (self.q // 2) == 1
        a = [jnp.where(low, pieces[i ^ 1], pieces[i]) for i in range(4)]
        return [jnp.where(high, a[i ^ 2], a[i]) for i in range(4)]

    def spread(self, rows):
        near = jnp.concatenate([rows, self.across(rows)], axis=0)
        return jnp.concatenate([near, self.core(near)], axis=0)

    def collect(self, left, weight, extra=None):
        half = left.shape[0] // 2

        def part(rows):
            value = matmul(rows, weight)
            return value

        far = part(left[half:]).astype(jnp.bfloat16)
        got = self.core(far)
        near = part(left[:half]) + got.astype(jnp.float32)
        quarter = half // 2
        passed = self.across(near[quarter:].astype(jnp.bfloat16))
        return near[:quarter] + passed.astype(jnp.float32)


def exchange_columns(fab, pieces):
    received = [pieces[0]] + [fab.rank(pieces[k], k) for k in range(1, TP)]
    return fab.natural(received)


def column_pieces(fab, weight, layer, k):
    rows, width = weight.shape[1:]
    chosen = (fab.q // 2 ^ (k // 2)) * 2 + (fab.q % 2 ^ (k % 2))
    view = weight[layer].reshape(rows, 2, TP, width // (2 * TP))
    return lax.dynamic_index_in_dim(view, chosen, 2, keepdims=False).reshape(rows, width // TP)


def gather_chunks(fab, own):
    row = [own] + [fab.over_z(own, k) for k in range(1, 4)]
    return row + [fab.over_y(v) for v in row]


def reduce_blocks(fab, left, right, left_block):
    wide = left.shape[1] // 2
    there = lax.dynamic_slice_in_dim(left, (1 - fab.y) * wide, wide, 1)
    here = lax.dynamic_slice_in_dim(left, fab.y * wide, wide, 1)
    sent = fab.over_y(matmul(there.T, right).astype(jnp.bfloat16))
    total = (matmul(here.T, right) + sent.astype(jnp.float32)).astype(jnp.bfloat16)
    blocks = total.reshape(4, wide // 4, right.shape[1])
    z = fab.z
    picked = [
        lax.dynamic_index_in_dim(blocks, (z // 2 ^ (k // 2)) * 2 + (z % 2 ^ (k % 2)), 0, keepdims=False)
        for k in range(4)
    ]
    result = picked[0].astype(jnp.float32)
    for k in range(1, 4):
        result = result + fab.over_z(picked[k], k).astype(jnp.float32)
    return result


def return_columns(fab, block):
    low = block.astype(jnp.bfloat16).reshape(TP, block.shape[0] // TP, block.shape[1])
    pieces = [
        lax.dynamic_index_in_dim(
            low, (fab.q // 2 ^ (k // 2)) * 2 + (fab.q % 2 ^ (k % 2)), 0, keepdims=False
        )
        for k in range(TP)
    ]
    return exchange_columns(fab, pieces)


def join_columns(pieces):
    rows, width = pieces[0].shape
    view = jnp.stack([p.reshape(rows, 2, width // 2) for p in pieces], axis=2)
    return view.reshape(rows, TP * width).astype(jnp.float32)


def inner_rsqrt(values):
    return lax.rsqrt(jnp.mean(values * values, axis=-1, keepdims=True) + EPSILON)


def fast_device(
    tokens, gain_attn, w_query, w_key, w_value, w_out, gain_ffn, w_gate, w_up, w_down, lengths, cotangent
):
    fab = Fabric()
    block, depth = tokens.shape
    group_tok = block * fab.z_size
    shard = w_query.shape[1]
    nat = jnp.arange(depth, dtype=jnp.int32)
    nat_p = (
        (nat // (depth // 2)) * (depth // 2)
        + (nat // shard % fab.z_size) * (TP * shard)
        + (nat // (shard * fab.z_size) % TP) * shard
        + nat % shard
    )
    to_inner = (nat_p[:, None] == nat[None, :]).astype(jnp.bfloat16)
    inward = lambda v: jnp.dot(v, to_inner, preferred_element_type=jnp.float32).astype(jnp.bfloat16)
    outward = lambda v: lax.dot_general(
        v, to_inner, (((1,), (1,)), ((), ())), preferred_element_type=jnp.float32
    )

    out_in = inward(w_out.reshape(-1, depth)).reshape(w_out.shape)
    down_in = inward(w_down.reshape(-1, depth)).reshape(w_down.shape)
    attn_own, ffn_own = [], []
    for layer in range(2):
        pieces = [
            jnp.concatenate([column_pieces(fab, w, layer, k) for w in (w_query, w_key, w_value)], axis=1)
            for k in range(TP)
        ]
        cols = exchange_columns(fab, pieces)
        width = cols[0].shape[1]
        own_out = out_in[layer]
        attn_own.append(jnp.concatenate(cols + [own_out[:, :width], own_out[:, width:]], axis=0))
        pieces = [
            jnp.concatenate([column_pieces(fab, w, layer, k) for w in (w_gate, w_up)], axis=1)
            for k in range(TP)
        ]
        cols = exchange_columns(fab, pieces)
        units = cols[0].shape[1] // 2
        dn = down_in[layer]
        dr = dn.shape[0]
        wide = jnp.concatenate([dn[: dr // 2, :units], dn[dr // 2 :, :units]], axis=1)
        rest = jnp.concatenate([dn[s * dr // 4 : (s + 1) * dr // 4, units:] for s in range(4)], axis=1)
        ffn_own.append(jnp.concatenate(cols + [wide, rest], axis=0))

    gains = lax.all_gather(
        jnp.concatenate([gain_attn, gain_ffn], axis=0), ("dp", "fsdp"), axis=0, tiled=False
    )
    gains = gains.reshape(2, TP, fab.z_size, 4, shard).transpose(3, 0, 2, 1, 4).reshape(4, depth)
    gains = gains.astype(jnp.float32)

    hidden = inward(fab.regroup(tokens)).astype(jnp.float32)
    cot = inward(fab.regroup(cotangent))
    lengths_row = fab.regroup(lengths)[0]

    segment, position = layout(lengths_row, group_tok)
    base = halves_swapped(fab.q)
    slots = (jnp.arange(TP) // 2 ^ base // 2) * 2 + (jnp.arange(TP) % 2 ^ base % 2)
    seg_blocks = segment.reshape(TP, block)
    row_seg = seg_blocks[:, :, None]
    col_seg = seg_blocks[:, None, :]
    pos_rows = jnp.take(position.reshape(TP, block), slots, axis=0).reshape(-1)
    halfway = HEAD_DIM // 2
    frequency = ROPE_BASE ** (-jnp.arange(halfway, dtype=jnp.float32) * 2.0 / HEAD_DIM)
    angles = pos_rows.astype(jnp.float32)[:, None] * frequency[None, :]
    cos_h, sin_h = jnp.cos(angles), jnp.sin(angles)
    heads = w_query.shape[2] // HEAD_DIM // TP
    kv_heads = w_key.shape[2] // HEAD_DIM // TP
    cosine = jnp.concatenate(
        [cos_h, cos_h] * (heads + kv_heads)
        + [jnp.ones((group_tok, kv_heads * HEAD_DIM), jnp.float32)],
        axis=1,
    )
    sine = jnp.concatenate(
        [-sin_h, sin_h] * (heads + kv_heads)
        + [jnp.zeros((group_tok, kv_heads * HEAD_DIM), jnp.float32)],
        axis=1,
    )

    places = jnp.arange(8, dtype=jnp.int32)
    order = (places // 4 ^ fab.y) * 4 + (places % 4 // 2 ^ fab.z // 2) * 2 + (places % 2 ^ fab.z % 2)
    saved, outs = [], []
    for layer in range(2):
        w_qkv, w_o = place_attn(order, gather_chunks(fab, attn_own[layer]), depth)
        w_g, w_u, w_d = place_ffn(order, gather_chunks(fab, ffn_own[layer]), depth)
        gain_a, gain_f = gains[layer], gains[2 + layer]
        normed = fab.spread((hidden * inner_rsqrt(hidden) * gain_a).astype(jnp.bfloat16))
        qkv = project_qkv(normed, w_qkv, cosine, sine)
        mixed, lse = attend_fwd(slots, qkv, row_seg, col_seg)
        middle = hidden + fab.collect(mixed, w_o)
        normed_ffn = fab.spread((middle * inner_rsqrt(middle) * gain_f).astype(jnp.bfloat16))
        gating = matmul(normed_ffn, w_g)
        upward = matmul(normed_ffn, w_u)
        activated = (jax.nn.silu(gating) * upward).astype(jnp.bfloat16)
        result = middle + fab.collect(activated, w_d)
        saved.append(
            (hidden, normed, qkv, mixed, lse, middle, normed_ffn,
             gating.astype(jnp.bfloat16), upward.astype(jnp.bfloat16), activated, w_qkv, w_o, w_g, w_u, w_d)
        )
        hidden = result
        outs.append(fab.regroup(outward(result.astype(jnp.bfloat16)).astype(jnp.bfloat16)))

    upstream = cot.astype(jnp.float32)
    grads = [None, None]
    gain_grads = [None] * 4
    for layer in (1, 0):
        (hid, normed, qkv, mixed, lse, middle, normed_ffn, gating, upward, activated,
         w_qkv, w_o, w_g, w_u, w_d) = saved[layer]
        gain_a, gain_f = gains[layer], gains[2 + layer]
        branch = fab.spread(upstream.astype(jnp.bfloat16))
        grad_act = matmul(branch, w_d.T)
        gating = gating.astype(jnp.float32)
        upward = upward.astype(jnp.float32)
        sig = jax.nn.sigmoid(gating)
        grad_gate = (grad_act * upward * sig * (1.0 + gating * (1.0 - sig))).astype(jnp.bfloat16)
        grad_up = (grad_act * gating * sig).astype(jnp.bfloat16)
        both = jnp.concatenate([grad_gate, grad_up], axis=1)
        down_grad = reduce_blocks(fab, activated, branch, None)
        gu_grad = reduce_blocks(fab, normed_ffn, both, None)
        w_gu = jnp.concatenate([w_g, w_u], axis=1)
        grad_normed_ffn = fab.collect(both, w_gu.T)
        part, gain_grads[2 + layer] = norm_back(middle, gain_f, grad_normed_ffn)
        grad_middle = upstream + part
        proj = fab.spread(grad_middle.astype(jnp.bfloat16))
        grad_mixed = matmul(proj, w_o.T).astype(jnp.bfloat16)
        out_grad = reduce_blocks(fab, mixed, proj, None)
        grad_qkv = attend_bwd(slots, qkv, grad_mixed, mixed, lse, row_seg, col_seg, cosine, sine)
        qkv_grad = reduce_blocks(fab, normed, grad_qkv, None)
        grad_normed = fab.collect(grad_qkv, w_qkv.T)
        part, gain_grads[layer] = norm_back(hid, gain_a, grad_normed)
        upstream = grad_middle + part
        gu_parts = return_columns(fab, gu_grad)
        units = gu_parts[0].shape[1] // 2
        qkv_parts = return_columns(fab, qkv_grad)
        qw, kw = heads * HEAD_DIM, kv_heads * HEAD_DIM
        grads[layer] = (
            join_columns([p[:, :qw] for p in qkv_parts]),
            join_columns([p[:, qw : qw + kw] for p in qkv_parts]),
            join_columns([p[:, qw + kw :] for p in qkv_parts]),
            outward(out_grad.astype(jnp.bfloat16)),
            join_columns([p[:, :units] for p in gu_parts]),
            join_columns([p[:, units:] for p in gu_parts]),
            outward(down_grad.astype(jnp.bfloat16)),
        )
    input_grad = fab.regroup(outward(upstream.astype(jnp.bfloat16)).astype(jnp.bfloat16)).astype(
        jnp.float32
    )
    gain_sums = lax.psum(jnp.stack(gain_grads), ("dp", "fsdp"))
    own_gain = lax.dynamic_slice_in_dim(
        gain_sums, (fab.y * fab.z_size + fab.z) * (TP * shard) + fab.q * shard, shard, 1
    )
    pair = lambda n: jnp.stack([grads[0][n], grads[1][n]])
    return (
        jnp.stack(outs),
        input_grad,
        own_gain[:2],
        pair(0),
        pair(1),
        pair(2),
        pair(3),
        own_gain[2:],
        pair(4),
        pair(5),
        pair(6),
    )


def per_device(*arrays):
    tokens, w_query, w_key, w_gate = arrays[0], arrays[2], arrays[3], arrays[7]
    dp_size, z_size = lax.axis_size("dp"), lax.axis_size("fsdp")
    suits = (
        dp_size == 2 * TP
        and z_size == TP
        and w_key.shape[2] // HEAD_DIM == dp_size
        and w_query.shape[2] == 2 * w_key.shape[2]
        and tokens.shape[0] % 128 == 0
        and w_query.shape[1] % 16 == 0
        and w_gate.shape[2] % (TP * dp_size * 128) == 0
    )
    return (fast_device if suits else general_device)(*arrays)


def solution(mesh):
    placed = (
        P(("dp", "fsdp"), None),
        P(None, ("dp", "fsdp")),
        P(None, ("dp", "fsdp"), None),
        P(None, ("dp", "fsdp"), None),
        P(None, ("dp", "fsdp"), None),
        P(None, ("dp", "fsdp"), None),
        P(None, ("dp", "fsdp")),
        P(None, ("dp", "fsdp"), None),
        P(None, ("dp", "fsdp"), None),
        P(None, ("dp", "fsdp"), None),
        P("dp", None),
        P(("dp", "fsdp"), None),
    )
    return jax.shard_map(
        per_device,
        mesh=mesh,
        in_specs=placed,
        out_specs=(
            P(None, ("dp", "fsdp"), None),
            P(("dp", "fsdp"), None),
            P(None, ("dp", "fsdp")),
            P(None, ("dp", "fsdp"), None),
            P(None, ("dp", "fsdp"), None),
            P(None, ("dp", "fsdp"), None),
            P(None, ("dp", "fsdp"), None),
            P(None, ("dp", "fsdp")),
            P(None, ("dp", "fsdp"), None),
            P(None, ("dp", "fsdp"), None),
            P(None, ("dp", "fsdp"), None),
        ),
        check_vma=False,
    )
```

```python
import functools
import math

import jax
import jax.numpy as jnp
from jax import lax
from jax.experimental import pallas as pl
from jax.experimental.pallas import tpu as pltpu
from jax.sharding import PartitionSpec as P

HEAD_DIM = 96


EPSILON = 1e-05
ROPE_BASE = 100000.0
NEGATIVE = -1e30


def layout(lengths_row, group_tok):
    places = jnp.arange(group_tok, dtype=jnp.int32)
    prompt_len = group_tok - jnp.sum(lengths_row)
    starts = prompt_len + jnp.cumsum(lengths_row) - lengths_row
    inside = places[:, None] >= starts[None, :]
    segment = jnp.sum(inside.astype(jnp.int32), axis=1)
    begins = jnp.max(jnp.where(inside, starts[None, :], 0), axis=1)
    position = jnp.where(segment > 0, places - begins + prompt_len, places)
    return (segment, position)


def rotate(values, position, direction):
    row_count = values.shape[0]
    shaped = values.reshape(row_count, -1, HEAD_DIM)
    halfway = HEAD_DIM // 2
    frequency = ROPE_BASE ** (-jnp.arange(halfway, dtype=jnp.float32) * 2.0 / HEAD_DIM)
    angles = position.astype(jnp.float32)[:, None] * frequency[None, :]
    cosine = jnp.cos(angles)[:, None, :]
    sine_part = direction * jnp.sin(angles)[:, None, :]
    first_half = shaped[..., :halfway]
    second_half = shaped[..., halfway:]
    turned = jnp.concatenate(
        [
            first_half * cosine - second_half * sine_part,
            second_half * cosine + first_half * sine_part,
        ],
        axis=-1,
    )
    return turned.reshape(values.shape)


def norm_apply(values, gain_vec):
    inv_rms = lax.rsqrt(jnp.mean(values * values, axis=-1, keepdims=True) + EPSILON)
    return values * inv_rms * gain_vec


def norm_back(values, gain_vec, incoming):
    inv_rms = lax.rsqrt(jnp.mean(values * values, axis=-1, keepdims=True) + EPSILON)
    weighted = incoming * gain_vec
    inner_sum = jnp.mean(weighted * values, axis=-1, keepdims=True)
    grad_values = inv_rms * weighted - values * inv_rms * inv_rms * inv_rms * inner_sum
    grad_gain = jnp.sum(incoming * values * inv_rms, axis=0)
    return (grad_values, grad_gain)


def matmul(left, right):
    return jnp.dot(left, right, preferred_element_type=jnp.float32)


def visibility(seg_rows, row_places, segment, places):
    same_seq = (seg_rows[:, None] == segment[None, :]) & (places[None, :] <= row_places[:, None])
    prompt_seen = (segment[None, :] == 0) & (seg_rows[:, None] > 0)
    return same_seq | prompt_seen


def head_slices(query_b, keys_all, head_index):
    row_count = query_b.shape[0]
    kv_width = keys_all.shape[1] // 2
    sharing = query_b.shape[1] // kv_width
    query_part = lax.dynamic_slice_in_dim(
        query_b, head_index * sharing * HEAD_DIM, sharing * HEAD_DIM, 1
    ).reshape(row_count, sharing, HEAD_DIM)
    key_part = lax.dynamic_slice_in_dim(keys_all, head_index * HEAD_DIM, HEAD_DIM, 1)
    value_part = lax.dynamic_slice_in_dim(keys_all, kv_width + head_index * HEAD_DIM, HEAD_DIM, 1)
    return (query_part, key_part, value_part)


def attend_forward(query_b, keys_all, visible):
    row_count = query_b.shape[0]
    kv_heads = keys_all.shape[1] // 2 // HEAD_DIM
    factor = 1.0 / math.sqrt(HEAD_DIM)

    def per_head(head_index):
        query_part, key_part, value_part = head_slices(query_b, keys_all, head_index)
        scores = (
            jnp.einsum("tgd,kd->gtk", query_part, key_part, preferred_element_type=jnp.float32)
            * factor
        )
        masked = jnp.where(visible[None], scores, NEGATIVE)
        peak_score = jnp.max(masked, axis=-1)
        exponent = jnp.where(visible[None], jnp.exp(masked - peak_score[..., None]), 0.0)
        totals = jnp.sum(exponent, axis=-1)
        probability = (exponent / totals[..., None]).astype(jnp.bfloat16)
        mixed_heads = jnp.einsum(
            "gtk,kd->tgd", probability, value_part, preferred_element_type=jnp.float32
        )
        return (mixed_heads.reshape(row_count, -1), peak_score, totals)

    mixed_heads, peak_score, totals = lax.map(per_head, jnp.arange(kv_heads, dtype=jnp.int32))
    return (jnp.transpose(mixed_heads, (1, 0, 2)).reshape(row_count, -1), peak_score, totals)


def attend_backward(query_b, keys_all, visible, peak_score, totals, grad_mixed):
    row_count = query_b.shape[0]
    kv_width = keys_all.shape[1] // 2
    kv_heads = kv_width // HEAD_DIM
    sharing = query_b.shape[1] // kv_width
    factor = 1.0 / math.sqrt(HEAD_DIM)

    def per_head(pieces):
        head_index, peak_head, total_head = pieces
        query_part, key_part, value_part = head_slices(query_b, keys_all, head_index)
        grad_part = lax.dynamic_slice_in_dim(
            grad_mixed, head_index * sharing * HEAD_DIM, sharing * HEAD_DIM, 1
        ).reshape(row_count, sharing, HEAD_DIM)
        scores = (
            jnp.einsum("tgd,kd->gtk", query_part, key_part, preferred_element_type=jnp.float32)
            * factor
        )
        masked = jnp.where(visible[None], scores, NEGATIVE)
        exponent = jnp.where(visible[None], jnp.exp(masked - peak_head[..., None]), 0.0)
        probability = exponent / total_head[..., None]
        prob_low = probability.astype(jnp.bfloat16)
        grad_probs = jnp.einsum(
            "tgd,kd->gtk", grad_part, value_part, preferred_element_type=jnp.float32
        )
        inner_sum = jnp.sum(probability * grad_probs, axis=-1, keepdims=True)
        grad_scores = (probability * (grad_probs - inner_sum)).astype(jnp.bfloat16)
        grad_query = (
            jnp.einsum("gtk,kd->tgd", grad_scores, key_part, preferred_element_type=jnp.float32)
            * factor
        )
        grad_key = (
            jnp.einsum("gtk,tgd->kd", grad_scores, query_part, preferred_element_type=jnp.float32)
            * factor
        )
        grad_value = jnp.einsum(
            "gtk,tgd->kd", prob_low, grad_part, preferred_element_type=jnp.float32
        )
        return (grad_query.reshape(row_count, -1), grad_key, grad_value)

    grad_query, grad_key, grad_value = lax.map(
        per_head, (jnp.arange(kv_heads, dtype=jnp.int32), peak_score, totals)
    )
    group_rows = keys_all.shape[0]
    key_terms = jnp.concatenate(
        [
            jnp.transpose(grad_key, (1, 0, 2)).reshape(group_rows, -1),
            jnp.transpose(grad_value, (1, 0, 2)).reshape(group_rows, -1),
        ],
        axis=1,
    )
    return (jnp.transpose(grad_query, (1, 0, 2)).reshape(row_count, -1), key_terms)


def fetch_attention(layer_index, gain_attn, w_query, w_key, w_value, w_out):
    return (
        lax.all_gather(gain_attn[layer_index], ("dp", "fsdp"), axis=0, tiled=True),
        lax.all_gather(w_query[layer_index], ("dp", "fsdp"), axis=0, tiled=True),
        lax.all_gather(w_key[layer_index], ("dp", "fsdp"), axis=0, tiled=True),
        lax.all_gather(w_value[layer_index], ("dp", "fsdp"), axis=0, tiled=True),
        lax.all_gather(w_out[layer_index], ("dp", "fsdp"), axis=0, tiled=True),
    )


def fetch_ffn(layer_index, gain_ffn, w_gate, w_up, w_down):
    return (
        lax.all_gather(gain_ffn[layer_index], ("dp", "fsdp"), axis=0, tiled=True),
        lax.all_gather(w_gate[layer_index], ("dp", "fsdp"), axis=0, tiled=True),
        lax.all_gather(w_up[layer_index], ("dp", "fsdp"), axis=0, tiled=True),
        lax.all_gather(w_down[layer_index], ("dp", "fsdp"), axis=0, tiled=True),
    )


def share_keys(stacked):
    return lax.all_gather(stacked, "fsdp", axis=0, tiled=True)


def layer_forward(hidden, attn_weights, ffn_weights, pos_rows, visible):
    gain_a, query_w, key_w, value_w, out_w = attn_weights
    gain_f, gate_w, upper_w, down_w = ffn_weights
    normed = norm_apply(hidden, gain_a.astype(jnp.float32)).astype(jnp.bfloat16)
    query_b = rotate(matmul(normed, query_w), pos_rows, 1.0).astype(jnp.bfloat16)
    key_b = rotate(matmul(normed, key_w), pos_rows, 1.0).astype(jnp.bfloat16)
    value_b = matmul(normed, value_w).astype(jnp.bfloat16)
    stacked = jnp.concatenate([key_b, value_b], axis=1)
    keys_all = share_keys(stacked)
    mixed_heads, peak_score, totals = attend_forward(query_b, keys_all, visible)
    mixed_b = mixed_heads.astype(jnp.bfloat16)
    middle = hidden + matmul(mixed_b, out_w)
    normed_ffn = norm_apply(middle, gain_f.astype(jnp.float32)).astype(jnp.bfloat16)
    gating = matmul(normed_ffn, gate_w)
    upward = matmul(normed_ffn, upper_w)
    activated = (jax.nn.silu(gating) * upward).astype(jnp.bfloat16)
    result = middle + matmul(activated, down_w)
    saved = (
        hidden,
        normed,
        query_b,
        stacked,
        keys_all,
        peak_score,
        totals,
        mixed_b,
        middle,
        normed_ffn,
        gating,
        upward,
        activated,
    )
    return (result, saved)


def layer_backward(upstream, saved, attn_weights, ffn_weights, keys_all, pos_rows, visible):
    (
        hidden,
        normed,
        query_b,
        stacked,
        unused_keys,
        peak_score,
        totals,
        mixed_b,
        middle,
        normed_ffn,
        gating,
        upward,
        activated,
    ) = saved
    gain_a, query_w, key_w, value_w, out_w = attn_weights
    gain_f, gate_w, upper_w, down_w = ffn_weights
    grad_branch = upstream.astype(jnp.bfloat16)
    grad_down_w = matmul(activated.T, grad_branch)
    grad_act = matmul(grad_branch, down_w.T)
    sigmoid_g = jax.nn.sigmoid(gating)
    grad_gate = (grad_act * upward * sigmoid_g * (1.0 + gating * (1.0 - sigmoid_g))).astype(
        jnp.bfloat16
    )
    grad_up = (grad_act * gating * sigmoid_g).astype(jnp.bfloat16)
    grad_gate_w = matmul(normed_ffn.T, grad_gate)
    grad_up_w = matmul(normed_ffn.T, grad_up)
    grad_normed_ffn = matmul(grad_gate, gate_w.T) + matmul(grad_up, upper_w.T)
    grad_middle_part, grad_gain_f = norm_back(middle, gain_f.astype(jnp.float32), grad_normed_ffn)
    ffn_blocks = (
        lax.psum_scatter(
            grad_gain_f.astype(jnp.bfloat16), "dp", scatter_dimension=0, tiled=True
        ).astype(jnp.float32),
        lax.psum_scatter(
            grad_gate_w.astype(jnp.bfloat16), "dp", scatter_dimension=0, tiled=True
        ).astype(jnp.float32),
        lax.psum_scatter(
            grad_up_w.astype(jnp.bfloat16), "dp", scatter_dimension=0, tiled=True
        ).astype(jnp.float32),
        lax.psum_scatter(
            grad_down_w.astype(jnp.bfloat16), "dp", scatter_dimension=0, tiled=True
        ).astype(jnp.float32),
    )
    ffn_grads = (
        lax.psum_scatter(
            ffn_blocks[0].astype(jnp.bfloat16), "fsdp", scatter_dimension=0, tiled=True
        ).astype(jnp.float32),
        lax.psum_scatter(
            ffn_blocks[1].astype(jnp.bfloat16), "fsdp", scatter_dimension=0, tiled=True
        ).astype(jnp.float32),
        lax.psum_scatter(
            ffn_blocks[2].astype(jnp.bfloat16), "fsdp", scatter_dimension=0, tiled=True
        ).astype(jnp.float32),
        lax.psum_scatter(
            ffn_blocks[3].astype(jnp.bfloat16), "fsdp", scatter_dimension=0, tiled=True
        ).astype(jnp.float32),
    )
    grad_middle = upstream + grad_middle_part
    grad_proj = grad_middle.astype(jnp.bfloat16)
    grad_out_w = matmul(mixed_b.T, grad_proj)
    grad_mixed = matmul(grad_proj, out_w.T).astype(jnp.bfloat16)
    grad_query_rot, key_terms = attend_backward(
        query_b, keys_all, visible, peak_score, totals, grad_mixed
    )
    key_grads = lax.psum_scatter(
        key_terms.astype(jnp.bfloat16), "fsdp", scatter_dimension=0, tiled=True
    ).astype(jnp.float32)
    kv_width = key_terms.shape[1] // 2
    grad_query = rotate(grad_query_rot, pos_rows, -1.0).astype(jnp.bfloat16)
    grad_key = rotate(key_grads[:, :kv_width], pos_rows, -1.0).astype(jnp.bfloat16)
    grad_value = key_grads[:, kv_width:].astype(jnp.bfloat16)
    grad_normed = (
        matmul(grad_query, query_w.T) + matmul(grad_key, key_w.T) + matmul(grad_value, value_w.T)
    )
    grad_query_w = matmul(normed.T, grad_query)
    grad_key_w = matmul(normed.T, grad_key)
    grad_value_w = matmul(normed.T, grad_value)
    grad_hidden_part, grad_gain_a = norm_back(hidden, gain_a.astype(jnp.float32), grad_normed)
    attn_blocks = (
        lax.psum_scatter(
            grad_gain_a.astype(jnp.bfloat16), "dp", scatter_dimension=0, tiled=True
        ).astype(jnp.float32),
        lax.psum_scatter(
            grad_query_w.astype(jnp.bfloat16), "dp", scatter_dimension=0, tiled=True
        ).astype(jnp.float32),
        lax.psum_scatter(
            grad_key_w.astype(jnp.bfloat16), "dp", scatter_dimension=0, tiled=True
        ).astype(jnp.float32),
        lax.psum_scatter(
            grad_value_w.astype(jnp.bfloat16), "dp", scatter_dimension=0, tiled=True
        ).astype(jnp.float32),
        lax.psum_scatter(
            grad_out_w.astype(jnp.bfloat16), "dp", scatter_dimension=0, tiled=True
        ).astype(jnp.float32),
    )
    attn_grads = (
        lax.psum_scatter(
            attn_blocks[0].astype(jnp.bfloat16), "fsdp", scatter_dimension=0, tiled=True
        ).astype(jnp.float32),
        lax.psum_scatter(
            attn_blocks[1].astype(jnp.bfloat16), "fsdp", scatter_dimension=0, tiled=True
        ).astype(jnp.float32),
        lax.psum_scatter(
            attn_blocks[2].astype(jnp.bfloat16), "fsdp", scatter_dimension=0, tiled=True
        ).astype(jnp.float32),
        lax.psum_scatter(
            attn_blocks[3].astype(jnp.bfloat16), "fsdp", scatter_dimension=0, tiled=True
        ).astype(jnp.float32),
        lax.psum_scatter(
            attn_blocks[4].astype(jnp.bfloat16), "fsdp", scatter_dimension=0, tiled=True
        ).astype(jnp.float32),
    )
    return (grad_middle + grad_hidden_part, attn_grads, ffn_grads)


def general_device(
    tokens,
    gain_attn,
    w_query,
    w_key,
    w_value,
    w_out,
    gain_ffn,
    w_gate,
    w_up,
    w_down,
    lengths,
    cotangent,
):
    tok_rows = tokens.shape[0]
    group_tok = tok_rows * lax.axis_size("fsdp")
    segment, position = layout(lengths[0], group_tok)
    first_row = lax.axis_index("fsdp") * tok_rows
    row_places = first_row + jnp.arange(tok_rows, dtype=jnp.int32)
    seg_rows = lax.dynamic_slice_in_dim(segment, first_row, tok_rows)
    pos_rows = lax.dynamic_slice_in_dim(position, first_row, tok_rows)
    visible = visibility(seg_rows, row_places, segment, jnp.arange(group_tok, dtype=jnp.int32))
    hidden = tokens.astype(jnp.float32)
    layer_store = []
    results = []
    for layer_index in range(2):
        attn_weights = fetch_attention(layer_index, gain_attn, w_query, w_key, w_value, w_out)
        ffn_weights = fetch_ffn(layer_index, gain_ffn, w_gate, w_up, w_down)
        hidden, saved = layer_forward(hidden, attn_weights, ffn_weights, pos_rows, visible)
        layer_store.append(saved)
        results.append(hidden.astype(jnp.bfloat16))
    upstream = cotangent.astype(jnp.float32)
    attn_list = []
    ffn_list = []
    for layer_index in (1, 0):
        attn_weights = fetch_attention(layer_index, gain_attn, w_query, w_key, w_value, w_out)
        ffn_weights = fetch_ffn(layer_index, gain_ffn, w_gate, w_up, w_down)
        saved = layer_store[layer_index]
        keys_all = share_keys(saved[3])
        upstream, attn_grads, ffn_grads = layer_backward(
            upstream, saved, attn_weights, ffn_weights, keys_all, pos_rows, visible
        )
        attn_list.append(attn_grads)
        ffn_list.append(ffn_grads)
    layer_outputs = jnp.stack(results)
    grad_gain_attn = jnp.stack([attn_list[1][0], attn_list[0][0]])
    grad_w_query = jnp.stack([attn_list[1][1], attn_list[0][1]])
    grad_w_key = jnp.stack([attn_list[1][2], attn_list[0][2]])
    grad_w_value = jnp.stack([attn_list[1][3], attn_list[0][3]])
    grad_w_out = jnp.stack([attn_list[1][4], attn_list[0][4]])
    grad_gain_ffn = jnp.stack([ffn_list[1][0], ffn_list[0][0]])
    grad_w_gate = jnp.stack([ffn_list[1][1], ffn_list[0][1]])
    grad_w_up = jnp.stack([ffn_list[1][2], ffn_list[0][2]])
    grad_w_down = jnp.stack([ffn_list[1][3], ffn_list[0][3]])
    return (
        layer_outputs,
        upstream,
        grad_gain_attn,
        grad_w_query,
        grad_w_key,
        grad_w_value,
        grad_w_out,
        grad_gain_ffn,
        grad_w_gate,
        grad_w_up,
        grad_w_down,
    )


TP = 4


def halves_swapped(value):
    return (value % 2) * 2 + value // 2


def flip_dp(dp_size, bits):
    return [(i, i ^ bits) for i in range(dp_size)]


def flip_z(z_size, bits):
    return [(i, i ^ bits) for i in range(z_size)]


def regroup_pairs(dp_size, z_size):
    pairs = []
    for high in range(dp_size // TP):
        for rank in range(TP):
            for z in range(z_size):
                new_dp = high * TP + halves_swapped(z)
                pairs.append(((high * TP + rank) * z_size + z, new_dp * z_size + halves_swapped(rank)))
    return pairs


def head_partner(values, halfway):
    width = values.shape[1]
    lane = lax.broadcasted_iota(jnp.int32, values.shape, 1)
    ahead = pltpu.roll(values, width - halfway, 1)
    behind = pltpu.roll(values, halfway, 1)
    return jnp.where(lane % HEAD_DIM < halfway, ahead, behind)


def qkv_kernel(rows_ref, weight_ref, cos_ref, sin_ref, out_ref):
    raw = jnp.dot(rows_ref[...], weight_ref[...], preferred_element_type=jnp.float32)
    turned = raw * cos_ref[...] + head_partner(raw, HEAD_DIM // 2) * sin_ref[...]
    out_ref[...] = turned.astype(jnp.bfloat16)


def project_qkv(rows, weight, cosine, sine):
    total, depth = rows.shape
    width = weight.shape[1]
    block = total // TP
    return pl.pallas_call(
        qkv_kernel,
        grid=(TP,),
        out_shape=jax.ShapeDtypeStruct((total, width), jnp.bfloat16),
        in_specs=[
            pl.BlockSpec((block, depth), lambda i: (i, 0)),
            pl.BlockSpec((depth, width), lambda i: (0, 0)),
            pl.BlockSpec((block, width), lambda i: (i, 0)),
            pl.BlockSpec((block, width), lambda i: (i, 0)),
        ],
        out_specs=pl.BlockSpec((block, width), lambda i: (i, 0)),
        compiler_params=pltpu.CompilerParams(vmem_limit_bytes=48 * 2**20),
        cost_estimate=pl.CostEstimate(
            flops=2 * total * depth * width,
            bytes_accessed=2 * total * depth + 2 * depth * width + 10 * total * width,
            transcendentals=0,
        ),
    )(rows, weight, cosine, sine)


def block_mask(row_seg, col_seg, same_block, block):
    visible = (row_seg == col_seg) | (col_seg == 0)
    if same_block:
        rows = lax.broadcasted_iota(jnp.int32, (block, block), 0)
        cols = lax.broadcasted_iota(jnp.int32, (block, block), 1)
        visible = visible & (cols <= rows)
    return visible


def attend_fwd_kernel(slot_ref, qkv_ref, row_seg_ref, col_seg_ref, mixed_ref, lse_ref):
    total, width = qkv_ref.shape
    block = total // TP
    q_heads = width // (2 * HEAD_DIM)
    kv_heads = q_heads // 2
    factor = 1.0 / math.sqrt(HEAD_DIM)
    key_at = q_heads * HEAD_DIM
    value_at = key_at + kv_heads * HEAD_DIM
    places = [pl.ds(pl.multiple_of(slot_ref[b] * block, block), block) for b in range(TP)]
    nt = (((1,), (1,)), ((), ()))
    for i in range(TP):
        row_seg = row_seg_ref[i]
        masks = [block_mask(row_seg, col_seg_ref[j], i == j, block) for j in range(i + 1)]
        lse_cols = []
        for h in range(q_heads):
            kv = h // 2
            query = qkv_ref[places[i], h * HEAD_DIM : (h + 1) * HEAD_DIM]
            scores = []
            for j in range(i + 1):
                key = qkv_ref[places[j], key_at + kv * HEAD_DIM : key_at + (kv + 1) * HEAD_DIM]
                s = lax.dot_general(query, key, nt, preferred_element_type=jnp.float32) * factor
                scores.append(jnp.where(masks[j], s, NEGATIVE))
            peak = scores[0].max(axis=1, keepdims=True)
            for s in scores[1:]:
                peak = jnp.maximum(peak, s.max(axis=1, keepdims=True))
            total_e = jnp.zeros((block, 1), jnp.float32)
            mixed = jnp.zeros((block, HEAD_DIM), jnp.float32)
            for j in range(i + 1):
                e = jnp.exp(scores[j] - peak)
                total_e = total_e + e.sum(axis=1, keepdims=True)
                value = qkv_ref[places[j], value_at + kv * HEAD_DIM : value_at + (kv + 1) * HEAD_DIM]
                mixed = mixed + jnp.dot(
                    e.astype(jnp.bfloat16), value, preferred_element_type=jnp.float32
                )
            mixed_ref[places[i], h * HEAD_DIM : (h + 1) * HEAD_DIM] = (mixed / total_e).astype(
                jnp.bfloat16
            )
            lse_ref[i, :, h : h + 1] = peak + jnp.log(total_e)


def attend_fwd(slots, qkv, row_seg, col_seg):
    total, width = qkv.shape
    block = total // TP
    q_heads = width // (2 * HEAD_DIM)
    whole = lambda shape: pl.BlockSpec(shape, lambda i, s: (0,) * len(shape))
    return pl.pallas_call(
        attend_fwd_kernel,
        out_shape=[
            jax.ShapeDtypeStruct((total, width // 2), jnp.bfloat16),
            jax.ShapeDtypeStruct((TP, block, q_heads), jnp.float32),
        ],
        grid_spec=pltpu.PrefetchScalarGridSpec(
            num_scalar_prefetch=1,
            grid=(1,),
            in_specs=[whole(qkv.shape), whole(row_seg.shape), whole(col_seg.shape)],
            out_specs=[whole((total, width // 2)), whole((TP, block, q_heads))],
        ),
        compiler_params=pltpu.CompilerParams(vmem_limit_bytes=48 * 2**20),
        cost_estimate=pl.CostEstimate(
            flops=4 * total * total * q_heads * HEAD_DIM,
            bytes_accessed=3 * total * width,
            transcendentals=total * total * q_heads // 2,
        ),
    )(slots, qkv, row_seg, col_seg)


def attend_bwd_kernel(
    slot_ref, qkv_ref, grad_ref, mixed_ref, lse_ref, row_seg_ref, col_seg_ref, cos_ref, sin_ref, out_ref, acc_ref
):
    total, width = qkv_ref.shape
    block = total // TP
    q_heads = width // (2 * HEAD_DIM)
    kv_heads = q_heads // 2
    factor = 1.0 / math.sqrt(HEAD_DIM)
    key_at = q_heads * HEAD_DIM
    value_at = key_at + kv_heads * HEAD_DIM
    places = [pl.ds(pl.multiple_of(slot_ref[b] * block, block), block) for b in range(TP)]
    nt = (((1,), (1,)), ((), ()))
    tn = (((0,), (0,)), ((), ()))
    acc_ref[:, key_at:] = jnp.zeros((total, width - key_at), jnp.float32)
    for i in range(TP):
        row_seg = row_seg_ref[i]
        masks = [block_mask(row_seg, col_seg_ref[j], i == j, block) for j in range(i + 1)]
        for h in range(q_heads):
            kv = h // 2
            lanes = slice(h * HEAD_DIM, (h + 1) * HEAD_DIM)
            query = qkv_ref[places[i], lanes]
            grad = grad_ref[places[i], lanes]
            lse = lse_ref[i, :, h : h + 1]
            inner = jnp.sum(
                grad.astype(jnp.float32) * mixed_ref[places[i], lanes].astype(jnp.float32),
                axis=1,
                keepdims=True,
            )
            grad_query = jnp.zeros((block, HEAD_DIM), jnp.float32)
            key_lanes = slice(key_at + kv * HEAD_DIM, key_at + (kv + 1) * HEAD_DIM)
            value_lanes = slice(value_at + kv * HEAD_DIM, value_at + (kv + 1) * HEAD_DIM)
            for j in range(i + 1):
                key = qkv_ref[places[j], key_lanes]
                value = qkv_ref[places[j], value_lanes]
                s = lax.dot_general(query, key, nt, preferred_element_type=jnp.float32) * factor
                prob = jnp.where(masks[j], jnp.exp(s - lse), 0.0)
                grad_prob = lax.dot_general(grad, value, nt, preferred_element_type=jnp.float32)
                grad_score = (prob * (grad_prob - inner)).astype(jnp.bfloat16)
                grad_query = grad_query + jnp.dot(
                    grad_score, key, preferred_element_type=jnp.float32
                )
                acc_ref[places[j], key_lanes] += (
                    lax.dot_general(grad_score, query, tn, preferred_element_type=jnp.float32)
                    * factor
                )
                acc_ref[places[j], value_lanes] += lax.dot_general(
                    prob.astype(jnp.bfloat16), grad, tn, preferred_element_type=jnp.float32
                )
            acc_ref[places[i], lanes] = grad_query * factor
    for b in range(TP):
        rows = slice(b * block, (b + 1) * block)
        acc = acc_ref[rows, :]
        turned = acc * cos_ref[rows, :] - head_partner(acc, HEAD_DIM // 2) * sin_ref[rows, :]
        out_ref[rows, :] = turned.astype(jnp.bfloat16)


def attend_bwd(slots, qkv, grad, mixed, lse, row_seg, col_seg, cosine, sine):
    total, width = qkv.shape
    q_heads = width // (2 * HEAD_DIM)
    operands = (qkv, grad, mixed, lse, row_seg, col_seg, cosine, sine)
    whole = lambda shape: pl.BlockSpec(shape, lambda i, s: (0,) * len(shape))
    return pl.pallas_call(
        attend_bwd_kernel,
        out_shape=jax.ShapeDtypeStruct((total, width), jnp.bfloat16),
        grid_spec=pltpu.PrefetchScalarGridSpec(
            num_scalar_prefetch=1,
            grid=(1,),
            in_specs=[whole(v.shape) for v in operands],
            out_specs=whole((total, width)),
            scratch_shapes=[pltpu.VMEM((total, width), jnp.float32)],
        ),
        compiler_params=pltpu.CompilerParams(vmem_limit_bytes=56 * 2**20),
        cost_estimate=pl.CostEstimate(
            flops=10 * total * total * q_heads * HEAD_DIM,
            bytes_accessed=12 * total * width,
            transcendentals=total * total * q_heads // 2,
        ),
    )(slots, *operands)


def place_attn_kernel(order_ref, chunk_ref, qkv_ref, out_ref):
    rows, half = qkv_ref.shape[0], out_ref.shape[1] // 2
    orows = out_ref.shape[0]
    qkv_ref[...] = chunk_ref[0, :rows]
    out_ref[:, :half] = chunk_ref[0, rows : rows + orows]
    out_ref[:, half:] = chunk_ref[0, rows + orows :]


def place_attn(order, chunks, depth):
    rows, width = chunks[0].shape
    col_rows = depth // 8
    orows = (rows - col_rows) // 2
    stacked = jnp.stack(chunks)
    return pl.pallas_call(
        place_attn_kernel,
        out_shape=[
            jax.ShapeDtypeStruct((depth, width), jnp.bfloat16),
            jax.ShapeDtypeStruct((orows * 8, width * 2), jnp.bfloat16),
        ],
        grid_spec=pltpu.PrefetchScalarGridSpec(
            num_scalar_prefetch=1,
            grid=(8,),
            in_specs=[pl.BlockSpec((1, rows, width), lambda r, o: (o[r], 0, 0))],
            out_specs=[
                pl.BlockSpec((col_rows, width), lambda r, o: (r, 0)),
                pl.BlockSpec((orows, width * 2), lambda r, o: (r, 0)),
            ],
        ),
        cost_estimate=pl.CostEstimate(flops=0, bytes_accessed=32 * rows * width, transcendentals=0),
    )(order, stacked)


def place_ffn_kernel(order_ref, chunk_ref, gate_ref, up_ref, down_ref):
    rows, units = gate_ref.shape
    drows = down_ref.shape[0]
    hd, qd = drows // 2, drows // 4
    gate_ref[...] = chunk_ref[0, :rows, :units]
    up_ref[...] = chunk_ref[0, :rows, units:]
    for s in range(2):
        down_ref[s * hd : (s + 1) * hd, :units] = chunk_ref[
            0, rows : rows + hd, s * units : (s + 1) * units
        ]
    for s in range(4):
        down_ref[s * qd : (s + 1) * qd, units:] = chunk_ref[
            0, rows + hd :, s * units // 2 : (s + 1) * units // 2
        ]


def place_ffn(order, chunks, depth):
    rows, width = chunks[0].shape
    col_rows = depth // 8
    units = width // 2
    drows = (rows - col_rows) * 4 // 3
    stacked = jnp.stack(chunks)
    return pl.pallas_call(
        place_ffn_kernel,
        out_shape=[
            jax.ShapeDtypeStruct((depth, units), jnp.bfloat16),
            jax.ShapeDtypeStruct((depth, units), jnp.bfloat16),
            jax.ShapeDtypeStruct((drows * 8, units * 3 // 2), jnp.bfloat16),
        ],
        grid_spec=pltpu.PrefetchScalarGridSpec(
            num_scalar_prefetch=1,
            grid=(8,),
            in_specs=[pl.BlockSpec((1, rows, width), lambda r, o: (o[r], 0, 0))],
            out_specs=[
                pl.BlockSpec((col_rows, units), lambda r, o: (r, 0)),
                pl.BlockSpec((col_rows, units), lambda r, o: (r, 0)),
                pl.BlockSpec((drows, units * 3 // 2), lambda r, o: (r, 0)),
            ],
        ),
        cost_estimate=pl.CostEstimate(flops=0, bytes_accessed=32 * rows * width, transcendentals=0),
    )(order, stacked)


class Fabric:
    def __init__(self):
        self.dp_size = lax.axis_size("dp")
        self.z_size = lax.axis_size("fsdp")
        dp = lax.axis_index("dp")
        self.z = lax.axis_index("fsdp")
        self.q = dp % TP
        self.y = dp // TP

    def rank(self, values, bits):
        return lax.ppermute(values, "dp", flip_dp(self.dp_size, bits))

    def core(self, values):
        return self.rank(values, 1)

    def across(self, values):
        return self.rank(values, 2)

    def over_y(self, values):
        return self.rank(values, TP)

    def over_z(self, values, bits):
        return lax.ppermute(values, "fsdp", flip_z(self.z_size, bits))

    def regroup(self, values):
        return lax.ppermute(values, ("dp", "fsdp"), regroup_pairs(self.dp_size, self.z_size))

    def natural(self, pieces):
        low, high = (self.q % 2) == 1, (self.q // 2) == 1
        a = [jnp.where(low, pieces[i ^ 1], pieces[i]) for i in range(4)]
        return [jnp.where(high, a[i ^ 2], a[i]) for i in range(4)]

    def spread(self, rows):
        near = jnp.concatenate([rows, self.across(rows)], axis=0)
        return jnp.concatenate([near, self.core(near)], axis=0)

    def collect(self, left, weight, extra=None):
        half = left.shape[0] // 2

        def part(rows):
            value = matmul(rows, weight)
            return value

        far = part(left[half:]).astype(jnp.bfloat16)
        got = self.core(far)
        near = part(left[:half]) + got.astype(jnp.float32)
        quarter = half // 2
        passed = self.across(near[quarter:].astype(jnp.bfloat16))
        return near[:quarter] + passed.astype(jnp.float32)


def exchange_columns(fab, pieces):
    received = [pieces[0]] + [fab.rank(pieces[k], k) for k in range(1, TP)]
    return fab.natural(received)


def column_pieces(fab, weight, layer, k):
    rows, width = weight.shape[1:]
    chosen = (fab.q // 2 ^ (k // 2)) * 2 + (fab.q % 2 ^ (k % 2))
    view = weight[layer].reshape(rows, 2, TP, width // (2 * TP))
    return lax.dynamic_index_in_dim(view, chosen, 2, keepdims=False).reshape(rows, width // TP)


def gather_chunks(fab, own):
    row = [own] + [fab.over_z(own, k) for k in range(1, 4)]
    return row + [fab.over_y(v) for v in row]


def reduce_blocks(fab, left, right, left_block):
    wide = left.shape[1] // 2
    there = lax.dynamic_slice_in_dim(left, (1 - fab.y) * wide, wide, 1)
    here = lax.dynamic_slice_in_dim(left, fab.y * wide, wide, 1)
    sent = fab.over_y(matmul(there.T, right).astype(jnp.bfloat16))
    total = (matmul(here.T, right) + sent.astype(jnp.float32)).astype(jnp.bfloat16)
    blocks = total.reshape(4, wide // 4, right.shape[1])
    z = fab.z
    picked = [
        lax.dynamic_index_in_dim(blocks, (z // 2 ^ (k // 2)) * 2 + (z % 2 ^ (k % 2)), 0, keepdims=False)
        for k in range(4)
    ]
    result = picked[0].astype(jnp.float32)
    for k in range(1, 4):
        result = result + fab.over_z(picked[k], k).astype(jnp.float32)
    return result


def return_columns(fab, block):
    low = block.astype(jnp.bfloat16).reshape(TP, block.shape[0] // TP, block.shape[1])
    pieces = [
        lax.dynamic_index_in_dim(
            low, (fab.q // 2 ^ (k // 2)) * 2 + (fab.q % 2 ^ (k % 2)), 0, keepdims=False
        )
        for k in range(TP)
    ]
    return exchange_columns(fab, pieces)


def join_columns(pieces):
    rows, width = pieces[0].shape
    view = jnp.stack([p.reshape(rows, 2, width // 2) for p in pieces], axis=2)
    return view.reshape(rows, TP * width).astype(jnp.float32)


def inner_rsqrt(values):
    return lax.rsqrt(jnp.mean(values * values, axis=-1, keepdims=True) + EPSILON)


MESH = pl.DeviceIdType.MESH
VMEM_LIMIT = 61 * 2**20
ANYWHERE = pl.BlockSpec(memory_space=pl.ANY)
IN_VMEM = pl.BlockSpec(memory_space=pltpu.VMEM)


class Net:
    def __init__(self, send_sems, recv_sems, local_sems):
        dp, z = lax.axis_index("dp"), lax.axis_index("fsdp")
        self.z = z
        self.q = lax.rem(dp, TP)
        self.y = lax.div(dp, TP)
        self.r = self.y * TP + z
        core = dp + 1 - 2 * lax.rem(dp, 2)
        across = dp + 2 - 4 * lax.rem(lax.div(dp, 2), 2)
        both = core + 2 - 4 * lax.rem(lax.div(dp, 2), 2)
        other = dp + TP - 2 * TP * lax.div(dp, TP)
        self.peer = {
            "core": (core, z),
            "x": (across, z),
            "both": (both, z),
            "y": (other, z),
            "z1": (dp, flip_index(z, 1)),
            "z2": (dp, flip_index(z, 2)),
            "z3": (dp, flip_index(z, 3)),
        }
        self.send_sems, self.recv_sems, self.local_sems = send_sems, recv_sems, local_sems
        self.n_remote = self.n_local = 0
        self.flying = []
        self.leaving = []

    def greet(self, names):
        barrier = pltpu.get_barrier_semaphore()
        for name in names:
            pl.semaphore_signal(barrier, inc=1, device_id=self.peer[name], device_id_type=MESH)
        pl.semaphore_wait(barrier, len(names))

    def remote(self, src, dst, name):
        n = self.n_remote
        self.n_remote += 1
        copy = pltpu.make_async_remote_copy(
            src_ref=src,
            dst_ref=dst,
            send_sem=self.send_sems.at[n],
            recv_sem=self.recv_sems.at[n],
            device_id=self.peer[name],
            device_id_type=MESH,
        )
        copy.start()
        return copy

    def local(self, src, dst):
        n = self.n_local
        self.n_local += 1
        copy = pltpu.make_async_copy(src, dst, self.local_sems.at[n])
        copy.start()
        return copy

    def keep(self, src, dst):
        self.leaving.append(self.local(src, dst))

    def finish(self):
        for copy in self.flying + self.leaving:
            copy.wait()
        self.flying, self.leaving = [], []

    def advance(self, moves):
        for copy in self.flying:
            copy.wait()
        self.flying = []
        for kind, ref, low, count in moves:
            if kind == "z":
                part = ref.at[self.r, pl.ds(low, count)]
                for k in (2, 3, 1):
                    self.flying.append(self.remote(part, part, f"z{k}"))
            else:
                part = ref.at[pl.ds(self.y * TP, TP), pl.ds(low, count)]
                self.flying.append(self.remote(part, part, "y"))


def flip_index(value, bits):
    low = lax.rem(value, 2)
    high = lax.div(value, 2)
    if bits & 1:
        low = 1 - low
    if bits & 2:
        high = 1 - high
    return high * 2 + low


def mixed_index(static, dynamic):
    return flip_index(dynamic, static)


def swap_index(value):
    return lax.rem(value, 2) * 2 + lax.div(value, 2)


def sems(remote, local):
    return [
        pltpu.SemaphoreType.DMA((max(remote, 1),)),
        pltpu.SemaphoreType.DMA((max(remote, 1),)),
        pltpu.SemaphoreType.DMA((max(local, 1),)),
    ]


def start_kernel(
    qkv_pack, gu_pack, out_own, down_own, gain_tile, cot,
    g_qkv0, g_qkv1, g_gu0, g_gu1, g_out0, g_out1, g_down0, g_down1, g_gain, branch,
    spread_buf, send_sems, recv_sems, local_sems,
):
    net = Net(send_sems, recv_sems, local_sems)
    shard = qkv_pack.shape[2]
    bring = net.local(cot, spread_buf.at[0])
    net.greet(("core", "x", "both", "y", "z1", "z2", "z3"))
    mine = pl.ds(pl.multiple_of(net.q * shard, shard), shard)
    r = net.r

    def columns(pack, layer, target):
        copies = []
        for name, bits in (("both", 3), ("x", 2), ("core", 1)):
            copies.append(
                net.remote(pack.at[layer, flip_index(net.q, bits)], target.at[r, mine], name)
            )
        copies.append(net.local(pack.at[layer, net.q], target.at[r, mine]))
        return copies

    first = columns(qkv_pack, 0, g_qkv0)
    for name in ("both", "x", "core"):
        first.append(net.remote(gain_tile, g_gain.at[r, net.q], name))
    first.append(net.local(gain_tile, g_gain.at[r, net.q]))
    placed = [
        net.local(out_own.at[0], g_out0.at[r]),
        net.local(out_own.at[1], g_out1.at[r]),
        net.local(down_own.at[0], g_down0.at[r]),
        net.local(down_own.at[1], g_down1.at[r]),
    ]
    out_first = [net.remote(out_own.at[0], g_out0.at[r], f"z{k}") for k in (2, 3, 1)]
    for copy in first:
        copy.wait()
    net.flying = []
    net.advance((("z", g_qkv0, 0, g_qkv0.shape[1]), ("z", g_gain, 0, TP)))
    second = columns(gu_pack, 0, g_gu0) + columns(qkv_pack, 1, g_qkv1) + columns(gu_pack, 1, g_gu1)
    bring.wait()
    over_x = net.remote(spread_buf.at[0], spread_buf.at[1], "x")
    over_core = net.remote(spread_buf.at[0], spread_buf.at[2], "core")
    for copy in out_first + placed:
        copy.wait()
    net.advance(
        (
            ("y", g_qkv0, 0, g_qkv0.shape[1]),
            ("y", g_gain, 0, TP),
            ("y", g_out0, 0, g_out0.shape[1]),
            ("z", g_down0, 0, g_down0.shape[1]),
        )
    )
    over_x.wait()
    forward = net.remote(spread_buf.at[1], spread_buf.at[3], "core")
    over_core.wait()
    forward.wait()
    net.keep(spread_buf, branch)
    for copy in second:
        copy.wait()
    net.finish()


def start_exchange(qkv_pack, gu_pack, out_own, down_own, gain_tile, cot):
    bf = jnp.bfloat16
    block, depth = cot.shape
    shard, qkv_width = qkv_pack.shape[2:]
    units = gu_pack.shape[3]
    outs = []
    for rows, width in (
        (TP * shard, qkv_width),
        (TP * shard, units),
        (shard, depth),
        (down_own.shape[1], depth),
    ):
        outs += [jax.ShapeDtypeStruct((2 * TP, rows, width), bf)] * 2
    outs.append(jax.ShapeDtypeStruct((2 * TP, TP) + gain_tile.shape, jnp.float32))
    outs.append(jax.ShapeDtypeStruct((TP, block, depth), bf))
    return pl.pallas_call(
        start_kernel,
        out_shape=outs,
        in_specs=[ANYWHERE] * 6,
        out_specs=[ANYWHERE] * 10,
        scratch_shapes=[pltpu.VMEM((TP, block, depth), bf)] + sems(40, 24),
        compiler_params=pltpu.CompilerParams(
            collective_id=1, has_side_effects=True, vmem_limit_bytes=VMEM_LIMIT
        ),
        cost_estimate=pl.CostEstimate(flops=0, bytes_accessed=300 * 2**20, transcendentals=0),
    )(qkv_pack, gu_pack, out_own, down_own, gain_tile, cot)


def attend_rows(net, block):
    base = swap_index(net.q)
    return [pl.ds(pl.multiple_of(mixed_index(b, base) * block, block), block) for b in range(TP)]


def attend_forward_block(net, qkv_ref, row_seg_ref, col_seg_ref, mixed_ref, lse_ref):
    total, width = qkv_ref.shape
    block = total // TP
    q_heads = width // (2 * HEAD_DIM)
    kv_heads = q_heads // 2
    factor = 1.0 / math.sqrt(HEAD_DIM)
    key_at = q_heads * HEAD_DIM
    value_at = key_at + kv_heads * HEAD_DIM
    places = attend_rows(net, block)
    nt = (((1,), (1,)), ((), ()))
    for i in range(TP):
        row_seg = row_seg_ref[i]
        masks = [block_mask(row_seg, col_seg_ref[j], i == j, block) for j in range(i + 1)]
        for h in range(q_heads):
            kv = h // 2
            query = qkv_ref[places[i], h * HEAD_DIM : (h + 1) * HEAD_DIM]
            scores = []
            for j in range(i + 1):
                key = qkv_ref[places[j], key_at + kv * HEAD_DIM : key_at + (kv + 1) * HEAD_DIM]
                s = lax.dot_general(query, key, nt, preferred_element_type=jnp.float32) * factor
                scores.append(jnp.where(masks[j], s, NEGATIVE))
            peak = scores[0].max(axis=1, keepdims=True)
            for s in scores[1:]:
                peak = jnp.maximum(peak, s.max(axis=1, keepdims=True))
            total_e = jnp.zeros((block, 1), jnp.float32)
            mixed = jnp.zeros((block, HEAD_DIM), jnp.float32)
            for j in range(i + 1):
                e = jnp.exp(scores[j] - peak)
                total_e = total_e + e.sum(axis=1, keepdims=True)
                value = qkv_ref[places[j], value_at + kv * HEAD_DIM : value_at + (kv + 1) * HEAD_DIM]
                mixed = mixed + jnp.dot(
                    e.astype(jnp.bfloat16), value, preferred_element_type=jnp.float32
                )
            mixed_ref[places[i], h * HEAD_DIM : (h + 1) * HEAD_DIM] = (mixed / total_e).astype(
                jnp.bfloat16
            )
            lse_ref[i, :, h : h + 1] = peak + jnp.log(total_e)


def normalize(values, gain_row):
    scale = lax.rsqrt(jnp.mean(values * values, axis=-1, keepdims=True) + EPSILON)
    return (values * scale * gain_row).astype(jnp.bfloat16)


def spread_begin(net, buf):
    return (net.remote(buf.at[0], buf.at[1], "x"), net.remote(buf.at[0], buf.at[2], "core"))


def spread_each(net, buf, begun, work):
    over_x, over_core = begun
    work(0)
    over_core.wait()
    work(2)
    over_x.wait()
    forward = net.remote(buf.at[1], buf.at[3], "core")
    work(1)
    forward.wait()
    work(3)


def collect(net, part, far_out, far_in, pass_out, pass_in):
    low = lambda v: v.astype(jnp.bfloat16)
    far_out[0] = low(part(3))
    first = net.remote(far_out.at[0], far_in.at[0], "core")
    near = part(1)
    first.wait()
    pass_out[...] = low(near + far_in[0].astype(jnp.float32))
    passed = net.remote(pass_out, pass_in, "x")
    far_out[1] = low(part(2))
    second = net.remote(far_out.at[1], far_in.at[1], "core")
    own = part(0)
    second.wait()
    own = own + far_in[1].astype(jnp.float32)
    passed.wait()
    return own + pass_in[...].astype(jnp.float32)


def forward_kernel(programs, n_moving, *refs):
    x_own, gain_a, gain_f, cos_ref, sin_ref, row_seg, col_seg = refs[:7]
    refs = refs[7 + n_moving :]
    moving, refs = refs[:n_moving], refs[n_moving:]
    (x_next, middle_ref, lse_ref, rows_out, qkv_out, mixed_out, ffn_rows_out, gate_out, up_out, act_out) = refs[:10]
    (rows, ffn_rows, w_qkv, w_o, w_gu, w_d, qkv, mixed, gate, up, act,
     far_out, far_in, pass_out, pass_in, send_sems, recv_sems, local_sems) = refs[10:]
    net = Net(send_sems, recv_sems, local_sems)
    steps = [[(kind, moving[n], low, count) for kind, n, low, count in step] for step in programs]
    block, depth = x_own.shape
    load_qkv = net.local(moving[0], w_qkv)
    load_o = net.local(moving[1], w_o)
    net.greet(("core", "x", "y", "z1", "z2", "z3"))
    net.advance(steps[0])
    rows[0] = normalize(x_own[...], gain_a[...])
    begun = spread_begin(net, rows)
    load_qkv.wait()

    def project(s):
        raw = jnp.dot(
            rows[s], w_qkv[...].reshape(depth, -1), preferred_element_type=jnp.float32
        )
        at = slice(s * block, (s + 1) * block)
        turned = raw * cos_ref[at, :] + head_partner(raw, HEAD_DIM // 2) * sin_ref[at, :]
        qkv[at, :] = turned.astype(jnp.bfloat16)

    spread_each(net, rows, begun, project)
    net.keep(rows, rows_out)
    net.keep(qkv, qkv_out)
    net.advance(steps[1])
    load_d = net.local(moving[3], w_d)
    attend_forward_block(net, qkv, row_seg, col_seg, mixed, lse_ref)
    net.keep(mixed, mixed_out)
    load_o.wait()

    def out_part(s):
        return jnp.dot(
            mixed[s * block : (s + 1) * block, :],
            w_o[...].reshape(-1, depth),
            preferred_element_type=jnp.float32,
        )

    middle = x_own[...] + collect(
        net, out_part, far_out, far_in.at[0], pass_out, pass_in.at[0]
    )
    middle_ref[...] = middle
    net.advance(steps[2])
    ffn_rows[0] = normalize(middle, gain_f[...])
    begun = spread_begin(net, ffn_rows)
    net.advance(steps[3])
    load_gu = net.local(moving[2], w_gu)
    load_d.wait()
    load_gu.wait()
    units = act.shape[2]

    def expand(s):
        value = ffn_rows[s]
        gating = jnp.dot(
            value, w_gu[:, :, :units].reshape(depth, units), preferred_element_type=jnp.float32
        )
        upward = jnp.dot(
            value, w_gu[:, :, units:].reshape(depth, units), preferred_element_type=jnp.float32
        )
        gate[s] = gating.astype(jnp.bfloat16)
        up[s] = upward.astype(jnp.bfloat16)
        act[s] = (gating * jax.nn.sigmoid(gating) * upward).astype(jnp.bfloat16)

    spread_each(net, ffn_rows, begun, expand)
    net.keep(ffn_rows, ffn_rows_out)
    net.keep(gate, gate_out)
    net.keep(up, up_out)
    net.keep(act, act_out)

    def down_part(s):
        return jnp.dot(act[s], w_d[...].reshape(-1, depth), preferred_element_type=jnp.float32)

    x_next[...] = middle_ref[...] + collect(
        net, down_part, far_out, far_in.at[1], pass_out, pass_in.at[1]
    )
    net.finish()


def forward_layer(programs, cid, x_own, gain_a, gain_f, cosine, sine, row_seg, col_seg, moving):
    bf, f32 = jnp.bfloat16, jnp.float32
    block, depth = x_own.shape
    total, qkv_width = cosine.shape
    units = moving[2].shape[2] // 2
    q_heads = qkv_width // (2 * HEAD_DIM)
    shape = jax.ShapeDtypeStruct
    outs = [shape(m.shape, m.dtype) for m in moving] + [
        shape((block, depth), f32),
        shape((block, depth), f32),
        shape((TP, block, q_heads), f32),
        shape((TP, block, depth), bf),
        shape((total, qkv_width), bf),
        shape((total, qkv_width // 2), bf),
        shape((TP, block, depth), bf),
        shape((TP, block, units), bf),
        shape((TP, block, units), bf),
        shape((TP, block, units), bf),
    ]
    n = len(moving)
    scratch = [
        pltpu.VMEM((TP, block, depth), bf),
        pltpu.VMEM((TP, block, depth), bf),
        pltpu.VMEM(moving[0].shape, bf),
        pltpu.VMEM(moving[1].shape, bf),
        pltpu.VMEM(moving[2].shape, bf),
        pltpu.VMEM(moving[3].shape, bf),
        pltpu.VMEM((total, qkv_width), bf),
        pltpu.VMEM((total, qkv_width // 2), bf),
        pltpu.VMEM((TP, block, units), bf),
        pltpu.VMEM((TP, block, units), bf),
        pltpu.VMEM((TP, block, units), bf),
        pltpu.VMEM((2, block, depth), bf),
        pltpu.VMEM((2, 2, block, depth), bf),
        pltpu.VMEM((block, depth), bf),
        pltpu.VMEM((2, block, depth), bf),
    ] + sems(64, 24)
    return pl.pallas_call(
        functools.partial(forward_kernel, programs, n),
        out_shape=outs,
        in_specs=[IN_VMEM] * 7 + [ANYWHERE] * n,
        out_specs=[ANYWHERE] * n + [IN_VMEM] * 3 + [ANYWHERE] * 7,
        scratch_shapes=scratch,
        input_output_aliases={7 + i: i for i in range(n)},
        compiler_params=pltpu.CompilerParams(
            collective_id=cid, has_side_effects=True, vmem_limit_bytes=VMEM_LIMIT
        ),
        cost_estimate=pl.CostEstimate(
            flops=16 * 10**9, bytes_accessed=400 * 2**20, transcendentals=10**7
        ),
    )(x_own, gain_a, gain_f, cosine, sine, row_seg, col_seg, *moving)


def column_pack(weights):
    parts = []
    for weight in weights:
        layers, rows, width = weight.shape
        view = weight.reshape(layers, rows, 2, TP, width // (2 * TP))
        parts.append(view.transpose(0, 3, 1, 2, 4).reshape(layers, TP, rows, width // TP))
    return jnp.concatenate(parts, axis=3)


def fast_device(
    tokens, gain_attn, w_query, w_key, w_value, w_out, gain_ffn, w_gate, w_up, w_down, lengths, cotangent
):
    fab = Fabric()
    block, depth = tokens.shape
    group_tok = block * fab.z_size
    shard = w_query.shape[1]
    nat = jnp.arange(depth, dtype=jnp.int32)
    nat_p = (
        (nat // (depth // 2)) * (depth // 2)
        + (nat // shard % fab.z_size) * (TP * shard)
        + (nat // (shard * fab.z_size) % TP) * shard
        + nat % shard
    )
    to_inner = (nat_p[:, None] == nat[None, :]).astype(jnp.bfloat16)
    inward = lambda v: jnp.dot(v, to_inner, preferred_element_type=jnp.float32).astype(jnp.bfloat16)
    outward = lambda v: lax.dot_general(
        v, to_inner, (((1,), (1,)), ((), ())), preferred_element_type=jnp.float32
    )

    out_in = inward(w_out.reshape(-1, depth)).reshape(w_out.shape)
    down_in = inward(w_down.reshape(-1, depth)).reshape(w_down.shape)
    gain_tile = jnp.pad(
        jnp.concatenate([gain_attn, gain_ffn], axis=0).astype(jnp.float32), ((0, 4), (0, 128 - shard))
    )
    hidden = inward(fab.regroup(tokens)).astype(jnp.float32)
    cot = inward(fab.regroup(cotangent))
    lengths_row = fab.regroup(lengths)[0]
    gains = None

    segment, position = layout(lengths_row, group_tok)
    base = halves_swapped(fab.q)
    slots = (jnp.arange(TP) // 2 ^ base // 2) * 2 + (jnp.arange(TP) % 2 ^ base % 2)
    seg_blocks = segment.reshape(TP, block)
    row_seg = seg_blocks[:, :, None]
    col_seg = seg_blocks[:, None, :]
    pos_rows = jnp.take(position.reshape(TP, block), slots, axis=0).reshape(-1)
    halfway = HEAD_DIM // 2
    frequency = ROPE_BASE ** (-jnp.arange(halfway, dtype=jnp.float32) * 2.0 / HEAD_DIM)
    angles = pos_rows.astype(jnp.float32)[:, None] * frequency[None, :]
    cos_h, sin_h = jnp.cos(angles), jnp.sin(angles)
    heads = w_query.shape[2] // HEAD_DIM // TP
    kv_heads = w_key.shape[2] // HEAD_DIM // TP
    cosine = jnp.concatenate(
        [cos_h, cos_h] * (heads + kv_heads)
        + [jnp.ones((group_tok, kv_heads * HEAD_DIM), jnp.float32)],
        axis=1,
    )
    sine = jnp.concatenate(
        [-sin_h, sin_h] * (heads + kv_heads)
        + [jnp.zeros((group_tok, kv_heads * HEAD_DIM), jnp.float32)],
        axis=1,
    )

    (g_qkv0, g_qkv1, g_gu0, g_gu1, g_out0, g_out1, g_down0, g_down1, g_gain, branch) = start_exchange(
        column_pack((w_query, w_key, w_value)), column_pack((w_gate, w_up)), out_in, down_in, gain_tile, cot
    )
    gains = jnp.transpose(g_gain[:, :, :4, :shard], (2, 0, 1, 3)).reshape(4, 1, depth)
    cols, drows, srows = TP * shard, g_down0.shape[1], shard
    half = cols // 2
    programs0 = (
        (("y", 3, 0, drows), ("z", 2, 0, half)),
        (("y", 2, 0, half), ("z", 2, half, half)),
        (("y", 2, half, half), ("z", 4, 0, cols), ("z", 5, 0, srows)),
        (("y", 4, 0, cols), ("y", 5, 0, srows), ("z", 7, 0, drows)),
    )
    programs1 = (
        (("y", 3, 0, drows), ("z", 2, 0, half)),
        (("y", 2, 0, half), ("z", 2, half, half)),
        (("y", 2, half, half),),
        (),
    )
    res = forward_layer(
        programs0, 2, hidden, gains[0], gains[2], cosine, sine, row_seg, col_seg,
        (g_qkv0, g_out0, g_gu0, g_down0, g_qkv1, g_out1, g_gu1, g_down1),
    )
    weights0, moving1, acts0 = res[:4], res[4:8], res[8:]
    res = forward_layer(
        programs1, 3, acts0[0], gains[1], gains[3], cosine, sine, row_seg, col_seg, moving1
    )
    weights1, acts1 = res[:4], res[4:]
    outs = [
        fab.regroup(outward(a[0].astype(jnp.bfloat16)).astype(jnp.bfloat16)) for a in (acts0, acts1)
    ]
    saved = []
    for hid, weights, acts in ((hidden, weights0, acts0), (acts0[0], weights1, acts1)):
        (x_next, middle, lse, normed, qkv, mixed, normed_ffn, gating, upward, activated) = acts
        flat = lambda v: v.reshape(-1, v.shape[-1])
        w_qkv, w_o, w_gu, w_d = (flat(w) for w in weights)
        units = w_gu.shape[1] // 2
        saved.append(
            (hid, flat(normed), qkv, mixed, lse, middle, flat(normed_ffn), flat(gating), flat(upward),
             flat(activated), w_qkv, w_o, w_gu[:, :units], w_gu[:, units:], w_d)
        )
    gains = gains[:, 0]

    upstream = cot.astype(jnp.float32)
    grads = [None, None]
    gain_grads = [None] * 4
    for layer in (1, 0):
        (hid, normed, qkv, mixed, lse, middle, normed_ffn, gating, upward, activated,
         w_qkv, w_o, w_g, w_u, w_d) = saved[layer]
        gain_a, gain_f = gains[layer], gains[2 + layer]
        branch = branch.reshape(-1, depth) if layer == 1 else fab.spread(upstream.astype(jnp.bfloat16))
        grad_act = matmul(branch, w_d.T)
        gating = gating.astype(jnp.float32)
        upward = upward.astype(jnp.float32)
        sig = jax.nn.sigmoid(gating)
        grad_gate = (grad_act * upward * sig * (1.0 + gating * (1.0 - sig))).astype(jnp.bfloat16)
        grad_up = (grad_act * gating * sig).astype(jnp.bfloat16)
        both = jnp.concatenate([grad_gate, grad_up], axis=1)
        down_grad = reduce_blocks(fab, activated, branch, None)
        gu_grad = reduce_blocks(fab, normed_ffn, both, None)
        w_gu = jnp.concatenate([w_g, w_u], axis=1)
        grad_normed_ffn = fab.collect(both, w_gu.T)
        part, gain_grads[2 + layer] = norm_back(middle, gain_f, grad_normed_ffn)
        grad_middle = upstream + part
        proj = fab.spread(grad_middle.astype(jnp.bfloat16))
        grad_mixed = matmul(proj, w_o.T).astype(jnp.bfloat16)
        out_grad = reduce_blocks(fab, mixed, proj, None)
        grad_qkv = attend_bwd(slots, qkv, grad_mixed, mixed, lse, row_seg, col_seg, cosine, sine)
        qkv_grad = reduce_blocks(fab, normed, grad_qkv, None)
        grad_normed = fab.collect(grad_qkv, w_qkv.T)
        part, gain_grads[layer] = norm_back(hid, gain_a, grad_normed)
        upstream = grad_middle + part
        gu_parts = return_columns(fab, gu_grad)
        units = gu_parts[0].shape[1] // 2
        qkv_parts = return_columns(fab, qkv_grad)
        qw, kw = heads * HEAD_DIM, kv_heads * HEAD_DIM
        grads[layer] = (
            join_columns([p[:, :qw] for p in qkv_parts]),
            join_columns([p[:, qw : qw + kw] for p in qkv_parts]),
            join_columns([p[:, qw + kw :] for p in qkv_parts]),
            outward(out_grad.astype(jnp.bfloat16)),
            join_columns([p[:, :units] for p in gu_parts]),
            join_columns([p[:, units:] for p in gu_parts]),
            outward(down_grad.astype(jnp.bfloat16)),
        )
    input_grad = fab.regroup(outward(upstream.astype(jnp.bfloat16)).astype(jnp.bfloat16)).astype(
        jnp.float32
    )
    gain_sums = lax.psum(jnp.stack(gain_grads), ("dp", "fsdp"))
    own_gain = lax.dynamic_slice_in_dim(
        gain_sums, (fab.y * fab.z_size + fab.z) * (TP * shard) + fab.q * shard, shard, 1
    )
    pair = lambda n: jnp.stack([grads[0][n], grads[1][n]])
    return (
        jnp.stack(outs),
        input_grad,
        own_gain[:2],
        pair(0),
        pair(1),
        pair(2),
        pair(3),
        own_gain[2:],
        pair(4),
        pair(5),
        pair(6),
    )


def per_device(*arrays):
    tokens, w_query, w_key, w_gate = arrays[0], arrays[2], arrays[3], arrays[7]
    dp_size, z_size = lax.axis_size("dp"), lax.axis_size("fsdp")
    suits = (
        dp_size == 2 * TP
        and z_size == TP
        and w_key.shape[2] // HEAD_DIM == dp_size
        and w_query.shape[2] == 2 * w_key.shape[2]
        and tokens.shape[0] % 128 == 0
        and w_query.shape[1] % 16 == 0
        and w_gate.shape[2] % (TP * dp_size * 128) == 0
    )
    return (fast_device if suits else general_device)(*arrays)


def solution(mesh):
    placed = (
        P(("dp", "fsdp"), None),
        P(None, ("dp", "fsdp")),
        P(None, ("dp", "fsdp"), None),
        P(None, ("dp", "fsdp"), None),
        P(None, ("dp", "fsdp"), None),
        P(None, ("dp", "fsdp"), None),
        P(None, ("dp", "fsdp")),
        P(None, ("dp", "fsdp"), None),
        P(None, ("dp", "fsdp"), None),
        P(None, ("dp", "fsdp"), None),
        P("dp", None),
        P(("dp", "fsdp"), None),
    )
    return jax.shard_map(
        per_device,
        mesh=mesh,
        in_specs=placed,
        out_specs=(
            P(None, ("dp", "fsdp"), None),
            P(("dp", "fsdp"), None),
            P(None, ("dp", "fsdp")),
            P(None, ("dp", "fsdp"), None),
            P(None, ("dp", "fsdp"), None),
            P(None, ("dp", "fsdp"), None),
            P(None, ("dp", "fsdp"), None),
            P(None, ("dp", "fsdp")),
            P(None, ("dp", "fsdp"), None),
            P(None, ("dp", "fsdp"), None),
            P(None, ("dp", "fsdp"), None),
        ),
        check_vma=False,
    )
```

```python
import functools
import math

import jax
import jax.numpy as jnp
from jax import lax
from jax.experimental import pallas as pl
from jax.experimental.pallas import tpu as pltpu
from jax.sharding import PartitionSpec as P

HEAD_DIM = 96


EPSILON = 1e-05
ROPE_BASE = 100000.0
NEGATIVE = -1e30


def layout(lengths_row, group_tok):
    places = jnp.arange(group_tok, dtype=jnp.int32)
    prompt_len = group_tok - jnp.sum(lengths_row)
    starts = prompt_len + jnp.cumsum(lengths_row) - lengths_row
    inside = places[:, None] >= starts[None, :]
    segment = jnp.sum(inside.astype(jnp.int32), axis=1)
    begins = jnp.max(jnp.where(inside, starts[None, :], 0), axis=1)
    position = jnp.where(segment > 0, places - begins + prompt_len, places)
    return (segment, position)


def rotate(values, position, direction):
    row_count = values.shape[0]
    shaped = values.reshape(row_count, -1, HEAD_DIM)
    halfway = HEAD_DIM // 2
    frequency = ROPE_BASE ** (-jnp.arange(halfway, dtype=jnp.float32) * 2.0 / HEAD_DIM)
    angles = position.astype(jnp.float32)[:, None] * frequency[None, :]
    cosine = jnp.cos(angles)[:, None, :]
    sine_part = direction * jnp.sin(angles)[:, None, :]
    first_half = shaped[..., :halfway]
    second_half = shaped[..., halfway:]
    turned = jnp.concatenate(
        [
            first_half * cosine - second_half * sine_part,
            second_half * cosine + first_half * sine_part,
        ],
        axis=-1,
    )
    return turned.reshape(values.shape)


def norm_apply(values, gain_vec):
    inv_rms = lax.rsqrt(jnp.mean(values * values, axis=-1, keepdims=True) + EPSILON)
    return values * inv_rms * gain_vec


def norm_back(values, gain_vec, incoming):
    inv_rms = lax.rsqrt(jnp.mean(values * values, axis=-1, keepdims=True) + EPSILON)
    weighted = incoming * gain_vec
    inner_sum = jnp.mean(weighted * values, axis=-1, keepdims=True)
    grad_values = inv_rms * weighted - values * inv_rms * inv_rms * inv_rms * inner_sum
    grad_gain = jnp.sum(incoming * values * inv_rms, axis=0)
    return (grad_values, grad_gain)


def matmul(left, right):
    return jnp.dot(left, right, preferred_element_type=jnp.float32)


def visibility(seg_rows, row_places, segment, places):
    same_seq = (seg_rows[:, None] == segment[None, :]) & (places[None, :] <= row_places[:, None])
    prompt_seen = (segment[None, :] == 0) & (seg_rows[:, None] > 0)
    return same_seq | prompt_seen


def head_slices(query_b, keys_all, head_index):
    row_count = query_b.shape[0]
    kv_width = keys_all.shape[1] // 2
    sharing = query_b.shape[1] // kv_width
    query_part = lax.dynamic_slice_in_dim(
        query_b, head_index * sharing * HEAD_DIM, sharing * HEAD_DIM, 1
    ).reshape(row_count, sharing, HEAD_DIM)
    key_part = lax.dynamic_slice_in_dim(keys_all, head_index * HEAD_DIM, HEAD_DIM, 1)
    value_part = lax.dynamic_slice_in_dim(keys_all, kv_width + head_index * HEAD_DIM, HEAD_DIM, 1)
    return (query_part, key_part, value_part)


def attend_forward(query_b, keys_all, visible):
    row_count = query_b.shape[0]
    kv_heads = keys_all.shape[1] // 2 // HEAD_DIM
    factor = 1.0 / math.sqrt(HEAD_DIM)

    def per_head(head_index):
        query_part, key_part, value_part = head_slices(query_b, keys_all, head_index)
        scores = (
            jnp.einsum("tgd,kd->gtk", query_part, key_part, preferred_element_type=jnp.float32)
            * factor
        )
        masked = jnp.where(visible[None], scores, NEGATIVE)
        peak_score = jnp.max(masked, axis=-1)
        exponent = jnp.where(visible[None], jnp.exp(masked - peak_score[..., None]), 0.0)
        totals = jnp.sum(exponent, axis=-1)
        probability = (exponent / totals[..., None]).astype(jnp.bfloat16)
        mixed_heads = jnp.einsum(
            "gtk,kd->tgd", probability, value_part, preferred_element_type=jnp.float32
        )
        return (mixed_heads.reshape(row_count, -1), peak_score, totals)

    mixed_heads, peak_score, totals = lax.map(per_head, jnp.arange(kv_heads, dtype=jnp.int32))
    return (jnp.transpose(mixed_heads, (1, 0, 2)).reshape(row_count, -1), peak_score, totals)


def attend_backward(query_b, keys_all, visible, peak_score, totals, grad_mixed):
    row_count = query_b.shape[0]
    kv_width = keys_all.shape[1] // 2
    kv_heads = kv_width // HEAD_DIM
    sharing = query_b.shape[1] // kv_width
    factor = 1.0 / math.sqrt(HEAD_DIM)

    def per_head(pieces):
        head_index, peak_head, total_head = pieces
        query_part, key_part, value_part = head_slices(query_b, keys_all, head_index)
        grad_part = lax.dynamic_slice_in_dim(
            grad_mixed, head_index * sharing * HEAD_DIM, sharing * HEAD_DIM, 1
        ).reshape(row_count, sharing, HEAD_DIM)
        scores = (
            jnp.einsum("tgd,kd->gtk", query_part, key_part, preferred_element_type=jnp.float32)
            * factor
        )
        masked = jnp.where(visible[None], scores, NEGATIVE)
        exponent = jnp.where(visible[None], jnp.exp(masked - peak_head[..., None]), 0.0)
        probability = exponent / total_head[..., None]
        prob_low = probability.astype(jnp.bfloat16)
        grad_probs = jnp.einsum(
            "tgd,kd->gtk", grad_part, value_part, preferred_element_type=jnp.float32
        )
        inner_sum = jnp.sum(probability * grad_probs, axis=-1, keepdims=True)
        grad_scores = (probability * (grad_probs - inner_sum)).astype(jnp.bfloat16)
        grad_query = (
            jnp.einsum("gtk,kd->tgd", grad_scores, key_part, preferred_element_type=jnp.float32)
            * factor
        )
        grad_key = (
            jnp.einsum("gtk,tgd->kd", grad_scores, query_part, preferred_element_type=jnp.float32)
            * factor
        )
        grad_value = jnp.einsum(
            "gtk,tgd->kd", prob_low, grad_part, preferred_element_type=jnp.float32
        )
        return (grad_query.reshape(row_count, -1), grad_key, grad_value)

    grad_query, grad_key, grad_value = lax.map(
        per_head, (jnp.arange(kv_heads, dtype=jnp.int32), peak_score, totals)
    )
    group_rows = keys_all.shape[0]
    key_terms = jnp.concatenate(
        [
            jnp.transpose(grad_key, (1, 0, 2)).reshape(group_rows, -1),
            jnp.transpose(grad_value, (1, 0, 2)).reshape(group_rows, -1),
        ],
        axis=1,
    )
    return (jnp.transpose(grad_query, (1, 0, 2)).reshape(row_count, -1), key_terms)


def fetch_attention(layer_index, gain_attn, w_query, w_key, w_value, w_out):
    return (
        lax.all_gather(gain_attn[layer_index], ("dp", "fsdp"), axis=0, tiled=True),
        lax.all_gather(w_query[layer_index], ("dp", "fsdp"), axis=0, tiled=True),
        lax.all_gather(w_key[layer_index], ("dp", "fsdp"), axis=0, tiled=True),
        lax.all_gather(w_value[layer_index], ("dp", "fsdp"), axis=0, tiled=True),
        lax.all_gather(w_out[layer_index], ("dp", "fsdp"), axis=0, tiled=True),
    )


def fetch_ffn(layer_index, gain_ffn, w_gate, w_up, w_down):
    return (
        lax.all_gather(gain_ffn[layer_index], ("dp", "fsdp"), axis=0, tiled=True),
        lax.all_gather(w_gate[layer_index], ("dp", "fsdp"), axis=0, tiled=True),
        lax.all_gather(w_up[layer_index], ("dp", "fsdp"), axis=0, tiled=True),
        lax.all_gather(w_down[layer_index], ("dp", "fsdp"), axis=0, tiled=True),
    )


def share_keys(stacked):
    return lax.all_gather(stacked, "fsdp", axis=0, tiled=True)


def layer_forward(hidden, attn_weights, ffn_weights, pos_rows, visible):
    gain_a, query_w, key_w, value_w, out_w = attn_weights
    gain_f, gate_w, upper_w, down_w = ffn_weights
    normed = norm_apply(hidden, gain_a.astype(jnp.float32)).astype(jnp.bfloat16)
    query_b = rotate(matmul(normed, query_w), pos_rows, 1.0).astype(jnp.bfloat16)
    key_b = rotate(matmul(normed, key_w), pos_rows, 1.0).astype(jnp.bfloat16)
    value_b = matmul(normed, value_w).astype(jnp.bfloat16)
    stacked = jnp.concatenate([key_b, value_b], axis=1)
    keys_all = share_keys(stacked)
    mixed_heads, peak_score, totals = attend_forward(query_b, keys_all, visible)
    mixed_b = mixed_heads.astype(jnp.bfloat16)
    middle = hidden + matmul(mixed_b, out_w)
    normed_ffn = norm_apply(middle, gain_f.astype(jnp.float32)).astype(jnp.bfloat16)
    gating = matmul(normed_ffn, gate_w)
    upward = matmul(normed_ffn, upper_w)
    activated = (jax.nn.silu(gating) * upward).astype(jnp.bfloat16)
    result = middle + matmul(activated, down_w)
    saved = (
        hidden,
        normed,
        query_b,
        stacked,
        keys_all,
        peak_score,
        totals,
        mixed_b,
        middle,
        normed_ffn,
        gating,
        upward,
        activated,
    )
    return (result, saved)


def layer_backward(upstream, saved, attn_weights, ffn_weights, keys_all, pos_rows, visible):
    (
        hidden,
        normed,
        query_b,
        stacked,
        unused_keys,
        peak_score,
        totals,
        mixed_b,
        middle,
        normed_ffn,
        gating,
        upward,
        activated,
    ) = saved
    gain_a, query_w, key_w, value_w, out_w = attn_weights
    gain_f, gate_w, upper_w, down_w = ffn_weights
    grad_branch = upstream.astype(jnp.bfloat16)
    grad_down_w = matmul(activated.T, grad_branch)
    grad_act = matmul(grad_branch, down_w.T)
    sigmoid_g = jax.nn.sigmoid(gating)
    grad_gate = (grad_act * upward * sigmoid_g * (1.0 + gating * (1.0 - sigmoid_g))).astype(
        jnp.bfloat16
    )
    grad_up = (grad_act * gating * sigmoid_g).astype(jnp.bfloat16)
    grad_gate_w = matmul(normed_ffn.T, grad_gate)
    grad_up_w = matmul(normed_ffn.T, grad_up)
    grad_normed_ffn = matmul(grad_gate, gate_w.T) + matmul(grad_up, upper_w.T)
    grad_middle_part, grad_gain_f = norm_back(middle, gain_f.astype(jnp.float32), grad_normed_ffn)
    ffn_blocks = (
        lax.psum_scatter(
            grad_gain_f.astype(jnp.bfloat16), "dp", scatter_dimension=0, tiled=True
        ).astype(jnp.float32),
        lax.psum_scatter(
            grad_gate_w.astype(jnp.bfloat16), "dp", scatter_dimension=0, tiled=True
        ).astype(jnp.float32),
        lax.psum_scatter(
            grad_up_w.astype(jnp.bfloat16), "dp", scatter_dimension=0, tiled=True
        ).astype(jnp.float32),
        lax.psum_scatter(
            grad_down_w.astype(jnp.bfloat16), "dp", scatter_dimension=0, tiled=True
        ).astype(jnp.float32),
    )
    ffn_grads = (
        lax.psum_scatter(
            ffn_blocks[0].astype(jnp.bfloat16), "fsdp", scatter_dimension=0, tiled=True
        ).astype(jnp.float32),
        lax.psum_scatter(
            ffn_blocks[1].astype(jnp.bfloat16), "fsdp", scatter_dimension=0, tiled=True
        ).astype(jnp.float32),
        lax.psum_scatter(
            ffn_blocks[2].astype(jnp.bfloat16), "fsdp", scatter_dimension=0, tiled=True
        ).astype(jnp.float32),
        lax.psum_scatter(
            ffn_blocks[3].astype(jnp.bfloat16), "fsdp", scatter_dimension=0, tiled=True
        ).astype(jnp.float32),
    )
    grad_middle = upstream + grad_middle_part
    grad_proj = grad_middle.astype(jnp.bfloat16)
    grad_out_w = matmul(mixed_b.T, grad_proj)
    grad_mixed = matmul(grad_proj, out_w.T).astype(jnp.bfloat16)
    grad_query_rot, key_terms = attend_backward(
        query_b, keys_all, visible, peak_score, totals, grad_mixed
    )
    key_grads = lax.psum_scatter(
        key_terms.astype(jnp.bfloat16), "fsdp", scatter_dimension=0, tiled=True
    ).astype(jnp.float32)
    kv_width = key_terms.shape[1] // 2
    grad_query = rotate(grad_query_rot, pos_rows, -1.0).astype(jnp.bfloat16)
    grad_key = rotate(key_grads[:, :kv_width], pos_rows, -1.0).astype(jnp.bfloat16)
    grad_value = key_grads[:, kv_width:].astype(jnp.bfloat16)
    grad_normed = (
        matmul(grad_query, query_w.T) + matmul(grad_key, key_w.T) + matmul(grad_value, value_w.T)
    )
    grad_query_w = matmul(normed.T, grad_query)
    grad_key_w = matmul(normed.T, grad_key)
    grad_value_w = matmul(normed.T, grad_value)
    grad_hidden_part, grad_gain_a = norm_back(hidden, gain_a.astype(jnp.float32), grad_normed)
    attn_blocks = (
        lax.psum_scatter(
            grad_gain_a.astype(jnp.bfloat16), "dp", scatter_dimension=0, tiled=True
        ).astype(jnp.float32),
        lax.psum_scatter(
            grad_query_w.astype(jnp.bfloat16), "dp", scatter_dimension=0, tiled=True
        ).astype(jnp.float32),
        lax.psum_scatter(
            grad_key_w.astype(jnp.bfloat16), "dp", scatter_dimension=0, tiled=True
        ).astype(jnp.float32),
        lax.psum_scatter(
            grad_value_w.astype(jnp.bfloat16), "dp", scatter_dimension=0, tiled=True
        ).astype(jnp.float32),
        lax.psum_scatter(
            grad_out_w.astype(jnp.bfloat16), "dp", scatter_dimension=0, tiled=True
        ).astype(jnp.float32),
    )
    attn_grads = (
        lax.psum_scatter(
            attn_blocks[0].astype(jnp.bfloat16), "fsdp", scatter_dimension=0, tiled=True
        ).astype(jnp.float32),
        lax.psum_scatter(
            attn_blocks[1].astype(jnp.bfloat16), "fsdp", scatter_dimension=0, tiled=True
        ).astype(jnp.float32),
        lax.psum_scatter(
            attn_blocks[2].astype(jnp.bfloat16), "fsdp", scatter_dimension=0, tiled=True
        ).astype(jnp.float32),
        lax.psum_scatter(
            attn_blocks[3].astype(jnp.bfloat16), "fsdp", scatter_dimension=0, tiled=True
        ).astype(jnp.float32),
        lax.psum_scatter(
            attn_blocks[4].astype(jnp.bfloat16), "fsdp", scatter_dimension=0, tiled=True
        ).astype(jnp.float32),
    )
    return (grad_middle + grad_hidden_part, attn_grads, ffn_grads)


def general_device(
    tokens,
    gain_attn,
    w_query,
    w_key,
    w_value,
    w_out,
    gain_ffn,
    w_gate,
    w_up,
    w_down,
    lengths,
    cotangent,
):
    tok_rows = tokens.shape[0]
    group_tok = tok_rows * lax.axis_size("fsdp")
    segment, position = layout(lengths[0], group_tok)
    first_row = lax.axis_index("fsdp") * tok_rows
    row_places = first_row + jnp.arange(tok_rows, dtype=jnp.int32)
    seg_rows = lax.dynamic_slice_in_dim(segment, first_row, tok_rows)
    pos_rows = lax.dynamic_slice_in_dim(position, first_row, tok_rows)
    visible = visibility(seg_rows, row_places, segment, jnp.arange(group_tok, dtype=jnp.int32))
    hidden = tokens.astype(jnp.float32)
    layer_store = []
    results = []
    for layer_index in range(2):
        attn_weights = fetch_attention(layer_index, gain_attn, w_query, w_key, w_value, w_out)
        ffn_weights = fetch_ffn(layer_index, gain_ffn, w_gate, w_up, w_down)
        hidden, saved = layer_forward(hidden, attn_weights, ffn_weights, pos_rows, visible)
        layer_store.append(saved)
        results.append(hidden.astype(jnp.bfloat16))
    upstream = cotangent.astype(jnp.float32)
    attn_list = []
    ffn_list = []
    for layer_index in (1, 0):
        attn_weights = fetch_attention(layer_index, gain_attn, w_query, w_key, w_value, w_out)
        ffn_weights = fetch_ffn(layer_index, gain_ffn, w_gate, w_up, w_down)
        saved = layer_store[layer_index]
        keys_all = share_keys(saved[3])
        upstream, attn_grads, ffn_grads = layer_backward(
            upstream, saved, attn_weights, ffn_weights, keys_all, pos_rows, visible
        )
        attn_list.append(attn_grads)
        ffn_list.append(ffn_grads)
    layer_outputs = jnp.stack(results)
    grad_gain_attn = jnp.stack([attn_list[1][0], attn_list[0][0]])
    grad_w_query = jnp.stack([attn_list[1][1], attn_list[0][1]])
    grad_w_key = jnp.stack([attn_list[1][2], attn_list[0][2]])
    grad_w_value = jnp.stack([attn_list[1][3], attn_list[0][3]])
    grad_w_out = jnp.stack([attn_list[1][4], attn_list[0][4]])
    grad_gain_ffn = jnp.stack([ffn_list[1][0], ffn_list[0][0]])
    grad_w_gate = jnp.stack([ffn_list[1][1], ffn_list[0][1]])
    grad_w_up = jnp.stack([ffn_list[1][2], ffn_list[0][2]])
    grad_w_down = jnp.stack([ffn_list[1][3], ffn_list[0][3]])
    return (
        layer_outputs,
        upstream,
        grad_gain_attn,
        grad_w_query,
        grad_w_key,
        grad_w_value,
        grad_w_out,
        grad_gain_ffn,
        grad_w_gate,
        grad_w_up,
        grad_w_down,
    )


TP = 4


def head_partner(values, halfway):
    width = values.shape[1]
    lane = lax.broadcasted_iota(jnp.int32, values.shape, 1)
    ahead = pltpu.roll(values, width - halfway, 1)
    behind = pltpu.roll(values, halfway, 1)
    return jnp.where(lane % HEAD_DIM < halfway, ahead, behind)


def block_mask(row_seg, col_seg, same_block, block):
    visible = (row_seg == col_seg) | (col_seg == 0)
    if same_block:
        rows = lax.broadcasted_iota(jnp.int32, (block, block), 0)
        cols = lax.broadcasted_iota(jnp.int32, (block, block), 1)
        visible = visible & (cols <= rows)
    return visible


MESH = pl.DeviceIdType.MESH
VMEM_LIMIT = 61 * 2**20
ANYWHERE = pl.BlockSpec(memory_space=pl.ANY)
IN_VMEM = pl.BlockSpec(memory_space=pltpu.VMEM)


class Net:
    def __init__(self, send_sems, recv_sems, local_sems):
        dp, z = lax.axis_index("dp"), lax.axis_index("fsdp")
        self.z = z
        self.q = lax.rem(dp, TP)
        self.y = lax.div(dp, TP)
        self.r = self.y * TP + z
        core = dp + 1 - 2 * lax.rem(dp, 2)
        across = dp + 2 - 4 * lax.rem(lax.div(dp, 2), 2)
        both = core + 2 - 4 * lax.rem(lax.div(dp, 2), 2)
        other = dp + TP - 2 * TP * lax.div(dp, TP)
        self.peer = {
            "core": (core, z),
            "x": (across, z),
            "both": (both, z),
            "y": (other, z),
            "z1": (dp, flip_index(z, 1)),
            "z2": (dp, flip_index(z, 2)),
            "z3": (dp, flip_index(z, 3)),
        }
        x, c = lax.div(self.q, 2), lax.rem(self.q, 2)
        high, low = lax.div(z, 2), lax.rem(z, 2)
        twisted = x + low - 2 * x * low
        self.peer["group"] = (self.y * TP + 2 * twisted + high, 2 * c + x)
        self.peer["home"] = (self.y * TP + 2 * low + high, 2 * c + twisted)
        self.alone = (self.peer["group"][0] == dp) & (self.peer["group"][1] == z)
        self.base = 2 * c + twisted
        self.send_sems, self.recv_sems, self.local_sems = send_sems, recv_sems, local_sems
        self.n_remote = self.n_local = 0
        self.flying = []
        self.leaving = []
        self.inner, self.outer = {}, {}

    def greet(self, names, regroup=None):
        barrier = pltpu.get_barrier_semaphore()
        for name in names:
            pl.semaphore_signal(barrier, inc=1, device_id=self.peer[name], device_id_type=MESH)
        if regroup is None:
            pl.semaphore_wait(barrier, len(names))
            return
        sender = self.peer["home" if regroup == "group" else "group"]

        @pl.when(jnp.logical_not(self.alone))
        def _():
            pl.semaphore_signal(barrier, inc=1, device_id=sender, device_id_type=MESH)
            pl.semaphore_wait(barrier, len(names) + 1)

        @pl.when(self.alone)
        def _():
            pl.semaphore_wait(barrier, len(names))

    def remote(self, src, dst, name):
        n = self.n_remote
        self.n_remote += 1
        copy = pltpu.make_async_remote_copy(
            src_ref=src,
            dst_ref=dst,
            send_sem=self.send_sems.at[n],
            recv_sem=self.recv_sems.at[n],
            device_id=self.peer[name],
            device_id_type=MESH,
        )
        copy.start()
        return copy

    def regroup(self, src, dst, name):
        n, k = self.n_remote, self.n_local
        self.n_remote += 1
        self.n_local += 1
        away = pltpu.make_async_remote_copy(
            src_ref=src,
            dst_ref=dst,
            send_sem=self.send_sems.at[n],
            recv_sem=self.recv_sems.at[n],
            device_id=self.peer[name],
            device_id_type=MESH,
        )
        here = pltpu.make_async_copy(src, dst, self.local_sems.at[k])
        copy = EitherCopy(self.alone, here, away)
        copy.start()
        return copy

    def local(self, src, dst):
        n = self.n_local
        self.n_local += 1
        copy = pltpu.make_async_copy(src, dst, self.local_sems.at[n])
        copy.start()
        return copy

    def keep(self, src, dst):
        self.leaving.append(self.local(src, dst))

    def finish(self):
        for copies in (*self.inner.values(), *self.outer.values(), self.flying, self.leaving):
            for copy in copies:
                copy.wait()
        self.inner, self.outer = {}, {}
        self.flying, self.leaving = [], []

    def arrived(self, ref):
        for pending in (self.inner, self.outer):
            for key in [k for k in pending if k[0] == id(ref)]:
                for copy in pending.pop(key):
                    copy.wait()

    def advance(self, moves):
        for stage, ref, low, count in moves:
            key = (id(ref), low)
            for copy in self.inner.pop(key, []):
                copy.wait()
            part = lambda bits: ref.at[self.y, pl.ds(low, count), flip_index(self.z, bits)]
            if stage == 1:
                sent = ((0, "z2"), (0, "z1"), (0, "y"))
            elif stage == 2:
                sent = ((2, "z1"), (1, "y"), (2, "y"))
            else:
                sent = ((3, "y"),)
            for bits, name in sent:
                pending = self.outer if name == "y" else self.inner
                pending.setdefault(key, []).append(self.remote(part(bits), part(bits), name))


class EitherCopy:
    def __init__(self, alone, here, away):
        self.alone, self.here, self.away = alone, here, away

    def start(self):
        pl.when(self.alone)(self.here.start)
        pl.when(jnp.logical_not(self.alone))(self.away.start)

    def wait(self):
        pl.when(self.alone)(self.here.wait)
        pl.when(jnp.logical_not(self.alone))(self.away.wait)


def flip_index(value, bits):
    low = lax.rem(value, 2)
    high = lax.div(value, 2)
    if bits & 1:
        low = 1 - low
    if bits & 2:
        high = 1 - high
    return high * 2 + low


def mixed_index(static, dynamic):
    return flip_index(dynamic, static)


def swap_index(value):
    return lax.rem(value, 2) * 2 + lax.div(value, 2)


def sems(remote, local):
    return [
        pltpu.SemaphoreType.DMA((max(remote, 1),)),
        pltpu.SemaphoreType.DMA((max(remote, 1),)),
        pltpu.SemaphoreType.DMA((max(local, 1),)),
    ]


PEERS = ("core", "x", "both", "y", "z1", "z2", "z3")
RANK_PEERS = (("core", 1), ("x", 2), ("both", 3))


def segments(lengths_ref, conts, group_tok, places):
    one = [lengths_ref[0:1, c : c + 1] for c in range(conts)]
    prompt = group_tok - sum(one)
    begin = prompt
    segment = jnp.zeros(places.shape, jnp.int32)
    begins = jnp.zeros(places.shape, jnp.int32)
    for c in range(conts):
        inside = places >= begin
        segment = segment + inside.astype(jnp.int32)
        begins = jnp.where(inside, jnp.maximum(begins, begin), begins)
        begin = begin + one[c]
    position = jnp.where(segment > 0, places - begins + prompt, places)
    return segment, position


def block_segments(lengths_ref, conts, block, index, row):
    shape = (block, 1) if row else (1, block)
    places = index * block + lax.broadcasted_iota(jnp.int32, shape, 0 if row else 1)
    return segments(lengths_ref, conts, TP * block, places)[0]


def start_kernel(
    conts, qkv_pack, w_gate, w_up, out_own, down_own, gain_tile, tokens, lengths, frequency, spread_cos, spread_sin,
    tok_out, cos_ref, sin_ref, len_out,
    g_qkv0, g_qkv1, g_gu0, g_gu1, g_out0, g_out1, g_down0, g_down1, g_gain,
    tok_buf, len_buf, send_sems, recv_sems, local_sems,
):
    net = Net(send_sems, recv_sems, local_sems)
    net.greet(PEERS, "group")
    bring = [net.regroup(lengths, len_buf, "group"), net.regroup(tokens, tok_buf, "group")]
    y, q, z = net.y, net.q, net.z
    step = w_gate.shape[2] // (2 * TP)

    def qkv_columns(layer, target):
        copies = [
            net.remote(qkv_pack.at[layer, flip_index(q, bits)], target.at[y, q, z], name)
            for name, bits in RANK_PEERS
        ]
        return copies + [net.local(qkv_pack.at[layer, q], target.at[y, q, z])]

    def gu_columns(layer, target):
        copies = []
        for name, bits in RANK_PEERS + ((None, 0),):
            for n, weight in enumerate((w_gate, w_up)):
                for half in range(2):
                    at = pl.multiple_of((half * TP + flip_index(q, bits)) * step, step)
                    src = weight.at[layer, :, pl.ds(at, step)]
                    dst = target.at[y, q, z, :, pl.ds((2 * n + half) * step, step)]
                    copies.append(net.local(src, dst) if name is None else net.remote(src, dst, name))
        return copies

    first = qkv_columns(0, g_qkv0)
    first += [net.remote(gain_tile, g_gain.at[y, q, z], name) for name, _ in RANK_PEERS]
    first.append(net.local(gain_tile, g_gain.at[y, q, z]))
    placed = [
        net.local(out_own.at[0], g_out0.at[y, 0, z]),
        net.local(down_own.at[0], g_down0.at[y, 0, z]),
        net.local(out_own.at[1], g_out1.at[y, 0, z]),
        net.local(down_own.at[1], g_down1.at[y, 0, z]),
    ]
    second = gu_columns(0, g_gu0)
    placed[0].wait()
    net.advance(((1, g_out0, 0, 1),))
    for copy in first:
        copy.wait()
    net.advance(((1, g_qkv0, 0, TP), (1, g_gain, 0, TP)))
    placed[1].wait()
    net.advance(((1, g_down0, 0, 1),))
    second += qkv_columns(1, g_qkv1) + gu_columns(1, g_gu1)
    bring[0].wait()
    block = tok_buf.shape[0]
    len_out[...] = len_buf[...]
    def table(s):
        places = mixed_index(s, net.base) * block + lax.broadcasted_iota(jnp.int32, (block, 1), 0)
        position = segments(len_buf, conts, TP * block, places)[1]
        angles = position.astype(jnp.float32) * frequency[...]
        at = slice(s * block, (s + 1) * block)
        for table_ref, values, lanes in (
            (cos_ref, jnp.cos(angles), spread_cos), (sin_ref, jnp.sin(angles), spread_sin)
        ):
            table_ref[at, :] = jnp.dot(
                values, lanes[...], precision=lax.Precision.HIGHEST, preferred_element_type=jnp.float32
            )

    table(0)
    net.advance(((2, g_out0, 0, 1), (2, g_qkv0, 0, TP), (2, g_gain, 0, TP)))
    table(1)
    net.advance(((3, g_out0, 0, 1), (3, g_qkv0, 0, TP), (3, g_gain, 0, TP), (2, g_down0, 0, 1)))
    table(2)
    table(3)
    bring[1].wait()
    tok_out[...] = tok_buf[...].astype(jnp.float32)
    for copy in placed[2:]:
        copy.wait()
    for copy in second:
        copy.wait()
    net.finish()


def start_exchange(conts, qkv_pack, w_gate, w_up, out_own, down_own, gain_tile, tokens, lengths, frequency, spread_cos, spread_sin):
    bf, f32 = jnp.bfloat16, jnp.float32
    shape = jax.ShapeDtypeStruct
    block, depth = tokens.shape
    shard, qkv_width = qkv_pack.shape[2:]
    units = w_gate.shape[2] // TP * 2
    outs = [
        shape((block, depth), f32),
        shape((TP * block, spread_cos.shape[1]), f32),
        shape((TP * block, spread_cos.shape[1]), f32),
        shape(lengths.shape, lengths.dtype),
    ]
    for ranks, rows, width in (
        (TP, shard, qkv_width),
        (TP, shard, units),
        (1, shard, depth),
        (1, down_own.shape[1], depth),
    ):
        outs += [shape((2, ranks, TP, rows, width), bf)] * 2
    outs.append(shape((2, TP, TP) + gain_tile.shape, f32))
    return pl.pallas_call(
        functools.partial(start_kernel, conts),
        out_shape=outs,
        in_specs=[IN_VMEM] * 11,
        out_specs=[IN_VMEM] * 4 + [ANYWHERE] * 9,
        scratch_shapes=[
            pltpu.VMEM((block, depth), bf),
            pltpu.VMEM(lengths.shape, lengths.dtype),
        ] + sems(80, 24),
        compiler_params=pltpu.CompilerParams(
            collective_id=1, has_side_effects=True, vmem_limit_bytes=VMEM_LIMIT
        ),
        cost_estimate=pl.CostEstimate(flops=0, bytes_accessed=300 * 2**20, transcendentals=0),
    )(qkv_pack, w_gate, w_up, out_own, down_own, gain_tile, tokens, lengths, frequency, spread_cos, spread_sin)


def attend_rows(net, block):
    return [
        pl.ds(pl.multiple_of(mixed_index(b, net.base) * block, block), block) for b in range(TP)
    ]


def attend_forward_block(net, qkv_ref, len_ref, conts, mixed_ref, lse_ref):
    total, width = qkv_ref.shape
    block = total // TP
    q_heads = width // (2 * HEAD_DIM)
    kv_heads = q_heads // 2
    factor = 1.0 / math.sqrt(HEAD_DIM)
    key_at = q_heads * HEAD_DIM
    value_at = key_at + kv_heads * HEAD_DIM
    places = attend_rows(net, block)
    nt = (((1,), (1,)), ((), ()))
    for i in range(TP):
        row_seg = block_segments(len_ref, conts, block, i, True)
        masks = [
            block_mask(row_seg, block_segments(len_ref, conts, block, j, False), i == j, block)
            for j in range(i + 1)
        ]
        for h in range(q_heads):
            kv = h // 2
            query = qkv_ref[places[i], h * HEAD_DIM : (h + 1) * HEAD_DIM]
            scores = []
            for j in range(i + 1):
                key = qkv_ref[places[j], key_at + kv * HEAD_DIM : key_at + (kv + 1) * HEAD_DIM]
                s = lax.dot_general(query, key, nt, preferred_element_type=jnp.float32) * factor
                scores.append(jnp.where(masks[j], s, NEGATIVE))
            peak = scores[0].max(axis=1, keepdims=True)
            for s in scores[1:]:
                peak = jnp.maximum(peak, s.max(axis=1, keepdims=True))
            total_e = jnp.zeros((block, 1), jnp.float32)
            mixed = jnp.zeros((block, HEAD_DIM), jnp.float32)
            for j in range(i + 1):
                e = jnp.exp(scores[j] - peak)
                total_e = total_e + e.sum(axis=1, keepdims=True)
                value = qkv_ref[places[j], value_at + kv * HEAD_DIM : value_at + (kv + 1) * HEAD_DIM]
                mixed = mixed + jnp.dot(
                    e.astype(jnp.bfloat16), value, preferred_element_type=jnp.float32
                )
            mixed_ref[places[i], h * HEAD_DIM : (h + 1) * HEAD_DIM] = (mixed / total_e).astype(
                jnp.bfloat16
            )
            lse_ref[i, :, h : h + 1] = peak + jnp.log(total_e)


def normalize(values, gain_row):
    scale = lax.rsqrt(jnp.mean(values * values, axis=-1, keepdims=True) + EPSILON)
    return (values * scale * gain_row).astype(jnp.bfloat16)


def spread_begin(net, buf):
    return (net.remote(buf.at[0], buf.at[1], "x"), net.remote(buf.at[0], buf.at[2], "core"))


def spread_each(net, buf, begun, work):
    over_x, over_core = begun
    work(0)
    over_core.wait()
    work(2)
    over_x.wait()
    forward = net.remote(buf.at[1], buf.at[3], "core")
    work(1)
    forward.wait()
    work(3)


def collect(net, part, far_out, far_in, pass_out, pass_in):
    low = lambda v: v.astype(jnp.bfloat16)
    far_out[0] = low(part(3))
    first = net.remote(far_out.at[0], far_in.at[0], "core")
    near = part(1)
    first.wait()
    pass_out[...] = low(near + far_in[0].astype(jnp.float32))
    passed = net.remote(pass_out, pass_in, "x")
    far_out[1] = low(part(2))
    second = net.remote(far_out.at[1], far_in.at[1], "core")
    own = part(0)
    second.wait()
    own = own + far_in[1].astype(jnp.float32)
    passed.wait()
    return own + pass_in[...].astype(jnp.float32)


def forward_kernel(programs, has_cot, conts, n_moving, *refs):
    x_own, gain_a, gain_f, cos_ref, sin_ref, lengths = refs[:6]
    refs = refs[6:]
    if has_cot:
        cot, refs = refs[0], refs[1:]
    refs = refs[n_moving:]
    moving, refs = refs[:n_moving], refs[n_moving:]
    (x_next, middle_ref, lse_ref, x_low, rows_out, qkv_out, mixed_out, ffn_rows_out, gate_out, up_out, act_out) = refs[:11]
    refs = refs[11:]
    if has_cot:
        branch_out, refs, branch = refs[0], refs[1:-1], refs[-1]
    (rows, ffn_rows, w_qkv, w_o, w_gu, w_d, qkv, mixed, gate, up, act,
     far_out, far_in, pass_out, pass_in, send_sems, recv_sems, local_sems) = refs
    net = Net(send_sems, recv_sems, local_sems)
    steps = [[(kind, moving[n], low, count) for kind, n, low, count in step] for step in programs]
    block, depth = x_own.shape
    load_qkv = net.local(moving[0], w_qkv)
    load_o = net.local(moving[1], w_o)
    net.greet(("core", "x", "y", "z1", "z2", "z3"), "group" if has_cot else None)
    net.advance(steps[0])
    if has_cot:
        bring = net.regroup(cot, branch.at[0], "group")
    rows[0] = normalize(x_own[...], gain_a[...])
    begun = spread_begin(net, rows)
    load_qkv.wait()

    def project(s):
        raw = jnp.dot(
            rows[s], w_qkv[...].reshape(depth, -1), preferred_element_type=jnp.float32
        )
        at = slice(s * block, (s + 1) * block)
        turned = raw * cos_ref[at, :] + head_partner(raw, HEAD_DIM // 2) * sin_ref[at, :]
        qkv[at, :] = turned.astype(jnp.bfloat16)

    spread_each(net, rows, begun, project)
    net.keep(rows, rows_out)
    net.keep(qkv, qkv_out)
    net.advance(steps[1])
    attend_forward_block(net, qkv, lengths, conts, mixed, lse_ref)
    net.keep(mixed, mixed_out)
    net.advance(steps[2])
    load_o.wait()

    def out_part(s):
        return jnp.dot(
            mixed[s * block : (s + 1) * block, :],
            w_o[...].reshape(-1, depth),
            preferred_element_type=jnp.float32,
        )

    middle = x_own[...] + collect(
        net, out_part, far_out, far_in.at[0], pass_out, pass_in.at[0]
    )
    middle_ref[...] = middle
    net.advance(steps[3])
    net.arrived(moving[3])
    load_d = net.local(moving[3], w_d)
    ffn_rows[0] = normalize(middle, gain_f[...])
    begun = spread_begin(net, ffn_rows)
    if has_cot:
        bring.wait()
        over_x, over_core = spread_begin(net, branch)
    net.arrived(moving[2])
    load_gu = net.local(moving[2], w_gu)
    net.advance(steps[4])
    load_d.wait()
    load_gu.wait()
    units = act.shape[2]

    def expand(s):
        value = ffn_rows[s]
        gating = jnp.dot(
            value, w_gu[:, :, :, :, :units].reshape(depth, units), preferred_element_type=jnp.float32
        )
        upward = jnp.dot(
            value, w_gu[:, :, :, :, units:].reshape(depth, units), preferred_element_type=jnp.float32
        )
        gate[s] = gating.astype(jnp.bfloat16)
        up[s] = upward.astype(jnp.bfloat16)
        act[s] = (gating * jax.nn.sigmoid(gating) * upward).astype(jnp.bfloat16)

    spread_each(net, ffn_rows, begun, expand)
    if has_cot:
        over_x.wait()
        forward = net.remote(branch.at[1], branch.at[3], "core")
    net.keep(ffn_rows, ffn_rows_out)
    net.keep(gate, gate_out)
    net.keep(up, up_out)
    net.keep(act, act_out)

    def down_part(s):
        return jnp.dot(act[s], w_d[...].reshape(-1, depth), preferred_element_type=jnp.float32)

    result = middle_ref[...] + collect_during(
        net,
        down_part,
        (far_out, far_in.at[1], pass_out, pass_in.at[1]),
        lambda: net.advance(steps[5]),
    )
    if has_cot:
        over_core.wait()
        forward.wait()
        net.keep(branch, branch_out)
    x_next[...] = result
    x_low[...] = result.astype(jnp.bfloat16)
    net.finish()


def forward_layer(programs, cot, cid, conts, x_own, gain_a, gain_f, cosine, sine, lengths, moving):
    bf, f32 = jnp.bfloat16, jnp.float32
    block, depth = x_own.shape
    total, qkv_width = cosine.shape
    units = moving[2].shape[4] // 2
    q_heads = qkv_width // (2 * HEAD_DIM)
    shape = jax.ShapeDtypeStruct
    outs = [shape(m.shape, m.dtype) for m in moving] + [
        shape((block, depth), f32),
        shape((block, depth), f32),
        shape((TP, block, q_heads), f32),
        shape((block, depth), bf),
        shape((TP, block, depth), bf),
        shape((total, qkv_width), bf),
        shape((total, qkv_width // 2), bf),
        shape((TP, block, depth), bf),
        shape((TP, block, units), bf),
        shape((TP, block, units), bf),
        shape((TP, block, units), bf),
    ]
    n = len(moving)
    given = [] if cot is None else [cot]
    c = len(given)
    outs += [shape((TP, block, depth), bf)] * c
    scratch = [
        pltpu.VMEM((TP, block, depth), bf),
        pltpu.VMEM((TP, block, depth), bf),
        pltpu.VMEM(moving[0].shape, bf),
        pltpu.VMEM(moving[1].shape, bf),
        pltpu.VMEM(moving[2].shape, bf),
        pltpu.VMEM(moving[3].shape, bf),
        pltpu.VMEM((total, qkv_width), bf),
        pltpu.VMEM((total, qkv_width // 2), bf),
        pltpu.VMEM((TP, block, units), bf),
        pltpu.VMEM((TP, block, units), bf),
        pltpu.VMEM((TP, block, units), bf),
        pltpu.VMEM((2, block, depth), bf),
        pltpu.VMEM((2, 2, block, depth), bf),
        pltpu.VMEM((block, depth), bf),
        pltpu.VMEM((2, block, depth), bf),
    ] + sems(80, 24) + [pltpu.VMEM((TP, block, depth), bf)] * c
    return pl.pallas_call(
        functools.partial(forward_kernel, programs, bool(c), conts, n),
        out_shape=outs,
        in_specs=[IN_VMEM] * (6 + c) + [ANYWHERE] * n,
        out_specs=[ANYWHERE] * n + [IN_VMEM] * 4 + [ANYWHERE] * (7 + c),
        scratch_shapes=scratch,
        input_output_aliases={6 + c + i: i for i in range(n)},
        compiler_params=pltpu.CompilerParams(
            collective_id=cid, has_side_effects=True, vmem_limit_bytes=VMEM_LIMIT
        ),
        cost_estimate=pl.CostEstimate(
            flops=16 * 10**9, bytes_accessed=400 * 2**20, transcendentals=10**7
        ),
    )(x_own, gain_a, gain_f, cosine, sine, lengths, *given, *moving)


def moved_shape(kind, source):
    shape = source.shape
    if kind in ("y", "whole_y"):
        kept = shape
    elif kind == "g":
        kept = shape
    elif kind == "zc":
        kept = (3, shape[0]) + shape[2:]
    elif kind in ("z", "t"):
        kept = (3,) + shape[1:]
    else:
        kept = (3,) + shape
    return jax.ShapeDtypeStruct(kept, source.dtype)


def begin_move(net, kind, source, target):
    if kind in ("y", "whole_y"):
        return [net.remote(source, target, "y")]
    if kind == "g":
        return [net.regroup(source, target, "home")]
    copies = []
    for name, bits in RANK_PEERS:
        if kind == "z":
            copies.append(
                net.remote(source.at[flip_index(net.z, bits)], target.at[bits - 1], f"z{bits}")
            )
        elif kind == "zc":
            copies.append(
                net.remote(source.at[:, flip_index(net.z, bits)], target.at[bits - 1], f"z{bits}")
            )
        elif kind == "whole_z":
            copies.append(net.remote(source, target.at[bits - 1], f"z{bits}"))
        elif kind == "t":
            copies.append(
                net.remote(source.at[flip_index(net.q, bits)], target.at[bits - 1], name)
            )
        else:
            copies.append(net.remote(source, target.at[bits - 1], name))
    return copies


def begin_moves(net, kinds, sources, targets):
    for kind, source, target in zip(kinds, sources, targets):
        net.flying += begin_move(net, kind, source, target)


def greet_all(net, kinds):
    net.greet(PEERS, "home" if "g" in kinds else None)


def move_kernel(kinds, *refs):
    n = len(kinds)
    net = Net(*refs[2 * n :])
    greet_all(net, kinds)
    begin_moves(net, kinds, refs[:n], refs[n : 2 * n])
    net.finish()


def run_moves(cid, moves):
    kinds = tuple(kind for kind, _ in moves)
    sources = [source for _, source in moves]
    return pl.pallas_call(
        functools.partial(move_kernel, kinds),
        out_shape=[moved_shape(kind, source) for kind, source in moves],
        in_specs=[ANYWHERE] * len(moves),
        out_specs=[ANYWHERE] * len(moves),
        scratch_shapes=sems(32, 4),
        compiler_params=pltpu.CompilerParams(
            collective_id=cid, has_side_effects=True, vmem_limit_bytes=VMEM_LIMIT
        ),
        cost_estimate=pl.CostEstimate(flops=0, bytes_accessed=200 * 2**20, transcendentals=0),
    )(*sources)


def norm_backward(values, gain_row, incoming):
    inv = lax.rsqrt(jnp.mean(values * values, axis=-1, keepdims=True) + EPSILON)
    weighted = incoming * gain_row
    inner = jnp.mean(weighted * values, axis=-1, keepdims=True)
    grad = inv * weighted - values * (inv * inv * inv * inner)
    return grad, jnp.sum(incoming * values * inv, axis=0, keepdims=True)


def collect_during(net, part, bufs, meanwhile):
    far_out, far_in, pass_out, pass_in = bufs
    low = lambda v: v.astype(jnp.bfloat16)
    far_out[0] = low(part(3))
    first = net.remote(far_out.at[0], far_in.at[0], "core")
    near = part(1)
    first.wait()
    pass_out[...] = low(near + far_in[0].astype(jnp.float32))
    passed = net.remote(pass_out, pass_in, "x")
    far_out[1] = low(part(2))
    second = net.remote(far_out.at[1], far_in.at[1], "core")
    own = part(0)
    second.wait()
    own = own + far_in[1].astype(jnp.float32)
    meanwhile()
    passed.wait()
    return own + pass_in[...].astype(jnp.float32)


NT = (((1,), (1,)), ((), ()))
TN = (((0,), (0,)), ((), ()))


def dot_nt(left, right):
    return lax.dot_general(left, right, NT, preferred_element_type=jnp.float32)


def dot_tn(left, right):
    return lax.dot_general(left, right, TN, preferred_element_type=jnp.float32)


def ffn_backward_kernel(kinds, given, *refs):
    n = len(kinds)
    middle, gain, source_in = refs[:3]
    acts, rows_in, gates, ups, mixed_in, wd_in, wgu_in, wo_in = refs[3:11]
    refs = refs[11:]
    sources, targets, refs = refs[:n], refs[n : 2 * n], refs[2 * n :]
    (grad_middle, gain_grad, dmixed_out, d_own, d_got, gu_own, gu_other, o_own, o_other) = refs[:9]
    (branch, proj, act, rows, gate, up, mixed, dmixed, w_d, w_gu, w_o, g_down, g_gu, g_out,
     far_out, far_in, pass_out, pass_in, send_sems, recv_sems, local_sems) = refs[9:]
    net = Net(send_sems, recv_sems, local_sems)
    block, depth = middle.shape
    units = act.shape[2]
    total = TP * block
    loads = {}
    if given:
        loads["branch"] = net.local(source_in, branch)
    for name, src, dst in (
        ("w_d", wd_in, w_d), ("gate", gates, gate), ("up", ups, up), ("act", acts, act),
        ("w_gu", wgu_in, w_gu), ("rows", rows_in, rows), ("w_o", wo_in, w_o), ("mixed", mixed_in, mixed),
    ):
        loads[name] = net.local(src, dst)
    greet_all(net, kinds)
    begin_moves(net, kinds, sources, targets)
    if given:
        loads["branch"].wait()
    else:
        branch[0] = source_in[...].astype(jnp.bfloat16)
        begun = spread_begin(net, branch)
    loads["w_d"].wait()
    loads["gate"].wait()
    loads["up"].wait()

    def through(s):
        grad_act = dot_nt(branch[s], w_d[...].reshape(units, depth))
        gating = gate[s].astype(jnp.float32)
        upward = up[s].astype(jnp.float32)
        sig = jax.nn.sigmoid(gating)
        shared = grad_act * sig
        gate[s] = (shared * upward * (1.0 + gating * (1.0 - sig))).astype(jnp.bfloat16)
        up[s] = (shared * gating).astype(jnp.bfloat16)

    if given:
        for s in (3, 1, 2, 0):
            through(s)
    else:
        spread_each(net, branch, begun, through)
    loads["act"].wait()
    theirs, ours = 1 - net.y, net.y
    drows, urows = g_down.shape[2], g_gu.shape[3]
    dwide, uwide = 2 * drows, 2 * TP * urows

    def down_half(side):
        def tile(m, carry):
            lanes = pl.ds(pl.multiple_of((side * 2 + m) * dwide, dwide), dwide)
            grad = dot_tn(act[:, :, lanes].reshape(total, dwide), branch[...].reshape(total, depth))
            g_down[side, pl.ds(2 * m, 2)] = grad.astype(jnp.bfloat16).reshape(2, drows, depth)
            return carry

        lax.fori_loop(0, 2, tile, 0)

    def gu_half(side):
        def tile(m, carry):
            lanes = pl.ds(pl.multiple_of((side * 2 + m) * uwide, uwide), uwide)
            left = rows[:, :, lanes].reshape(total, uwide)
            for ref, at in ((gate, 0), (up, units)):
                grad = dot_tn(left, ref[...].reshape(total, units)).astype(jnp.bfloat16)
                g_gu[side, pl.ds(2 * m, 2), :, :, at : at + units] = grad.reshape(2, TP, urows, units)
            return carry

        lax.fori_loop(0, 2, tile, 0)

    down_half(theirs)
    net.flying.append(net.remote(g_down.at[theirs], d_got, "y"))
    loads["w_gu"].wait()
    loads["rows"].wait()

    def back(s):
        return dot_nt(gate[s], w_gu[:, :, :, :, :units].reshape(depth, units)) + dot_nt(
            up[s], w_gu[:, :, :, :, units:].reshape(depth, units)
        )

    def meanwhile():
        gu_half(theirs)
        net.keep(g_gu.at[theirs], gu_other)
        gu_half(ours)
        net.keep(g_gu.at[ours], gu_own)
        down_half(ours)
        net.keep(g_down.at[ours], d_own)

    incoming = collect_during(net, back, (far_out, far_in, pass_out, pass_in), meanwhile)
    part, gain_part = norm_backward(middle[...], gain[...], incoming)
    gain_grad[...] = gain_part
    grad_mid = (branch[0].astype(jnp.float32) if given else source_in[...]) + part
    grad_middle[...] = grad_mid
    proj[0] = grad_mid.astype(jnp.bfloat16)
    begun = spread_begin(net, proj)
    loads["w_o"].wait()
    loads["mixed"].wait()

    def mix_back(s):
        dmixed[s * block : (s + 1) * block, :] = dot_nt(
            proj[s], w_o[...].reshape(-1, depth)
        ).astype(jnp.bfloat16)

    spread_each(net, proj, begun, mix_back)
    net.keep(dmixed, dmixed_out)
    grad = dot_tn(mixed[...], proj[...].reshape(total, depth)).astype(jnp.bfloat16)
    g_out[...] = grad.reshape(g_out.shape)
    net.keep(g_out.at[ours], o_own)
    net.keep(g_out.at[theirs], o_other)
    net.finish()


def ffn_backward(cid, moves, source, given, middle, gain, acts, rows, gates, ups, mixed, w_d, w_gu, w_o):
    bf, f32 = jnp.bfloat16, jnp.float32
    shape = jax.ShapeDtypeStruct
    block, depth = middle.shape
    units = gates.shape[2]
    total, mixed_width = mixed.shape
    kinds = tuple(kind for kind, _ in moves)
    sources = [source for _, source in moves]
    n = len(moves)
    drows, urows, orows = w_d.shape[3], w_gu.shape[3], w_o.shape[3]
    outs = [moved_shape(kind, source) for kind, source in moves] + [
        shape((block, depth), f32),
        shape((1, depth), f32),
        shape((total, mixed_width), bf),
        shape((TP, drows, depth), bf),
        shape((TP, drows, depth), bf),
        shape((TP, TP, urows, 2 * units), bf),
        shape((TP, TP, urows, 2 * units), bf),
        shape((TP, orows, depth), bf),
        shape((TP, orows, depth), bf),
    ]
    scratch = [
        pltpu.VMEM((TP, block, depth), bf),
        pltpu.VMEM((TP, block, depth), bf),
        pltpu.VMEM((TP, block, units), bf),
        pltpu.VMEM((TP, block, depth), bf),
        pltpu.VMEM((TP, block, units), bf),
        pltpu.VMEM((TP, block, units), bf),
        pltpu.VMEM((total, mixed_width), bf),
        pltpu.VMEM((total, mixed_width), bf),
        pltpu.VMEM(w_d.shape, bf),
        pltpu.VMEM(w_gu.shape, bf),
        pltpu.VMEM(w_o.shape, bf),
        pltpu.VMEM((2, TP, drows, depth), bf),
        pltpu.VMEM((2, TP, TP, urows, 2 * units), bf),
        pltpu.VMEM((2, TP, orows, depth), bf),
        pltpu.VMEM((2, block, depth), bf),
        pltpu.VMEM((2, block, depth), bf),
        pltpu.VMEM((block, depth), bf),
        pltpu.VMEM((block, depth), bf),
    ] + sems(48, 20)
    operands = [middle, gain, source, acts, rows, gates, ups, mixed, w_d, w_gu, w_o]
    return pl.pallas_call(
        functools.partial(ffn_backward_kernel, kinds, given),
        out_shape=outs,
        in_specs=[IN_VMEM] * 2 + [ANYWHERE if given else IN_VMEM] + [ANYWHERE] * (8 + n),
        out_specs=[ANYWHERE] * n + [IN_VMEM] * 2 + [ANYWHERE] * 7,
        scratch_shapes=scratch,
        compiler_params=pltpu.CompilerParams(
            collective_id=cid, has_side_effects=True, vmem_limit_bytes=VMEM_LIMIT
        ),
        cost_estimate=pl.CostEstimate(
            flops=24 * 10**9, bytes_accessed=200 * 2**20, transcendentals=10**6
        ),
    )(*operands, *sources)


def attend_backward_block(net, qkv_ref, grad_ref, mixed_ref, lse_ref, len_ref, conts, acc_ref):
    total, width = qkv_ref.shape
    block = total // TP
    q_heads = width // (2 * HEAD_DIM)
    kv_heads = q_heads // 2
    factor = 1.0 / math.sqrt(HEAD_DIM)
    key_at = q_heads * HEAD_DIM
    value_at = key_at + kv_heads * HEAD_DIM
    places = attend_rows(net, block)
    acc_ref[:, key_at:] = jnp.zeros((total, width - key_at), jnp.float32)
    for i in range(TP):
        row_seg = block_segments(len_ref, conts, block, i, True)
        masks = [
            block_mask(row_seg, block_segments(len_ref, conts, block, j, False), i == j, block)
            for j in range(i + 1)
        ]
        for h in range(q_heads):
            kv = h // 2
            lanes = slice(h * HEAD_DIM, (h + 1) * HEAD_DIM)
            query = qkv_ref[places[i], lanes]
            grad = grad_ref[places[i], lanes]
            lse = lse_ref[i, :, h : h + 1]
            inner = jnp.sum(
                grad.astype(jnp.float32) * mixed_ref[places[i], lanes].astype(jnp.float32),
                axis=1,
                keepdims=True,
            )
            grad_query = jnp.zeros((block, HEAD_DIM), jnp.float32)
            key_lanes = slice(key_at + kv * HEAD_DIM, key_at + (kv + 1) * HEAD_DIM)
            value_lanes = slice(value_at + kv * HEAD_DIM, value_at + (kv + 1) * HEAD_DIM)
            for j in range(i + 1):
                key = qkv_ref[places[j], key_lanes]
                value = qkv_ref[places[j], value_lanes]
                s = dot_nt(query, key) * factor
                prob = jnp.where(masks[j], jnp.exp(s - lse), 0.0)
                grad_prob = dot_nt(grad, value)
                grad_score = (prob * (grad_prob - inner)).astype(jnp.bfloat16)
                grad_query = grad_query + jnp.dot(
                    grad_score, key, preferred_element_type=jnp.float32
                )
                acc_ref[places[j], key_lanes] += dot_tn(grad_score, query) * factor
                acc_ref[places[j], value_lanes] += dot_tn(prob.astype(jnp.bfloat16), grad)
            acc_ref[places[i], lanes] = grad_query * factor


def attn_backward_kernel(kinds, conts, *refs):
    n = len(kinds)
    (grad_middle, hidden, gain, qkv, dmixed, mixed, lse, lengths, cos_ref, sin_ref) = refs[:10]
    rows_in, w_in = refs[10:12]
    sources, targets, refs = refs[12 : 12 + n], refs[12 + n : 12 + 2 * n], refs[12 + 2 * n :]
    upstream, up_low, gain_grad, qkv_own, qkv_other = refs[:5]
    (acc, dqkv, rows, w_qkv, g_qkv, far_out, far_in, pass_out, pass_in,
     send_sems, recv_sems, local_sems) = refs[5:]
    net = Net(send_sems, recv_sems, local_sems)
    block, depth = hidden.shape
    total = TP * block
    load_rows = net.local(rows_in, rows)
    load_w = net.local(w_in, w_qkv)
    greet_all(net, kinds)
    begin_moves(net, kinds, sources, targets)
    attend_backward_block(net, qkv, dmixed, mixed, lse, lengths, conts, acc)
    for s in range(TP):
        at = slice(s * block, (s + 1) * block)
        value = acc[at, :]
        turned = value * cos_ref[at, :] - head_partner(value, HEAD_DIM // 2) * sin_ref[at, :]
        dqkv[at, :] = turned.astype(jnp.bfloat16)
    load_w.wait()
    load_rows.wait()
    urows = g_qkv.shape[2]
    wide = 2 * TP * urows

    def back(s):
        return dot_nt(dqkv[s * block : (s + 1) * block, :], w_qkv[...].reshape(depth, -1))

    def meanwhile():
        def tile(m, carry):
            lanes = pl.ds(pl.multiple_of(m * wide, wide), wide)
            grad = dot_tn(rows[:, :, lanes].reshape(total, wide), dqkv[...])
            g_qkv[pl.ds(2 * m, 2)] = grad.astype(jnp.bfloat16).reshape(2, TP, urows, -1)
            return carry

        lax.fori_loop(0, TP, tile, 0)
        net.keep(g_qkv.at[pl.ds(net.y * TP, TP)], qkv_own)
        net.keep(g_qkv.at[pl.ds((1 - net.y) * TP, TP)], qkv_other)

    incoming = collect_during(net, back, (far_out, far_in, pass_out, pass_in), meanwhile)
    part, gain_part = norm_backward(hidden[...], gain[...], incoming)
    gain_grad[...] = gain_part
    result = grad_middle[...] + part
    upstream[...] = result
    up_low[...] = result.astype(jnp.bfloat16)
    net.finish()


def attn_backward(
    cid, moves, conts, grad_middle, hidden, gain, qkv, dmixed, mixed, lse, lengths, cosine, sine, rows, w_qkv
):
    bf, f32 = jnp.bfloat16, jnp.float32
    shape = jax.ShapeDtypeStruct
    block, depth = hidden.shape
    total, width = qkv.shape
    kinds = tuple(kind for kind, _ in moves)
    sources = [source for _, source in moves]
    n = len(moves)
    urows = w_qkv.shape[3]
    outs = [moved_shape(kind, source) for kind, source in moves] + [
        shape((block, depth), f32),
        shape((block, depth), bf),
        shape((1, depth), f32),
        shape((TP, TP, urows, width), bf),
        shape((TP, TP, urows, width), bf),
    ]
    scratch = [
        pltpu.VMEM((total, width), f32),
        pltpu.VMEM((total, width), bf),
        pltpu.VMEM((TP, block, depth), bf),
        pltpu.VMEM(w_qkv.shape, bf),
        pltpu.VMEM((2 * TP, TP, urows, width), bf),
        pltpu.VMEM((2, block, depth), bf),
        pltpu.VMEM((2, block, depth), bf),
        pltpu.VMEM((block, depth), bf),
        pltpu.VMEM((block, depth), bf),
    ] + sems(48, 8)
    return pl.pallas_call(
        functools.partial(attn_backward_kernel, kinds, conts),
        out_shape=outs,
        in_specs=[IN_VMEM] * 10 + [ANYWHERE] * (2 + n),
        out_specs=[ANYWHERE] * n + [IN_VMEM] * 3 + [ANYWHERE] * 2,
        scratch_shapes=scratch,
        compiler_params=pltpu.CompilerParams(
            collective_id=cid, has_side_effects=True, vmem_limit_bytes=VMEM_LIMIT
        ),
        cost_estimate=pl.CostEstimate(
            flops=16 * 10**9, bytes_accessed=200 * 2**20, transcendentals=10**7
        ),
    )(grad_middle, hidden, gain, qkv, dmixed, mixed, lse, lengths, cosine, sine, rows, w_qkv, *sources)


def add_low(own, got):
    return (own.astype(jnp.float32) + got.astype(jnp.float32)).astype(jnp.bfloat16)


def z_total(summed, got, axis):
    own = lax.dynamic_index_in_dim(summed, lax.axis_index("fsdp"), axis, keepdims=False)
    return (own.astype(jnp.float32) + jnp.sum(got.astype(jnp.float32), axis=0)).astype(jnp.bfloat16)


def end_kernel(step, qw, kw, *refs):
    layers, refs = refs[:16], refs[16:]
    x_outs, back, refs = refs[:2], refs[2], refs[3:]
    out_x, out_back, out_q, out_k, out_v, out_o, out_g, out_u, out_d = refs
    q = lax.rem(lax.axis_index("dp"), TP)
    z = lax.axis_index("fsdp")
    low, high = lax.rem(q, 2) == 1, lax.div(q, 2) == 1

    def columns(blocks, got):
        pieces = [blocks[q]] + [got[k] for k in range(3)]
        a = [jnp.where(low, pieces[i ^ 1], pieces[i]) for i in range(4)]
        return [jnp.where(high, a[i ^ 2], a[i]).astype(jnp.float32) for i in range(4)]

    def lay(target, layer, pieces, at, width):
        half = width // 2
        for n, piece in enumerate(pieces):
            for side in range(2):
                to = (side * TP + n) * half
                target[layer, :, to : to + half] = piece[:, at + side * half : at + (side + 1) * half]

    for layer in range(2):
        bqkv, tqkv, bgu, tgu, so, ro, sd, rd = layers[8 * layer : 8 * layer + 8]
        pieces = columns(bqkv, tqkv)
        lay(out_q, layer, pieces, 0, qw)
        lay(out_k, layer, pieces, qw, kw)
        lay(out_v, layer, pieces, qw + kw, kw)
        pieces = columns(bgu, tgu)
        lay(out_g, layer, pieces, 0, 2 * step)
        lay(out_u, layer, pieces, 2 * step, 2 * step)
        for summed, got, target in ((so, ro, out_o), (sd, rd, out_d)):
            value = summed[z].astype(jnp.float32)
            for k in range(3):
                value = value + got[k].astype(jnp.float32)
            target[layer] = value
        out_x[layer] = x_outs[layer][...]
    out_back[...] = back[...].astype(jnp.float32)


def end_assembly(step, qw, kw, pieces, x_outs, back):
    f32 = jnp.float32
    shape = jax.ShapeDtypeStruct
    block, depth = back.shape
    rows = pieces[0].shape[1]
    drows = pieces[6].shape[1]
    outs = [
        shape((2, block, depth), jnp.bfloat16),
        shape((block, depth), f32),
        shape((2, rows, TP * qw), f32),
        shape((2, rows, TP * kw), f32),
        shape((2, rows, TP * kw), f32),
        shape((2, rows, depth), f32),
        shape((2, rows, TP * 2 * step), f32),
        shape((2, rows, TP * 2 * step), f32),
        shape((2, drows, depth), f32),
    ]
    return pl.pallas_call(
        functools.partial(end_kernel, step, qw, kw),
        out_shape=outs,
        in_specs=[IN_VMEM] * 19,
        out_specs=[IN_VMEM] * 9,
        compiler_params=pltpu.CompilerParams(vmem_limit_bytes=VMEM_LIMIT),
    )(*pieces, *x_outs, back)


def column_pack(weights):
    parts = []
    for weight in weights:
        layers, rows, width = weight.shape
        view = weight.reshape(layers, rows, 2, TP, width // (2 * TP))
        parts.append(view.transpose(0, 3, 1, 2, 4).reshape(layers, TP, rows, width // TP))
    return jnp.concatenate(parts, axis=3)


def fast_device(
    tokens, gain_attn, w_query, w_key, w_value, w_out, gain_ffn, w_gate, w_up, w_down, lengths, cotangent
):
    depth = tokens.shape[1]
    shard = w_query.shape[1]
    conts = lengths.shape[1]
    halfway = HEAD_DIM // 2
    qw, kw = w_query.shape[2] // TP, w_key.shape[2] // TP
    step = w_gate.shape[2] // (2 * TP)
    frequency = ROPE_BASE ** (-jnp.arange(halfway, dtype=jnp.float32) * 2.0 / HEAD_DIM)
    lane = jnp.arange(128)[:, None]
    column = jnp.arange(qw + 2 * kw)[None]
    turned = column < qw + kw
    frequency = jnp.pad(frequency, (0, 128 - halfway))[None]
    picks = (lane == jnp.where(turned, column % halfway, halfway)).astype(jnp.float32)
    signed = picks * jnp.where(turned, jnp.where(column % HEAD_DIM < halfway, -1.0, 1.0), 0.0)
    gain_tile = jnp.pad(
        jnp.concatenate([gain_attn, gain_ffn], axis=0).astype(jnp.float32), ((0, 4), (0, 128 - shard))
    )
    len_tile = jnp.pad(lengths, ((0, 7), (0, 128 - conts)))
    (hidden, cosine, sine, lens, g_qkv0, g_qkv1, g_gu0, g_gu1, g_out0, g_out1, g_down0, g_down1, g_gain) = (
        start_exchange(
            conts, column_pack((w_query, w_key, w_value)), w_gate, w_up, w_out, w_down, gain_tile,
            tokens, len_tile, frequency, picks, signed,
        )
    )
    gains = jnp.transpose(g_gain[..., :4, :shard], (3, 0, 1, 2, 4)).reshape(4, 1, depth)
    qkv, out, gu, down, qkv_next, out_next, gu_next, down_next = range(8)
    programs0 = (
        ((3, down, 0, 1), (1, gu, 0, 2), (1, gu, 2, 2)),
        ((2, gu, 0, 2),),
        ((2, gu, 2, 2), (3, gu, 0, 2)),
        ((3, gu, 2, 2), (1, qkv_next, 0, 4), (1, out_next, 0, 1)),
        ((2, qkv_next, 0, 4), (2, out_next, 0, 1), (1, down_next, 0, 1), (1, gu_next, 0, 2)),
        ((3, qkv_next, 0, 4), (3, out_next, 0, 1), (2, down_next, 0, 1)),
    )
    programs1 = (
        ((3, down, 0, 1), (2, gu, 0, 2), (1, gu, 2, 2)),
        ((3, gu, 0, 2), (2, gu, 2, 2)),
        (),
        ((3, gu, 2, 2),),
        (),
        (),
    )
    tables = (cosine, sine, lens)
    res = forward_layer(
        programs0, cotangent, 2, conts, hidden, gains[0], gains[2], *tables,
        (g_qkv0, g_out0, g_gu0, g_down0, g_qkv1, g_out1, g_gu1, g_down1),
    )
    weights0, moving1, acts0 = res[:4], res[4:8], res[8:]
    (x1, mid0, lse0, low1, rows0, qkv0, mix0, frows0, gate0, up0, act0, branch) = acts0
    res = forward_layer(programs1, None, 3, conts, x1, gains[1], gains[3], *tables, moving1)
    weights1, acts1 = res[:4], res[4:]
    (x2, mid1, lse1, low2, rows1, qkv1, mix1, frows1, gate1, up1, act1) = acts1

    (low1_back, gmid1, ggf1, dmix1, d_own, d_got, gu_own, gu_other, o_own, o_other) = ffn_backward(
        4, (("g", low1),), branch, True, mid1, gains[3], act1, frows1, gate1, up1, mix1,
        weights1[3], weights1[2], weights1[1],
    )
    sd1 = add_low(d_own, d_got)
    (gu_got, o_got, rd1, low2_back, up_1, _, gga1, qkv_own1, qkv_other1) = attn_backward(
        5, (("y", gu_other), ("y", o_other), ("z", sd1), ("g", low2)), conts,
        gmid1, x1, gains[1], qkv1, dmix1, mix1, lse1, lens, cosine, sine, rows1, weights1[0],
    )
    sgu1 = add_low(gu_own, gu_got)
    so1 = add_low(o_own, o_got)
    (qkv_got1, rgu1, ro1, gmid0, ggf0, dmix0, d_own0, d_got0, gu_own0, gu_other0, o_own0, o_other0) = ffn_backward(
        6, (("y", qkv_other1), ("zc", sgu1), ("z", so1)), up_1, False, mid0, gains[2], act0, frows0, gate0, up0, mix0,
        weights0[3], weights0[2], weights0[1],
    )
    sqkv1 = add_low(qkv_own1, qkv_got1)
    sd0 = add_low(d_own0, d_got0)
    bgu1 = z_total(sgu1, rgu1, 1)
    (gu_got0, o_got0, rqkv1, rd0, tgu1, _, up_low, gga0, qkv_own0, qkv_other0) = attn_backward(
        7, (("y", gu_other0), ("y", o_other0), ("zc", sqkv1), ("z", sd0), ("t", bgu1)), conts,
        gmid0, hidden, gains[0], qkv0, dmix0, mix0, lse0, lens, cosine, sine, rows0, weights0[0],
    )
    sgu0 = add_low(gu_own0, gu_got0)
    so0 = add_low(o_own0, o_got0)
    bqkv1 = z_total(sqkv1, rqkv1, 1)
    gain_part = jnp.concatenate([gga0, gga1, ggf0, ggf1, jnp.zeros((4, depth), jnp.float32)], axis=0)
    (qkv_got0, rgu0, ro0, tqkv1, gain_t, back) = run_moves(
        8,
        (("y", qkv_other0), ("zc", sgu0), ("z", so0), ("t", bqkv1), ("whole_t", gain_part), ("g", up_low)),
    )
    sqkv0 = add_low(qkv_own0, qkv_got0)
    bgu0 = z_total(sgu0, rgu0, 1)
    gain_part = gain_part + jnp.sum(gain_t, axis=0)
    (rqkv0, tgu0, gain_z) = run_moves(9, (("zc", sqkv0), ("t", bgu0), ("whole_z", gain_part)))
    bqkv0 = z_total(sqkv0, rqkv0, 1)
    gain_part = gain_part + jnp.sum(gain_z, axis=0)
    (tqkv0, gain_y) = run_moves(10, (("t", bqkv0), ("whole_y", gain_part)))
    gain_sums = (gain_part + gain_y)[:4]
    device = lax.axis_index("dp") * lax.axis_size("fsdp") + lax.axis_index("fsdp")
    own_gain = lax.dynamic_slice_in_dim(gain_sums, device * shard, shard, 1)
    (out_x, out_back, grad_q, grad_k, grad_v, grad_o, grad_g, grad_u, grad_d) = end_assembly(
        step, qw, kw,
        (bqkv0, tqkv0, bgu0, tgu0, so0, ro0, sd0, rd0, bqkv1, tqkv1, bgu1, tgu1, so1, ro1, sd1, rd1),
        (low1_back, low2_back), back,
    )
    return (
        out_x, out_back, own_gain[:2], grad_q, grad_k, grad_v, grad_o, own_gain[2:], grad_g, grad_u, grad_d,
    )


def per_device(*arrays):
    tokens, w_query, w_key, w_gate = arrays[0], arrays[2], arrays[3], arrays[7]
    dp_size, z_size = lax.axis_size("dp"), lax.axis_size("fsdp")
    suits = (
        dp_size == 2 * TP
        and z_size == TP
        and w_key.shape[2] // HEAD_DIM == dp_size
        and w_query.shape[2] == 2 * w_key.shape[2]
        and tokens.shape[0] % 128 == 0
        and w_query.shape[1] % 16 == 0
        and w_gate.shape[2] % (TP * dp_size * 128) == 0
    )
    return (fast_device if suits else general_device)(*arrays)


def solution(mesh):
    placed = (
        P(("dp", "fsdp"), None),
        P(None, ("dp", "fsdp")),
        P(None, ("dp", "fsdp"), None),
        P(None, ("dp", "fsdp"), None),
        P(None, ("dp", "fsdp"), None),
        P(None, ("dp", "fsdp"), None),
        P(None, ("dp", "fsdp")),
        P(None, ("dp", "fsdp"), None),
        P(None, ("dp", "fsdp"), None),
        P(None, ("dp", "fsdp"), None),
        P("dp", None),
        P(("dp", "fsdp"), None),
    )
    return jax.shard_map(
        per_device,
        mesh=mesh,
        in_specs=placed,
        out_specs=(
            P(None, ("dp", "fsdp"), None),
            P(("dp", "fsdp"), None),
            P(None, ("dp", "fsdp")),
            P(None, ("dp", "fsdp"), None),
            P(None, ("dp", "fsdp"), None),
            P(None, ("dp", "fsdp"), None),
            P(None, ("dp", "fsdp"), None),
            P(None, ("dp", "fsdp")),
            P(None, ("dp", "fsdp"), None),
            P(None, ("dp", "fsdp"), None),
            P(None, ("dp", "fsdp"), None),
        ),
        check_vma=False,
    )
```

```python
import functools
import math

import jax
import jax.numpy as jnp
from jax import lax
from jax.experimental import pallas as pl
from jax.experimental.pallas import tpu as pltpu
from jax.sharding import PartitionSpec as P

HEAD_DIM = 96


EPSILON = 1e-05
ROPE_BASE = 100000.0
NEGATIVE = -1e30


def layout(lengths_row, group_tok):
    places = jnp.arange(group_tok, dtype=jnp.int32)
    prompt_len = group_tok - jnp.sum(lengths_row)
    starts = prompt_len + jnp.cumsum(lengths_row) - lengths_row
    inside = places[:, None] >= starts[None, :]
    segment = jnp.sum(inside.astype(jnp.int32), axis=1)
    begins = jnp.max(jnp.where(inside, starts[None, :], 0), axis=1)
    position = jnp.where(segment > 0, places - begins + prompt_len, places)
    return (segment, position)


def rotate(values, position, direction):
    row_count = values.shape[0]
    shaped = values.reshape(row_count, -1, HEAD_DIM)
    halfway = HEAD_DIM // 2
    frequency = ROPE_BASE ** (-jnp.arange(halfway, dtype=jnp.float32) * 2.0 / HEAD_DIM)
    angles = position.astype(jnp.float32)[:, None] * frequency[None, :]
    cosine = jnp.cos(angles)[:, None, :]
    sine_part = direction * jnp.sin(angles)[:, None, :]
    first_half = shaped[..., :halfway]
    second_half = shaped[..., halfway:]
    turned = jnp.concatenate(
        [
            first_half * cosine - second_half * sine_part,
            second_half * cosine + first_half * sine_part,
        ],
        axis=-1,
    )
    return turned.reshape(values.shape)


def norm_apply(values, gain_vec):
    inv_rms = lax.rsqrt(jnp.mean(values * values, axis=-1, keepdims=True) + EPSILON)
    return values * inv_rms * gain_vec


def norm_back(values, gain_vec, incoming):
    inv_rms = lax.rsqrt(jnp.mean(values * values, axis=-1, keepdims=True) + EPSILON)
    weighted = incoming * gain_vec
    inner_sum = jnp.mean(weighted * values, axis=-1, keepdims=True)
    grad_values = inv_rms * weighted - values * inv_rms * inv_rms * inv_rms * inner_sum
    grad_gain = jnp.sum(incoming * values * inv_rms, axis=0)
    return (grad_values, grad_gain)


def matmul(left, right):
    return jnp.dot(left, right, preferred_element_type=jnp.float32)


def visibility(seg_rows, row_places, segment, places):
    same_seq = (seg_rows[:, None] == segment[None, :]) & (places[None, :] <= row_places[:, None])
    prompt_seen = (segment[None, :] == 0) & (seg_rows[:, None] > 0)
    return same_seq | prompt_seen


def head_slices(query_b, keys_all, head_index):
    row_count = query_b.shape[0]
    kv_width = keys_all.shape[1] // 2
    sharing = query_b.shape[1] // kv_width
    query_part = lax.dynamic_slice_in_dim(
        query_b, head_index * sharing * HEAD_DIM, sharing * HEAD_DIM, 1
    ).reshape(row_count, sharing, HEAD_DIM)
    key_part = lax.dynamic_slice_in_dim(keys_all, head_index * HEAD_DIM, HEAD_DIM, 1)
    value_part = lax.dynamic_slice_in_dim(keys_all, kv_width + head_index * HEAD_DIM, HEAD_DIM, 1)
    return (query_part, key_part, value_part)


def attend_forward(query_b, keys_all, visible):
    row_count = query_b.shape[0]
    kv_heads = keys_all.shape[1] // 2 // HEAD_DIM
    factor = 1.0 / math.sqrt(HEAD_DIM)

    def per_head(head_index):
        query_part, key_part, value_part = head_slices(query_b, keys_all, head_index)
        scores = (
            jnp.einsum("tgd,kd->gtk", query_part, key_part, preferred_element_type=jnp.float32)
            * factor
        )
        masked = jnp.where(visible[None], scores, NEGATIVE)
        peak_score = jnp.max(masked, axis=-1)
        exponent = jnp.where(visible[None], jnp.exp(masked - peak_score[..., None]), 0.0)
        totals = jnp.sum(exponent, axis=-1)
        probability = (exponent / totals[..., None]).astype(jnp.bfloat16)
        mixed_heads = jnp.einsum(
            "gtk,kd->tgd", probability, value_part, preferred_element_type=jnp.float32
        )
        return (mixed_heads.reshape(row_count, -1), peak_score, totals)

    mixed_heads, peak_score, totals = lax.map(per_head, jnp.arange(kv_heads, dtype=jnp.int32))
    return (jnp.transpose(mixed_heads, (1, 0, 2)).reshape(row_count, -1), peak_score, totals)


def attend_backward(query_b, keys_all, visible, peak_score, totals, grad_mixed):
    row_count = query_b.shape[0]
    kv_width = keys_all.shape[1] // 2
    kv_heads = kv_width // HEAD_DIM
    sharing = query_b.shape[1] // kv_width
    factor = 1.0 / math.sqrt(HEAD_DIM)

    def per_head(pieces):
        head_index, peak_head, total_head = pieces
        query_part, key_part, value_part = head_slices(query_b, keys_all, head_index)
        grad_part = lax.dynamic_slice_in_dim(
            grad_mixed, head_index * sharing * HEAD_DIM, sharing * HEAD_DIM, 1
        ).reshape(row_count, sharing, HEAD_DIM)
        scores = (
            jnp.einsum("tgd,kd->gtk", query_part, key_part, preferred_element_type=jnp.float32)
            * factor
        )
        masked = jnp.where(visible[None], scores, NEGATIVE)
        exponent = jnp.where(visible[None], jnp.exp(masked - peak_head[..., None]), 0.0)
        probability = exponent / total_head[..., None]
        prob_low = probability.astype(jnp.bfloat16)
        grad_probs = jnp.einsum(
            "tgd,kd->gtk", grad_part, value_part, preferred_element_type=jnp.float32
        )
        inner_sum = jnp.sum(probability * grad_probs, axis=-1, keepdims=True)
        grad_scores = (probability * (grad_probs - inner_sum)).astype(jnp.bfloat16)
        grad_query = (
            jnp.einsum("gtk,kd->tgd", grad_scores, key_part, preferred_element_type=jnp.float32)
            * factor
        )
        grad_key = (
            jnp.einsum("gtk,tgd->kd", grad_scores, query_part, preferred_element_type=jnp.float32)
            * factor
        )
        grad_value = jnp.einsum(
            "gtk,tgd->kd", prob_low, grad_part, preferred_element_type=jnp.float32
        )
        return (grad_query.reshape(row_count, -1), grad_key, grad_value)

    grad_query, grad_key, grad_value = lax.map(
        per_head, (jnp.arange(kv_heads, dtype=jnp.int32), peak_score, totals)
    )
    group_rows = keys_all.shape[0]
    key_terms = jnp.concatenate(
        [
            jnp.transpose(grad_key, (1, 0, 2)).reshape(group_rows, -1),
            jnp.transpose(grad_value, (1, 0, 2)).reshape(group_rows, -1),
        ],
        axis=1,
    )
    return (jnp.transpose(grad_query, (1, 0, 2)).reshape(row_count, -1), key_terms)


def fetch_attention(layer_index, gain_attn, w_query, w_key, w_value, w_out):
    return (
        lax.all_gather(gain_attn[layer_index], ("dp", "fsdp"), axis=0, tiled=True),
        lax.all_gather(w_query[layer_index], ("dp", "fsdp"), axis=0, tiled=True),
        lax.all_gather(w_key[layer_index], ("dp", "fsdp"), axis=0, tiled=True),
        lax.all_gather(w_value[layer_index], ("dp", "fsdp"), axis=0, tiled=True),
        lax.all_gather(w_out[layer_index], ("dp", "fsdp"), axis=0, tiled=True),
    )


def fetch_ffn(layer_index, gain_ffn, w_gate, w_up, w_down):
    return (
        lax.all_gather(gain_ffn[layer_index], ("dp", "fsdp"), axis=0, tiled=True),
        lax.all_gather(w_gate[layer_index], ("dp", "fsdp"), axis=0, tiled=True),
        lax.all_gather(w_up[layer_index], ("dp", "fsdp"), axis=0, tiled=True),
        lax.all_gather(w_down[layer_index], ("dp", "fsdp"), axis=0, tiled=True),
    )


def share_keys(stacked):
    return lax.all_gather(stacked, "fsdp", axis=0, tiled=True)


def layer_forward(hidden, attn_weights, ffn_weights, pos_rows, visible):
    gain_a, query_w, key_w, value_w, out_w = attn_weights
    gain_f, gate_w, upper_w, down_w = ffn_weights
    normed = norm_apply(hidden, gain_a.astype(jnp.float32)).astype(jnp.bfloat16)
    query_b = rotate(matmul(normed, query_w), pos_rows, 1.0).astype(jnp.bfloat16)
    key_b = rotate(matmul(normed, key_w), pos_rows, 1.0).astype(jnp.bfloat16)
    value_b = matmul(normed, value_w).astype(jnp.bfloat16)
    stacked = jnp.concatenate([key_b, value_b], axis=1)
    keys_all = share_keys(stacked)
    mixed_heads, peak_score, totals = attend_forward(query_b, keys_all, visible)
    mixed_b = mixed_heads.astype(jnp.bfloat16)
    middle = hidden + matmul(mixed_b, out_w)
    normed_ffn = norm_apply(middle, gain_f.astype(jnp.float32)).astype(jnp.bfloat16)
    gating = matmul(normed_ffn, gate_w)
    upward = matmul(normed_ffn, upper_w)
    activated = (jax.nn.silu(gating) * upward).astype(jnp.bfloat16)
    result = middle + matmul(activated, down_w)
    saved = (
        hidden,
        normed,
        query_b,
        stacked,
        keys_all,
        peak_score,
        totals,
        mixed_b,
        middle,
        normed_ffn,
        gating,
        upward,
        activated,
    )
    return (result, saved)


def layer_backward(upstream, saved, attn_weights, ffn_weights, keys_all, pos_rows, visible):
    (
        hidden,
        normed,
        query_b,
        stacked,
        unused_keys,
        peak_score,
        totals,
        mixed_b,
        middle,
        normed_ffn,
        gating,
        upward,
        activated,
    ) = saved
    gain_a, query_w, key_w, value_w, out_w = attn_weights
    gain_f, gate_w, upper_w, down_w = ffn_weights
    grad_branch = upstream.astype(jnp.bfloat16)
    grad_down_w = matmul(activated.T, grad_branch)
    grad_act = matmul(grad_branch, down_w.T)
    sigmoid_g = jax.nn.sigmoid(gating)
    grad_gate = (grad_act * upward * sigmoid_g * (1.0 + gating * (1.0 - sigmoid_g))).astype(
        jnp.bfloat16
    )
    grad_up = (grad_act * gating * sigmoid_g).astype(jnp.bfloat16)
    grad_gate_w = matmul(normed_ffn.T, grad_gate)
    grad_up_w = matmul(normed_ffn.T, grad_up)
    grad_normed_ffn = matmul(grad_gate, gate_w.T) + matmul(grad_up, upper_w.T)
    grad_middle_part, grad_gain_f = norm_back(middle, gain_f.astype(jnp.float32), grad_normed_ffn)
    ffn_blocks = (
        lax.psum_scatter(
            grad_gain_f.astype(jnp.bfloat16), "dp", scatter_dimension=0, tiled=True
        ).astype(jnp.float32),
        lax.psum_scatter(
            grad_gate_w.astype(jnp.bfloat16), "dp", scatter_dimension=0, tiled=True
        ).astype(jnp.float32),
        lax.psum_scatter(
            grad_up_w.astype(jnp.bfloat16), "dp", scatter_dimension=0, tiled=True
        ).astype(jnp.float32),
        lax.psum_scatter(
            grad_down_w.astype(jnp.bfloat16), "dp", scatter_dimension=0, tiled=True
        ).astype(jnp.float32),
    )
    ffn_grads = (
        lax.psum_scatter(
            ffn_blocks[0].astype(jnp.bfloat16), "fsdp", scatter_dimension=0, tiled=True
        ).astype(jnp.float32),
        lax.psum_scatter(
            ffn_blocks[1].astype(jnp.bfloat16), "fsdp", scatter_dimension=0, tiled=True
        ).astype(jnp.float32),
        lax.psum_scatter(
            ffn_blocks[2].astype(jnp.bfloat16), "fsdp", scatter_dimension=0, tiled=True
        ).astype(jnp.float32),
        lax.psum_scatter(
            ffn_blocks[3].astype(jnp.bfloat16), "fsdp", scatter_dimension=0, tiled=True
        ).astype(jnp.float32),
    )
    grad_middle = upstream + grad_middle_part
    grad_proj = grad_middle.astype(jnp.bfloat16)
    grad_out_w = matmul(mixed_b.T, grad_proj)
    grad_mixed = matmul(grad_proj, out_w.T).astype(jnp.bfloat16)
    grad_query_rot, key_terms = attend_backward(
        query_b, keys_all, visible, peak_score, totals, grad_mixed
    )
    key_grads = lax.psum_scatter(
        key_terms.astype(jnp.bfloat16), "fsdp", scatter_dimension=0, tiled=True
    ).astype(jnp.float32)
    kv_width = key_terms.shape[1] // 2
    grad_query = rotate(grad_query_rot, pos_rows, -1.0).astype(jnp.bfloat16)
    grad_key = rotate(key_grads[:, :kv_width], pos_rows, -1.0).astype(jnp.bfloat16)
    grad_value = key_grads[:, kv_width:].astype(jnp.bfloat16)
    grad_normed = (
        matmul(grad_query, query_w.T) + matmul(grad_key, key_w.T) + matmul(grad_value, value_w.T)
    )
    grad_query_w = matmul(normed.T, grad_query)
    grad_key_w = matmul(normed.T, grad_key)
    grad_value_w = matmul(normed.T, grad_value)
    grad_hidden_part, grad_gain_a = norm_back(hidden, gain_a.astype(jnp.float32), grad_normed)
    attn_blocks = (
        lax.psum_scatter(
            grad_gain_a.astype(jnp.bfloat16), "dp", scatter_dimension=0, tiled=True
        ).astype(jnp.float32),
        lax.psum_scatter(
            grad_query_w.astype(jnp.bfloat16), "dp", scatter_dimension=0, tiled=True
        ).astype(jnp.float32),
        lax.psum_scatter(
            grad_key_w.astype(jnp.bfloat16), "dp", scatter_dimension=0, tiled=True
        ).astype(jnp.float32),
        lax.psum_scatter(
            grad_value_w.astype(jnp.bfloat16), "dp", scatter_dimension=0, tiled=True
        ).astype(jnp.float32),
        lax.psum_scatter(
            grad_out_w.astype(jnp.bfloat16), "dp", scatter_dimension=0, tiled=True
        ).astype(jnp.float32),
    )
    attn_grads = (
        lax.psum_scatter(
            attn_blocks[0].astype(jnp.bfloat16), "fsdp", scatter_dimension=0, tiled=True
        ).astype(jnp.float32),
        lax.psum_scatter(
            attn_blocks[1].astype(jnp.bfloat16), "fsdp", scatter_dimension=0, tiled=True
        ).astype(jnp.float32),
        lax.psum_scatter(
            attn_blocks[2].astype(jnp.bfloat16), "fsdp", scatter_dimension=0, tiled=True
        ).astype(jnp.float32),
        lax.psum_scatter(
            attn_blocks[3].astype(jnp.bfloat16), "fsdp", scatter_dimension=0, tiled=True
        ).astype(jnp.float32),
        lax.psum_scatter(
            attn_blocks[4].astype(jnp.bfloat16), "fsdp", scatter_dimension=0, tiled=True
        ).astype(jnp.float32),
    )
    return (grad_middle + grad_hidden_part, attn_grads, ffn_grads)


def general_device(
    tokens,
    gain_attn,
    w_query,
    w_key,
    w_value,
    w_out,
    gain_ffn,
    w_gate,
    w_up,
    w_down,
    lengths,
    cotangent,
):
    tok_rows = tokens.shape[0]
    group_tok = tok_rows * lax.axis_size("fsdp")
    segment, position = layout(lengths[0], group_tok)
    first_row = lax.axis_index("fsdp") * tok_rows
    row_places = first_row + jnp.arange(tok_rows, dtype=jnp.int32)
    seg_rows = lax.dynamic_slice_in_dim(segment, first_row, tok_rows)
    pos_rows = lax.dynamic_slice_in_dim(position, first_row, tok_rows)
    visible = visibility(seg_rows, row_places, segment, jnp.arange(group_tok, dtype=jnp.int32))
    hidden = tokens.astype(jnp.float32)
    layer_store = []
    results = []
    for layer_index in range(2):
        attn_weights = fetch_attention(layer_index, gain_attn, w_query, w_key, w_value, w_out)
        ffn_weights = fetch_ffn(layer_index, gain_ffn, w_gate, w_up, w_down)
        hidden, saved = layer_forward(hidden, attn_weights, ffn_weights, pos_rows, visible)
        layer_store.append(saved)
        results.append(hidden.astype(jnp.bfloat16))
    upstream = cotangent.astype(jnp.float32)
    attn_list = []
    ffn_list = []
    for layer_index in (1, 0):
        attn_weights = fetch_attention(layer_index, gain_attn, w_query, w_key, w_value, w_out)
        ffn_weights = fetch_ffn(layer_index, gain_ffn, w_gate, w_up, w_down)
        saved = layer_store[layer_index]
        keys_all = share_keys(saved[3])
        upstream, attn_grads, ffn_grads = layer_backward(
            upstream, saved, attn_weights, ffn_weights, keys_all, pos_rows, visible
        )
        attn_list.append(attn_grads)
        ffn_list.append(ffn_grads)
    layer_outputs = jnp.stack(results)
    grad_gain_attn = jnp.stack([attn_list[1][0], attn_list[0][0]])
    grad_w_query = jnp.stack([attn_list[1][1], attn_list[0][1]])
    grad_w_key = jnp.stack([attn_list[1][2], attn_list[0][2]])
    grad_w_value = jnp.stack([attn_list[1][3], attn_list[0][3]])
    grad_w_out = jnp.stack([attn_list[1][4], attn_list[0][4]])
    grad_gain_ffn = jnp.stack([ffn_list[1][0], ffn_list[0][0]])
    grad_w_gate = jnp.stack([ffn_list[1][1], ffn_list[0][1]])
    grad_w_up = jnp.stack([ffn_list[1][2], ffn_list[0][2]])
    grad_w_down = jnp.stack([ffn_list[1][3], ffn_list[0][3]])
    return (
        layer_outputs,
        upstream,
        grad_gain_attn,
        grad_w_query,
        grad_w_key,
        grad_w_value,
        grad_w_out,
        grad_gain_ffn,
        grad_w_gate,
        grad_w_up,
        grad_w_down,
    )


TP = 4


def head_partner(values, halfway):
    width = values.shape[1]
    lane = lax.broadcasted_iota(jnp.int32, values.shape, 1)
    ahead = pltpu.roll(values, width - halfway, 1)
    behind = pltpu.roll(values, halfway, 1)
    return jnp.where(lane % HEAD_DIM < halfway, ahead, behind)


def block_mask(row_seg, col_seg, same_block, block):
    visible = (row_seg == col_seg) | (col_seg == 0)
    if same_block:
        rows = lax.broadcasted_iota(jnp.int32, (block, block), 0)
        cols = lax.broadcasted_iota(jnp.int32, (block, block), 1)
        visible = visible & (cols <= rows)
    return visible


MESH = pl.DeviceIdType.MESH
VMEM_LIMIT = 61 * 2**20
ANYWHERE = pl.BlockSpec(memory_space=pl.ANY)
IN_VMEM = pl.BlockSpec(memory_space=pltpu.VMEM)


class Net:
    def __init__(self, send_sems, recv_sems, local_sems):
        dp, z = lax.axis_index("dp"), lax.axis_index("fsdp")
        self.z = z
        self.q = lax.rem(dp, TP)
        self.y = lax.div(dp, TP)
        self.r = self.y * TP + z
        core = dp + 1 - 2 * lax.rem(dp, 2)
        across = dp + 2 - 4 * lax.rem(lax.div(dp, 2), 2)
        both = core + 2 - 4 * lax.rem(lax.div(dp, 2), 2)
        other = dp + TP - 2 * TP * lax.div(dp, TP)
        self.peer = {
            "core": (core, z),
            "x": (across, z),
            "both": (both, z),
            "y": (other, z),
            "z1": (dp, flip_index(z, 1)),
            "z2": (dp, flip_index(z, 2)),
            "z3": (dp, flip_index(z, 3)),
        }
        x, c = lax.div(self.q, 2), lax.rem(self.q, 2)
        high, low = lax.div(z, 2), lax.rem(z, 2)
        twisted = x + low - 2 * x * low
        self.peer["group"] = (self.y * TP + 2 * twisted + high, 2 * c + x)
        self.peer["home"] = (self.y * TP + 2 * low + high, 2 * c + twisted)
        self.alone = (self.peer["group"][0] == dp) & (self.peer["group"][1] == z)
        self.base = 2 * c + twisted
        self.send_sems, self.recv_sems, self.local_sems = send_sems, recv_sems, local_sems
        self.n_remote = self.n_local = 0
        self.flying = []
        self.leaving = []
        self.inner, self.outer = {}, {}

    def greet(self, names, regroup=None):
        barrier = pltpu.get_barrier_semaphore()
        for name in names:
            pl.semaphore_signal(barrier, inc=1, device_id=self.peer[name], device_id_type=MESH)
        if regroup is None:
            pl.semaphore_wait(barrier, len(names))
            return
        sender = self.peer["home" if regroup == "group" else "group"]

        @pl.when(jnp.logical_not(self.alone))
        def _():
            pl.semaphore_signal(barrier, inc=1, device_id=sender, device_id_type=MESH)
            pl.semaphore_wait(barrier, len(names) + 1)

        @pl.when(self.alone)
        def _():
            pl.semaphore_wait(barrier, len(names))

    def remote(self, src, dst, name):
        n = self.n_remote
        self.n_remote += 1
        copy = pltpu.make_async_remote_copy(
            src_ref=src,
            dst_ref=dst,
            send_sem=self.send_sems.at[n],
            recv_sem=self.recv_sems.at[n],
            device_id=self.peer[name],
            device_id_type=MESH,
        )
        copy.start()
        return copy

    def regroup(self, src, dst, name):
        n, k = self.n_remote, self.n_local
        self.n_remote += 1
        self.n_local += 1
        away = pltpu.make_async_remote_copy(
            src_ref=src,
            dst_ref=dst,
            send_sem=self.send_sems.at[n],
            recv_sem=self.recv_sems.at[n],
            device_id=self.peer[name],
            device_id_type=MESH,
        )
        here = pltpu.make_async_copy(src, dst, self.local_sems.at[k])
        copy = EitherCopy(self.alone, here, away)
        copy.start()
        return copy

    def local(self, src, dst):
        n = self.n_local
        self.n_local += 1
        copy = pltpu.make_async_copy(src, dst, self.local_sems.at[n])
        copy.start()
        return copy

    def keep(self, src, dst):
        self.leaving.append(self.local(src, dst))

    def finish(self):
        for copies in (*self.inner.values(), *self.outer.values(), self.flying, self.leaving):
            for copy in copies:
                copy.wait()
        self.inner, self.outer = {}, {}
        self.flying, self.leaving = [], []

    def arrived(self, ref):
        for pending in (self.inner, self.outer):
            for key in [k for k in pending if k[0] == id(ref)]:
                for copy in pending.pop(key):
                    copy.wait()

    def advance(self, moves):
        for stage, ref, low, count in moves:
            key = (id(ref), low)
            for copy in self.inner.pop(key, []):
                copy.wait()
            part = lambda bits: ref.at[self.y, pl.ds(low, count), flip_index(self.z, bits)]
            if stage == 1:
                sent = ((0, "z2"), (0, "z1"), (0, "y"))
            elif stage == 4:
                sent = ((0, "y"),)
            elif stage == 5:
                sent = ((0, "z2"), (0, "z1"))
            elif stage == 2:
                sent = ((2, "z1"), (1, "y"), (2, "y"))
            else:
                sent = ((3, "y"),)
            for bits, name in sent:
                pending = self.outer if name == "y" else self.inner
                pending.setdefault(key, []).append(self.remote(part(bits), part(bits), name))


class EitherCopy:
    def __init__(self, alone, here, away):
        self.alone, self.here, self.away = alone, here, away

    def start(self):
        pl.when(self.alone)(self.here.start)
        pl.when(jnp.logical_not(self.alone))(self.away.start)

    def wait(self):
        pl.when(self.alone)(self.here.wait)
        pl.when(jnp.logical_not(self.alone))(self.away.wait)


def flip_index(value, bits):
    low = lax.rem(value, 2)
    high = lax.div(value, 2)
    if bits & 1:
        low = 1 - low
    if bits & 2:
        high = 1 - high
    return high * 2 + low


def mixed_index(static, dynamic):
    return flip_index(dynamic, static)


def swap_index(value):
    return lax.rem(value, 2) * 2 + lax.div(value, 2)


def sems(remote, local):
    return [
        pltpu.SemaphoreType.DMA((max(remote, 1),)),
        pltpu.SemaphoreType.DMA((max(remote, 1),)),
        pltpu.SemaphoreType.DMA((max(local, 1),)),
    ]


PEERS = ("core", "x", "both", "y", "z1", "z2", "z3")
RANK_PEERS = (("core", 1), ("x", 2), ("both", 3))


def segments(lengths_ref, conts, group_tok, places):
    one = [lengths_ref[0:1, c : c + 1] for c in range(conts)]
    prompt = group_tok - sum(one)
    begin = prompt
    segment = jnp.zeros(places.shape, jnp.int32)
    begins = jnp.zeros(places.shape, jnp.int32)
    for c in range(conts):
        inside = places >= begin
        segment = segment + inside.astype(jnp.int32)
        begins = jnp.where(inside, jnp.maximum(begins, begin), begins)
        begin = begin + one[c]
    position = jnp.where(segment > 0, places - begins + prompt, places)
    return segment, position


def block_segments(lengths_ref, conts, block, index, row):
    shape = (block, 1) if row else (1, block)
    places = index * block + lax.broadcasted_iota(jnp.int32, shape, 0 if row else 1)
    return segments(lengths_ref, conts, TP * block, places)[0]


def start_kernel(
    conts, qkv_pack, w_gate, w_up, out_own, down_own, gain_tile, tokens, lengths, frequency, spread_cos, spread_sin,
    tok_out, cos_ref, sin_ref, len_out,
    g_qkv0, g_qkv1, g_gu0, g_gu1, g_out0, g_out1, g_down0, g_down1, g_gain,
    tok_buf, len_buf, send_sems, recv_sems, local_sems,
):
    net = Net(send_sems, recv_sems, local_sems)
    net.greet(PEERS, "group")
    bring = [net.regroup(lengths, len_buf, "group"), net.regroup(tokens, tok_buf, "group")]
    y, q, z = net.y, net.q, net.z
    step = w_gate.shape[2] // (2 * TP)

    def qkv_columns(layer, target):
        copies = [
            net.remote(qkv_pack.at[layer, flip_index(q, bits)], target.at[y, q, z], name)
            for name, bits in RANK_PEERS
        ]
        return copies + [net.local(qkv_pack.at[layer, q], target.at[y, q, z])]

    def gu_columns(layer, target):
        copies = []
        for name, bits in RANK_PEERS + ((None, 0),):
            for n, weight in enumerate((w_gate, w_up)):
                for half in range(2):
                    at = pl.multiple_of((half * TP + flip_index(q, bits)) * step, step)
                    src = weight.at[layer, :, pl.ds(at, step)]
                    dst = target.at[y, q, z, :, pl.ds((2 * n + half) * step, step)]
                    copies.append(net.local(src, dst) if name is None else net.remote(src, dst, name))
        return copies

    first = qkv_columns(0, g_qkv0)
    first += [net.remote(gain_tile, g_gain.at[y, q, z], name) for name, _ in RANK_PEERS]
    first.append(net.local(gain_tile, g_gain.at[y, q, z]))
    placed = [
        net.local(out_own.at[0], g_out0.at[y, 0, z]),
        net.local(down_own.at[0], g_down0.at[y, 0, z]),
        net.local(out_own.at[1], g_out1.at[y, 0, z]),
        net.local(down_own.at[1], g_down1.at[y, 0, z]),
    ]
    second = gu_columns(0, g_gu0)
    placed[0].wait()
    net.advance(((1, g_out0, 0, 1),))
    for copy in first:
        copy.wait()
    net.advance(((1, g_qkv0, 0, TP), (1, g_gain, 0, TP)))
    placed[1].wait()
    net.advance(((1, g_down0, 0, 1),))
    second += qkv_columns(1, g_qkv1) + gu_columns(1, g_gu1)
    bring[0].wait()
    block = tok_buf.shape[0]
    len_out[...] = len_buf[...]
    def table(s):
        places = mixed_index(s, net.base) * block + lax.broadcasted_iota(jnp.int32, (block, 1), 0)
        position = segments(len_buf, conts, TP * block, places)[1]
        angles = position.astype(jnp.float32) * frequency[...]
        at = slice(s * block, (s + 1) * block)
        for table_ref, values, lanes in (
            (cos_ref, jnp.cos(angles), spread_cos), (sin_ref, jnp.sin(angles), spread_sin)
        ):
            table_ref[at, :] = jnp.dot(
                values, lanes[...], precision=lax.Precision.HIGHEST, preferred_element_type=jnp.float32
            )

    table(0)
    net.advance(((2, g_out0, 0, 1), (2, g_qkv0, 0, TP), (2, g_gain, 0, TP)))
    for copy in second[:16] + placed[2:]:
        copy.wait()
    second = second[16:]
    net.advance(((4, g_gu0, 0, TP), (4, g_down1, 0, 1), (4, g_out1, 0, 1)))
    table(1)
    net.advance(((3, g_out0, 0, 1), (3, g_qkv0, 0, TP), (3, g_gain, 0, TP), (2, g_down0, 0, 1)))
    table(2)
    table(3)
    bring[1].wait()
    tok_out[...] = tok_buf[...].astype(jnp.float32)
    for copy in second:
        copy.wait()
    net.finish()


def start_exchange(conts, qkv_pack, w_gate, w_up, out_own, down_own, gain_tile, tokens, lengths, frequency, spread_cos, spread_sin):
    bf, f32 = jnp.bfloat16, jnp.float32
    shape = jax.ShapeDtypeStruct
    block, depth = tokens.shape
    shard, qkv_width = qkv_pack.shape[2:]
    units = w_gate.shape[2] // TP * 2
    outs = [
        shape((block, depth), f32),
        shape((TP * block, spread_cos.shape[1]), f32),
        shape((TP * block, spread_cos.shape[1]), f32),
        shape(lengths.shape, lengths.dtype),
    ]
    for ranks, rows, width in (
        (TP, shard, qkv_width),
        (TP, shard, units),
        (1, shard, depth),
        (1, down_own.shape[1], depth),
    ):
        outs += [shape((2, ranks, TP, rows, width), bf)] * 2
    outs.append(shape((2, TP, TP) + gain_tile.shape, f32))
    return pl.pallas_call(
        functools.partial(start_kernel, conts),
        out_shape=outs,
        in_specs=[IN_VMEM] * 11,
        out_specs=[IN_VMEM] * 4 + [ANYWHERE] * 9,
        scratch_shapes=[
            pltpu.VMEM((block, depth), bf),
            pltpu.VMEM(lengths.shape, lengths.dtype),
        ] + sems(80, 24),
        compiler_params=pltpu.CompilerParams(
            collective_id=1, has_side_effects=True, vmem_limit_bytes=VMEM_LIMIT
        ),
        cost_estimate=pl.CostEstimate(flops=0, bytes_accessed=300 * 2**20, transcendentals=0),
    )(qkv_pack, w_gate, w_up, out_own, down_own, gain_tile, tokens, lengths, frequency, spread_cos, spread_sin)


def attend_rows(net, block):
    return [
        pl.ds(pl.multiple_of(mixed_index(b, net.base) * block, block), block) for b in range(TP)
    ]


def attend_forward_block(net, qkv_ref, len_ref, conts, mixed_ref, lse_ref):
    total, width = qkv_ref.shape
    block = total // TP
    q_heads = width // (2 * HEAD_DIM)
    kv_heads = q_heads // 2
    factor = 1.0 / math.sqrt(HEAD_DIM)
    key_at = q_heads * HEAD_DIM
    value_at = key_at + kv_heads * HEAD_DIM
    places = attend_rows(net, block)
    nt = (((1,), (1,)), ((), ()))
    for i in range(TP):
        row_seg = block_segments(len_ref, conts, block, i, True)
        masks = [
            block_mask(row_seg, block_segments(len_ref, conts, block, j, False), i == j, block)
            for j in range(i + 1)
        ]
        for h in range(q_heads):
            kv = h // 2
            query = qkv_ref[places[i], h * HEAD_DIM : (h + 1) * HEAD_DIM]
            scores = []
            for j in range(i + 1):
                key = qkv_ref[places[j], key_at + kv * HEAD_DIM : key_at + (kv + 1) * HEAD_DIM]
                s = lax.dot_general(query, key, nt, preferred_element_type=jnp.float32) * factor
                scores.append(jnp.where(masks[j], s, NEGATIVE))
            peak = scores[0].max(axis=1, keepdims=True)
            for s in scores[1:]:
                peak = jnp.maximum(peak, s.max(axis=1, keepdims=True))
            total_e = jnp.zeros((block, 1), jnp.float32)
            mixed = jnp.zeros((block, HEAD_DIM), jnp.float32)
            for j in range(i + 1):
                e = jnp.exp(scores[j] - peak)
                total_e = total_e + e.sum(axis=1, keepdims=True)
                value = qkv_ref[places[j], value_at + kv * HEAD_DIM : value_at + (kv + 1) * HEAD_DIM]
                mixed = mixed + jnp.dot(
                    e.astype(jnp.bfloat16), value, preferred_element_type=jnp.float32
                )
            mixed_ref[places[i], h * HEAD_DIM : (h + 1) * HEAD_DIM] = (mixed / total_e).astype(
                jnp.bfloat16
            )
            lse_ref[i, :, h : h + 1] = peak + jnp.log(total_e)


def normalize(values, gain_row):
    scale = lax.rsqrt(jnp.mean(values * values, axis=-1, keepdims=True) + EPSILON)
    return (values * scale * gain_row).astype(jnp.bfloat16)


def spread_begin(net, buf):
    return (net.remote(buf.at[0], buf.at[1], "x"), net.remote(buf.at[0], buf.at[2], "core"))


def spread_each(net, buf, begun, work):
    over_x, over_core = begun
    work(0)
    over_core.wait()
    work(2)
    over_x.wait()
    forward = net.remote(buf.at[1], buf.at[3], "core")
    work(1)
    forward.wait()
    work(3)


def collect(net, part, far_out, far_in, pass_out, pass_in):
    low = lambda v: v.astype(jnp.bfloat16)
    far_out[0] = low(part(3))
    first = net.remote(far_out.at[0], far_in.at[0], "core")
    near = part(1)
    first.wait()
    pass_out[...] = low(near + far_in[0].astype(jnp.float32))
    passed = net.remote(pass_out, pass_in, "x")
    far_out[1] = low(part(2))
    second = net.remote(far_out.at[1], far_in.at[1], "core")
    own = part(0)
    second.wait()
    own = own + far_in[1].astype(jnp.float32)
    passed.wait()
    return own + pass_in[...].astype(jnp.float32)


def forward_kernel(programs, has_cot, conts, n_moving, *refs):
    x_own, gain_a, gain_f, cos_ref, sin_ref, lengths = refs[:6]
    refs = refs[6:]
    if has_cot:
        cot, refs = refs[0], refs[1:]
    refs = refs[n_moving:]
    moving, refs = refs[:n_moving], refs[n_moving:]
    (x_next, middle_ref, lse_ref, x_low, rows_out, qkv_out, mixed_out, ffn_rows_out, gate_out, up_out, act_out) = refs[:11]
    refs = refs[11:]
    if has_cot:
        branch_out, refs, branch = refs[0], refs[1:-1], refs[-1]
    (rows, ffn_rows, w_qkv, w_o, w_gu, w_d, qkv, mixed, gate, up, act,
     far_out, far_in, pass_out, pass_in, send_sems, recv_sems, local_sems) = refs
    net = Net(send_sems, recv_sems, local_sems)
    steps = [[(kind, moving[n], low, count) for kind, n, low, count in step] for step in programs]
    block, depth = x_own.shape
    load_qkv = net.local(moving[0], w_qkv)
    load_o = net.local(moving[1], w_o)
    net.greet(("core", "x", "y", "z1", "z2", "z3"), "group" if has_cot else None)
    net.advance(steps[0])
    if has_cot:
        bring = net.regroup(cot, branch.at[0], "group")
    rows[0] = normalize(x_own[...], gain_a[...])
    begun = spread_begin(net, rows)
    load_qkv.wait()

    def project(s):
        raw = jnp.dot(
            rows[s], w_qkv[...].reshape(depth, -1), preferred_element_type=jnp.float32
        )
        at = slice(s * block, (s + 1) * block)
        turned = raw * cos_ref[at, :] + head_partner(raw, HEAD_DIM // 2) * sin_ref[at, :]
        qkv[at, :] = turned.astype(jnp.bfloat16)

    spread_each(net, rows, begun, project)
    net.keep(rows, rows_out)
    net.keep(qkv, qkv_out)
    net.advance(steps[1])
    attend_forward_block(net, qkv, lengths, conts, mixed, lse_ref)
    net.keep(mixed, mixed_out)
    net.advance(steps[2])
    load_o.wait()

    def out_part(s):
        return jnp.dot(
            mixed[s * block : (s + 1) * block, :],
            w_o[...].reshape(-1, depth),
            preferred_element_type=jnp.float32,
        )

    middle = x_own[...] + collect(
        net, out_part, far_out, far_in.at[0], pass_out, pass_in.at[0]
    )
    middle_ref[...] = middle
    net.advance(steps[3])
    net.arrived(moving[3])
    load_d = net.local(moving[3], w_d)
    ffn_rows[0] = normalize(middle, gain_f[...])
    begun = spread_begin(net, ffn_rows)
    if has_cot:
        bring.wait()
        over_x, over_core = spread_begin(net, branch)
    net.arrived(moving[2])
    load_gu = net.local(moving[2], w_gu)
    net.advance(steps[4])
    load_d.wait()
    load_gu.wait()
    units = act.shape[2]

    def expand(s):
        value = ffn_rows[s]
        gating = jnp.dot(
            value, w_gu[:, :, :, :, :units].reshape(depth, units), preferred_element_type=jnp.float32
        )
        upward = jnp.dot(
            value, w_gu[:, :, :, :, units:].reshape(depth, units), preferred_element_type=jnp.float32
        )
        gate[s] = gating.astype(jnp.bfloat16)
        up[s] = upward.astype(jnp.bfloat16)
        act[s] = (gating * jax.nn.sigmoid(gating) * upward).astype(jnp.bfloat16)

    spread_each(net, ffn_rows, begun, expand)
    if has_cot:
        over_x.wait()
        forward = net.remote(branch.at[1], branch.at[3], "core")
    net.keep(ffn_rows, ffn_rows_out)
    net.keep(gate, gate_out)
    net.keep(up, up_out)
    net.keep(act, act_out)

    def down_part(s):
        return jnp.dot(act[s], w_d[...].reshape(-1, depth), preferred_element_type=jnp.float32)

    result = middle_ref[...] + collect_during(
        net,
        down_part,
        (far_out, far_in.at[1], pass_out, pass_in.at[1]),
        lambda: net.advance(steps[5]),
    )
    if has_cot:
        over_core.wait()
        forward.wait()
        net.keep(branch, branch_out)
    x_next[...] = result
    x_low[...] = result.astype(jnp.bfloat16)
    net.finish()


def forward_layer(programs, cot, cid, conts, x_own, gain_a, gain_f, cosine, sine, lengths, moving):
    bf, f32 = jnp.bfloat16, jnp.float32
    block, depth = x_own.shape
    total, qkv_width = cosine.shape
    units = moving[2].shape[4] // 2
    q_heads = qkv_width // (2 * HEAD_DIM)
    shape = jax.ShapeDtypeStruct
    outs = [shape(m.shape, m.dtype) for m in moving] + [
        shape((block, depth), f32),
        shape((block, depth), f32),
        shape((TP, block, q_heads), f32),
        shape((block, depth), bf),
        shape((TP, block, depth), bf),
        shape((total, qkv_width), bf),
        shape((total, qkv_width // 2), bf),
        shape((TP, block, depth), bf),
        shape((TP, block, units), bf),
        shape((TP, block, units), bf),
        shape((TP, block, units), bf),
    ]
    n = len(moving)
    given = [] if cot is None else [cot]
    c = len(given)
    outs += [shape((TP, block, depth), bf)] * c
    scratch = [
        pltpu.VMEM((TP, block, depth), bf),
        pltpu.VMEM((TP, block, depth), bf),
        pltpu.VMEM(moving[0].shape, bf),
        pltpu.VMEM(moving[1].shape, bf),
        pltpu.VMEM(moving[2].shape, bf),
        pltpu.VMEM(moving[3].shape, bf),
        pltpu.VMEM((total, qkv_width), bf),
        pltpu.VMEM((total, qkv_width // 2), bf),
        pltpu.VMEM((TP, block, units), bf),
        pltpu.VMEM((TP, block, units), bf),
        pltpu.VMEM((TP, block, units), bf),
        pltpu.VMEM((2, block, depth), bf),
        pltpu.VMEM((2, 2, block, depth), bf),
        pltpu.VMEM((block, depth), bf),
        pltpu.VMEM((2, block, depth), bf),
    ] + sems(80, 24) + [pltpu.VMEM((TP, block, depth), bf)] * c
    return pl.pallas_call(
        functools.partial(forward_kernel, programs, bool(c), conts, n),
        out_shape=outs,
        in_specs=[IN_VMEM] * (6 + c) + [ANYWHERE] * n,
        out_specs=[ANYWHERE] * n + [IN_VMEM] * 4 + [ANYWHERE] * (7 + c),
        scratch_shapes=scratch,
        input_output_aliases={6 + c + i: i for i in range(n)},
        compiler_params=pltpu.CompilerParams(
            collective_id=cid, has_side_effects=True, vmem_limit_bytes=VMEM_LIMIT
        ),
        cost_estimate=pl.CostEstimate(
            flops=16 * 10**9, bytes_accessed=400 * 2**20, transcendentals=10**7
        ),
    )(x_own, gain_a, gain_f, cosine, sine, lengths, *given, *moving)


def moved_shape(kind, source):
    shape = source.shape
    if kind in ("y", "whole_y"):
        kept = shape
    elif kind == "g":
        kept = shape
    elif kind == "zc":
        kept = (3, shape[0]) + shape[2:]
    elif kind in ("z", "t"):
        kept = (3,) + shape[1:]
    else:
        kept = (3,) + shape
    return jax.ShapeDtypeStruct(kept, source.dtype)


def begin_move(net, kind, source, target):
    if kind in ("y", "whole_y"):
        return [net.remote(source, target, "y")]
    if kind == "g":
        return [net.regroup(source, target, "home")]
    copies = []
    for name, bits in RANK_PEERS:
        if kind == "z":
            copies.append(
                net.remote(source.at[flip_index(net.z, bits)], target.at[bits - 1], f"z{bits}")
            )
        elif kind == "zc":
            copies.append(
                net.remote(source.at[:, flip_index(net.z, bits)], target.at[bits - 1], f"z{bits}")
            )
        elif kind == "whole_z":
            copies.append(net.remote(source, target.at[bits - 1], f"z{bits}"))
        elif kind == "t":
            copies.append(
                net.remote(source.at[flip_index(net.q, bits)], target.at[bits - 1], name)
            )
        else:
            copies.append(net.remote(source, target.at[bits - 1], name))
    return copies


def begin_moves(net, kinds, sources, targets):
    for kind, source, target in zip(kinds, sources, targets):
        net.flying += begin_move(net, kind, source, target)


def greet_all(net, kinds):
    net.greet(PEERS, "home" if "g" in kinds else None)


def tail_kernel(
    gain_part, sgu_in, so_in, qkv_own_in, qkv_other, bqkv, up_low,
    gain_out, out_sum, b_gu, b_qkv, t_gu, t_qkv, t_qkv1, back,
    sgu, so, s_qkv, qkv_got, gu_one, gu_pass, gu_two, o_one, o_pass, o_two, q_one, q_pass, q_two,
    gain_t, gain_a, gain_z, gain_b, gain_y, send_sems, recv_sems, local_sems,
):
    net = Net(send_sems, recv_sems, local_sems)
    f32, bf = jnp.float32, jnp.bfloat16
    z, q = net.z, net.q
    z1, z2, z3 = (flip_index(z, bits) for bits in (1, 2, 3))
    loads = [net.local(sgu_in, sgu), net.local(so_in, so), net.local(qkv_own_in, s_qkv)]
    net.greet(PEERS, "home")
    over_y = net.remote(qkv_other, qkv_got, "y")

    def first_hop(source, target, part):
        return [
            net.remote(source.at[part + (z3,)], target.at[(1,) + part], "z1"),
            net.remote(source.at[part + (z1,)], target.at[(0,) + part], "z1"),
        ]

    halves = [(pl.ds(0, 2),), (pl.ds(2, 2),)]
    gu_first = [first_hop(sgu_in, gu_one, part) for part in halves]
    o_first = first_hop(so_in, o_one, ())
    gains = [net.remote(gain_part, gain_t.at[bits - 1], name) for name, bits in RANK_PEERS]
    net.flying += begin_move(net, "t", bqkv, t_qkv1)
    net.flying += begin_move(net, "g", up_low, back)
    for copy in loads:
        copy.wait()
    over_y.wait()
    s_qkv[...] = (s_qkv[...].astype(f32) + qkv_got[...].astype(f32)).astype(bf)
    every = (pl.ds(0, TP),)
    q_first = first_hop(s_qkv, q_one, every)
    for copy in gains:
        copy.wait()
    gain_a[...] = gain_part[...] + gain_t[0] + gain_t[1] + gain_t[2]
    gains = [net.remote(gain_a, gain_z.at[bits - 1], f"z{bits}") for bits in (1, 2, 3)]

    def second_hop(own, one, passing, two, part, first):
        first[0].wait()
        passing[part or (Ellipsis,)] = (
            own[part + (z2,)].astype(f32) + one[(1,) + part].astype(f32)
        ).astype(bf)
        at = (lambda ref: ref.at[part]) if part else (lambda ref: ref)
        return net.remote(at(passing), at(two), "z2")

    gu_second = [
        second_hop(sgu, gu_one, gu_pass, gu_two, part, first) for part, first in zip(halves, gu_first)
    ]
    o_second = second_hop(so, o_one, o_pass, o_two, (), o_first)
    q_second = second_hop(s_qkv, q_one, q_pass, q_two, every, q_first)
    for copy in gains:
        copy.wait()
    gain_b[...] = gain_a[...] + gain_z[0] + gain_z[1] + gain_z[2]
    gain_over_y = net.remote(gain_b, gain_y, "y")

    def total(own, one, two, part):
        whole = part or (Ellipsis,)
        return (
            own[part + (z,)].astype(f32) + one[(0,) + part].astype(f32) + two[whole].astype(f32)
        )

    for part, first, second in zip(halves, gu_first, gu_second):
        first[1].wait()
        second.wait()
        b_gu[part] = total(sgu, gu_one, gu_two, part).astype(bf)
    net.flying += begin_move(net, "t", b_gu, t_gu)
    o_first[1].wait()
    o_second.wait()
    out_sum[...] = total(so, o_one, o_two, ())
    q_first[1].wait()
    q_second.wait()
    b_qkv[...] = total(s_qkv, q_one, q_two, every).astype(bf)
    net.flying += begin_move(net, "t", b_qkv, t_qkv)
    gain_over_y.wait()
    gain_out[...] = gain_b[...] + gain_y[...]
    net.finish()


def run_tail(cid, gain_part, sgu, so, qkv_own, qkv_other, bqkv, up_low):
    bf, f32 = jnp.bfloat16, jnp.float32
    shape = jax.ShapeDtypeStruct
    gu_block = (TP,) + sgu.shape[2:]
    o_block = so.shape[1:]
    q_block = (TP,) + qkv_own.shape[2:]
    three = lambda block: (3,) + block[1:]
    return pl.pallas_call(
        tail_kernel,
        out_shape=[
            shape(gain_part.shape, f32),
            shape(o_block, f32),
            shape(gu_block, bf),
            shape(q_block, bf),
            shape(three(gu_block), bf),
            shape(three(q_block), bf),
            shape(three(q_block), bf),
            shape(up_low.shape, bf),
        ],
        in_specs=[IN_VMEM] + [ANYWHERE] * 6,
        out_specs=[IN_VMEM] * 4 + [ANYWHERE] * 4,
        scratch_shapes=[
            pltpu.VMEM(sgu.shape, bf),
            pltpu.VMEM(so.shape, bf),
            pltpu.VMEM(qkv_own.shape, bf),
            pltpu.VMEM(qkv_own.shape, bf),
        ]
        + [
            pltpu.VMEM(dims, bf)
            for block in (gu_block, o_block, q_block)
            for dims in ((2,) + block, block, block)
        ]
        + [
            pltpu.VMEM(dims, f32)
            for dims in (
                (3,) + gain_part.shape, gain_part.shape, (3,) + gain_part.shape, gain_part.shape, gain_part.shape
            )
        ]
        + sems(48, 8),
        compiler_params=pltpu.CompilerParams(
            collective_id=cid, has_side_effects=True, vmem_limit_bytes=VMEM_LIMIT
        ),
        cost_estimate=pl.CostEstimate(flops=0, bytes_accessed=200 * 2**20, transcendentals=0),
    )(gain_part, sgu, so, qkv_own, qkv_other, bqkv, up_low)


def norm_backward(values, gain_row, incoming):
    inv = lax.rsqrt(jnp.mean(values * values, axis=-1, keepdims=True) + EPSILON)
    weighted = incoming * gain_row
    inner = jnp.mean(weighted * values, axis=-1, keepdims=True)
    grad = inv * weighted - values * (inv * inv * inv * inner)
    return grad, jnp.sum(incoming * values * inv, axis=0, keepdims=True)


def collect_during(net, part, bufs, meanwhile):
    far_out, far_in, pass_out, pass_in = bufs
    low = lambda v: v.astype(jnp.bfloat16)
    far_out[0] = low(part(3))
    first = net.remote(far_out.at[0], far_in.at[0], "core")
    near = part(1)
    first.wait()
    pass_out[...] = low(near + far_in[0].astype(jnp.float32))
    passed = net.remote(pass_out, pass_in, "x")
    far_out[1] = low(part(2))
    second = net.remote(far_out.at[1], far_in.at[1], "core")
    own = part(0)
    second.wait()
    own = own + far_in[1].astype(jnp.float32)
    meanwhile()
    passed.wait()
    return own + pass_in[...].astype(jnp.float32)


NT = (((1,), (1,)), ((), ()))
TN = (((0,), (0,)), ((), ()))


def dot_nt(left, right):
    return lax.dot_general(left, right, NT, preferred_element_type=jnp.float32)


def dot_tn(left, right):
    return lax.dot_general(left, right, TN, preferred_element_type=jnp.float32)


def ffn_backward_kernel(kinds, given, *refs):
    n = len(kinds)
    middle, gain, source_in = refs[:3]
    acts, rows_in, gates, ups, mixed_in, wd_in, wgu_in, wo_in = refs[3:11]
    refs = refs[11:]
    sources, targets, refs = refs[:n], refs[n : 2 * n], refs[2 * n :]
    (grad_middle, gain_grad, dmixed_out, d_own, d_got, gu_own, gu_other, o_own, o_other) = refs[:9]
    (branch, proj, act, rows, gate, up, mixed, dmixed, w_d, w_gu, w_o, g_down, g_gu, g_out,
     far_out, far_in, pass_out, pass_in, send_sems, recv_sems, local_sems) = refs[9:]
    net = Net(send_sems, recv_sems, local_sems)
    block, depth = middle.shape
    units = act.shape[2]
    total = TP * block
    loads = {}
    if given:
        loads["branch"] = net.local(source_in, branch)
    for name, src, dst in (
        ("w_d", wd_in, w_d), ("gate", gates, gate), ("up", ups, up), ("act", acts, act),
        ("w_gu", wgu_in, w_gu), ("rows", rows_in, rows), ("w_o", wo_in, w_o), ("mixed", mixed_in, mixed),
    ):
        loads[name] = net.local(src, dst)
    greet_all(net, kinds)
    begin_moves(net, kinds, sources, targets)
    if given:
        loads["branch"].wait()
    else:
        branch[0] = source_in[...].astype(jnp.bfloat16)
        begun = spread_begin(net, branch)
    loads["w_d"].wait()
    loads["gate"].wait()
    loads["up"].wait()

    def through(s):
        grad_act = dot_nt(branch[s], w_d[...].reshape(units, depth))
        gating = gate[s].astype(jnp.float32)
        upward = up[s].astype(jnp.float32)
        sig = jax.nn.sigmoid(gating)
        shared = grad_act * sig
        gate[s] = (shared * upward * (1.0 + gating * (1.0 - sig))).astype(jnp.bfloat16)
        up[s] = (shared * gating).astype(jnp.bfloat16)

    if given:
        for s in (3, 1, 2, 0):
            through(s)
    else:
        spread_each(net, branch, begun, through)
    loads["act"].wait()
    theirs, ours = 1 - net.y, net.y
    drows, urows = g_down.shape[2], g_gu.shape[3]
    dwide, uwide = 2 * drows, 2 * TP * urows

    def down_half(side):
        def tile(m, carry):
            lanes = pl.ds(pl.multiple_of((side * 2 + m) * dwide, dwide), dwide)
            grad = dot_tn(act[:, :, lanes].reshape(total, dwide), branch[...].reshape(total, depth))
            g_down[side, pl.ds(2 * m, 2)] = grad.astype(jnp.bfloat16).reshape(2, drows, depth)
            return carry

        lax.fori_loop(0, 2, tile, 0)

    def gu_half(side):
        def tile(m, carry):
            lanes = pl.ds(pl.multiple_of((side * 2 + m) * uwide, uwide), uwide)
            left = rows[:, :, lanes].reshape(total, uwide)
            for ref, at in ((gate, 0), (up, units)):
                grad = dot_tn(left, ref[...].reshape(total, units)).astype(jnp.bfloat16)
                g_gu[side, pl.ds(2 * m, 2), :, :, at : at + units] = grad.reshape(2, TP, urows, units)
            return carry

        lax.fori_loop(0, 2, tile, 0)

    down_half(theirs)
    net.flying.append(net.remote(g_down.at[theirs], d_got, "y"))
    loads["w_gu"].wait()
    loads["rows"].wait()

    def back(s):
        return dot_nt(gate[s], w_gu[:, :, :, :, :units].reshape(depth, units)) + dot_nt(
            up[s], w_gu[:, :, :, :, units:].reshape(depth, units)
        )

    def meanwhile():
        gu_half(theirs)
        net.keep(g_gu.at[theirs], gu_other)
        gu_half(ours)
        net.keep(g_gu.at[ours], gu_own)
        down_half(ours)
        net.keep(g_down.at[ours], d_own)

    incoming = collect_during(net, back, (far_out, far_in, pass_out, pass_in), meanwhile)
    part, gain_part = norm_backward(middle[...], gain[...], incoming)
    gain_grad[...] = gain_part
    grad_mid = (branch[0].astype(jnp.float32) if given else source_in[...]) + part
    grad_middle[...] = grad_mid
    proj[0] = grad_mid.astype(jnp.bfloat16)
    begun = spread_begin(net, proj)
    loads["w_o"].wait()
    loads["mixed"].wait()

    def mix_back(s):
        dmixed[s * block : (s + 1) * block, :] = dot_nt(
            proj[s], w_o[...].reshape(-1, depth)
        ).astype(jnp.bfloat16)

    spread_each(net, proj, begun, mix_back)
    net.keep(dmixed, dmixed_out)
    grad = dot_tn(mixed[...], proj[...].reshape(total, depth)).astype(jnp.bfloat16)
    g_out[...] = grad.reshape(g_out.shape)
    net.keep(g_out.at[ours], o_own)
    net.keep(g_out.at[theirs], o_other)
    net.finish()


def ffn_backward(cid, moves, source, given, middle, gain, acts, rows, gates, ups, mixed, w_d, w_gu, w_o):
    bf, f32 = jnp.bfloat16, jnp.float32
    shape = jax.ShapeDtypeStruct
    block, depth = middle.shape
    units = gates.shape[2]
    total, mixed_width = mixed.shape
    kinds = tuple(kind for kind, _ in moves)
    sources = [source for _, source in moves]
    n = len(moves)
    drows, urows, orows = w_d.shape[3], w_gu.shape[3], w_o.shape[3]
    outs = [moved_shape(kind, source) for kind, source in moves] + [
        shape((block, depth), f32),
        shape((1, depth), f32),
        shape((total, mixed_width), bf),
        shape((TP, drows, depth), bf),
        shape((TP, drows, depth), bf),
        shape((TP, TP, urows, 2 * units), bf),
        shape((TP, TP, urows, 2 * units), bf),
        shape((TP, orows, depth), bf),
        shape((TP, orows, depth), bf),
    ]
    scratch = [
        pltpu.VMEM((TP, block, depth), bf),
        pltpu.VMEM((TP, block, depth), bf),
        pltpu.VMEM((TP, block, units), bf),
        pltpu.VMEM((TP, block, depth), bf),
        pltpu.VMEM((TP, block, units), bf),
        pltpu.VMEM((TP, block, units), bf),
        pltpu.VMEM((total, mixed_width), bf),
        pltpu.VMEM((total, mixed_width), bf),
        pltpu.VMEM(w_d.shape, bf),
        pltpu.VMEM(w_gu.shape, bf),
        pltpu.VMEM(w_o.shape, bf),
        pltpu.VMEM((2, TP, drows, depth), bf),
        pltpu.VMEM((2, TP, TP, urows, 2 * units), bf),
        pltpu.VMEM((2, TP, orows, depth), bf),
        pltpu.VMEM((2, block, depth), bf),
        pltpu.VMEM((2, block, depth), bf),
        pltpu.VMEM((block, depth), bf),
        pltpu.VMEM((block, depth), bf),
    ] + sems(48, 20)
    operands = [middle, gain, source, acts, rows, gates, ups, mixed, w_d, w_gu, w_o]
    return pl.pallas_call(
        functools.partial(ffn_backward_kernel, kinds, given),
        out_shape=outs,
        in_specs=[IN_VMEM] * 2 + [ANYWHERE if given else IN_VMEM] + [ANYWHERE] * (8 + n),
        out_specs=[ANYWHERE] * n + [IN_VMEM] * 2 + [ANYWHERE] * 7,
        scratch_shapes=scratch,
        compiler_params=pltpu.CompilerParams(
            collective_id=cid, has_side_effects=True, vmem_limit_bytes=VMEM_LIMIT
        ),
        cost_estimate=pl.CostEstimate(
            flops=24 * 10**9, bytes_accessed=200 * 2**20, transcendentals=10**6
        ),
    )(*operands, *sources)


def attend_backward_block(net, qkv_ref, grad_ref, mixed_ref, lse_ref, len_ref, conts, acc_ref):
    total, width = qkv_ref.shape
    block = total // TP
    q_heads = width // (2 * HEAD_DIM)
    kv_heads = q_heads // 2
    factor = 1.0 / math.sqrt(HEAD_DIM)
    key_at = q_heads * HEAD_DIM
    value_at = key_at + kv_heads * HEAD_DIM
    places = attend_rows(net, block)
    acc_ref[:, key_at:] = jnp.zeros((total, width - key_at), jnp.float32)
    for i in range(TP):
        row_seg = block_segments(len_ref, conts, block, i, True)
        masks = [
            block_mask(row_seg, block_segments(len_ref, conts, block, j, False), i == j, block)
            for j in range(i + 1)
        ]
        for h in range(q_heads):
            kv = h // 2
            lanes = slice(h * HEAD_DIM, (h + 1) * HEAD_DIM)
            query = qkv_ref[places[i], lanes]
            grad = grad_ref[places[i], lanes]
            lse = lse_ref[i, :, h : h + 1]
            inner = jnp.sum(
                grad.astype(jnp.float32) * mixed_ref[places[i], lanes].astype(jnp.float32),
                axis=1,
                keepdims=True,
            )
            grad_query = jnp.zeros((block, HEAD_DIM), jnp.float32)
            key_lanes = slice(key_at + kv * HEAD_DIM, key_at + (kv + 1) * HEAD_DIM)
            value_lanes = slice(value_at + kv * HEAD_DIM, value_at + (kv + 1) * HEAD_DIM)
            for j in range(i + 1):
                key = qkv_ref[places[j], key_lanes]
                value = qkv_ref[places[j], value_lanes]
                s = dot_nt(query, key) * factor
                prob = jnp.where(masks[j], jnp.exp(s - lse), 0.0)
                grad_prob = dot_nt(grad, value)
                grad_score = (prob * (grad_prob - inner)).astype(jnp.bfloat16)
                grad_query = grad_query + jnp.dot(
                    grad_score, key, preferred_element_type=jnp.float32
                )
                acc_ref[places[j], key_lanes] += dot_tn(grad_score, query) * factor
                acc_ref[places[j], value_lanes] += dot_tn(prob.astype(jnp.bfloat16), grad)
            acc_ref[places[i], lanes] = grad_query * factor


def attn_backward_kernel(kinds, conts, *refs):
    n = len(kinds)
    (grad_middle, hidden, gain, qkv, dmixed, mixed, lse, lengths, cos_ref, sin_ref) = refs[:10]
    rows_in, w_in = refs[10:12]
    sources, targets, refs = refs[12 : 12 + n], refs[12 + n : 12 + 2 * n], refs[12 + 2 * n :]
    upstream, up_low, gain_grad, qkv_own, qkv_other = refs[:5]
    (acc, dqkv, rows, w_qkv, g_qkv, far_out, far_in, pass_out, pass_in,
     send_sems, recv_sems, local_sems) = refs[5:]
    net = Net(send_sems, recv_sems, local_sems)
    block, depth = hidden.shape
    total = TP * block
    load_rows = net.local(rows_in, rows)
    load_w = net.local(w_in, w_qkv)
    greet_all(net, kinds)
    begin_moves(net, kinds, sources, targets)
    attend_backward_block(net, qkv, dmixed, mixed, lse, lengths, conts, acc)
    for s in range(TP):
        at = slice(s * block, (s + 1) * block)
        value = acc[at, :]
        turned = value * cos_ref[at, :] - head_partner(value, HEAD_DIM // 2) * sin_ref[at, :]
        dqkv[at, :] = turned.astype(jnp.bfloat16)
    load_w.wait()
    load_rows.wait()
    urows = g_qkv.shape[2]
    wide = 2 * TP * urows

    def back(s):
        return dot_nt(dqkv[s * block : (s + 1) * block, :], w_qkv[...].reshape(depth, -1))

    def meanwhile():
        def tile(m, carry):
            lanes = pl.ds(pl.multiple_of(m * wide, wide), wide)
            grad = dot_tn(rows[:, :, lanes].reshape(total, wide), dqkv[...])
            g_qkv[pl.ds(2 * m, 2)] = grad.astype(jnp.bfloat16).reshape(2, TP, urows, -1)
            return carry

        lax.fori_loop(0, TP, tile, 0)
        net.keep(g_qkv.at[pl.ds(net.y * TP, TP)], qkv_own)
        net.keep(g_qkv.at[pl.ds((1 - net.y) * TP, TP)], qkv_other)

    incoming = collect_during(net, back, (far_out, far_in, pass_out, pass_in), meanwhile)
    part, gain_part = norm_backward(hidden[...], gain[...], incoming)
    gain_grad[...] = gain_part
    result = grad_middle[...] + part
    upstream[...] = result
    up_low[...] = result.astype(jnp.bfloat16)
    net.finish()


def attn_backward(
    cid, moves, conts, grad_middle, hidden, gain, qkv, dmixed, mixed, lse, lengths, cosine, sine, rows, w_qkv
):
    bf, f32 = jnp.bfloat16, jnp.float32
    shape = jax.ShapeDtypeStruct
    block, depth = hidden.shape
    total, width = qkv.shape
    kinds = tuple(kind for kind, _ in moves)
    sources = [source for _, source in moves]
    n = len(moves)
    urows = w_qkv.shape[3]
    outs = [moved_shape(kind, source) for kind, source in moves] + [
        shape((block, depth), f32),
        shape((block, depth), bf),
        shape((1, depth), f32),
        shape((TP, TP, urows, width), bf),
        shape((TP, TP, urows, width), bf),
    ]
    scratch = [
        pltpu.VMEM((total, width), f32),
        pltpu.VMEM((total, width), bf),
        pltpu.VMEM((TP, block, depth), bf),
        pltpu.VMEM(w_qkv.shape, bf),
        pltpu.VMEM((2 * TP, TP, urows, width), bf),
        pltpu.VMEM((2, block, depth), bf),
        pltpu.VMEM((2, block, depth), bf),
        pltpu.VMEM((block, depth), bf),
        pltpu.VMEM((block, depth), bf),
    ] + sems(48, 8)
    return pl.pallas_call(
        functools.partial(attn_backward_kernel, kinds, conts),
        out_shape=outs,
        in_specs=[IN_VMEM] * 10 + [ANYWHERE] * (2 + n),
        out_specs=[ANYWHERE] * n + [IN_VMEM] * 3 + [ANYWHERE] * 2,
        scratch_shapes=scratch,
        compiler_params=pltpu.CompilerParams(
            collective_id=cid, has_side_effects=True, vmem_limit_bytes=VMEM_LIMIT
        ),
        cost_estimate=pl.CostEstimate(
            flops=16 * 10**9, bytes_accessed=200 * 2**20, transcendentals=10**7
        ),
    )(grad_middle, hidden, gain, qkv, dmixed, mixed, lse, lengths, cosine, sine, rows, w_qkv, *sources)


def add_low(own, got):
    return (own.astype(jnp.float32) + got.astype(jnp.float32)).astype(jnp.bfloat16)


def z_total(summed, got, axis):
    own = lax.dynamic_index_in_dim(summed, lax.axis_index("fsdp"), axis, keepdims=False)
    return (own.astype(jnp.float32) + jnp.sum(got.astype(jnp.float32), axis=0)).astype(jnp.bfloat16)


def end_kernel(step, qw, kw, *refs):
    layers, refs = (refs[:7], refs[7:15]), refs[15:]
    x_outs, back, refs = refs[:2], refs[2], refs[3:]
    out_x, out_back, out_q, out_k, out_v, out_o, out_g, out_u, out_d = refs
    q = lax.rem(lax.axis_index("dp"), TP)
    z = lax.axis_index("fsdp")
    low, high = lax.rem(q, 2) == 1, lax.div(q, 2) == 1

    def columns(blocks, got):
        pieces = [blocks[q]] + [got[k] for k in range(3)]
        a = [jnp.where(low, pieces[i ^ 1], pieces[i]) for i in range(4)]
        return [jnp.where(high, a[i ^ 2], a[i]).astype(jnp.float32) for i in range(4)]

    def lay(target, layer, pieces, at, width):
        half = width // 2
        for n, piece in enumerate(pieces):
            for side in range(2):
                to = (side * TP + n) * half
                target[layer, :, to : to + half] = piece[:, at + side * half : at + (side + 1) * half]

    for layer in range(2):
        bqkv, tqkv, bgu, tgu = layers[layer][:4]
        pieces = columns(bqkv, tqkv)
        lay(out_q, layer, pieces, 0, qw)
        lay(out_k, layer, pieces, qw, kw)
        lay(out_v, layer, pieces, qw + kw, kw)
        pieces = columns(bgu, tgu)
        lay(out_g, layer, pieces, 0, 2 * step)
        lay(out_u, layer, pieces, 2 * step, 2 * step)
        sums = [(*layers[layer][-2:], out_d)]
        if layer == 0:
            out_o[0] = layers[0][4][...]
        else:
            sums.append((*layers[1][4:6], out_o))
        for summed, got, target in sums:
            value = summed[z].astype(jnp.float32)
            for k in range(3):
                value = value + got[k].astype(jnp.float32)
            target[layer] = value
        out_x[layer] = x_outs[layer][...]
    out_back[...] = back[...].astype(jnp.float32)


def end_assembly(step, qw, kw, pieces, x_outs, back):
    f32 = jnp.float32
    shape = jax.ShapeDtypeStruct
    block, depth = back.shape
    rows = pieces[0].shape[1]
    drows = pieces[5].shape[1]
    outs = [
        shape((2, block, depth), jnp.bfloat16),
        shape((block, depth), f32),
        shape((2, rows, TP * qw), f32),
        shape((2, rows, TP * kw), f32),
        shape((2, rows, TP * kw), f32),
        shape((2, rows, depth), f32),
        shape((2, rows, TP * 2 * step), f32),
        shape((2, rows, TP * 2 * step), f32),
        shape((2, drows, depth), f32),
    ]
    return pl.pallas_call(
        functools.partial(end_kernel, step, qw, kw),
        out_shape=outs,
        in_specs=[IN_VMEM] * 18,
        out_specs=[IN_VMEM] * 9,
        compiler_params=pltpu.CompilerParams(vmem_limit_bytes=VMEM_LIMIT),
    )(*pieces, *x_outs, back)


def column_pack(weights):
    parts = []
    for weight in weights:
        layers, rows, width = weight.shape
        view = weight.reshape(layers, rows, 2, TP, width // (2 * TP))
        parts.append(view.transpose(0, 3, 1, 2, 4).reshape(layers, TP, rows, width // TP))
    return jnp.concatenate(parts, axis=3)


def fast_device(
    tokens, gain_attn, w_query, w_key, w_value, w_out, gain_ffn, w_gate, w_up, w_down, lengths, cotangent
):
    depth = tokens.shape[1]
    shard = w_query.shape[1]
    conts = lengths.shape[1]
    halfway = HEAD_DIM // 2
    qw, kw = w_query.shape[2] // TP, w_key.shape[2] // TP
    step = w_gate.shape[2] // (2 * TP)
    frequency = ROPE_BASE ** (-jnp.arange(halfway, dtype=jnp.float32) * 2.0 / HEAD_DIM)
    lane = jnp.arange(128)[:, None]
    column = jnp.arange(qw + 2 * kw)[None]
    turned = column < qw + kw
    frequency = jnp.pad(frequency, (0, 128 - halfway))[None]
    picks = (lane == jnp.where(turned, column % halfway, halfway)).astype(jnp.float32)
    signed = picks * jnp.where(turned, jnp.where(column % HEAD_DIM < halfway, -1.0, 1.0), 0.0)
    gain_tile = jnp.pad(
        jnp.concatenate([gain_attn, gain_ffn], axis=0).astype(jnp.float32), ((0, 4), (0, 128 - shard))
    )
    len_tile = jnp.pad(lengths, ((0, 7), (0, 128 - conts)))
    (hidden, cosine, sine, lens, g_qkv0, g_qkv1, g_gu0, g_gu1, g_out0, g_out1, g_down0, g_down1, g_gain) = (
        start_exchange(
            conts, column_pack((w_query, w_key, w_value)), w_gate, w_up, w_out, w_down, gain_tile,
            tokens, len_tile, frequency, picks, signed,
        )
    )
    gains = jnp.transpose(g_gain[..., :4, :shard], (3, 0, 1, 2, 4)).reshape(4, 1, depth)
    qkv, out, gu, down, qkv_next, out_next, gu_next, down_next = range(8)
    programs0 = (
        ((3, down, 0, 1), (5, gu, 0, 2), (5, gu, 2, 2)),
        ((2, gu, 0, 2),),
        ((2, gu, 2, 2), (3, gu, 0, 2)),
        ((3, gu, 2, 2), (1, qkv_next, 0, 4), (5, out_next, 0, 1)),
        ((2, qkv_next, 0, 4), (2, out_next, 0, 1), (5, down_next, 0, 1), (1, gu_next, 0, 2)),
        ((3, qkv_next, 0, 4), (3, out_next, 0, 1), (2, down_next, 0, 1)),
    )
    programs1 = (
        ((3, down, 0, 1), (2, gu, 0, 2), (1, gu, 2, 2)),
        ((3, gu, 0, 2), (2, gu, 2, 2)),
        (),
        ((3, gu, 2, 2),),
        (),
        (),
    )
    tables = (cosine, sine, lens)
    res = forward_layer(
        programs0, cotangent, 2, conts, hidden, gains[0], gains[2], *tables,
        (g_qkv0, g_out0, g_gu0, g_down0, g_qkv1, g_out1, g_gu1, g_down1),
    )
    weights0, moving1, acts0 = res[:4], res[4:8], res[8:]
    (x1, mid0, lse0, low1, rows0, qkv0, mix0, frows0, gate0, up0, act0, branch) = acts0
    res = forward_layer(programs1, None, 3, conts, x1, gains[1], gains[3], *tables, moving1)
    weights1, acts1 = res[:4], res[4:]
    (x2, mid1, lse1, low2, rows1, qkv1, mix1, frows1, gate1, up1, act1) = acts1

    (low1_back, gmid1, ggf1, dmix1, d_own, d_got, gu_own, gu_other, o_own, o_other) = ffn_backward(
        4, (("g", low1),), branch, True, mid1, gains[3], act1, frows1, gate1, up1, mix1,
        weights1[3], weights1[2], weights1[1],
    )
    sd1 = add_low(d_own, d_got)
    (gu_got, o_got, rd1, low2_back, up_1, _, gga1, qkv_own1, qkv_other1) = attn_backward(
        5, (("y", gu_other), ("y", o_other), ("z", sd1), ("g", low2)), conts,
        gmid1, x1, gains[1], qkv1, dmix1, mix1, lse1, lens, cosine, sine, rows1, weights1[0],
    )
    sgu1 = add_low(gu_own, gu_got)
    so1 = add_low(o_own, o_got)
    (qkv_got1, rgu1, ro1, gmid0, ggf0, dmix0, d_own0, d_got0, gu_own0, gu_other0, o_own0, o_other0) = ffn_backward(
        6, (("y", qkv_other1), ("zc", sgu1), ("z", so1)), up_1, False, mid0, gains[2], act0, frows0, gate0, up0, mix0,
        weights0[3], weights0[2], weights0[1],
    )
    sqkv1 = add_low(qkv_own1, qkv_got1)
    sd0 = add_low(d_own0, d_got0)
    bgu1 = z_total(sgu1, rgu1, 1)
    (gu_got0, o_got0, rqkv1, rd0, tgu1, _, up_low, gga0, qkv_own0, qkv_other0) = attn_backward(
        7, (("y", gu_other0), ("y", o_other0), ("zc", sqkv1), ("z", sd0), ("t", bgu1)), conts,
        gmid0, hidden, gains[0], qkv0, dmix0, mix0, lse0, lens, cosine, sine, rows0, weights0[0],
    )
    sgu0 = add_low(gu_own0, gu_got0)
    so0 = add_low(o_own0, o_got0)
    bqkv1 = z_total(sqkv1, rqkv1, 1)
    gain_part = jnp.concatenate([gga0, gga1, ggf0, ggf1, jnp.zeros((4, depth), jnp.float32)], axis=0)
    (gain_sums, osum0, bgu0, bqkv0, tgu0, tqkv0, tqkv1, back) = run_tail(
        8, gain_part, sgu0, so0, qkv_own0, qkv_other0, bqkv1, up_low
    )
    gain_sums = gain_sums[:4]
    device = lax.axis_index("dp") * lax.axis_size("fsdp") + lax.axis_index("fsdp")
    own_gain = lax.dynamic_slice_in_dim(gain_sums, device * shard, shard, 1)
    (out_x, out_back, grad_q, grad_k, grad_v, grad_o, grad_g, grad_u, grad_d) = end_assembly(
        step, qw, kw,
        (bqkv0, tqkv0, bgu0, tgu0, osum0, sd0, rd0, bqkv1, tqkv1, bgu1, tgu1, so1, ro1, sd1, rd1),
        (low1_back, low2_back), back,
    )
    return (
        out_x, out_back, own_gain[:2], grad_q, grad_k, grad_v, grad_o, own_gain[2:], grad_g, grad_u, grad_d,
    )


def per_device(*arrays):
    tokens, w_query, w_key, w_gate = arrays[0], arrays[2], arrays[3], arrays[7]
    dp_size, z_size = lax.axis_size("dp"), lax.axis_size("fsdp")
    suits = (
        dp_size == 2 * TP
        and z_size == TP
        and w_key.shape[2] // HEAD_DIM == dp_size
        and w_query.shape[2] == 2 * w_key.shape[2]
        and tokens.shape[0] % 128 == 0
        and w_query.shape[1] % 16 == 0
        and w_gate.shape[2] % (TP * dp_size * 128) == 0
    )
    return (fast_device if suits else general_device)(*arrays)


def solution(mesh):
    placed = (
        P(("dp", "fsdp"), None),
        P(None, ("dp", "fsdp")),
        P(None, ("dp", "fsdp"), None),
        P(None, ("dp", "fsdp"), None),
        P(None, ("dp", "fsdp"), None),
        P(None, ("dp", "fsdp"), None),
        P(None, ("dp", "fsdp")),
        P(None, ("dp", "fsdp"), None),
        P(None, ("dp", "fsdp"), None),
        P(None, ("dp", "fsdp"), None),
        P("dp", None),
        P(("dp", "fsdp"), None),
    )
    return jax.shard_map(
        per_device,
        mesh=mesh,
        in_specs=placed,
        out_specs=(
            P(None, ("dp", "fsdp"), None),
            P(("dp", "fsdp"), None),
            P(None, ("dp", "fsdp")),
            P(None, ("dp", "fsdp"), None),
            P(None, ("dp", "fsdp"), None),
            P(None, ("dp", "fsdp"), None),
            P(None, ("dp", "fsdp"), None),
            P(None, ("dp", "fsdp")),
            P(None, ("dp", "fsdp"), None),
            P(None, ("dp", "fsdp"), None),
            P(None, ("dp", "fsdp"), None),
        ),
        check_vma=False,
    )
```

```python
import functools
import math

import jax
import jax.numpy as jnp
from jax import lax
from jax.experimental import pallas as pl
from jax.experimental.pallas import tpu as pltpu
from jax.sharding import PartitionSpec as P

HEAD_DIM = 96


EPSILON = 1e-05
ROPE_BASE = 100000.0
NEGATIVE = -1e30


def layout(lengths_row, group_tok):
    places = jnp.arange(group_tok, dtype=jnp.int32)
    prompt_len = group_tok - jnp.sum(lengths_row)
    starts = prompt_len + jnp.cumsum(lengths_row) - lengths_row
    inside = places[:, None] >= starts[None, :]
    segment = jnp.sum(inside.astype(jnp.int32), axis=1)
    begins = jnp.max(jnp.where(inside, starts[None, :], 0), axis=1)
    position = jnp.where(segment > 0, places - begins + prompt_len, places)
    return (segment, position)


def rotate(values, position, direction):
    row_count = values.shape[0]
    shaped = values.reshape(row_count, -1, HEAD_DIM)
    halfway = HEAD_DIM // 2
    frequency = ROPE_BASE ** (-jnp.arange(halfway, dtype=jnp.float32) * 2.0 / HEAD_DIM)
    angles = position.astype(jnp.float32)[:, None] * frequency[None, :]
    cosine = jnp.cos(angles)[:, None, :]
    sine_part = direction * jnp.sin(angles)[:, None, :]
    first_half = shaped[..., :halfway]
    second_half = shaped[..., halfway:]
    turned = jnp.concatenate(
        [
            first_half * cosine - second_half * sine_part,
            second_half * cosine + first_half * sine_part,
        ],
        axis=-1,
    )
    return turned.reshape(values.shape)


def norm_apply(values, gain_vec):
    inv_rms = lax.rsqrt(jnp.mean(values * values, axis=-1, keepdims=True) + EPSILON)
    return values * inv_rms * gain_vec


def norm_back(values, gain_vec, incoming):
    inv_rms = lax.rsqrt(jnp.mean(values * values, axis=-1, keepdims=True) + EPSILON)
    weighted = incoming * gain_vec
    inner_sum = jnp.mean(weighted * values, axis=-1, keepdims=True)
    grad_values = inv_rms * weighted - values * inv_rms * inv_rms * inv_rms * inner_sum
    grad_gain = jnp.sum(incoming * values * inv_rms, axis=0)
    return (grad_values, grad_gain)


def matmul(left, right):
    return jnp.dot(left, right, preferred_element_type=jnp.float32)


def visibility(seg_rows, row_places, segment, places):
    same_seq = (seg_rows[:, None] == segment[None, :]) & (places[None, :] <= row_places[:, None])
    prompt_seen = (segment[None, :] == 0) & (seg_rows[:, None] > 0)
    return same_seq | prompt_seen


def head_slices(query_b, keys_all, head_index):
    row_count = query_b.shape[0]
    kv_width = keys_all.shape[1] // 2
    sharing = query_b.shape[1] // kv_width
    query_part = lax.dynamic_slice_in_dim(
        query_b, head_index * sharing * HEAD_DIM, sharing * HEAD_DIM, 1
    ).reshape(row_count, sharing, HEAD_DIM)
    key_part = lax.dynamic_slice_in_dim(keys_all, head_index * HEAD_DIM, HEAD_DIM, 1)
    value_part = lax.dynamic_slice_in_dim(keys_all, kv_width + head_index * HEAD_DIM, HEAD_DIM, 1)
    return (query_part, key_part, value_part)


def attend_forward(query_b, keys_all, visible):
    row_count = query_b.shape[0]
    kv_heads = keys_all.shape[1] // 2 // HEAD_DIM
    factor = 1.0 / math.sqrt(HEAD_DIM)

    def per_head(head_index):
        query_part, key_part, value_part = head_slices(query_b, keys_all, head_index)
        scores = (
            jnp.einsum("tgd,kd->gtk", query_part, key_part, preferred_element_type=jnp.float32)
            * factor
        )
        masked = jnp.where(visible[None], scores, NEGATIVE)
        peak_score = jnp.max(masked, axis=-1)
        exponent = jnp.where(visible[None], jnp.exp(masked - peak_score[..., None]), 0.0)
        totals = jnp.sum(exponent, axis=-1)
        probability = (exponent / totals[..., None]).astype(jnp.bfloat16)
        mixed_heads = jnp.einsum(
            "gtk,kd->tgd", probability, value_part, preferred_element_type=jnp.float32
        )
        return (mixed_heads.reshape(row_count, -1), peak_score, totals)

    mixed_heads, peak_score, totals = lax.map(per_head, jnp.arange(kv_heads, dtype=jnp.int32))
    return (jnp.transpose(mixed_heads, (1, 0, 2)).reshape(row_count, -1), peak_score, totals)


def attend_backward(query_b, keys_all, visible, peak_score, totals, grad_mixed):
    row_count = query_b.shape[0]
    kv_width = keys_all.shape[1] // 2
    kv_heads = kv_width // HEAD_DIM
    sharing = query_b.shape[1] // kv_width
    factor = 1.0 / math.sqrt(HEAD_DIM)

    def per_head(pieces):
        head_index, peak_head, total_head = pieces
        query_part, key_part, value_part = head_slices(query_b, keys_all, head_index)
        grad_part = lax.dynamic_slice_in_dim(
            grad_mixed, head_index * sharing * HEAD_DIM, sharing * HEAD_DIM, 1
        ).reshape(row_count, sharing, HEAD_DIM)
        scores = (
            jnp.einsum("tgd,kd->gtk", query_part, key_part, preferred_element_type=jnp.float32)
            * factor
        )
        masked = jnp.where(visible[None], scores, NEGATIVE)
        exponent = jnp.where(visible[None], jnp.exp(masked - peak_head[..., None]), 0.0)
        probability = exponent / total_head[..., None]
        prob_low = probability.astype(jnp.bfloat16)
        grad_probs = jnp.einsum(
            "tgd,kd->gtk", grad_part, value_part, preferred_element_type=jnp.float32
        )
        inner_sum = jnp.sum(probability * grad_probs, axis=-1, keepdims=True)
        grad_scores = (probability * (grad_probs - inner_sum)).astype(jnp.bfloat16)
        grad_query = (
            jnp.einsum("gtk,kd->tgd", grad_scores, key_part, preferred_element_type=jnp.float32)
            * factor
        )
        grad_key = (
            jnp.einsum("gtk,tgd->kd", grad_scores, query_part, preferred_element_type=jnp.float32)
            * factor
        )
        grad_value = jnp.einsum(
            "gtk,tgd->kd", prob_low, grad_part, preferred_element_type=jnp.float32
        )
        return (grad_query.reshape(row_count, -1), grad_key, grad_value)

    grad_query, grad_key, grad_value = lax.map(
        per_head, (jnp.arange(kv_heads, dtype=jnp.int32), peak_score, totals)
    )
    group_rows = keys_all.shape[0]
    key_terms = jnp.concatenate(
        [
            jnp.transpose(grad_key, (1, 0, 2)).reshape(group_rows, -1),
            jnp.transpose(grad_value, (1, 0, 2)).reshape(group_rows, -1),
        ],
        axis=1,
    )
    return (jnp.transpose(grad_query, (1, 0, 2)).reshape(row_count, -1), key_terms)


def fetch_attention(layer_index, gain_attn, w_query, w_key, w_value, w_out):
    return (
        lax.all_gather(gain_attn[layer_index], ("dp", "fsdp"), axis=0, tiled=True),
        lax.all_gather(w_query[layer_index], ("dp", "fsdp"), axis=0, tiled=True),
        lax.all_gather(w_key[layer_index], ("dp", "fsdp"), axis=0, tiled=True),
        lax.all_gather(w_value[layer_index], ("dp", "fsdp"), axis=0, tiled=True),
        lax.all_gather(w_out[layer_index], ("dp", "fsdp"), axis=0, tiled=True),
    )


def fetch_ffn(layer_index, gain_ffn, w_gate, w_up, w_down):
    return (
        lax.all_gather(gain_ffn[layer_index], ("dp", "fsdp"), axis=0, tiled=True),
        lax.all_gather(w_gate[layer_index], ("dp", "fsdp"), axis=0, tiled=True),
        lax.all_gather(w_up[layer_index], ("dp", "fsdp"), axis=0, tiled=True),
        lax.all_gather(w_down[layer_index], ("dp", "fsdp"), axis=0, tiled=True),
    )


def share_keys(stacked):
    return lax.all_gather(stacked, "fsdp", axis=0, tiled=True)


def layer_forward(hidden, attn_weights, ffn_weights, pos_rows, visible):
    gain_a, query_w, key_w, value_w, out_w = attn_weights
    gain_f, gate_w, upper_w, down_w = ffn_weights
    normed = norm_apply(hidden, gain_a.astype(jnp.float32)).astype(jnp.bfloat16)
    query_b = rotate(matmul(normed, query_w), pos_rows, 1.0).astype(jnp.bfloat16)
    key_b = rotate(matmul(normed, key_w), pos_rows, 1.0).astype(jnp.bfloat16)
    value_b = matmul(normed, value_w).astype(jnp.bfloat16)
    stacked = jnp.concatenate([key_b, value_b], axis=1)
    keys_all = share_keys(stacked)
    mixed_heads, peak_score, totals = attend_forward(query_b, keys_all, visible)
    mixed_b = mixed_heads.astype(jnp.bfloat16)
    middle = hidden + matmul(mixed_b, out_w)
    normed_ffn = norm_apply(middle, gain_f.astype(jnp.float32)).astype(jnp.bfloat16)
    gating = matmul(normed_ffn, gate_w)
    upward = matmul(normed_ffn, upper_w)
    activated = (jax.nn.silu(gating) * upward).astype(jnp.bfloat16)
    result = middle + matmul(activated, down_w)
    saved = (
        hidden,
        normed,
        query_b,
        stacked,
        keys_all,
        peak_score,
        totals,
        mixed_b,
        middle,
        normed_ffn,
        gating,
        upward,
        activated,
    )
    return (result, saved)


def layer_backward(upstream, saved, attn_weights, ffn_weights, keys_all, pos_rows, visible):
    (
        hidden,
        normed,
        query_b,
        stacked,
        unused_keys,
        peak_score,
        totals,
        mixed_b,
        middle,
        normed_ffn,
        gating,
        upward,
        activated,
    ) = saved
    gain_a, query_w, key_w, value_w, out_w = attn_weights
    gain_f, gate_w, upper_w, down_w = ffn_weights
    grad_branch = upstream.astype(jnp.bfloat16)
    grad_down_w = matmul(activated.T, grad_branch)
    grad_act = matmul(grad_branch, down_w.T)
    sigmoid_g = jax.nn.sigmoid(gating)
    grad_gate = (grad_act * upward * sigmoid_g * (1.0 + gating * (1.0 - sigmoid_g))).astype(
        jnp.bfloat16
    )
    grad_up = (grad_act * gating * sigmoid_g).astype(jnp.bfloat16)
    grad_gate_w = matmul(normed_ffn.T, grad_gate)
    grad_up_w = matmul(normed_ffn.T, grad_up)
    grad_normed_ffn = matmul(grad_gate, gate_w.T) + matmul(grad_up, upper_w.T)
    grad_middle_part, grad_gain_f = norm_back(middle, gain_f.astype(jnp.float32), grad_normed_ffn)
    ffn_blocks = (
        lax.psum_scatter(
            grad_gain_f.astype(jnp.bfloat16), "dp", scatter_dimension=0, tiled=True
        ).astype(jnp.float32),
        lax.psum_scatter(
            grad_gate_w.astype(jnp.bfloat16), "dp", scatter_dimension=0, tiled=True
        ).astype(jnp.float32),
        lax.psum_scatter(
            grad_up_w.astype(jnp.bfloat16), "dp", scatter_dimension=0, tiled=True
        ).astype(jnp.float32),
        lax.psum_scatter(
            grad_down_w.astype(jnp.bfloat16), "dp", scatter_dimension=0, tiled=True
        ).astype(jnp.float32),
    )
    ffn_grads = (
        lax.psum_scatter(
            ffn_blocks[0].astype(jnp.bfloat16), "fsdp", scatter_dimension=0, tiled=True
        ).astype(jnp.float32),
        lax.psum_scatter(
            ffn_blocks[1].astype(jnp.bfloat16), "fsdp", scatter_dimension=0, tiled=True
        ).astype(jnp.float32),
        lax.psum_scatter(
            ffn_blocks[2].astype(jnp.bfloat16), "fsdp", scatter_dimension=0, tiled=True
        ).astype(jnp.float32),
        lax.psum_scatter(
            ffn_blocks[3].astype(jnp.bfloat16), "fsdp", scatter_dimension=0, tiled=True
        ).astype(jnp.float32),
    )
    grad_middle = upstream + grad_middle_part
    grad_proj = grad_middle.astype(jnp.bfloat16)
    grad_out_w = matmul(mixed_b.T, grad_proj)
    grad_mixed = matmul(grad_proj, out_w.T).astype(jnp.bfloat16)
    grad_query_rot, key_terms = attend_backward(
        query_b, keys_all, visible, peak_score, totals, grad_mixed
    )
    key_grads = lax.psum_scatter(
        key_terms.astype(jnp.bfloat16), "fsdp", scatter_dimension=0, tiled=True
    ).astype(jnp.float32)
    kv_width = key_terms.shape[1] // 2
    grad_query = rotate(grad_query_rot, pos_rows, -1.0).astype(jnp.bfloat16)
    grad_key = rotate(key_grads[:, :kv_width], pos_rows, -1.0).astype(jnp.bfloat16)
    grad_value = key_grads[:, kv_width:].astype(jnp.bfloat16)
    grad_normed = (
        matmul(grad_query, query_w.T) + matmul(grad_key, key_w.T) + matmul(grad_value, value_w.T)
    )
    grad_query_w = matmul(normed.T, grad_query)
    grad_key_w = matmul(normed.T, grad_key)
    grad_value_w = matmul(normed.T, grad_value)
    grad_hidden_part, grad_gain_a = norm_back(hidden, gain_a.astype(jnp.float32), grad_normed)
    attn_blocks = (
        lax.psum_scatter(
            grad_gain_a.astype(jnp.bfloat16), "dp", scatter_dimension=0, tiled=True
        ).astype(jnp.float32),
        lax.psum_scatter(
            grad_query_w.astype(jnp.bfloat16), "dp", scatter_dimension=0, tiled=True
        ).astype(jnp.float32),
        lax.psum_scatter(
            grad_key_w.astype(jnp.bfloat16), "dp", scatter_dimension=0, tiled=True
        ).astype(jnp.float32),
        lax.psum_scatter(
            grad_value_w.astype(jnp.bfloat16), "dp", scatter_dimension=0, tiled=True
        ).astype(jnp.float32),
        lax.psum_scatter(
            grad_out_w.astype(jnp.bfloat16), "dp", scatter_dimension=0, tiled=True
        ).astype(jnp.float32),
    )
    attn_grads = (
        lax.psum_scatter(
            attn_blocks[0].astype(jnp.bfloat16), "fsdp", scatter_dimension=0, tiled=True
        ).astype(jnp.float32),
        lax.psum_scatter(
            attn_blocks[1].astype(jnp.bfloat16), "fsdp", scatter_dimension=0, tiled=True
        ).astype(jnp.float32),
        lax.psum_scatter(
            attn_blocks[2].astype(jnp.bfloat16), "fsdp", scatter_dimension=0, tiled=True
        ).astype(jnp.float32),
        lax.psum_scatter(
            attn_blocks[3].astype(jnp.bfloat16), "fsdp", scatter_dimension=0, tiled=True
        ).astype(jnp.float32),
        lax.psum_scatter(
            attn_blocks[4].astype(jnp.bfloat16), "fsdp", scatter_dimension=0, tiled=True
        ).astype(jnp.float32),
    )
    return (grad_middle + grad_hidden_part, attn_grads, ffn_grads)


def general_device(
    tokens,
    gain_attn,
    w_query,
    w_key,
    w_value,
    w_out,
    gain_ffn,
    w_gate,
    w_up,
    w_down,
    lengths,
    cotangent,
):
    tok_rows = tokens.shape[0]
    group_tok = tok_rows * lax.axis_size("fsdp")
    segment, position = layout(lengths[0], group_tok)
    first_row = lax.axis_index("fsdp") * tok_rows
    row_places = first_row + jnp.arange(tok_rows, dtype=jnp.int32)
    seg_rows = lax.dynamic_slice_in_dim(segment, first_row, tok_rows)
    pos_rows = lax.dynamic_slice_in_dim(position, first_row, tok_rows)
    visible = visibility(seg_rows, row_places, segment, jnp.arange(group_tok, dtype=jnp.int32))
    hidden = tokens.astype(jnp.float32)
    layer_store = []
    results = []
    for layer_index in range(2):
        attn_weights = fetch_attention(layer_index, gain_attn, w_query, w_key, w_value, w_out)
        ffn_weights = fetch_ffn(layer_index, gain_ffn, w_gate, w_up, w_down)
        hidden, saved = layer_forward(hidden, attn_weights, ffn_weights, pos_rows, visible)
        layer_store.append(saved)
        results.append(hidden.astype(jnp.bfloat16))
    upstream = cotangent.astype(jnp.float32)
    attn_list = []
    ffn_list = []
    for layer_index in (1, 0):
        attn_weights = fetch_attention(layer_index, gain_attn, w_query, w_key, w_value, w_out)
        ffn_weights = fetch_ffn(layer_index, gain_ffn, w_gate, w_up, w_down)
        saved = layer_store[layer_index]
        keys_all = share_keys(saved[3])
        upstream, attn_grads, ffn_grads = layer_backward(
            upstream, saved, attn_weights, ffn_weights, keys_all, pos_rows, visible
        )
        attn_list.append(attn_grads)
        ffn_list.append(ffn_grads)
    layer_outputs = jnp.stack(results)
    grad_gain_attn = jnp.stack([attn_list[1][0], attn_list[0][0]])
    grad_w_query = jnp.stack([attn_list[1][1], attn_list[0][1]])
    grad_w_key = jnp.stack([attn_list[1][2], attn_list[0][2]])
    grad_w_value = jnp.stack([attn_list[1][3], attn_list[0][3]])
    grad_w_out = jnp.stack([attn_list[1][4], attn_list[0][4]])
    grad_gain_ffn = jnp.stack([ffn_list[1][0], ffn_list[0][0]])
    grad_w_gate = jnp.stack([ffn_list[1][1], ffn_list[0][1]])
    grad_w_up = jnp.stack([ffn_list[1][2], ffn_list[0][2]])
    grad_w_down = jnp.stack([ffn_list[1][3], ffn_list[0][3]])
    return (
        layer_outputs,
        upstream,
        grad_gain_attn,
        grad_w_query,
        grad_w_key,
        grad_w_value,
        grad_w_out,
        grad_gain_ffn,
        grad_w_gate,
        grad_w_up,
        grad_w_down,
    )


TP = 4


def head_partner(values, halfway):
    width = values.shape[1]
    lane = lax.broadcasted_iota(jnp.int32, values.shape, 1)
    ahead = pltpu.roll(values, width - halfway, 1)
    behind = pltpu.roll(values, halfway, 1)
    return jnp.where(lane % HEAD_DIM < halfway, ahead, behind)


def block_mask(row_seg, col_seg, same_block, block):
    visible = (row_seg == col_seg) | (col_seg == 0)
    if same_block:
        rows = lax.broadcasted_iota(jnp.int32, (block, block), 0)
        cols = lax.broadcasted_iota(jnp.int32, (block, block), 1)
        visible = visible & (cols <= rows)
    return visible


MESH = pl.DeviceIdType.MESH
VMEM_LIMIT = 61 * 2**20
ANYWHERE = pl.BlockSpec(memory_space=pl.ANY)
IN_VMEM = pl.BlockSpec(memory_space=pltpu.VMEM)


class Net:
    def __init__(self, send_sems, recv_sems, local_sems):
        dp, z = lax.axis_index("dp"), lax.axis_index("fsdp")
        self.z = z
        self.q = lax.rem(dp, TP)
        self.y = lax.div(dp, TP)
        self.r = self.y * TP + z
        core = dp + 1 - 2 * lax.rem(dp, 2)
        across = dp + 2 - 4 * lax.rem(lax.div(dp, 2), 2)
        both = core + 2 - 4 * lax.rem(lax.div(dp, 2), 2)
        other = dp + TP - 2 * TP * lax.div(dp, TP)
        self.peer = {
            "core": (core, z),
            "x": (across, z),
            "both": (both, z),
            "y": (other, z),
            "z1": (dp, flip_index(z, 1)),
            "z2": (dp, flip_index(z, 2)),
            "z3": (dp, flip_index(z, 3)),
        }
        x, c = lax.div(self.q, 2), lax.rem(self.q, 2)
        high, low = lax.div(z, 2), lax.rem(z, 2)
        twisted = x + low - 2 * x * low
        self.peer["group"] = (self.y * TP + 2 * twisted + high, 2 * c + x)
        self.peer["home"] = (self.y * TP + 2 * low + high, 2 * c + twisted)
        self.alone = (self.peer["group"][0] == dp) & (self.peer["group"][1] == z)
        self.base = 2 * c + twisted
        self.send_sems, self.recv_sems, self.local_sems = send_sems, recv_sems, local_sems
        self.n_remote = self.n_local = 0
        self.flying = []
        self.leaving = []
        self.inner, self.outer = {}, {}

    def greet(self, names, regroup=None):
        barrier = pltpu.get_barrier_semaphore()
        for name in names:
            pl.semaphore_signal(barrier, inc=1, device_id=self.peer[name], device_id_type=MESH)
        if regroup is None:
            pl.semaphore_wait(barrier, len(names))
            return
        sender = self.peer["home" if regroup == "group" else "group"]

        @pl.when(jnp.logical_not(self.alone))
        def _():
            pl.semaphore_signal(barrier, inc=1, device_id=sender, device_id_type=MESH)
            pl.semaphore_wait(barrier, len(names) + 1)

        @pl.when(self.alone)
        def _():
            pl.semaphore_wait(barrier, len(names))

    def remote(self, src, dst, name):
        n = self.n_remote
        self.n_remote += 1
        copy = pltpu.make_async_remote_copy(
            src_ref=src,
            dst_ref=dst,
            send_sem=self.send_sems.at[n],
            recv_sem=self.recv_sems.at[n],
            device_id=self.peer[name],
            device_id_type=MESH,
        )
        copy.start()
        return copy

    def regroup(self, src, dst, name):
        n, k = self.n_remote, self.n_local
        self.n_remote += 1
        self.n_local += 1
        away = pltpu.make_async_remote_copy(
            src_ref=src,
            dst_ref=dst,
            send_sem=self.send_sems.at[n],
            recv_sem=self.recv_sems.at[n],
            device_id=self.peer[name],
            device_id_type=MESH,
        )
        here = pltpu.make_async_copy(src, dst, self.local_sems.at[k])
        copy = EitherCopy(self.alone, here, away)
        copy.start()
        return copy

    def local(self, src, dst):
        n = self.n_local
        self.n_local += 1
        copy = pltpu.make_async_copy(src, dst, self.local_sems.at[n])
        copy.start()
        return copy

    def keep(self, src, dst):
        self.leaving.append(self.local(src, dst))

    def finish(self):
        for copies in (*self.inner.values(), *self.outer.values(), self.flying, self.leaving):
            for copy in copies:
                copy.wait()
        self.inner, self.outer = {}, {}
        self.flying, self.leaving = [], []

    def arrived(self, ref):
        for pending in (self.inner, self.outer):
            for key in [k for k in pending if k[0] == id(ref)]:
                for copy in pending.pop(key):
                    copy.wait()

    def advance(self, moves):
        for stage, ref, low, count in moves:
            key = (id(ref), low)
            for copy in self.inner.pop(key, []):
                copy.wait()
            part = lambda bits: ref.at[self.y, pl.ds(low, count), flip_index(self.z, bits)]
            if stage == 1:
                sent = ((0, "z2"), (0, "z1"), (0, "y"))
            elif stage == 4:
                sent = ((0, "y"),)
            elif stage == 5:
                sent = ((0, "z2"), (0, "z1"))
            elif stage == 2:
                sent = ((2, "z1"), (1, "y"), (2, "y"))
            else:
                sent = ((3, "y"),)
            for bits, name in sent:
                pending = self.outer if name == "y" else self.inner
                pending.setdefault(key, []).append(self.remote(part(bits), part(bits), name))


class EitherCopy:
    def __init__(self, alone, here, away):
        self.alone, self.here, self.away = alone, here, away

    def start(self):
        pl.when(self.alone)(self.here.start)
        pl.when(jnp.logical_not(self.alone))(self.away.start)

    def wait(self):
        pl.when(self.alone)(self.here.wait)
        pl.when(jnp.logical_not(self.alone))(self.away.wait)


def flip_index(value, bits):
    low = lax.rem(value, 2)
    high = lax.div(value, 2)
    if bits & 1:
        low = 1 - low
    if bits & 2:
        high = 1 - high
    return high * 2 + low


def mixed_index(static, dynamic):
    return flip_index(dynamic, static)


def swap_index(value):
    return lax.rem(value, 2) * 2 + lax.div(value, 2)


def sems(remote, local):
    return [
        pltpu.SemaphoreType.DMA((max(remote, 1),)),
        pltpu.SemaphoreType.DMA((max(remote, 1),)),
        pltpu.SemaphoreType.DMA((max(local, 1),)),
    ]


PEERS = ("core", "x", "both", "y", "z1", "z2", "z3")
RANK_PEERS = (("core", 1), ("x", 2), ("both", 3))


def segments(lengths_ref, conts, group_tok, places):
    one = [lengths_ref[0:1, c : c + 1] for c in range(conts)]
    prompt = group_tok - sum(one)
    begin = prompt
    segment = jnp.zeros(places.shape, jnp.int32)
    begins = jnp.zeros(places.shape, jnp.int32)
    for c in range(conts):
        inside = places >= begin
        segment = segment + inside.astype(jnp.int32)
        begins = jnp.where(inside, jnp.maximum(begins, begin), begins)
        begin = begin + one[c]
    position = jnp.where(segment > 0, places - begins + prompt, places)
    return segment, position


def block_segments(lengths_ref, conts, block, index, row):
    shape = (block, 1) if row else (1, block)
    places = index * block + lax.broadcasted_iota(jnp.int32, shape, 0 if row else 1)
    return segments(lengths_ref, conts, TP * block, places)[0]


def start_kernel(
    conts, qkv_pack, w_gate, w_up, out_own, down_own, gain_tile, tokens, lengths, frequency, spread_cos, spread_sin,
    tok_out, cos_ref, sin_ref, len_out,
    g_qkv0, g_qkv1, g_gu0, g_gu1, g_out0, g_out1, g_down0, g_down1, g_gain,
    tok_buf, len_buf, send_sems, recv_sems, local_sems,
):
    net = Net(send_sems, recv_sems, local_sems)
    net.greet(PEERS, "group")
    bring = [net.regroup(lengths, len_buf, "group"), net.regroup(tokens, tok_buf, "group")]
    y, q, z = net.y, net.q, net.z
    step = w_gate.shape[2] // (2 * TP)

    def qkv_columns(layer, target):
        copies = [
            net.remote(qkv_pack.at[layer, flip_index(q, bits)], target.at[y, q, z], name)
            for name, bits in RANK_PEERS
        ]
        return copies + [net.local(qkv_pack.at[layer, q], target.at[y, q, z])]

    def gu_columns(layer, target):
        copies = []
        for name, bits in RANK_PEERS + ((None, 0),):
            for n, weight in enumerate((w_gate, w_up)):
                for half in range(2):
                    at = pl.multiple_of((half * TP + flip_index(q, bits)) * step, step)
                    src = weight.at[layer, :, pl.ds(at, step)]
                    dst = target.at[y, q, z, :, pl.ds((2 * n + half) * step, step)]
                    copies.append(net.local(src, dst) if name is None else net.remote(src, dst, name))
        return copies

    first = qkv_columns(0, g_qkv0)
    first += [net.remote(gain_tile, g_gain.at[y, q, z], name) for name, _ in RANK_PEERS]
    first.append(net.local(gain_tile, g_gain.at[y, q, z]))
    placed = [
        net.local(out_own.at[0], g_out0.at[y, 0, z]),
        net.local(down_own.at[0], g_down0.at[y, 0, z]),
        net.local(out_own.at[1], g_out1.at[y, 0, z]),
        net.local(down_own.at[1], g_down1.at[y, 0, z]),
    ]
    second = gu_columns(0, g_gu0)
    placed[0].wait()
    net.advance(((1, g_out0, 0, 1),))
    for copy in first:
        copy.wait()
    net.advance(((1, g_qkv0, 0, TP), (1, g_gain, 0, TP)))
    placed[1].wait()
    net.advance(((1, g_down0, 0, 1),))
    second += qkv_columns(1, g_qkv1) + gu_columns(1, g_gu1)
    bring[0].wait()
    block = tok_buf.shape[0]
    len_out[...] = len_buf[...]
    def table(s):
        places = mixed_index(s, net.base) * block + lax.broadcasted_iota(jnp.int32, (block, 1), 0)
        position = segments(len_buf, conts, TP * block, places)[1]
        angles = position.astype(jnp.float32) * frequency[...]
        at = slice(s * block, (s + 1) * block)
        for table_ref, values, lanes in (
            (cos_ref, jnp.cos(angles), spread_cos), (sin_ref, jnp.sin(angles), spread_sin)
        ):
            table_ref[at, :] = jnp.dot(
                values, lanes[...], precision=lax.Precision.HIGHEST, preferred_element_type=jnp.float32
            )

    table(0)
    net.advance(((2, g_out0, 0, 1), (2, g_qkv0, 0, TP), (2, g_gain, 0, TP)))
    for copy in second[:16]:
        copy.wait()
    second = second[16:] + placed[2:]
    net.advance(((4, g_gu0, 0, TP),))
    table(1)
    net.advance(((3, g_out0, 0, 1), (3, g_qkv0, 0, TP), (3, g_gain, 0, TP), (2, g_down0, 0, 1)))
    table(2)
    table(3)
    bring[1].wait()
    tok_out[...] = tok_buf[...].astype(jnp.float32)
    for copy in second:
        copy.wait()
    net.finish()


def start_exchange(conts, qkv_pack, w_gate, w_up, out_own, down_own, gain_tile, tokens, lengths, frequency, spread_cos, spread_sin):
    bf, f32 = jnp.bfloat16, jnp.float32
    shape = jax.ShapeDtypeStruct
    block, depth = tokens.shape
    shard, qkv_width = qkv_pack.shape[2:]
    units = w_gate.shape[2] // TP * 2
    outs = [
        shape((block, depth), f32),
        shape((TP * block, spread_cos.shape[1]), f32),
        shape((TP * block, spread_cos.shape[1]), f32),
        shape(lengths.shape, lengths.dtype),
    ]
    for ranks, rows, width in (
        (TP, shard, qkv_width),
        (TP, shard, units),
        (1, shard, depth),
        (1, down_own.shape[1], depth),
    ):
        outs += [shape((2, ranks, TP, rows, width), bf)] * 2
    outs.append(shape((2, TP, TP) + gain_tile.shape, f32))
    return pl.pallas_call(
        functools.partial(start_kernel, conts),
        out_shape=outs,
        in_specs=[IN_VMEM] * 11,
        out_specs=[IN_VMEM] * 4 + [ANYWHERE] * 9,
        scratch_shapes=[
            pltpu.VMEM((block, depth), bf),
            pltpu.VMEM(lengths.shape, lengths.dtype),
        ] + sems(80, 24),
        compiler_params=pltpu.CompilerParams(
            collective_id=1, has_side_effects=True, vmem_limit_bytes=VMEM_LIMIT
        ),
        cost_estimate=pl.CostEstimate(flops=0, bytes_accessed=300 * 2**20, transcendentals=0),
    )(qkv_pack, w_gate, w_up, out_own, down_own, gain_tile, tokens, lengths, frequency, spread_cos, spread_sin)


def attend_rows(net, block):
    return [
        pl.ds(pl.multiple_of(mixed_index(b, net.base) * block, block), block) for b in range(TP)
    ]


def attend_forward_block(net, qkv_ref, len_ref, conts, mixed_ref, lse_ref):
    total, width = qkv_ref.shape
    block = total // TP
    q_heads = width // (2 * HEAD_DIM)
    kv_heads = q_heads // 2
    factor = 1.0 / math.sqrt(HEAD_DIM)
    key_at = q_heads * HEAD_DIM
    value_at = key_at + kv_heads * HEAD_DIM
    places = attend_rows(net, block)
    nt = (((1,), (1,)), ((), ()))
    for i in range(TP):
        row_seg = block_segments(len_ref, conts, block, i, True)
        masks = [
            block_mask(row_seg, block_segments(len_ref, conts, block, j, False), i == j, block)
            for j in range(i + 1)
        ]
        for h in range(q_heads):
            kv = h // 2
            query = qkv_ref[places[i], h * HEAD_DIM : (h + 1) * HEAD_DIM]
            scores = []
            for j in range(i + 1):
                key = qkv_ref[places[j], key_at + kv * HEAD_DIM : key_at + (kv + 1) * HEAD_DIM]
                s = lax.dot_general(query, key, nt, preferred_element_type=jnp.float32) * factor
                scores.append(jnp.where(masks[j], s, NEGATIVE))
            peak = scores[0].max(axis=1, keepdims=True)
            for s in scores[1:]:
                peak = jnp.maximum(peak, s.max(axis=1, keepdims=True))
            total_e = jnp.zeros((block, 1), jnp.float32)
            mixed = jnp.zeros((block, HEAD_DIM), jnp.float32)
            for j in range(i + 1):
                e = jnp.exp(scores[j] - peak)
                total_e = total_e + e.sum(axis=1, keepdims=True)
                value = qkv_ref[places[j], value_at + kv * HEAD_DIM : value_at + (kv + 1) * HEAD_DIM]
                mixed = mixed + jnp.dot(
                    e.astype(jnp.bfloat16), value, preferred_element_type=jnp.float32
                )
            mixed_ref[places[i], h * HEAD_DIM : (h + 1) * HEAD_DIM] = (mixed / total_e).astype(
                jnp.bfloat16
            )
            lse_ref[i, :, h : h + 1] = peak + jnp.log(total_e)


def normalize(values, gain_row):
    scale = lax.rsqrt(jnp.mean(values * values, axis=-1, keepdims=True) + EPSILON)
    return (values * scale * gain_row).astype(jnp.bfloat16)


def spread_begin(net, buf):
    return (net.remote(buf.at[0], buf.at[1], "x"), net.remote(buf.at[0], buf.at[2], "core"))


def spread_each(net, buf, begun, work):
    over_x, over_core = begun
    work(0)
    over_core.wait()
    work(2)
    over_x.wait()
    forward = net.remote(buf.at[1], buf.at[3], "core")
    work(1)
    forward.wait()
    work(3)


def collect(net, part, far_out, far_in, pass_out, pass_in):
    low = lambda v: v.astype(jnp.bfloat16)
    far_out[0] = low(part(3))
    first = net.remote(far_out.at[0], far_in.at[0], "core")
    near = part(1)
    first.wait()
    pass_out[...] = low(near + far_in[0].astype(jnp.float32))
    passed = net.remote(pass_out, pass_in, "x")
    far_out[1] = low(part(2))
    second = net.remote(far_out.at[1], far_in.at[1], "core")
    own = part(0)
    second.wait()
    own = own + far_in[1].astype(jnp.float32)
    passed.wait()
    return own + pass_in[...].astype(jnp.float32)


def forward_kernel(programs, has_cot, conts, n_moving, *refs):
    x_own, gain_a, gain_f, cos_ref, sin_ref, lengths = refs[:6]
    refs = refs[6:]
    if has_cot:
        cot, refs = refs[0], refs[1:]
    refs = refs[n_moving:]
    moving, refs = refs[:n_moving], refs[n_moving:]
    (x_next, middle_ref, lse_ref, x_low, rows_out, qkv_out, mixed_out, ffn_rows_out, gate_out, up_out, act_out) = refs[:11]
    refs = refs[11:]
    if has_cot:
        branch_out, refs, branch = refs[0], refs[1:-1], refs[-1]
    (rows, ffn_rows, w_qkv, w_o, w_gu, w_d, qkv, mixed, gate, up, act,
     far_out, far_in, pass_out, pass_in, send_sems, recv_sems, local_sems) = refs
    net = Net(send_sems, recv_sems, local_sems)
    steps = [[(kind, moving[n], low, count) for kind, n, low, count in step] for step in programs]
    block, depth = x_own.shape
    load_qkv = net.local(moving[0], w_qkv)
    load_o = net.local(moving[1], w_o)
    net.greet(("core", "x", "y", "z1", "z2", "z3"), "group" if has_cot else None)
    net.advance(steps[0])
    if has_cot:
        bring = net.regroup(cot, branch.at[0], "group")
    rows[0] = normalize(x_own[...], gain_a[...])
    begun = spread_begin(net, rows)
    load_qkv.wait()

    def project(s):
        raw = jnp.dot(
            rows[s], w_qkv[...].reshape(depth, -1), preferred_element_type=jnp.float32
        )
        at = slice(s * block, (s + 1) * block)
        turned = raw * cos_ref[at, :] + head_partner(raw, HEAD_DIM // 2) * sin_ref[at, :]
        qkv[at, :] = turned.astype(jnp.bfloat16)

    spread_each(net, rows, begun, project)
    net.keep(rows, rows_out)
    net.keep(qkv, qkv_out)
    net.advance(steps[1])
    attend_forward_block(net, qkv, lengths, conts, mixed, lse_ref)
    net.keep(mixed, mixed_out)
    net.advance(steps[2])
    load_o.wait()

    def out_part(s):
        return jnp.dot(
            mixed[s * block : (s + 1) * block, :],
            w_o[...].reshape(-1, depth),
            preferred_element_type=jnp.float32,
        )

    middle = x_own[...] + collect(
        net, out_part, far_out, far_in.at[0], pass_out, pass_in.at[0]
    )
    middle_ref[...] = middle
    net.advance(steps[3])
    net.arrived(moving[3])
    load_d = net.local(moving[3], w_d)
    ffn_rows[0] = normalize(middle, gain_f[...])
    begun = spread_begin(net, ffn_rows)
    if has_cot:
        bring.wait()
        over_x, over_core = spread_begin(net, branch)
    net.arrived(moving[2])
    load_gu = net.local(moving[2], w_gu)
    net.advance(steps[4])
    load_d.wait()
    load_gu.wait()
    units = act.shape[2]

    def expand(s):
        value = ffn_rows[s]
        gating = jnp.dot(
            value, w_gu[:, :, :, :, :units].reshape(depth, units), preferred_element_type=jnp.float32
        )
        upward = jnp.dot(
            value, w_gu[:, :, :, :, units:].reshape(depth, units), preferred_element_type=jnp.float32
        )
        gate[s] = gating.astype(jnp.bfloat16)
        up[s] = upward.astype(jnp.bfloat16)
        act[s] = (gating * jax.nn.sigmoid(gating) * upward).astype(jnp.bfloat16)

    spread_each(net, ffn_rows, begun, expand)
    if has_cot:
        over_x.wait()
        forward = net.remote(branch.at[1], branch.at[3], "core")
    net.keep(ffn_rows, ffn_rows_out)
    net.keep(gate, gate_out)
    net.keep(up, up_out)
    net.keep(act, act_out)

    def down_part(s):
        return jnp.dot(act[s], w_d[...].reshape(-1, depth), preferred_element_type=jnp.float32)

    result = middle_ref[...] + collect_during(
        net,
        down_part,
        (far_out, far_in.at[1], pass_out, pass_in.at[1]),
        lambda: net.advance(steps[5]),
    )
    if has_cot:
        over_core.wait()
        forward.wait()
        net.keep(branch, branch_out)
    x_next[...] = result
    x_low[...] = result.astype(jnp.bfloat16)
    net.finish()


def forward_layer(programs, cot, cid, conts, x_own, gain_a, gain_f, cosine, sine, lengths, moving):
    bf, f32 = jnp.bfloat16, jnp.float32
    block, depth = x_own.shape
    total, qkv_width = cosine.shape
    units = moving[2].shape[4] // 2
    q_heads = qkv_width // (2 * HEAD_DIM)
    shape = jax.ShapeDtypeStruct
    outs = [shape(m.shape, m.dtype) for m in moving] + [
        shape((block, depth), f32),
        shape((block, depth), f32),
        shape((TP, block, q_heads), f32),
        shape((block, depth), bf),
        shape((TP, block, depth), bf),
        shape((total, qkv_width), bf),
        shape((total, qkv_width // 2), bf),
        shape((TP, block, depth), bf),
        shape((TP, block, units), bf),
        shape((TP, block, units), bf),
        shape((TP, block, units), bf),
    ]
    n = len(moving)
    given = [] if cot is None else [cot]
    c = len(given)
    outs += [shape((TP, block, depth), bf)] * c
    scratch = [
        pltpu.VMEM((TP, block, depth), bf),
        pltpu.VMEM((TP, block, depth), bf),
        pltpu.VMEM(moving[0].shape, bf),
        pltpu.VMEM(moving[1].shape, bf),
        pltpu.VMEM(moving[2].shape, bf),
        pltpu.VMEM(moving[3].shape, bf),
        pltpu.VMEM((total, qkv_width), bf),
        pltpu.VMEM((total, qkv_width // 2), bf),
        pltpu.VMEM((TP, block, units), bf),
        pltpu.VMEM((TP, block, units), bf),
        pltpu.VMEM((TP, block, units), bf),
        pltpu.VMEM((2, block, depth), bf),
        pltpu.VMEM((2, 2, block, depth), bf),
        pltpu.VMEM((block, depth), bf),
        pltpu.VMEM((2, block, depth), bf),
    ] + sems(80, 24) + [pltpu.VMEM((TP, block, depth), bf)] * c
    return pl.pallas_call(
        functools.partial(forward_kernel, programs, bool(c), conts, n),
        out_shape=outs,
        in_specs=[IN_VMEM] * (6 + c) + [ANYWHERE] * n,
        out_specs=[ANYWHERE] * n + [IN_VMEM] * 4 + [ANYWHERE] * (7 + c),
        scratch_shapes=scratch,
        input_output_aliases={6 + c + i: i for i in range(n)},
        compiler_params=pltpu.CompilerParams(
            collective_id=cid, has_side_effects=True, vmem_limit_bytes=VMEM_LIMIT
        ),
        cost_estimate=pl.CostEstimate(
            flops=16 * 10**9, bytes_accessed=400 * 2**20, transcendentals=10**7
        ),
    )(x_own, gain_a, gain_f, cosine, sine, lengths, *given, *moving)


def moved_shape(kind, source):
    shape = source.shape
    if kind in ("y", "whole_y"):
        kept = shape
    elif kind == "g":
        kept = shape
    elif kind == "zc":
        kept = (3, shape[0]) + shape[2:]
    elif kind in ("z", "t"):
        kept = (3,) + shape[1:]
    else:
        kept = (3,) + shape
    return jax.ShapeDtypeStruct(kept, source.dtype)


def begin_move(net, kind, source, target):
    if kind in ("y", "whole_y"):
        return [net.remote(source, target, "y")]
    if kind == "g":
        return [net.regroup(source, target, "home")]
    copies = []
    for name, bits in RANK_PEERS:
        if kind == "z":
            copies.append(
                net.remote(source.at[flip_index(net.z, bits)], target.at[bits - 1], f"z{bits}")
            )
        elif kind == "zc":
            copies.append(
                net.remote(source.at[:, flip_index(net.z, bits)], target.at[bits - 1], f"z{bits}")
            )
        elif kind == "whole_z":
            copies.append(net.remote(source, target.at[bits - 1], f"z{bits}"))
        elif kind == "t":
            copies.append(
                net.remote(source.at[flip_index(net.q, bits)], target.at[bits - 1], name)
            )
        else:
            copies.append(net.remote(source, target.at[bits - 1], name))
    return copies


def begin_moves(net, kinds, sources, targets):
    for kind, source, target in zip(kinds, sources, targets):
        net.flying += begin_move(net, kind, source, target)


def greet_all(net, kinds):
    net.greet(PEERS, "home" if "g" in kinds else None)


def tail_kernel(
    gain_part, sgu_in, o_own_in, o_other, qkv_own_in, qkv_other, bqkv, up_low,
    gain_out, out_sum, b_gu, b_qkv, t_gu, t_qkv, t_qkv1, back,
    sgu, so, s_qkv, qkv_got, o_got, gu_one, gu_pass, gu_two, o_one, o_pass, o_two, q_one, q_pass, q_two,
    gain_t, gain_a, gain_z, gain_b, gain_y, send_sems, recv_sems, local_sems,
):
    net = Net(send_sems, recv_sems, local_sems)
    f32, bf = jnp.float32, jnp.bfloat16
    z, q = net.z, net.q
    z1, z2, z3 = (flip_index(z, bits) for bits in (1, 2, 3))
    loads = [net.local(sgu_in, sgu), net.local(o_own_in, so), net.local(qkv_own_in, s_qkv)]
    net.greet(PEERS, "home")
    over_y = [net.remote(o_other, o_got, "y"), net.remote(qkv_other, qkv_got, "y")]

    def first_hop(source, target, part):
        return [
            net.remote(source.at[part + (z3,)], target.at[(1,) + part], "z1"),
            net.remote(source.at[part + (z1,)], target.at[(0,) + part], "z1"),
        ]

    halves = [(pl.ds(0, 2),), (pl.ds(2, 2),)]
    gu_first = [first_hop(sgu_in, gu_one, part) for part in halves]
    gains = [net.remote(gain_part, gain_t.at[bits - 1], name) for name, bits in RANK_PEERS]
    net.flying += begin_move(net, "t", bqkv, t_qkv1)
    net.flying += begin_move(net, "g", up_low, back)
    for copy in loads:
        copy.wait()
    over_y[0].wait()
    so[...] = (so[...].astype(f32) + o_got[...].astype(f32)).astype(bf)
    o_first = first_hop(so, o_one, ())
    over_y[1].wait()
    s_qkv[...] = (s_qkv[...].astype(f32) + qkv_got[...].astype(f32)).astype(bf)
    every = (pl.ds(0, TP),)
    q_first = first_hop(s_qkv, q_one, every)
    for copy in gains:
        copy.wait()
    gain_a[...] = gain_part[...] + gain_t[0] + gain_t[1] + gain_t[2]
    gains = [net.remote(gain_a, gain_z.at[bits - 1], f"z{bits}") for bits in (1, 2, 3)]

    def second_hop(own, one, passing, two, part, first):
        first[0].wait()
        passing[part or (Ellipsis,)] = (
            own[part + (z2,)].astype(f32) + one[(1,) + part].astype(f32)
        ).astype(bf)
        at = (lambda ref: ref.at[part]) if part else (lambda ref: ref)
        return net.remote(at(passing), at(two), "z2")

    gu_second = [
        second_hop(sgu, gu_one, gu_pass, gu_two, part, first) for part, first in zip(halves, gu_first)
    ]
    o_second = second_hop(so, o_one, o_pass, o_two, (), o_first)
    q_second = second_hop(s_qkv, q_one, q_pass, q_two, every, q_first)
    for copy in gains:
        copy.wait()
    gain_b[...] = gain_a[...] + gain_z[0] + gain_z[1] + gain_z[2]
    gain_over_y = net.remote(gain_b, gain_y, "y")

    def total(own, one, two, part):
        whole = part or (Ellipsis,)
        return (
            own[part + (z,)].astype(f32) + one[(0,) + part].astype(f32) + two[whole].astype(f32)
        )

    for part, first, second in zip(halves, gu_first, gu_second):
        first[1].wait()
        second.wait()
        b_gu[part] = total(sgu, gu_one, gu_two, part).astype(bf)
    net.flying += begin_move(net, "t", b_gu, t_gu)
    o_first[1].wait()
    o_second.wait()
    out_sum[...] = total(so, o_one, o_two, ())
    q_first[1].wait()
    q_second.wait()
    b_qkv[...] = total(s_qkv, q_one, q_two, every).astype(bf)
    net.flying += begin_move(net, "t", b_qkv, t_qkv)
    gain_over_y.wait()
    gain_out[...] = gain_b[...] + gain_y[...]
    net.finish()


def run_tail(cid, gain_part, sgu, so, o_other, qkv_own, qkv_other, bqkv, up_low):
    bf, f32 = jnp.bfloat16, jnp.float32
    shape = jax.ShapeDtypeStruct
    gu_block = (TP,) + sgu.shape[2:]
    o_block = so.shape[1:]
    q_block = (TP,) + qkv_own.shape[2:]
    three = lambda block: (3,) + block[1:]
    return pl.pallas_call(
        tail_kernel,
        out_shape=[
            shape(gain_part.shape, f32),
            shape(o_block, f32),
            shape(gu_block, bf),
            shape(q_block, bf),
            shape(three(gu_block), bf),
            shape(three(q_block), bf),
            shape(three(q_block), bf),
            shape(up_low.shape, bf),
        ],
        in_specs=[IN_VMEM] + [ANYWHERE] * 7,
        out_specs=[IN_VMEM] * 4 + [ANYWHERE] * 4,
        scratch_shapes=[
            pltpu.VMEM(sgu.shape, bf),
            pltpu.VMEM(so.shape, bf),
            pltpu.VMEM(qkv_own.shape, bf),
            pltpu.VMEM(qkv_own.shape, bf),
            pltpu.VMEM(so.shape, bf),
        ]
        + [
            pltpu.VMEM(dims, bf)
            for block in (gu_block, o_block, q_block)
            for dims in ((2,) + block, block, block)
        ]
        + [
            pltpu.VMEM(dims, f32)
            for dims in (
                (3,) + gain_part.shape, gain_part.shape, (3,) + gain_part.shape, gain_part.shape, gain_part.shape
            )
        ]
        + sems(48, 8),
        compiler_params=pltpu.CompilerParams(
            collective_id=cid, has_side_effects=True, vmem_limit_bytes=VMEM_LIMIT
        ),
        cost_estimate=pl.CostEstimate(flops=0, bytes_accessed=200 * 2**20, transcendentals=0),
    )(gain_part, sgu, so, o_other, qkv_own, qkv_other, bqkv, up_low)


def norm_backward(values, gain_row, incoming):
    inv = lax.rsqrt(jnp.mean(values * values, axis=-1, keepdims=True) + EPSILON)
    weighted = incoming * gain_row
    inner = jnp.mean(weighted * values, axis=-1, keepdims=True)
    grad = inv * weighted - values * (inv * inv * inv * inner)
    return grad, jnp.sum(incoming * values * inv, axis=0, keepdims=True)


def collect_during(net, part, bufs, meanwhile):
    far_out, far_in, pass_out, pass_in = bufs
    low = lambda v: v.astype(jnp.bfloat16)
    far_out[0] = low(part(3))
    first = net.remote(far_out.at[0], far_in.at[0], "core")
    near = part(1)
    first.wait()
    pass_out[...] = low(near + far_in[0].astype(jnp.float32))
    passed = net.remote(pass_out, pass_in, "x")
    far_out[1] = low(part(2))
    second = net.remote(far_out.at[1], far_in.at[1], "core")
    own = part(0)
    second.wait()
    own = own + far_in[1].astype(jnp.float32)
    meanwhile()
    passed.wait()
    return own + pass_in[...].astype(jnp.float32)


NT = (((1,), (1,)), ((), ()))
TN = (((0,), (0,)), ((), ()))


def dot_nt(left, right):
    return lax.dot_general(left, right, NT, preferred_element_type=jnp.float32)


def dot_tn(left, right):
    return lax.dot_general(left, right, TN, preferred_element_type=jnp.float32)


def ffn_backward_kernel(kinds, given, *refs):
    n = len(kinds)
    middle, gain, source_in = refs[:3]
    acts, rows_in, gates, ups, mixed_in, wd_in, wgu_in, wo_in = refs[3:11]
    refs = refs[11:]
    sources, targets, refs = refs[:n], refs[n : 2 * n], refs[2 * n :]
    (grad_middle, gain_grad, dmixed_out, d_own, d_got, gu_own, gu_other, o_own, o_other) = refs[:9]
    (branch, proj, act, rows, gate, up, mixed, dmixed, w_d, w_gu, w_o, g_down, g_gu, g_out,
     far_out, far_in, pass_out, pass_in, send_sems, recv_sems, local_sems) = refs[9:]
    net = Net(send_sems, recv_sems, local_sems)
    block, depth = middle.shape
    units = act.shape[2]
    total = TP * block
    loads = {}
    if given:
        loads["branch"] = net.local(source_in, branch)
    for name, src, dst in (
        ("w_d", wd_in, w_d), ("gate", gates, gate), ("up", ups, up), ("act", acts, act),
        ("w_gu", wgu_in, w_gu), ("rows", rows_in, rows), ("w_o", wo_in, w_o), ("mixed", mixed_in, mixed),
    ):
        loads[name] = net.local(src, dst)
    greet_all(net, kinds)
    begin_moves(net, kinds, sources, targets)
    if given:
        loads["branch"].wait()
    else:
        branch[0] = source_in[...].astype(jnp.bfloat16)
        begun = spread_begin(net, branch)
    loads["w_d"].wait()
    loads["gate"].wait()
    loads["up"].wait()

    def through(s):
        grad_act = dot_nt(branch[s], w_d[...].reshape(units, depth))
        gating = gate[s].astype(jnp.float32)
        upward = up[s].astype(jnp.float32)
        sig = jax.nn.sigmoid(gating)
        shared = grad_act * sig
        gate[s] = (shared * upward * (1.0 + gating * (1.0 - sig))).astype(jnp.bfloat16)
        up[s] = (shared * gating).astype(jnp.bfloat16)

    if given:
        for s in (3, 1, 2, 0):
            through(s)
    else:
        spread_each(net, branch, begun, through)
    loads["act"].wait()
    theirs, ours = 1 - net.y, net.y
    drows, urows = g_down.shape[2], g_gu.shape[3]
    dwide, uwide = 2 * drows, 2 * TP * urows

    def down_half(side):
        def tile(m, carry):
            lanes = pl.ds(pl.multiple_of((side * 2 + m) * dwide, dwide), dwide)
            grad = dot_tn(act[:, :, lanes].reshape(total, dwide), branch[...].reshape(total, depth))
            g_down[side, pl.ds(2 * m, 2)] = grad.astype(jnp.bfloat16).reshape(2, drows, depth)
            return carry

        lax.fori_loop(0, 2, tile, 0)

    def gu_half(side):
        def tile(m, carry):
            lanes = pl.ds(pl.multiple_of((side * 2 + m) * uwide, uwide), uwide)
            left = rows[:, :, lanes].reshape(total, uwide)
            for ref, at in ((gate, 0), (up, units)):
                grad = dot_tn(left, ref[...].reshape(total, units)).astype(jnp.bfloat16)
                g_gu[side, pl.ds(2 * m, 2), :, :, at : at + units] = grad.reshape(2, TP, urows, units)
            return carry

        lax.fori_loop(0, 2, tile, 0)

    down_half(theirs)
    net.flying.append(net.remote(g_down.at[theirs], d_got, "y"))
    loads["w_gu"].wait()
    loads["rows"].wait()

    def back(s):
        return dot_nt(gate[s], w_gu[:, :, :, :, :units].reshape(depth, units)) + dot_nt(
            up[s], w_gu[:, :, :, :, units:].reshape(depth, units)
        )

    def meanwhile():
        gu_half(theirs)
        net.keep(g_gu.at[theirs], gu_other)
        gu_half(ours)
        net.keep(g_gu.at[ours], gu_own)
        down_half(ours)
        net.keep(g_down.at[ours], d_own)

    incoming = collect_during(net, back, (far_out, far_in, pass_out, pass_in), meanwhile)
    part, gain_part = norm_backward(middle[...], gain[...], incoming)
    gain_grad[...] = gain_part
    grad_mid = (branch[0].astype(jnp.float32) if given else source_in[...]) + part
    grad_middle[...] = grad_mid
    proj[0] = grad_mid.astype(jnp.bfloat16)
    begun = spread_begin(net, proj)
    loads["w_o"].wait()
    loads["mixed"].wait()

    def mix_back(s):
        dmixed[s * block : (s + 1) * block, :] = dot_nt(
            proj[s], w_o[...].reshape(-1, depth)
        ).astype(jnp.bfloat16)

    spread_each(net, proj, begun, mix_back)
    net.keep(dmixed, dmixed_out)
    grad = dot_tn(mixed[...], proj[...].reshape(total, depth)).astype(jnp.bfloat16)
    g_out[...] = grad.reshape(g_out.shape)
    net.keep(g_out.at[ours], o_own)
    net.keep(g_out.at[theirs], o_other)
    net.finish()


def ffn_backward(cid, moves, source, given, middle, gain, acts, rows, gates, ups, mixed, w_d, w_gu, w_o):
    bf, f32 = jnp.bfloat16, jnp.float32
    shape = jax.ShapeDtypeStruct
    block, depth = middle.shape
    units = gates.shape[2]
    total, mixed_width = mixed.shape
    kinds = tuple(kind for kind, _ in moves)
    sources = [source for _, source in moves]
    n = len(moves)
    drows, urows, orows = w_d.shape[3], w_gu.shape[3], w_o.shape[3]
    outs = [moved_shape(kind, source) for kind, source in moves] + [
        shape((block, depth), f32),
        shape((1, depth), f32),
        shape((total, mixed_width), bf),
        shape((TP, drows, depth), bf),
        shape((TP, drows, depth), bf),
        shape((TP, TP, urows, 2 * units), bf),
        shape((TP, TP, urows, 2 * units), bf),
        shape((TP, orows, depth), bf),
        shape((TP, orows, depth), bf),
    ]
    scratch = [
        pltpu.VMEM((TP, block, depth), bf),
        pltpu.VMEM((TP, block, depth), bf),
        pltpu.VMEM((TP, block, units), bf),
        pltpu.VMEM((TP, block, depth), bf),
        pltpu.VMEM((TP, block, units), bf),
        pltpu.VMEM((TP, block, units), bf),
        pltpu.VMEM((total, mixed_width), bf),
        pltpu.VMEM((total, mixed_width), bf),
        pltpu.VMEM(w_d.shape, bf),
        pltpu.VMEM(w_gu.shape, bf),
        pltpu.VMEM(w_o.shape, bf),
        pltpu.VMEM((2, TP, drows, depth), bf),
        pltpu.VMEM((2, TP, TP, urows, 2 * units), bf),
        pltpu.VMEM((2, TP, orows, depth), bf),
        pltpu.VMEM((2, block, depth), bf),
        pltpu.VMEM((2, block, depth), bf),
        pltpu.VMEM((block, depth), bf),
        pltpu.VMEM((block, depth), bf),
    ] + sems(48, 20)
    operands = [middle, gain, source, acts, rows, gates, ups, mixed, w_d, w_gu, w_o]
    return pl.pallas_call(
        functools.partial(ffn_backward_kernel, kinds, given),
        out_shape=outs,
        in_specs=[IN_VMEM] * 2 + [ANYWHERE if given else IN_VMEM] + [ANYWHERE] * (8 + n),
        out_specs=[ANYWHERE] * n + [IN_VMEM] * 2 + [ANYWHERE] * 7,
        scratch_shapes=scratch,
        compiler_params=pltpu.CompilerParams(
            collective_id=cid, has_side_effects=True, vmem_limit_bytes=VMEM_LIMIT
        ),
        cost_estimate=pl.CostEstimate(
            flops=24 * 10**9, bytes_accessed=200 * 2**20, transcendentals=10**6
        ),
    )(*operands, *sources)


def attend_backward_block(net, qkv_ref, grad_ref, mixed_ref, lse_ref, len_ref, conts, acc_ref):
    total, width = qkv_ref.shape
    block = total // TP
    q_heads = width // (2 * HEAD_DIM)
    kv_heads = q_heads // 2
    factor = 1.0 / math.sqrt(HEAD_DIM)
    key_at = q_heads * HEAD_DIM
    value_at = key_at + kv_heads * HEAD_DIM
    places = attend_rows(net, block)
    acc_ref[:, key_at:] = jnp.zeros((total, width - key_at), jnp.float32)
    for i in range(TP):
        row_seg = block_segments(len_ref, conts, block, i, True)
        masks = [
            block_mask(row_seg, block_segments(len_ref, conts, block, j, False), i == j, block)
            for j in range(i + 1)
        ]
        for h in range(q_heads):
            kv = h // 2
            lanes = slice(h * HEAD_DIM, (h + 1) * HEAD_DIM)
            query = qkv_ref[places[i], lanes]
            grad = grad_ref[places[i], lanes]
            lse = lse_ref[i, :, h : h + 1]
            inner = jnp.sum(
                grad.astype(jnp.float32) * mixed_ref[places[i], lanes].astype(jnp.float32),
                axis=1,
                keepdims=True,
            )
            grad_query = jnp.zeros((block, HEAD_DIM), jnp.float32)
            key_lanes = slice(key_at + kv * HEAD_DIM, key_at + (kv + 1) * HEAD_DIM)
            value_lanes = slice(value_at + kv * HEAD_DIM, value_at + (kv + 1) * HEAD_DIM)
            for j in range(i + 1):
                key = qkv_ref[places[j], key_lanes]
                value = qkv_ref[places[j], value_lanes]
                s = dot_nt(query, key) * factor
                prob = jnp.where(masks[j], jnp.exp(s - lse), 0.0)
                grad_prob = dot_nt(grad, value)
                grad_score = (prob * (grad_prob - inner)).astype(jnp.bfloat16)
                grad_query = grad_query + jnp.dot(
                    grad_score, key, preferred_element_type=jnp.float32
                )
                acc_ref[places[j], key_lanes] += dot_tn(grad_score, query) * factor
                acc_ref[places[j], value_lanes] += dot_tn(prob.astype(jnp.bfloat16), grad)
            acc_ref[places[i], lanes] = grad_query * factor


def attn_backward_kernel(kinds, conts, *refs):
    n = len(kinds)
    (grad_middle, hidden, gain, qkv, dmixed, mixed, lse, lengths, cos_ref, sin_ref) = refs[:10]
    rows_in, w_in = refs[10:12]
    sources, targets, refs = refs[12 : 12 + n], refs[12 + n : 12 + 2 * n], refs[12 + 2 * n :]
    upstream, up_low, gain_grad, qkv_own, qkv_other = refs[:5]
    (acc, dqkv, rows, w_qkv, g_qkv, far_out, far_in, pass_out, pass_in,
     send_sems, recv_sems, local_sems) = refs[5:]
    net = Net(send_sems, recv_sems, local_sems)
    block, depth = hidden.shape
    total = TP * block
    load_rows = net.local(rows_in, rows)
    load_w = net.local(w_in, w_qkv)
    greet_all(net, kinds)
    begin_moves(net, kinds, sources, targets)
    attend_backward_block(net, qkv, dmixed, mixed, lse, lengths, conts, acc)
    for s in range(TP):
        at = slice(s * block, (s + 1) * block)
        value = acc[at, :]
        turned = value * cos_ref[at, :] - head_partner(value, HEAD_DIM // 2) * sin_ref[at, :]
        dqkv[at, :] = turned.astype(jnp.bfloat16)
    load_w.wait()
    load_rows.wait()
    urows = g_qkv.shape[2]
    wide = 2 * TP * urows

    def back(s):
        return dot_nt(dqkv[s * block : (s + 1) * block, :], w_qkv[...].reshape(depth, -1))

    def meanwhile():
        def tile(m, carry):
            lanes = pl.ds(pl.multiple_of(m * wide, wide), wide)
            grad = dot_tn(rows[:, :, lanes].reshape(total, wide), dqkv[...])
            g_qkv[pl.ds(2 * m, 2)] = grad.astype(jnp.bfloat16).reshape(2, TP, urows, -1)
            return carry

        lax.fori_loop(0, TP, tile, 0)
        net.keep(g_qkv.at[pl.ds(net.y * TP, TP)], qkv_own)
        net.keep(g_qkv.at[pl.ds((1 - net.y) * TP, TP)], qkv_other)

    incoming = collect_during(net, back, (far_out, far_in, pass_out, pass_in), meanwhile)
    part, gain_part = norm_backward(hidden[...], gain[...], incoming)
    gain_grad[...] = gain_part
    result = grad_middle[...] + part
    upstream[...] = result
    up_low[...] = result.astype(jnp.bfloat16)
    net.finish()


def attn_backward(
    cid, moves, conts, grad_middle, hidden, gain, qkv, dmixed, mixed, lse, lengths, cosine, sine, rows, w_qkv
):
    bf, f32 = jnp.bfloat16, jnp.float32
    shape = jax.ShapeDtypeStruct
    block, depth = hidden.shape
    total, width = qkv.shape
    kinds = tuple(kind for kind, _ in moves)
    sources = [source for _, source in moves]
    n = len(moves)
    urows = w_qkv.shape[3]
    outs = [moved_shape(kind, source) for kind, source in moves] + [
        shape((block, depth), f32),
        shape((block, depth), bf),
        shape((1, depth), f32),
        shape((TP, TP, urows, width), bf),
        shape((TP, TP, urows, width), bf),
    ]
    scratch = [
        pltpu.VMEM((total, width), f32),
        pltpu.VMEM((total, width), bf),
        pltpu.VMEM((TP, block, depth), bf),
        pltpu.VMEM(w_qkv.shape, bf),
        pltpu.VMEM((2 * TP, TP, urows, width), bf),
        pltpu.VMEM((2, block, depth), bf),
        pltpu.VMEM((2, block, depth), bf),
        pltpu.VMEM((block, depth), bf),
        pltpu.VMEM((block, depth), bf),
    ] + sems(48, 8)
    return pl.pallas_call(
        functools.partial(attn_backward_kernel, kinds, conts),
        out_shape=outs,
        in_specs=[IN_VMEM] * 10 + [ANYWHERE] * (2 + n),
        out_specs=[ANYWHERE] * n + [IN_VMEM] * 3 + [ANYWHERE] * 2,
        scratch_shapes=scratch,
        compiler_params=pltpu.CompilerParams(
            collective_id=cid, has_side_effects=True, vmem_limit_bytes=VMEM_LIMIT
        ),
        cost_estimate=pl.CostEstimate(
            flops=16 * 10**9, bytes_accessed=200 * 2**20, transcendentals=10**7
        ),
    )(grad_middle, hidden, gain, qkv, dmixed, mixed, lse, lengths, cosine, sine, rows, w_qkv, *sources)


def add_low(own, got):
    return (own.astype(jnp.float32) + got.astype(jnp.float32)).astype(jnp.bfloat16)


def z_total(summed, got, axis):
    own = lax.dynamic_index_in_dim(summed, lax.axis_index("fsdp"), axis, keepdims=False)
    return (own.astype(jnp.float32) + jnp.sum(got.astype(jnp.float32), axis=0)).astype(jnp.bfloat16)


def end_kernel(step, qw, kw, *refs):
    layers, refs = (refs[:7], refs[7:15]), refs[15:]
    x_outs, back, refs = refs[:2], refs[2], refs[3:]
    out_x, out_back, out_q, out_k, out_v, out_o, out_g, out_u, out_d = refs
    q = lax.rem(lax.axis_index("dp"), TP)
    z = lax.axis_index("fsdp")
    low, high = lax.rem(q, 2) == 1, lax.div(q, 2) == 1

    def columns(blocks, got):
        pieces = [blocks[q]] + [got[k] for k in range(3)]
        a = [jnp.where(low, pieces[i ^ 1], pieces[i]) for i in range(4)]
        return [jnp.where(high, a[i ^ 2], a[i]).astype(jnp.float32) for i in range(4)]

    def lay(target, layer, pieces, at, width):
        half = width // 2
        for n, piece in enumerate(pieces):
            for side in range(2):
                to = (side * TP + n) * half
                target[layer, :, to : to + half] = piece[:, at + side * half : at + (side + 1) * half]

    for layer in range(2):
        bqkv, tqkv, bgu, tgu = layers[layer][:4]
        pieces = columns(bqkv, tqkv)
        lay(out_q, layer, pieces, 0, qw)
        lay(out_k, layer, pieces, qw, kw)
        lay(out_v, layer, pieces, qw + kw, kw)
        pieces = columns(bgu, tgu)
        lay(out_g, layer, pieces, 0, 2 * step)
        lay(out_u, layer, pieces, 2 * step, 2 * step)
        sums = [(*layers[layer][-2:], out_d)]
        if layer == 0:
            out_o[0] = layers[0][4][...]
        else:
            sums.append((*layers[1][4:6], out_o))
        for summed, got, target in sums:
            value = summed[z].astype(jnp.float32)
            for k in range(3):
                value = value + got[k].astype(jnp.float32)
            target[layer] = value
        out_x[layer] = x_outs[layer][...]
    out_back[...] = back[...].astype(jnp.float32)


def end_assembly(step, qw, kw, pieces, x_outs, back):
    f32 = jnp.float32
    shape = jax.ShapeDtypeStruct
    block, depth = back.shape
    rows = pieces[0].shape[1]
    drows = pieces[5].shape[1]
    outs = [
        shape((2, block, depth), jnp.bfloat16),
        shape((block, depth), f32),
        shape((2, rows, TP * qw), f32),
        shape((2, rows, TP * kw), f32),
        shape((2, rows, TP * kw), f32),
        shape((2, rows, depth), f32),
        shape((2, rows, TP * 2 * step), f32),
        shape((2, rows, TP * 2 * step), f32),
        shape((2, drows, depth), f32),
    ]
    return pl.pallas_call(
        functools.partial(end_kernel, step, qw, kw),
        out_shape=outs,
        in_specs=[IN_VMEM] * 18,
        out_specs=[IN_VMEM] * 9,
        compiler_params=pltpu.CompilerParams(vmem_limit_bytes=VMEM_LIMIT),
    )(*pieces, *x_outs, back)


def column_pack(weights):
    parts = []
    for weight in weights:
        layers, rows, width = weight.shape
        view = weight.reshape(layers, rows, 2, TP, width // (2 * TP))
        parts.append(view.transpose(0, 3, 1, 2, 4).reshape(layers, TP, rows, width // TP))
    return jnp.concatenate(parts, axis=3)


def fast_device(
    tokens, gain_attn, w_query, w_key, w_value, w_out, gain_ffn, w_gate, w_up, w_down, lengths, cotangent
):
    depth = tokens.shape[1]
    shard = w_query.shape[1]
    conts = lengths.shape[1]
    halfway = HEAD_DIM // 2
    qw, kw = w_query.shape[2] // TP, w_key.shape[2] // TP
    step = w_gate.shape[2] // (2 * TP)
    frequency = ROPE_BASE ** (-jnp.arange(halfway, dtype=jnp.float32) * 2.0 / HEAD_DIM)
    lane = jnp.arange(128)[:, None]
    column = jnp.arange(qw + 2 * kw)[None]
    turned = column < qw + kw
    frequency = jnp.pad(frequency, (0, 128 - halfway))[None]
    picks = (lane == jnp.where(turned, column % halfway, halfway)).astype(jnp.float32)
    signed = picks * jnp.where(turned, jnp.where(column % HEAD_DIM < halfway, -1.0, 1.0), 0.0)
    gain_tile = jnp.pad(
        jnp.concatenate([gain_attn, gain_ffn], axis=0).astype(jnp.float32), ((0, 4), (0, 128 - shard))
    )
    len_tile = jnp.pad(lengths, ((0, 7), (0, 128 - conts)))
    (hidden, cosine, sine, lens, g_qkv0, g_qkv1, g_gu0, g_gu1, g_out0, g_out1, g_down0, g_down1, g_gain) = (
        start_exchange(
            conts, column_pack((w_query, w_key, w_value)), w_gate, w_up, w_out, w_down, gain_tile,
            tokens, len_tile, frequency, picks, signed,
        )
    )
    gains = jnp.transpose(g_gain[..., :4, :shard], (3, 0, 1, 2, 4)).reshape(4, 1, depth)
    qkv, out, gu, down, qkv_next, out_next, gu_next, down_next = range(8)
    programs0 = (
        ((3, down, 0, 1), (5, gu, 0, 2), (5, gu, 2, 2)),
        ((2, gu, 0, 2),),
        ((2, gu, 2, 2), (3, gu, 0, 2)),
        ((3, gu, 2, 2), (1, qkv_next, 0, 4), (1, out_next, 0, 1)),
        ((2, qkv_next, 0, 4), (2, out_next, 0, 1), (1, down_next, 0, 1)),
        ((3, qkv_next, 0, 4), (3, out_next, 0, 1), (2, down_next, 0, 1)),
    )
    programs1 = (
        ((3, down, 0, 1), (1, gu, 0, 2), (1, gu, 2, 2)),
        ((2, gu, 0, 2),),
        ((2, gu, 2, 2), (3, gu, 0, 2)),
        ((3, gu, 2, 2),),
        (),
        (),
    )
    tables = (cosine, sine, lens)
    res = forward_layer(
        programs0, None, 2, conts, hidden, gains[0], gains[2], *tables,
        (g_qkv0, g_out0, g_gu0, g_down0, g_qkv1, g_out1, g_gu1, g_down1),
    )
    weights0, moving1, acts0 = res[:4], res[4:8], res[8:]
    (x1, mid0, lse0, low1, rows0, qkv0, mix0, frows0, gate0, up0, act0) = acts0
    res = forward_layer(programs1, cotangent, 3, conts, x1, gains[1], gains[3], *tables, moving1)
    weights1, acts1 = res[:4], res[4:]
    (x2, mid1, lse1, low2, rows1, qkv1, mix1, frows1, gate1, up1, act1, branch) = acts1

    (low1_back, gmid1, ggf1, dmix1, d_own, d_got, gu_own, gu_other, o_own, o_other) = ffn_backward(
        4, (("g", low1),), branch, True, mid1, gains[3], act1, frows1, gate1, up1, mix1,
        weights1[3], weights1[2], weights1[1],
    )
    sd1 = add_low(d_own, d_got)
    (gu_got, rd1, low2_back, up_1, _, gga1, qkv_own1, qkv_other1) = attn_backward(
        5, (("y", gu_other), ("z", sd1), ("g", low2)), conts,
        gmid1, x1, gains[1], qkv1, dmix1, mix1, lse1, lens, cosine, sine, rows1, weights1[0],
    )
    sgu1 = add_low(gu_own, gu_got)
    (qkv_got1, o_got, rgu1, gmid0, ggf0, dmix0, d_own0, d_got0, gu_own0, gu_other0, o_own0, o_other0) = ffn_backward(
        6, (("y", qkv_other1), ("y", o_other), ("zc", sgu1)), up_1, False, mid0, gains[2], act0, frows0, gate0, up0, mix0,
        weights0[3], weights0[2], weights0[1],
    )
    sqkv1 = add_low(qkv_own1, qkv_got1)
    so1 = add_low(o_own, o_got)
    sd0 = add_low(d_own0, d_got0)
    bgu1 = z_total(sgu1, rgu1, 1)
    (gu_got0, rqkv1, rd0, ro1, tgu1, _, up_low, gga0, qkv_own0, qkv_other0) = attn_backward(
        7, (("y", gu_other0), ("zc", sqkv1), ("z", sd0), ("z", so1), ("t", bgu1)), conts,
        gmid0, hidden, gains[0], qkv0, dmix0, mix0, lse0, lens, cosine, sine, rows0, weights0[0],
    )
    sgu0 = add_low(gu_own0, gu_got0)
    bqkv1 = z_total(sqkv1, rqkv1, 1)
    gain_part = jnp.concatenate([gga0, gga1, ggf0, ggf1, jnp.zeros((4, depth), jnp.float32)], axis=0)
    (gain_sums, osum0, bgu0, bqkv0, tgu0, tqkv0, tqkv1, back) = run_tail(
        8, gain_part, sgu0, o_own0, o_other0, qkv_own0, qkv_other0, bqkv1, up_low
    )
    gain_sums = gain_sums[:4]
    device = lax.axis_index("dp") * lax.axis_size("fsdp") + lax.axis_index("fsdp")
    own_gain = lax.dynamic_slice_in_dim(gain_sums, device * shard, shard, 1)
    (out_x, out_back, grad_q, grad_k, grad_v, grad_o, grad_g, grad_u, grad_d) = end_assembly(
        step, qw, kw,
        (bqkv0, tqkv0, bgu0, tgu0, osum0, sd0, rd0, bqkv1, tqkv1, bgu1, tgu1, so1, ro1, sd1, rd1),
        (low1_back, low2_back), back,
    )
    return (
        out_x, out_back, own_gain[:2], grad_q, grad_k, grad_v, grad_o, own_gain[2:], grad_g, grad_u, grad_d,
    )


def per_device(*arrays):
    tokens, w_query, w_key, w_gate = arrays[0], arrays[2], arrays[3], arrays[7]
    dp_size, z_size = lax.axis_size("dp"), lax.axis_size("fsdp")
    suits = (
        dp_size == 2 * TP
        and z_size == TP
        and w_key.shape[2] // HEAD_DIM == dp_size
        and w_query.shape[2] == 2 * w_key.shape[2]
        and tokens.shape[0] % 128 == 0
        and w_query.shape[1] % 16 == 0
        and w_gate.shape[2] % (TP * dp_size * 128) == 0
    )
    return (fast_device if suits else general_device)(*arrays)


def solution(mesh):
    placed = (
        P(("dp", "fsdp"), None),
        P(None, ("dp", "fsdp")),
        P(None, ("dp", "fsdp"), None),
        P(None, ("dp", "fsdp"), None),
        P(None, ("dp", "fsdp"), None),
        P(None, ("dp", "fsdp"), None),
        P(None, ("dp", "fsdp")),
        P(None, ("dp", "fsdp"), None),
        P(None, ("dp", "fsdp"), None),
        P(None, ("dp", "fsdp"), None),
        P("dp", None),
        P(("dp", "fsdp"), None),
    )
    return jax.shard_map(
        per_device,
        mesh=mesh,
        in_specs=placed,
        out_specs=(
            P(None, ("dp", "fsdp"), None),
            P(("dp", "fsdp"), None),
            P(None, ("dp", "fsdp")),
            P(None, ("dp", "fsdp"), None),
            P(None, ("dp", "fsdp"), None),
            P(None, ("dp", "fsdp"), None),
            P(None, ("dp", "fsdp"), None),
            P(None, ("dp", "fsdp")),
            P(None, ("dp", "fsdp"), None),
            P(None, ("dp", "fsdp"), None),
            P(None, ("dp", "fsdp"), None),
        ),
        check_vma=False,
    )
```

```python
import functools
import math

import jax
import jax.numpy as jnp
from jax import lax
from jax.experimental import pallas as pl
from jax.experimental.pallas import tpu as pltpu
from jax.sharding import PartitionSpec as P

HEAD_DIM = 96


EPSILON = 1e-05
ROPE_BASE = 100000.0
NEGATIVE = -1e30


def layout(lengths_row, group_tok):
    places = jnp.arange(group_tok, dtype=jnp.int32)
    prompt_len = group_tok - jnp.sum(lengths_row)
    starts = prompt_len + jnp.cumsum(lengths_row) - lengths_row
    inside = places[:, None] >= starts[None, :]
    segment = jnp.sum(inside.astype(jnp.int32), axis=1)
    begins = jnp.max(jnp.where(inside, starts[None, :], 0), axis=1)
    position = jnp.where(segment > 0, places - begins + prompt_len, places)
    return (segment, position)


def rotate(values, position, direction):
    row_count = values.shape[0]
    shaped = values.reshape(row_count, -1, HEAD_DIM)
    halfway = HEAD_DIM // 2
    frequency = ROPE_BASE ** (-jnp.arange(halfway, dtype=jnp.float32) * 2.0 / HEAD_DIM)
    angles = position.astype(jnp.float32)[:, None] * frequency[None, :]
    cosine = jnp.cos(angles)[:, None, :]
    sine_part = direction * jnp.sin(angles)[:, None, :]
    first_half = shaped[..., :halfway]
    second_half = shaped[..., halfway:]
    turned = jnp.concatenate(
        [
            first_half * cosine - second_half * sine_part,
            second_half * cosine + first_half * sine_part,
        ],
        axis=-1,
    )
    return turned.reshape(values.shape)


def norm_apply(values, gain_vec):
    inv_rms = lax.rsqrt(jnp.mean(values * values, axis=-1, keepdims=True) + EPSILON)
    return values * inv_rms * gain_vec


def norm_back(values, gain_vec, incoming):
    inv_rms = lax.rsqrt(jnp.mean(values * values, axis=-1, keepdims=True) + EPSILON)
    weighted = incoming * gain_vec
    inner_sum = jnp.mean(weighted * values, axis=-1, keepdims=True)
    grad_values = inv_rms * weighted - values * inv_rms * inv_rms * inv_rms * inner_sum
    grad_gain = jnp.sum(incoming * values * inv_rms, axis=0)
    return (grad_values, grad_gain)


def matmul(left, right):
    return jnp.dot(left, right, preferred_element_type=jnp.float32)


def visibility(seg_rows, row_places, segment, places):
    same_seq = (seg_rows[:, None] == segment[None, :]) & (places[None, :] <= row_places[:, None])
    prompt_seen = (segment[None, :] == 0) & (seg_rows[:, None] > 0)
    return same_seq | prompt_seen


def head_slices(query_b, keys_all, head_index):
    row_count = query_b.shape[0]
    kv_width = keys_all.shape[1] // 2
    sharing = query_b.shape[1] // kv_width
    query_part = lax.dynamic_slice_in_dim(
        query_b, head_index * sharing * HEAD_DIM, sharing * HEAD_DIM, 1
    ).reshape(row_count, sharing, HEAD_DIM)
    key_part = lax.dynamic_slice_in_dim(keys_all, head_index * HEAD_DIM, HEAD_DIM, 1)
    value_part = lax.dynamic_slice_in_dim(keys_all, kv_width + head_index * HEAD_DIM, HEAD_DIM, 1)
    return (query_part, key_part, value_part)


def attend_forward(query_b, keys_all, visible):
    row_count = query_b.shape[0]
    kv_heads = keys_all.shape[1] // 2 // HEAD_DIM
    factor = 1.0 / math.sqrt(HEAD_DIM)

    def per_head(head_index):
        query_part, key_part, value_part = head_slices(query_b, keys_all, head_index)
        scores = (
            jnp.einsum("tgd,kd->gtk", query_part, key_part, preferred_element_type=jnp.float32)
            * factor
        )
        masked = jnp.where(visible[None], scores, NEGATIVE)
        peak_score = jnp.max(masked, axis=-1)
        exponent = jnp.where(visible[None], jnp.exp(masked - peak_score[..., None]), 0.0)
        totals = jnp.sum(exponent, axis=-1)
        probability = (exponent / totals[..., None]).astype(jnp.bfloat16)
        mixed_heads = jnp.einsum(
            "gtk,kd->tgd", probability, value_part, preferred_element_type=jnp.float32
        )
        return (mixed_heads.reshape(row_count, -1), peak_score, totals)

    mixed_heads, peak_score, totals = lax.map(per_head, jnp.arange(kv_heads, dtype=jnp.int32))
    return (jnp.transpose(mixed_heads, (1, 0, 2)).reshape(row_count, -1), peak_score, totals)


def attend_backward(query_b, keys_all, visible, peak_score, totals, grad_mixed):
    row_count = query_b.shape[0]
    kv_width = keys_all.shape[1] // 2
    kv_heads = kv_width // HEAD_DIM
    sharing = query_b.shape[1] // kv_width
    factor = 1.0 / math.sqrt(HEAD_DIM)

    def per_head(pieces):
        head_index, peak_head, total_head = pieces
        query_part, key_part, value_part = head_slices(query_b, keys_all, head_index)
        grad_part = lax.dynamic_slice_in_dim(
            grad_mixed, head_index * sharing * HEAD_DIM, sharing * HEAD_DIM, 1
        ).reshape(row_count, sharing, HEAD_DIM)
        scores = (
            jnp.einsum("tgd,kd->gtk", query_part, key_part, preferred_element_type=jnp.float32)
            * factor
        )
        masked = jnp.where(visible[None], scores, NEGATIVE)
        exponent = jnp.where(visible[None], jnp.exp(masked - peak_head[..., None]), 0.0)
        probability = exponent / total_head[..., None]
        prob_low = probability.astype(jnp.bfloat16)
        grad_probs = jnp.einsum(
            "tgd,kd->gtk", grad_part, value_part, preferred_element_type=jnp.float32
        )
        inner_sum = jnp.sum(probability * grad_probs, axis=-1, keepdims=True)
        grad_scores = (probability * (grad_probs - inner_sum)).astype(jnp.bfloat16)
        grad_query = (
            jnp.einsum("gtk,kd->tgd", grad_scores, key_part, preferred_element_type=jnp.float32)
            * factor
        )
        grad_key = (
            jnp.einsum("gtk,tgd->kd", grad_scores, query_part, preferred_element_type=jnp.float32)
            * factor
        )
        grad_value = jnp.einsum(
            "gtk,tgd->kd", prob_low, grad_part, preferred_element_type=jnp.float32
        )
        return (grad_query.reshape(row_count, -1), grad_key, grad_value)

    grad_query, grad_key, grad_value = lax.map(
        per_head, (jnp.arange(kv_heads, dtype=jnp.int32), peak_score, totals)
    )
    group_rows = keys_all.shape[0]
    key_terms = jnp.concatenate(
        [
            jnp.transpose(grad_key, (1, 0, 2)).reshape(group_rows, -1),
            jnp.transpose(grad_value, (1, 0, 2)).reshape(group_rows, -1),
        ],
        axis=1,
    )
    return (jnp.transpose(grad_query, (1, 0, 2)).reshape(row_count, -1), key_terms)


def fetch_attention(layer_index, gain_attn, w_query, w_key, w_value, w_out):
    return (
        lax.all_gather(gain_attn[layer_index], ("dp", "fsdp"), axis=0, tiled=True),
        lax.all_gather(w_query[layer_index], ("dp", "fsdp"), axis=0, tiled=True),
        lax.all_gather(w_key[layer_index], ("dp", "fsdp"), axis=0, tiled=True),
        lax.all_gather(w_value[layer_index], ("dp", "fsdp"), axis=0, tiled=True),
        lax.all_gather(w_out[layer_index], ("dp", "fsdp"), axis=0, tiled=True),
    )


def fetch_ffn(layer_index, gain_ffn, w_gate, w_up, w_down):
    return (
        lax.all_gather(gain_ffn[layer_index], ("dp", "fsdp"), axis=0, tiled=True),
        lax.all_gather(w_gate[layer_index], ("dp", "fsdp"), axis=0, tiled=True),
        lax.all_gather(w_up[layer_index], ("dp", "fsdp"), axis=0, tiled=True),
        lax.all_gather(w_down[layer_index], ("dp", "fsdp"), axis=0, tiled=True),
    )


def share_keys(stacked):
    return lax.all_gather(stacked, "fsdp", axis=0, tiled=True)


def layer_forward(hidden, attn_weights, ffn_weights, pos_rows, visible):
    gain_a, query_w, key_w, value_w, out_w = attn_weights
    gain_f, gate_w, upper_w, down_w = ffn_weights
    normed = norm_apply(hidden, gain_a.astype(jnp.float32)).astype(jnp.bfloat16)
    query_b = rotate(matmul(normed, query_w), pos_rows, 1.0).astype(jnp.bfloat16)
    key_b = rotate(matmul(normed, key_w), pos_rows, 1.0).astype(jnp.bfloat16)
    value_b = matmul(normed, value_w).astype(jnp.bfloat16)
    stacked = jnp.concatenate([key_b, value_b], axis=1)
    keys_all = share_keys(stacked)
    mixed_heads, peak_score, totals = attend_forward(query_b, keys_all, visible)
    mixed_b = mixed_heads.astype(jnp.bfloat16)
    middle = hidden + matmul(mixed_b, out_w)
    normed_ffn = norm_apply(middle, gain_f.astype(jnp.float32)).astype(jnp.bfloat16)
    gating = matmul(normed_ffn, gate_w)
    upward = matmul(normed_ffn, upper_w)
    activated = (jax.nn.silu(gating) * upward).astype(jnp.bfloat16)
    result = middle + matmul(activated, down_w)
    saved = (
        hidden,
        normed,
        query_b,
        stacked,
        keys_all,
        peak_score,
        totals,
        mixed_b,
        middle,
        normed_ffn,
        gating,
        upward,
        activated,
    )
    return (result, saved)


def layer_backward(upstream, saved, attn_weights, ffn_weights, keys_all, pos_rows, visible):
    (
        hidden,
        normed,
        query_b,
        stacked,
        unused_keys,
        peak_score,
        totals,
        mixed_b,
        middle,
        normed_ffn,
        gating,
        upward,
        activated,
    ) = saved
    gain_a, query_w, key_w, value_w, out_w = attn_weights
    gain_f, gate_w, upper_w, down_w = ffn_weights
    grad_branch = upstream.astype(jnp.bfloat16)
    grad_down_w = matmul(activated.T, grad_branch)
    grad_act = matmul(grad_branch, down_w.T)
    sigmoid_g = jax.nn.sigmoid(gating)
    grad_gate = (grad_act * upward * sigmoid_g * (1.0 + gating * (1.0 - sigmoid_g))).astype(
        jnp.bfloat16
    )
    grad_up = (grad_act * gating * sigmoid_g).astype(jnp.bfloat16)
    grad_gate_w = matmul(normed_ffn.T, grad_gate)
    grad_up_w = matmul(normed_ffn.T, grad_up)
    grad_normed_ffn = matmul(grad_gate, gate_w.T) + matmul(grad_up, upper_w.T)
    grad_middle_part, grad_gain_f = norm_back(middle, gain_f.astype(jnp.float32), grad_normed_ffn)
    ffn_blocks = (
        lax.psum_scatter(
            grad_gain_f.astype(jnp.bfloat16), "dp", scatter_dimension=0, tiled=True
        ).astype(jnp.float32),
        lax.psum_scatter(
            grad_gate_w.astype(jnp.bfloat16), "dp", scatter_dimension=0, tiled=True
        ).astype(jnp.float32),
        lax.psum_scatter(
            grad_up_w.astype(jnp.bfloat16), "dp", scatter_dimension=0, tiled=True
        ).astype(jnp.float32),
        lax.psum_scatter(
            grad_down_w.astype(jnp.bfloat16), "dp", scatter_dimension=0, tiled=True
        ).astype(jnp.float32),
    )
    ffn_grads = (
        lax.psum_scatter(
            ffn_blocks[0].astype(jnp.bfloat16), "fsdp", scatter_dimension=0, tiled=True
        ).astype(jnp.float32),
        lax.psum_scatter(
            ffn_blocks[1].astype(jnp.bfloat16), "fsdp", scatter_dimension=0, tiled=True
        ).astype(jnp.float32),
        lax.psum_scatter(
            ffn_blocks[2].astype(jnp.bfloat16), "fsdp", scatter_dimension=0, tiled=True
        ).astype(jnp.float32),
        lax.psum_scatter(
            ffn_blocks[3].astype(jnp.bfloat16), "fsdp", scatter_dimension=0, tiled=True
        ).astype(jnp.float32),
    )
    grad_middle = upstream + grad_middle_part
    grad_proj = grad_middle.astype(jnp.bfloat16)
    grad_out_w = matmul(mixed_b.T, grad_proj)
    grad_mixed = matmul(grad_proj, out_w.T).astype(jnp.bfloat16)
    grad_query_rot, key_terms = attend_backward(
        query_b, keys_all, visible, peak_score, totals, grad_mixed
    )
    key_grads = lax.psum_scatter(
        key_terms.astype(jnp.bfloat16), "fsdp", scatter_dimension=0, tiled=True
    ).astype(jnp.float32)
    kv_width = key_terms.shape[1] // 2
    grad_query = rotate(grad_query_rot, pos_rows, -1.0).astype(jnp.bfloat16)
    grad_key = rotate(key_grads[:, :kv_width], pos_rows, -1.0).astype(jnp.bfloat16)
    grad_value = key_grads[:, kv_width:].astype(jnp.bfloat16)
    grad_normed = (
        matmul(grad_query, query_w.T) + matmul(grad_key, key_w.T) + matmul(grad_value, value_w.T)
    )
    grad_query_w = matmul(normed.T, grad_query)
    grad_key_w = matmul(normed.T, grad_key)
    grad_value_w = matmul(normed.T, grad_value)
    grad_hidden_part, grad_gain_a = norm_back(hidden, gain_a.astype(jnp.float32), grad_normed)
    attn_blocks = (
        lax.psum_scatter(
            grad_gain_a.astype(jnp.bfloat16), "dp", scatter_dimension=0, tiled=True
        ).astype(jnp.float32),
        lax.psum_scatter(
            grad_query_w.astype(jnp.bfloat16), "dp", scatter_dimension=0, tiled=True
        ).astype(jnp.float32),
        lax.psum_scatter(
            grad_key_w.astype(jnp.bfloat16), "dp", scatter_dimension=0, tiled=True
        ).astype(jnp.float32),
        lax.psum_scatter(
            grad_value_w.astype(jnp.bfloat16), "dp", scatter_dimension=0, tiled=True
        ).astype(jnp.float32),
        lax.psum_scatter(
            grad_out_w.astype(jnp.bfloat16), "dp", scatter_dimension=0, tiled=True
        ).astype(jnp.float32),
    )
    attn_grads = (
        lax.psum_scatter(
            attn_blocks[0].astype(jnp.bfloat16), "fsdp", scatter_dimension=0, tiled=True
        ).astype(jnp.float32),
        lax.psum_scatter(
            attn_blocks[1].astype(jnp.bfloat16), "fsdp", scatter_dimension=0, tiled=True
        ).astype(jnp.float32),
        lax.psum_scatter(
            attn_blocks[2].astype(jnp.bfloat16), "fsdp", scatter_dimension=0, tiled=True
        ).astype(jnp.float32),
        lax.psum_scatter(
            attn_blocks[3].astype(jnp.bfloat16), "fsdp", scatter_dimension=0, tiled=True
        ).astype(jnp.float32),
        lax.psum_scatter(
            attn_blocks[4].astype(jnp.bfloat16), "fsdp", scatter_dimension=0, tiled=True
        ).astype(jnp.float32),
    )
    return (grad_middle + grad_hidden_part, attn_grads, ffn_grads)


def general_device(
    tokens,
    gain_attn,
    w_query,
    w_key,
    w_value,
    w_out,
    gain_ffn,
    w_gate,
    w_up,
    w_down,
    lengths,
    cotangent,
):
    tok_rows = tokens.shape[0]
    group_tok = tok_rows * lax.axis_size("fsdp")
    segment, position = layout(lengths[0], group_tok)
    first_row = lax.axis_index("fsdp") * tok_rows
    row_places = first_row + jnp.arange(tok_rows, dtype=jnp.int32)
    seg_rows = lax.dynamic_slice_in_dim(segment, first_row, tok_rows)
    pos_rows = lax.dynamic_slice_in_dim(position, first_row, tok_rows)
    visible = visibility(seg_rows, row_places, segment, jnp.arange(group_tok, dtype=jnp.int32))
    hidden = tokens.astype(jnp.float32)
    layer_store = []
    results = []
    for layer_index in range(2):
        attn_weights = fetch_attention(layer_index, gain_attn, w_query, w_key, w_value, w_out)
        ffn_weights = fetch_ffn(layer_index, gain_ffn, w_gate, w_up, w_down)
        hidden, saved = layer_forward(hidden, attn_weights, ffn_weights, pos_rows, visible)
        layer_store.append(saved)
        results.append(hidden.astype(jnp.bfloat16))
    upstream = cotangent.astype(jnp.float32)
    attn_list = []
    ffn_list = []
    for layer_index in (1, 0):
        attn_weights = fetch_attention(layer_index, gain_attn, w_query, w_key, w_value, w_out)
        ffn_weights = fetch_ffn(layer_index, gain_ffn, w_gate, w_up, w_down)
        saved = layer_store[layer_index]
        keys_all = share_keys(saved[3])
        upstream, attn_grads, ffn_grads = layer_backward(
            upstream, saved, attn_weights, ffn_weights, keys_all, pos_rows, visible
        )
        attn_list.append(attn_grads)
        ffn_list.append(ffn_grads)
    layer_outputs = jnp.stack(results)
    grad_gain_attn = jnp.stack([attn_list[1][0], attn_list[0][0]])
    grad_w_query = jnp.stack([attn_list[1][1], attn_list[0][1]])
    grad_w_key = jnp.stack([attn_list[1][2], attn_list[0][2]])
    grad_w_value = jnp.stack([attn_list[1][3], attn_list[0][3]])
    grad_w_out = jnp.stack([attn_list[1][4], attn_list[0][4]])
    grad_gain_ffn = jnp.stack([ffn_list[1][0], ffn_list[0][0]])
    grad_w_gate = jnp.stack([ffn_list[1][1], ffn_list[0][1]])
    grad_w_up = jnp.stack([ffn_list[1][2], ffn_list[0][2]])
    grad_w_down = jnp.stack([ffn_list[1][3], ffn_list[0][3]])
    return (
        layer_outputs,
        upstream,
        grad_gain_attn,
        grad_w_query,
        grad_w_key,
        grad_w_value,
        grad_w_out,
        grad_gain_ffn,
        grad_w_gate,
        grad_w_up,
        grad_w_down,
    )


TP = 4


def head_partner(values, halfway):
    width = values.shape[1]
    lane = lax.broadcasted_iota(jnp.int32, values.shape, 1)
    ahead = pltpu.roll(values, width - halfway, 1)
    behind = pltpu.roll(values, halfway, 1)
    return jnp.where(lane % HEAD_DIM < halfway, ahead, behind)


def block_mask(row_seg, col_seg, same_block, block):
    visible = (row_seg == col_seg) | (col_seg == 0)
    if same_block:
        rows = lax.broadcasted_iota(jnp.int32, (block, block), 0)
        cols = lax.broadcasted_iota(jnp.int32, (block, block), 1)
        visible = visible & (cols <= rows)
    return visible


MESH = pl.DeviceIdType.MESH
VMEM_LIMIT = 61 * 2**20
ANYWHERE = pl.BlockSpec(memory_space=pl.ANY)
IN_VMEM = pl.BlockSpec(memory_space=pltpu.VMEM)


class Net:
    def __init__(self, send_sems, recv_sems, local_sems):
        dp, z = lax.axis_index("dp"), lax.axis_index("fsdp")
        self.z = z
        self.q = lax.rem(dp, TP)
        self.y = lax.div(dp, TP)
        self.r = self.y * TP + z
        core = dp + 1 - 2 * lax.rem(dp, 2)
        across = dp + 2 - 4 * lax.rem(lax.div(dp, 2), 2)
        both = core + 2 - 4 * lax.rem(lax.div(dp, 2), 2)
        other = dp + TP - 2 * TP * lax.div(dp, TP)
        self.peer = {
            "core": (core, z),
            "x": (across, z),
            "both": (both, z),
            "y": (other, z),
            "z1": (dp, flip_index(z, 1)),
            "z2": (dp, flip_index(z, 2)),
            "z3": (dp, flip_index(z, 3)),
        }
        x, c = lax.div(self.q, 2), lax.rem(self.q, 2)
        high, low = lax.div(z, 2), lax.rem(z, 2)
        twisted = x + low - 2 * x * low
        self.peer["group"] = (self.y * TP + 2 * twisted + high, 2 * c + x)
        self.peer["home"] = (self.y * TP + 2 * low + high, 2 * c + twisted)
        self.alone = (self.peer["group"][0] == dp) & (self.peer["group"][1] == z)
        self.base = 2 * c + twisted
        self.send_sems, self.recv_sems, self.local_sems = send_sems, recv_sems, local_sems
        self.n_remote = self.n_local = 0
        self.flying = []
        self.leaving = []
        self.inner, self.outer = {}, {}

    def greet(self, names, regroup=None):
        barrier = pltpu.get_barrier_semaphore()
        for name in names:
            pl.semaphore_signal(barrier, inc=1, device_id=self.peer[name], device_id_type=MESH)
        if regroup is None:
            pl.semaphore_wait(barrier, len(names))
            return
        sender = self.peer["home" if regroup == "group" else "group"]

        @pl.when(jnp.logical_not(self.alone))
        def _():
            pl.semaphore_signal(barrier, inc=1, device_id=sender, device_id_type=MESH)
            pl.semaphore_wait(barrier, len(names) + 1)

        @pl.when(self.alone)
        def _():
            pl.semaphore_wait(barrier, len(names))

    def remote(self, src, dst, name):
        n = self.n_remote
        self.n_remote += 1
        copy = pltpu.make_async_remote_copy(
            src_ref=src,
            dst_ref=dst,
            send_sem=self.send_sems.at[n],
            recv_sem=self.recv_sems.at[n],
            device_id=self.peer[name],
            device_id_type=MESH,
        )
        copy.start()
        return copy

    def regroup(self, src, dst, name):
        n, k = self.n_remote, self.n_local
        self.n_remote += 1
        self.n_local += 1
        away = pltpu.make_async_remote_copy(
            src_ref=src,
            dst_ref=dst,
            send_sem=self.send_sems.at[n],
            recv_sem=self.recv_sems.at[n],
            device_id=self.peer[name],
            device_id_type=MESH,
        )
        here = pltpu.make_async_copy(src, dst, self.local_sems.at[k])
        copy = EitherCopy(self.alone, here, away)
        copy.start()
        return copy

    def local(self, src, dst):
        n = self.n_local
        self.n_local += 1
        copy = pltpu.make_async_copy(src, dst, self.local_sems.at[n])
        copy.start()
        return copy

    def keep(self, src, dst):
        self.leaving.append(self.local(src, dst))

    def finish(self):
        for copies in (*self.inner.values(), *self.outer.values(), self.flying, self.leaving):
            for copy in copies:
                copy.wait()
        self.inner, self.outer = {}, {}
        self.flying, self.leaving = [], []

    def arrived(self, ref):
        for pending in (self.inner, self.outer):
            for key in [k for k in pending if k[0] == id(ref)]:
                for copy in pending.pop(key):
                    copy.wait()

    def advance(self, moves):
        for stage, ref, low, count in moves:
            key = (id(ref), low)
            for copy in self.inner.pop(key, []):
                copy.wait()
            part = lambda bits: ref.at[self.y, pl.ds(low, count), flip_index(self.z, bits)]
            if stage == 1:
                sent = ((0, "z2"), (0, "z1"), (0, "y"))
            elif stage == 4:
                sent = ((0, "y"),)
            elif stage == 5:
                sent = ((0, "z2"), (0, "z1"))
            elif stage == 2:
                sent = ((2, "z1"), (1, "y"), (2, "y"))
            else:
                sent = ((3, "y"),)
            for bits, name in sent:
                pending = self.outer if name == "y" else self.inner
                pending.setdefault(key, []).append(self.remote(part(bits), part(bits), name))


class EitherCopy:
    def __init__(self, alone, here, away):
        self.alone, self.here, self.away = alone, here, away

    def start(self):
        pl.when(self.alone)(self.here.start)
        pl.when(jnp.logical_not(self.alone))(self.away.start)

    def wait(self):
        pl.when(self.alone)(self.here.wait)
        pl.when(jnp.logical_not(self.alone))(self.away.wait)


def flip_index(value, bits):
    low = lax.rem(value, 2)
    high = lax.div(value, 2)
    if bits & 1:
        low = 1 - low
    if bits & 2:
        high = 1 - high
    return high * 2 + low


def mixed_index(static, dynamic):
    return flip_index(dynamic, static)


def swap_index(value):
    return lax.rem(value, 2) * 2 + lax.div(value, 2)


def sems(remote, local):
    return [
        pltpu.SemaphoreType.DMA((max(remote, 1),)),
        pltpu.SemaphoreType.DMA((max(remote, 1),)),
        pltpu.SemaphoreType.DMA((max(local, 1),)),
    ]


PEERS = ("core", "x", "both", "y", "z1", "z2", "z3")
RANK_PEERS = (("core", 1), ("x", 2), ("both", 3))


def segments(lengths_ref, conts, group_tok, places):
    one = [lengths_ref[0:1, c : c + 1] for c in range(conts)]
    prompt = group_tok - sum(one)
    begin = prompt
    segment = jnp.zeros(places.shape, jnp.int32)
    begins = jnp.zeros(places.shape, jnp.int32)
    for c in range(conts):
        inside = places >= begin
        segment = segment + inside.astype(jnp.int32)
        begins = jnp.where(inside, jnp.maximum(begins, begin), begins)
        begin = begin + one[c]
    position = jnp.where(segment > 0, places - begins + prompt, places)
    return segment, position


def block_segments(lengths_ref, conts, block, index, row):
    shape = (block, 1) if row else (1, block)
    places = index * block + lax.broadcasted_iota(jnp.int32, shape, 0 if row else 1)
    return segments(lengths_ref, conts, TP * block, places)[0]


def start_kernel(
    conts, qkv_pack, w_gate, w_up, out_own, down_own, gain_tile, tokens, lengths, frequency, spread_cos, spread_sin,
    tok_out, cos_ref, sin_ref, len_out,
    g_qkv0, g_qkv1, g_gu0, g_gu1, g_out0, g_out1, g_down0, g_down1, g_gain,
    tok_buf, len_buf, send_sems, recv_sems, local_sems,
):
    net = Net(send_sems, recv_sems, local_sems)
    net.greet(PEERS, "group")
    bring = [net.regroup(lengths, len_buf, "group"), net.regroup(tokens, tok_buf, "group")]
    y, q, z = net.y, net.q, net.z
    step = w_gate.shape[2] // (2 * TP)

    def qkv_columns(layer, target):
        copies = [
            net.remote(qkv_pack.at[layer, flip_index(q, bits)], target.at[y, q, z], name)
            for name, bits in RANK_PEERS
        ]
        return copies + [net.local(qkv_pack.at[layer, q], target.at[y, q, z])]

    def gu_columns(layer, target):
        copies = []
        for name, bits in RANK_PEERS + ((None, 0),):
            for n, weight in enumerate((w_gate, w_up)):
                for half in range(2):
                    at = pl.multiple_of((half * TP + flip_index(q, bits)) * step, step)
                    src = weight.at[layer, :, pl.ds(at, step)]
                    dst = target.at[y, q, z, :, pl.ds((2 * n + half) * step, step)]
                    copies.append(net.local(src, dst) if name is None else net.remote(src, dst, name))
        return copies

    first = qkv_columns(0, g_qkv0)
    first += [net.remote(gain_tile, g_gain.at[y, q, z], name) for name, _ in RANK_PEERS]
    first.append(net.local(gain_tile, g_gain.at[y, q, z]))
    placed = [
        net.local(out_own.at[0], g_out0.at[y, 0, z]),
        net.local(down_own.at[0], g_down0.at[y, 0, z]),
        net.local(out_own.at[1], g_out1.at[y, 0, z]),
        net.local(down_own.at[1], g_down1.at[y, 0, z]),
    ]
    second = gu_columns(0, g_gu0)
    placed[0].wait()
    net.advance(((1, g_out0, 0, 1),))
    for copy in first:
        copy.wait()
    net.advance(((1, g_qkv0, 0, TP), (1, g_gain, 0, TP)))
    placed[1].wait()
    net.advance(((1, g_down0, 0, 1),))
    second += qkv_columns(1, g_qkv1) + gu_columns(1, g_gu1)
    bring[0].wait()
    block = tok_buf.shape[0]
    len_out[...] = len_buf[...]
    def table(s):
        places = mixed_index(s, net.base) * block + lax.broadcasted_iota(jnp.int32, (block, 1), 0)
        position = segments(len_buf, conts, TP * block, places)[1]
        angles = position.astype(jnp.float32) * frequency[...]
        at = slice(s * block, (s + 1) * block)
        for table_ref, values, lanes in (
            (cos_ref, jnp.cos(angles), spread_cos), (sin_ref, jnp.sin(angles), spread_sin)
        ):
            table_ref[at, :] = jnp.dot(
                values, lanes[...], precision=lax.Precision.HIGHEST, preferred_element_type=jnp.float32
            )

    table(0)
    net.advance(((2, g_out0, 0, 1), (2, g_qkv0, 0, TP), (2, g_gain, 0, TP)))
    second += placed[2:]
    table(1)
    net.advance(((3, g_out0, 0, 1), (3, g_qkv0, 0, TP), (3, g_gain, 0, TP), (2, g_down0, 0, 1)))
    table(2)
    table(3)
    bring[1].wait()
    tok_out[...] = tok_buf[...].astype(jnp.float32)
    for copy in second:
        copy.wait()
    net.finish()


def start_exchange(conts, qkv_pack, w_gate, w_up, out_own, down_own, gain_tile, tokens, lengths, frequency, spread_cos, spread_sin):
    bf, f32 = jnp.bfloat16, jnp.float32
    shape = jax.ShapeDtypeStruct
    block, depth = tokens.shape
    shard, qkv_width = qkv_pack.shape[2:]
    units = w_gate.shape[2] // TP * 2
    outs = [
        shape((block, depth), f32),
        shape((TP * block, spread_cos.shape[1]), f32),
        shape((TP * block, spread_cos.shape[1]), f32),
        shape(lengths.shape, lengths.dtype),
    ]
    for ranks, rows, width in (
        (TP, shard, qkv_width),
        (TP, shard, units),
        (1, shard, depth),
        (1, down_own.shape[1], depth),
    ):
        outs += [shape((2, ranks, TP, rows, width), bf)] * 2
    outs.append(shape((2, TP, TP) + gain_tile.shape, f32))
    return pl.pallas_call(
        functools.partial(start_kernel, conts),
        out_shape=outs,
        in_specs=[IN_VMEM] * 11,
        out_specs=[IN_VMEM] * 4 + [ANYWHERE] * 9,
        scratch_shapes=[
            pltpu.VMEM((block, depth), bf),
            pltpu.VMEM(lengths.shape, lengths.dtype),
        ] + sems(80, 24),
        compiler_params=pltpu.CompilerParams(
            collective_id=1, has_side_effects=True, vmem_limit_bytes=VMEM_LIMIT
        ),
        cost_estimate=pl.CostEstimate(flops=0, bytes_accessed=300 * 2**20, transcendentals=0),
    )(qkv_pack, w_gate, w_up, out_own, down_own, gain_tile, tokens, lengths, frequency, spread_cos, spread_sin)


def attend_rows(net, block):
    return [
        pl.ds(pl.multiple_of(mixed_index(b, net.base) * block, block), block) for b in range(TP)
    ]


def attend_forward_block(net, qkv_ref, len_ref, conts, mixed_ref, lse_ref):
    total, width = qkv_ref.shape
    block = total // TP
    q_heads = width // (2 * HEAD_DIM)
    kv_heads = q_heads // 2
    factor = 1.0 / math.sqrt(HEAD_DIM)
    key_at = q_heads * HEAD_DIM
    value_at = key_at + kv_heads * HEAD_DIM
    places = attend_rows(net, block)
    nt = (((1,), (1,)), ((), ()))
    for i in range(TP):
        row_seg = block_segments(len_ref, conts, block, i, True)
        masks = [
            block_mask(row_seg, block_segments(len_ref, conts, block, j, False), i == j, block)
            for j in range(i + 1)
        ]
        for h in range(q_heads):
            kv = h // 2
            query = qkv_ref[places[i], h * HEAD_DIM : (h + 1) * HEAD_DIM]
            scores = []
            for j in range(i + 1):
                key = qkv_ref[places[j], key_at + kv * HEAD_DIM : key_at + (kv + 1) * HEAD_DIM]
                s = lax.dot_general(query, key, nt, preferred_element_type=jnp.float32) * factor
                scores.append(jnp.where(masks[j], s, NEGATIVE))
            peak = scores[0].max(axis=1, keepdims=True)
            for s in scores[1:]:
                peak = jnp.maximum(peak, s.max(axis=1, keepdims=True))
            total_e = jnp.zeros((block, 1), jnp.float32)
            mixed = jnp.zeros((block, HEAD_DIM), jnp.float32)
            for j in range(i + 1):
                e = jnp.exp(scores[j] - peak)
                total_e = total_e + e.sum(axis=1, keepdims=True)
                value = qkv_ref[places[j], value_at + kv * HEAD_DIM : value_at + (kv + 1) * HEAD_DIM]
                mixed = mixed + jnp.dot(
                    e.astype(jnp.bfloat16), value, preferred_element_type=jnp.float32
                )
            mixed_ref[places[i], h * HEAD_DIM : (h + 1) * HEAD_DIM] = (mixed / total_e).astype(
                jnp.bfloat16
            )
            lse_ref[i, :, h : h + 1] = peak + jnp.log(total_e)


def normalize(values, gain_row):
    scale = lax.rsqrt(jnp.mean(values * values, axis=-1, keepdims=True) + EPSILON)
    return (values * scale * gain_row).astype(jnp.bfloat16)


def spread_begin(net, buf):
    return (net.remote(buf.at[0], buf.at[1], "x"), net.remote(buf.at[0], buf.at[2], "core"))


def spread_each(net, buf, begun, work):
    over_x, over_core = begun
    work(0)
    over_core.wait()
    work(2)
    over_x.wait()
    forward = net.remote(buf.at[1], buf.at[3], "core")
    work(1)
    forward.wait()
    work(3)


def collect(net, part, far_out, far_in, pass_out, pass_in):
    low = lambda v: v.astype(jnp.bfloat16)
    far_out[0] = low(part(3))
    first = net.remote(far_out.at[0], far_in.at[0], "core")
    near = part(1)
    first.wait()
    pass_out[...] = low(near + far_in[0].astype(jnp.float32))
    passed = net.remote(pass_out, pass_in, "x")
    far_out[1] = low(part(2))
    second = net.remote(far_out.at[1], far_in.at[1], "core")
    own = part(0)
    second.wait()
    own = own + far_in[1].astype(jnp.float32)
    passed.wait()
    return own + pass_in[...].astype(jnp.float32)


def forward_kernel(programs, has_cot, conts, n_moving, *refs):
    x_own, gain_a, gain_f, cos_ref, sin_ref, lengths = refs[:6]
    refs = refs[6:]
    if has_cot:
        cot, refs = refs[0], refs[1:]
    refs = refs[n_moving:]
    moving, refs = refs[:n_moving], refs[n_moving:]
    (x_next, middle_ref, lse_ref, x_low, rows_out, qkv_out, mixed_out, ffn_rows_out, gate_out, up_out, act_out) = refs[:11]
    refs = refs[11:]
    if has_cot:
        branch_out, refs, branch = refs[0], refs[1:-1], refs[-1]
    (rows, ffn_rows, w_qkv, w_o, w_gu, w_d, qkv, mixed, gate, up, act,
     far_out, far_in, pass_out, pass_in, send_sems, recv_sems, local_sems) = refs
    net = Net(send_sems, recv_sems, local_sems)
    steps = [[(kind, moving[n], low, count) for kind, n, low, count in step] for step in programs]
    block, depth = x_own.shape
    load_qkv = net.local(moving[0], w_qkv)
    load_o = net.local(moving[1], w_o)
    net.greet(("core", "x", "y", "z1", "z2", "z3"), "group" if has_cot else None)
    net.advance(steps[0])
    rows[0] = normalize(x_own[...], gain_a[...])
    begun = spread_begin(net, rows)
    load_qkv.wait()

    def project(s):
        raw = jnp.dot(
            rows[s], w_qkv[...].reshape(depth, -1), preferred_element_type=jnp.float32
        )
        at = slice(s * block, (s + 1) * block)
        turned = raw * cos_ref[at, :] + head_partner(raw, HEAD_DIM // 2) * sin_ref[at, :]
        qkv[at, :] = turned.astype(jnp.bfloat16)

    spread_each(net, rows, begun, project)
    net.keep(rows, rows_out)
    net.keep(qkv, qkv_out)
    net.advance(steps[1])
    if has_cot:
        bring = net.regroup(cot, branch.at[0], "group")
    attend_forward_block(net, qkv, lengths, conts, mixed, lse_ref)
    net.keep(mixed, mixed_out)
    net.advance(steps[2])
    load_o.wait()

    def out_part(s):
        return jnp.dot(
            mixed[s * block : (s + 1) * block, :],
            w_o[...].reshape(-1, depth),
            preferred_element_type=jnp.float32,
        )

    middle = x_own[...] + collect(
        net, out_part, far_out, far_in.at[0], pass_out, pass_in.at[0]
    )
    middle_ref[...] = middle
    net.advance(steps[3])
    net.arrived(moving[3])
    load_d = net.local(moving[3], w_d)
    ffn_rows[0] = normalize(middle, gain_f[...])
    begun = spread_begin(net, ffn_rows)
    if has_cot:
        bring.wait()
        over_x, over_core = spread_begin(net, branch)
    net.arrived(moving[2])
    load_gu = net.local(moving[2], w_gu)
    net.advance(steps[4])
    load_d.wait()
    load_gu.wait()
    units = act.shape[2]

    def expand(s):
        value = ffn_rows[s]
        gating = jnp.dot(
            value, w_gu[:, :, :, :, :units].reshape(depth, units), preferred_element_type=jnp.float32
        )
        upward = jnp.dot(
            value, w_gu[:, :, :, :, units:].reshape(depth, units), preferred_element_type=jnp.float32
        )
        gate[s] = gating.astype(jnp.bfloat16)
        up[s] = upward.astype(jnp.bfloat16)
        act[s] = (gating * jax.nn.sigmoid(gating) * upward).astype(jnp.bfloat16)

    spread_each(net, ffn_rows, begun, expand)
    if has_cot:
        over_x.wait()
        forward = net.remote(branch.at[1], branch.at[3], "core")
    net.keep(ffn_rows, ffn_rows_out)
    net.keep(gate, gate_out)
    net.keep(up, up_out)
    net.keep(act, act_out)

    def down_part(s):
        return jnp.dot(act[s], w_d[...].reshape(-1, depth), preferred_element_type=jnp.float32)

    result = middle_ref[...] + collect_during(
        net,
        down_part,
        (far_out, far_in.at[1], pass_out, pass_in.at[1]),
        lambda: net.advance(steps[5]),
    )
    if has_cot:
        over_core.wait()
        forward.wait()
        net.keep(branch, branch_out)
    x_next[...] = result
    x_low[...] = result.astype(jnp.bfloat16)
    net.finish()


def forward_layer(programs, cot, cid, conts, x_own, gain_a, gain_f, cosine, sine, lengths, moving):
    bf, f32 = jnp.bfloat16, jnp.float32
    block, depth = x_own.shape
    total, qkv_width = cosine.shape
    units = moving[2].shape[4] // 2
    q_heads = qkv_width // (2 * HEAD_DIM)
    shape = jax.ShapeDtypeStruct
    outs = [shape(m.shape, m.dtype) for m in moving] + [
        shape((block, depth), f32),
        shape((block, depth), f32),
        shape((TP, block, q_heads), f32),
        shape((block, depth), bf),
        shape((TP, block, depth), bf),
        shape((total, qkv_width), bf),
        shape((total, qkv_width // 2), bf),
        shape((TP, block, depth), bf),
        shape((TP, block, units), bf),
        shape((TP, block, units), bf),
        shape((TP, block, units), bf),
    ]
    n = len(moving)
    given = [] if cot is None else [cot]
    c = len(given)
    outs += [shape((TP, block, depth), bf)] * c
    scratch = [
        pltpu.VMEM((TP, block, depth), bf),
        pltpu.VMEM((TP, block, depth), bf),
        pltpu.VMEM(moving[0].shape, bf),
        pltpu.VMEM(moving[1].shape, bf),
        pltpu.VMEM(moving[2].shape, bf),
        pltpu.VMEM(moving[3].shape, bf),
        pltpu.VMEM((total, qkv_width), bf),
        pltpu.VMEM((total, qkv_width // 2), bf),
        pltpu.VMEM((TP, block, units), bf),
        pltpu.VMEM((TP, block, units), bf),
        pltpu.VMEM((TP, block, units), bf),
        pltpu.VMEM((2, block, depth), bf),
        pltpu.VMEM((2, 2, block, depth), bf),
        pltpu.VMEM((block, depth), bf),
        pltpu.VMEM((2, block, depth), bf),
    ] + sems(80, 24) + [pltpu.VMEM((TP, block, depth), bf)] * c
    return pl.pallas_call(
        functools.partial(forward_kernel, programs, bool(c), conts, n),
        out_shape=outs,
        in_specs=[IN_VMEM] * (6 + c) + [ANYWHERE] * n,
        out_specs=[ANYWHERE] * n + [IN_VMEM] * 4 + [ANYWHERE] * (7 + c),
        scratch_shapes=scratch,
        input_output_aliases={6 + c + i: i for i in range(n)},
        compiler_params=pltpu.CompilerParams(
            collective_id=cid, has_side_effects=True, vmem_limit_bytes=VMEM_LIMIT
        ),
        cost_estimate=pl.CostEstimate(
            flops=16 * 10**9, bytes_accessed=400 * 2**20, transcendentals=10**7
        ),
    )(x_own, gain_a, gain_f, cosine, sine, lengths, *given, *moving)


def moved_shape(kind, source):
    shape = source.shape
    if kind in ("y", "whole_y"):
        kept = shape
    elif kind == "g":
        kept = shape
    elif kind == "zc":
        kept = (3, shape[0]) + shape[2:]
    elif kind in ("z", "t"):
        kept = (3,) + shape[1:]
    else:
        kept = (3,) + shape
    return jax.ShapeDtypeStruct(kept, source.dtype)


def begin_move(net, kind, source, target):
    if kind in ("y", "whole_y"):
        return [net.remote(source, target, "y")]
    if kind == "g":
        return [net.regroup(source, target, "home")]
    copies = []
    for name, bits in RANK_PEERS:
        if kind == "z":
            copies.append(
                net.remote(source.at[flip_index(net.z, bits)], target.at[bits - 1], f"z{bits}")
            )
        elif kind == "zc":
            copies.append(
                net.remote(source.at[:, flip_index(net.z, bits)], target.at[bits - 1], f"z{bits}")
            )
        elif kind == "whole_z":
            copies.append(net.remote(source, target.at[bits - 1], f"z{bits}"))
        elif kind == "t":
            copies.append(
                net.remote(source.at[flip_index(net.q, bits)], target.at[bits - 1], name)
            )
        else:
            copies.append(net.remote(source, target.at[bits - 1], name))
    return copies


def begin_moves(net, kinds, sources, targets):
    for kind, source, target in zip(kinds, sources, targets):
        net.flying += begin_move(net, kind, source, target)


def greet_all(net, kinds):
    net.greet(PEERS, "home" if "g" in kinds else None)


def tail_kernel(
    gain_part, sgu_in, o_own_in, o_other, qkv_own_in, qkv_other, bqkv, up_low,
    gain_out, out_sum, b_gu, b_qkv, t_gu, t_qkv, t_qkv1, back,
    sgu, so, s_qkv, qkv_got, o_got, gu_one, gu_pass, gu_two, o_one, o_pass, o_two, q_one, q_pass, q_two,
    gain_t, gain_a, gain_z, gain_b, gain_y, send_sems, recv_sems, local_sems,
):
    net = Net(send_sems, recv_sems, local_sems)
    f32, bf = jnp.float32, jnp.bfloat16
    z, q = net.z, net.q
    z1, z2, z3 = (flip_index(z, bits) for bits in (1, 2, 3))
    loads = [net.local(sgu_in, sgu), net.local(o_own_in, so), net.local(qkv_own_in, s_qkv)]
    net.greet(PEERS, "home")
    over_y = [net.remote(o_other, o_got, "y"), net.remote(qkv_other, qkv_got, "y")]

    def first_hop(source, target, part):
        return [
            net.remote(source.at[part + (z3,)], target.at[(1,) + part], "z1"),
            net.remote(source.at[part + (z1,)], target.at[(0,) + part], "z1"),
        ]

    halves = [(pl.ds(0, 2),), (pl.ds(2, 2),)]
    gu_first = [first_hop(sgu_in, gu_one, part) for part in halves]
    gains = [net.remote(gain_part, gain_t.at[bits - 1], name) for name, bits in RANK_PEERS]
    net.flying += begin_move(net, "t", bqkv, t_qkv1)
    net.flying += begin_move(net, "g", up_low, back)
    for copy in loads:
        copy.wait()
    over_y[0].wait()
    so[...] = (so[...].astype(f32) + o_got[...].astype(f32)).astype(bf)
    o_first = first_hop(so, o_one, ())
    over_y[1].wait()
    s_qkv[...] = (s_qkv[...].astype(f32) + qkv_got[...].astype(f32)).astype(bf)
    every = (pl.ds(0, TP),)
    q_first = first_hop(s_qkv, q_one, every)
    for copy in gains:
        copy.wait()
    gain_a[...] = gain_part[...] + gain_t[0] + gain_t[1] + gain_t[2]
    gains = [net.remote(gain_a, gain_z.at[bits - 1], f"z{bits}") for bits in (1, 2, 3)]

    def second_hop(own, one, passing, two, part, first):
        first[0].wait()
        passing[part or (Ellipsis,)] = (
            own[part + (z2,)].astype(f32) + one[(1,) + part].astype(f32)
        ).astype(bf)
        at = (lambda ref: ref.at[part]) if part else (lambda ref: ref)
        return net.remote(at(passing), at(two), "z2")

    gu_second = [
        second_hop(sgu, gu_one, gu_pass, gu_two, part, first) for part, first in zip(halves, gu_first)
    ]
    o_second = second_hop(so, o_one, o_pass, o_two, (), o_first)
    q_second = second_hop(s_qkv, q_one, q_pass, q_two, every, q_first)
    for copy in gains:
        copy.wait()
    gain_b[...] = gain_a[...] + gain_z[0] + gain_z[1] + gain_z[2]
    gain_over_y = net.remote(gain_b, gain_y, "y")

    def total(own, one, two, part):
        whole = part or (Ellipsis,)
        return (
            own[part + (z,)].astype(f32) + one[(0,) + part].astype(f32) + two[whole].astype(f32)
        )

    for part, first, second in zip(halves, gu_first, gu_second):
        first[1].wait()
        second.wait()
        b_gu[part] = total(sgu, gu_one, gu_two, part).astype(bf)
    net.flying += begin_move(net, "t", b_gu, t_gu)
    o_first[1].wait()
    o_second.wait()
    out_sum[...] = total(so, o_one, o_two, ())
    q_first[1].wait()
    q_second.wait()
    b_qkv[...] = total(s_qkv, q_one, q_two, every).astype(bf)
    net.flying += begin_move(net, "t", b_qkv, t_qkv)
    gain_over_y.wait()
    gain_out[...] = gain_b[...] + gain_y[...]
    net.finish()


def run_tail(cid, gain_part, sgu, so, o_other, qkv_own, qkv_other, bqkv, up_low):
    bf, f32 = jnp.bfloat16, jnp.float32
    shape = jax.ShapeDtypeStruct
    gu_block = (TP,) + sgu.shape[2:]
    o_block = so.shape[1:]
    q_block = (TP,) + qkv_own.shape[2:]
    three = lambda block: (3,) + block[1:]
    return pl.pallas_call(
        tail_kernel,
        out_shape=[
            shape(gain_part.shape, f32),
            shape(o_block, f32),
            shape(gu_block, bf),
            shape(q_block, bf),
            shape(three(gu_block), bf),
            shape(three(q_block), bf),
            shape(three(q_block), bf),
            shape(up_low.shape, bf),
        ],
        in_specs=[IN_VMEM] + [ANYWHERE] * 7,
        out_specs=[IN_VMEM] * 4 + [ANYWHERE] * 4,
        scratch_shapes=[
            pltpu.VMEM(sgu.shape, bf),
            pltpu.VMEM(so.shape, bf),
            pltpu.VMEM(qkv_own.shape, bf),
            pltpu.VMEM(qkv_own.shape, bf),
            pltpu.VMEM(so.shape, bf),
        ]
        + [
            pltpu.VMEM(dims, bf)
            for block in (gu_block, o_block, q_block)
            for dims in ((2,) + block, block, block)
        ]
        + [
            pltpu.VMEM(dims, f32)
            for dims in (
                (3,) + gain_part.shape, gain_part.shape, (3,) + gain_part.shape, gain_part.shape, gain_part.shape
            )
        ]
        + sems(48, 8),
        compiler_params=pltpu.CompilerParams(
            collective_id=cid, has_side_effects=True, vmem_limit_bytes=VMEM_LIMIT
        ),
        cost_estimate=pl.CostEstimate(flops=0, bytes_accessed=200 * 2**20, transcendentals=0),
    )(gain_part, sgu, so, o_other, qkv_own, qkv_other, bqkv, up_low)


def norm_backward(values, gain_row, incoming):
    inv = lax.rsqrt(jnp.mean(values * values, axis=-1, keepdims=True) + EPSILON)
    weighted = incoming * gain_row
    inner = jnp.mean(weighted * values, axis=-1, keepdims=True)
    grad = inv * weighted - values * (inv * inv * inv * inner)
    return grad, jnp.sum(incoming * values * inv, axis=0, keepdims=True)


def collect_during(net, part, bufs, meanwhile):
    far_out, far_in, pass_out, pass_in = bufs
    low = lambda v: v.astype(jnp.bfloat16)
    far_out[0] = low(part(3))
    first = net.remote(far_out.at[0], far_in.at[0], "core")
    near = part(1)
    first.wait()
    pass_out[...] = low(near + far_in[0].astype(jnp.float32))
    passed = net.remote(pass_out, pass_in, "x")
    far_out[1] = low(part(2))
    second = net.remote(far_out.at[1], far_in.at[1], "core")
    own = part(0)
    second.wait()
    own = own + far_in[1].astype(jnp.float32)
    meanwhile()
    passed.wait()
    return own + pass_in[...].astype(jnp.float32)


NT = (((1,), (1,)), ((), ()))
TN = (((0,), (0,)), ((), ()))


def dot_nt(left, right):
    return lax.dot_general(left, right, NT, preferred_element_type=jnp.float32)


def dot_tn(left, right):
    return lax.dot_general(left, right, TN, preferred_element_type=jnp.float32)


def ffn_backward_kernel(kinds, given, *refs):
    n = len(kinds)
    middle, gain, source_in = refs[:3]
    acts, rows_in, gates, ups, mixed_in, wd_in, wgu_in, wo_in = refs[3:11]
    refs = refs[11:]
    sources, targets, refs = refs[:n], refs[n : 2 * n], refs[2 * n :]
    (grad_middle, gain_grad, dmixed_out, d_own, d_got, gu_own, gu_other, o_own, o_other) = refs[:9]
    (branch, proj, act, rows, gate, up, mixed, dmixed, w_d, w_gu, w_o, g_down, g_gu, g_out,
     far_out, far_in, pass_out, pass_in, send_sems, recv_sems, local_sems) = refs[9:]
    net = Net(send_sems, recv_sems, local_sems)
    block, depth = middle.shape
    units = act.shape[2]
    total = TP * block
    loads = {}
    if given:
        loads["branch"] = net.local(source_in, branch)
    for name, src, dst in (
        ("w_d", wd_in, w_d), ("gate", gates, gate), ("up", ups, up), ("act", acts, act),
        ("w_gu", wgu_in, w_gu), ("rows", rows_in, rows), ("w_o", wo_in, w_o), ("mixed", mixed_in, mixed),
    ):
        loads[name] = net.local(src, dst)
    greet_all(net, kinds)
    begin_moves(net, kinds, sources, targets)
    if given:
        loads["branch"].wait()
    else:
        branch[0] = source_in[...].astype(jnp.bfloat16)
        begun = spread_begin(net, branch)
    loads["w_d"].wait()
    loads["gate"].wait()
    loads["up"].wait()

    def through(s):
        grad_act = dot_nt(branch[s], w_d[...].reshape(units, depth))
        gating = gate[s].astype(jnp.float32)
        upward = up[s].astype(jnp.float32)
        sig = jax.nn.sigmoid(gating)
        shared = grad_act * sig
        gate[s] = (shared * upward * (1.0 + gating * (1.0 - sig))).astype(jnp.bfloat16)
        up[s] = (shared * gating).astype(jnp.bfloat16)

    if given:
        for s in (3, 1, 2, 0):
            through(s)
    else:
        spread_each(net, branch, begun, through)
    loads["act"].wait()
    theirs, ours = 1 - net.y, net.y
    drows, urows = g_down.shape[2], g_gu.shape[3]
    dwide, uwide = 2 * drows, 2 * TP * urows

    def down_half(side):
        def tile(m, carry):
            lanes = pl.ds(pl.multiple_of((side * 2 + m) * dwide, dwide), dwide)
            grad = dot_tn(act[:, :, lanes].reshape(total, dwide), branch[...].reshape(total, depth))
            g_down[side, pl.ds(2 * m, 2)] = grad.astype(jnp.bfloat16).reshape(2, drows, depth)
            return carry

        lax.fori_loop(0, 2, tile, 0)

    def gu_half(side):
        def tile(m, carry):
            lanes = pl.ds(pl.multiple_of((side * 2 + m) * uwide, uwide), uwide)
            left = rows[:, :, lanes].reshape(total, uwide)
            for ref, at in ((gate, 0), (up, units)):
                grad = dot_tn(left, ref[...].reshape(total, units)).astype(jnp.bfloat16)
                g_gu[side, pl.ds(2 * m, 2), :, :, at : at + units] = grad.reshape(2, TP, urows, units)
            return carry

        lax.fori_loop(0, 2, tile, 0)

    down_half(theirs)
    net.flying.append(net.remote(g_down.at[theirs], d_got, "y"))
    loads["w_gu"].wait()
    loads["rows"].wait()

    def back(s):
        return dot_nt(gate[s], w_gu[:, :, :, :, :units].reshape(depth, units)) + dot_nt(
            up[s], w_gu[:, :, :, :, units:].reshape(depth, units)
        )

    def meanwhile():
        gu_half(theirs)
        net.keep(g_gu.at[theirs], gu_other)
        gu_half(ours)
        net.keep(g_gu.at[ours], gu_own)
        down_half(ours)
        net.keep(g_down.at[ours], d_own)

    incoming = collect_during(net, back, (far_out, far_in, pass_out, pass_in), meanwhile)
    part, gain_part = norm_backward(middle[...], gain[...], incoming)
    gain_grad[...] = gain_part
    grad_mid = (branch[0].astype(jnp.float32) if given else source_in[...]) + part
    grad_middle[...] = grad_mid
    proj[0] = grad_mid.astype(jnp.bfloat16)
    begun = spread_begin(net, proj)
    loads["w_o"].wait()
    loads["mixed"].wait()

    def mix_back(s):
        dmixed[s * block : (s + 1) * block, :] = dot_nt(
            proj[s], w_o[...].reshape(-1, depth)
        ).astype(jnp.bfloat16)

    spread_each(net, proj, begun, mix_back)
    net.keep(dmixed, dmixed_out)
    grad = dot_tn(mixed[...], proj[...].reshape(total, depth)).astype(jnp.bfloat16)
    g_out[...] = grad.reshape(g_out.shape)
    net.keep(g_out.at[ours], o_own)
    net.keep(g_out.at[theirs], o_other)
    net.finish()


def ffn_backward(cid, moves, source, given, middle, gain, acts, rows, gates, ups, mixed, w_d, w_gu, w_o):
    bf, f32 = jnp.bfloat16, jnp.float32
    shape = jax.ShapeDtypeStruct
    block, depth = middle.shape
    units = gates.shape[2]
    total, mixed_width = mixed.shape
    kinds = tuple(kind for kind, _ in moves)
    sources = [source for _, source in moves]
    n = len(moves)
    drows, urows, orows = w_d.shape[3], w_gu.shape[3], w_o.shape[3]
    outs = [moved_shape(kind, source) for kind, source in moves] + [
        shape((block, depth), f32),
        shape((1, depth), f32),
        shape((total, mixed_width), bf),
        shape((TP, drows, depth), bf),
        shape((TP, drows, depth), bf),
        shape((TP, TP, urows, 2 * units), bf),
        shape((TP, TP, urows, 2 * units), bf),
        shape((TP, orows, depth), bf),
        shape((TP, orows, depth), bf),
    ]
    scratch = [
        pltpu.VMEM((TP, block, depth), bf),
        pltpu.VMEM((TP, block, depth), bf),
        pltpu.VMEM((TP, block, units), bf),
        pltpu.VMEM((TP, block, depth), bf),
        pltpu.VMEM((TP, block, units), bf),
        pltpu.VMEM((TP, block, units), bf),
        pltpu.VMEM((total, mixed_width), bf),
        pltpu.VMEM((total, mixed_width), bf),
        pltpu.VMEM(w_d.shape, bf),
        pltpu.VMEM(w_gu.shape, bf),
        pltpu.VMEM(w_o.shape, bf),
        pltpu.VMEM((2, TP, drows, depth), bf),
        pltpu.VMEM((2, TP, TP, urows, 2 * units), bf),
        pltpu.VMEM((2, TP, orows, depth), bf),
        pltpu.VMEM((2, block, depth), bf),
        pltpu.VMEM((2, block, depth), bf),
        pltpu.VMEM((block, depth), bf),
        pltpu.VMEM((block, depth), bf),
    ] + sems(48, 20)
    operands = [middle, gain, source, acts, rows, gates, ups, mixed, w_d, w_gu, w_o]
    return pl.pallas_call(
        functools.partial(ffn_backward_kernel, kinds, given),
        out_shape=outs,
        in_specs=[IN_VMEM] * 2 + [ANYWHERE if given else IN_VMEM] + [ANYWHERE] * (8 + n),
        out_specs=[ANYWHERE] * n + [IN_VMEM] * 2 + [ANYWHERE] * 7,
        scratch_shapes=scratch,
        compiler_params=pltpu.CompilerParams(
            collective_id=cid, has_side_effects=True, vmem_limit_bytes=VMEM_LIMIT
        ),
        cost_estimate=pl.CostEstimate(
            flops=24 * 10**9, bytes_accessed=200 * 2**20, transcendentals=10**6
        ),
    )(*operands, *sources)


def attend_backward_block(net, qkv_ref, grad_ref, mixed_ref, lse_ref, len_ref, conts, acc_ref):
    total, width = qkv_ref.shape
    block = total // TP
    q_heads = width // (2 * HEAD_DIM)
    kv_heads = q_heads // 2
    factor = 1.0 / math.sqrt(HEAD_DIM)
    key_at = q_heads * HEAD_DIM
    value_at = key_at + kv_heads * HEAD_DIM
    places = attend_rows(net, block)
    acc_ref[:, key_at:] = jnp.zeros((total, width - key_at), jnp.float32)
    for i in range(TP):
        row_seg = block_segments(len_ref, conts, block, i, True)
        masks = [
            block_mask(row_seg, block_segments(len_ref, conts, block, j, False), i == j, block)
            for j in range(i + 1)
        ]
        for h in range(q_heads):
            kv = h // 2
            lanes = slice(h * HEAD_DIM, (h + 1) * HEAD_DIM)
            query = qkv_ref[places[i], lanes]
            grad = grad_ref[places[i], lanes]
            lse = lse_ref[i, :, h : h + 1]
            inner = jnp.sum(
                grad.astype(jnp.float32) * mixed_ref[places[i], lanes].astype(jnp.float32),
                axis=1,
                keepdims=True,
            )
            grad_query = jnp.zeros((block, HEAD_DIM), jnp.float32)
            key_lanes = slice(key_at + kv * HEAD_DIM, key_at + (kv + 1) * HEAD_DIM)
            value_lanes = slice(value_at + kv * HEAD_DIM, value_at + (kv + 1) * HEAD_DIM)
            for j in range(i + 1):
                key = qkv_ref[places[j], key_lanes]
                value = qkv_ref[places[j], value_lanes]
                s = dot_nt(query, key) * factor
                prob = jnp.where(masks[j], jnp.exp(s - lse), 0.0)
                grad_prob = dot_nt(grad, value)
                grad_score = (prob * (grad_prob - inner)).astype(jnp.bfloat16)
                grad_query = grad_query + jnp.dot(
                    grad_score, key, preferred_element_type=jnp.float32
                )
                acc_ref[places[j], key_lanes] += dot_tn(grad_score, query) * factor
                acc_ref[places[j], value_lanes] += dot_tn(prob.astype(jnp.bfloat16), grad)
            acc_ref[places[i], lanes] = grad_query * factor


def attn_backward_kernel(kinds, conts, *refs):
    n = len(kinds)
    (grad_middle, hidden, gain, qkv, dmixed, mixed, lse, lengths, cos_ref, sin_ref) = refs[:10]
    rows_in, w_in = refs[10:12]
    sources, targets, refs = refs[12 : 12 + n], refs[12 + n : 12 + 2 * n], refs[12 + 2 * n :]
    upstream, up_low, gain_grad, qkv_own, qkv_other = refs[:5]
    (acc, dqkv, rows, w_qkv, g_qkv, far_out, far_in, pass_out, pass_in,
     send_sems, recv_sems, local_sems) = refs[5:]
    net = Net(send_sems, recv_sems, local_sems)
    block, depth = hidden.shape
    total = TP * block
    load_rows = net.local(rows_in, rows)
    load_w = net.local(w_in, w_qkv)
    greet_all(net, kinds)
    begin_moves(net, kinds, sources, targets)
    attend_backward_block(net, qkv, dmixed, mixed, lse, lengths, conts, acc)
    for s in range(TP):
        at = slice(s * block, (s + 1) * block)
        value = acc[at, :]
        turned = value * cos_ref[at, :] - head_partner(value, HEAD_DIM // 2) * sin_ref[at, :]
        dqkv[at, :] = turned.astype(jnp.bfloat16)
    load_w.wait()
    load_rows.wait()
    urows = g_qkv.shape[2]
    wide = 2 * TP * urows

    def back(s):
        return dot_nt(dqkv[s * block : (s + 1) * block, :], w_qkv[...].reshape(depth, -1))

    def meanwhile():
        def tile(m, carry):
            lanes = pl.ds(pl.multiple_of(m * wide, wide), wide)
            grad = dot_tn(rows[:, :, lanes].reshape(total, wide), dqkv[...])
            g_qkv[pl.ds(2 * m, 2)] = grad.astype(jnp.bfloat16).reshape(2, TP, urows, -1)
            return carry

        lax.fori_loop(0, TP, tile, 0)
        net.keep(g_qkv.at[pl.ds(net.y * TP, TP)], qkv_own)
        net.keep(g_qkv.at[pl.ds((1 - net.y) * TP, TP)], qkv_other)

    incoming = collect_during(net, back, (far_out, far_in, pass_out, pass_in), meanwhile)
    part, gain_part = norm_backward(hidden[...], gain[...], incoming)
    gain_grad[...] = gain_part
    result = grad_middle[...] + part
    upstream[...] = result
    up_low[...] = result.astype(jnp.bfloat16)
    net.finish()


def attn_backward(
    cid, moves, conts, grad_middle, hidden, gain, qkv, dmixed, mixed, lse, lengths, cosine, sine, rows, w_qkv
):
    bf, f32 = jnp.bfloat16, jnp.float32
    shape = jax.ShapeDtypeStruct
    block, depth = hidden.shape
    total, width = qkv.shape
    kinds = tuple(kind for kind, _ in moves)
    sources = [source for _, source in moves]
    n = len(moves)
    urows = w_qkv.shape[3]
    outs = [moved_shape(kind, source) for kind, source in moves] + [
        shape((block, depth), f32),
        shape((block, depth), bf),
        shape((1, depth), f32),
        shape((TP, TP, urows, width), bf),
        shape((TP, TP, urows, width), bf),
    ]
    scratch = [
        pltpu.VMEM((total, width), f32),
        pltpu.VMEM((total, width), bf),
        pltpu.VMEM((TP, block, depth), bf),
        pltpu.VMEM(w_qkv.shape, bf),
        pltpu.VMEM((2 * TP, TP, urows, width), bf),
        pltpu.VMEM((2, block, depth), bf),
        pltpu.VMEM((2, block, depth), bf),
        pltpu.VMEM((block, depth), bf),
        pltpu.VMEM((block, depth), bf),
    ] + sems(48, 8)
    return pl.pallas_call(
        functools.partial(attn_backward_kernel, kinds, conts),
        out_shape=outs,
        in_specs=[IN_VMEM] * 10 + [ANYWHERE] * (2 + n),
        out_specs=[ANYWHERE] * n + [IN_VMEM] * 3 + [ANYWHERE] * 2,
        scratch_shapes=scratch,
        compiler_params=pltpu.CompilerParams(
            collective_id=cid, has_side_effects=True, vmem_limit_bytes=VMEM_LIMIT
        ),
        cost_estimate=pl.CostEstimate(
            flops=16 * 10**9, bytes_accessed=200 * 2**20, transcendentals=10**7
        ),
    )(grad_middle, hidden, gain, qkv, dmixed, mixed, lse, lengths, cosine, sine, rows, w_qkv, *sources)


def add_low(own, got):
    return (own.astype(jnp.float32) + got.astype(jnp.float32)).astype(jnp.bfloat16)


def z_total(summed, got, axis):
    own = lax.dynamic_index_in_dim(summed, lax.axis_index("fsdp"), axis, keepdims=False)
    return (own.astype(jnp.float32) + jnp.sum(got.astype(jnp.float32), axis=0)).astype(jnp.bfloat16)


def end_kernel(step, qw, kw, *refs):
    layers, refs = (refs[:7], refs[7:15]), refs[15:]
    x_outs, back, refs = refs[:2], refs[2], refs[3:]
    out_x, out_back, out_q, out_k, out_v, out_o, out_g, out_u, out_d = refs
    q = lax.rem(lax.axis_index("dp"), TP)
    z = lax.axis_index("fsdp")
    low, high = lax.rem(q, 2) == 1, lax.div(q, 2) == 1

    def columns(blocks, got):
        pieces = [blocks[q]] + [got[k] for k in range(3)]
        a = [jnp.where(low, pieces[i ^ 1], pieces[i]) for i in range(4)]
        return [jnp.where(high, a[i ^ 2], a[i]).astype(jnp.float32) for i in range(4)]

    def lay(target, layer, pieces, at, width):
        half = width // 2
        for n, piece in enumerate(pieces):
            for side in range(2):
                to = (side * TP + n) * half
                target[layer, :, to : to + half] = piece[:, at + side * half : at + (side + 1) * half]

    for layer in range(2):
        bqkv, tqkv, bgu, tgu = layers[layer][:4]
        pieces = columns(bqkv, tqkv)
        lay(out_q, layer, pieces, 0, qw)
        lay(out_k, layer, pieces, qw, kw)
        lay(out_v, layer, pieces, qw + kw, kw)
        pieces = columns(bgu, tgu)
        lay(out_g, layer, pieces, 0, 2 * step)
        lay(out_u, layer, pieces, 2 * step, 2 * step)
        sums = [(*layers[layer][-2:], out_d)]
        if layer == 0:
            out_o[0] = layers[0][4][...]
        else:
            sums.append((*layers[1][4:6], out_o))
        for summed, got, target in sums:
            value = summed[z].astype(jnp.float32)
            for k in range(3):
                value = value + got[k].astype(jnp.float32)
            target[layer] = value
        out_x[layer] = x_outs[layer][...]
    out_back[...] = back[...].astype(jnp.float32)


def end_assembly(step, qw, kw, pieces, x_outs, back):
    f32 = jnp.float32
    shape = jax.ShapeDtypeStruct
    block, depth = back.shape
    rows = pieces[0].shape[1]
    drows = pieces[5].shape[1]
    outs = [
        shape((2, block, depth), jnp.bfloat16),
        shape((block, depth), f32),
        shape((2, rows, TP * qw), f32),
        shape((2, rows, TP * kw), f32),
        shape((2, rows, TP * kw), f32),
        shape((2, rows, depth), f32),
        shape((2, rows, TP * 2 * step), f32),
        shape((2, rows, TP * 2 * step), f32),
        shape((2, drows, depth), f32),
    ]
    return pl.pallas_call(
        functools.partial(end_kernel, step, qw, kw),
        out_shape=outs,
        in_specs=[IN_VMEM] * 18,
        out_specs=[IN_VMEM] * 9,
        compiler_params=pltpu.CompilerParams(vmem_limit_bytes=VMEM_LIMIT),
    )(*pieces, *x_outs, back)


def column_pack(weights):
    parts = []
    for weight in weights:
        layers, rows, width = weight.shape
        view = weight.reshape(layers, rows, 2, TP, width // (2 * TP))
        parts.append(view.transpose(0, 3, 1, 2, 4).reshape(layers, TP, rows, width // TP))
    return jnp.concatenate(parts, axis=3)


def fast_device(
    tokens, gain_attn, w_query, w_key, w_value, w_out, gain_ffn, w_gate, w_up, w_down, lengths, cotangent
):
    depth = tokens.shape[1]
    shard = w_query.shape[1]
    conts = lengths.shape[1]
    halfway = HEAD_DIM // 2
    qw, kw = w_query.shape[2] // TP, w_key.shape[2] // TP
    step = w_gate.shape[2] // (2 * TP)
    frequency = ROPE_BASE ** (-jnp.arange(halfway, dtype=jnp.float32) * 2.0 / HEAD_DIM)
    lane = jnp.arange(128)[:, None]
    column = jnp.arange(qw + 2 * kw)[None]
    turned = column < qw + kw
    frequency = jnp.pad(frequency, (0, 128 - halfway))[None]
    picks = (lane == jnp.where(turned, column % halfway, halfway)).astype(jnp.float32)
    signed = picks * jnp.where(turned, jnp.where(column % HEAD_DIM < halfway, -1.0, 1.0), 0.0)
    gain_tile = jnp.pad(
        jnp.concatenate([gain_attn, gain_ffn], axis=0).astype(jnp.float32), ((0, 4), (0, 128 - shard))
    )
    len_tile = jnp.pad(lengths, ((0, 7), (0, 128 - conts)))
    (hidden, cosine, sine, lens, g_qkv0, g_qkv1, g_gu0, g_gu1, g_out0, g_out1, g_down0, g_down1, g_gain) = (
        start_exchange(
            conts, column_pack((w_query, w_key, w_value)), w_gate, w_up, w_out, w_down, gain_tile,
            tokens, len_tile, frequency, picks, signed,
        )
    )
    gains = jnp.transpose(g_gain[..., :4, :shard], (3, 0, 1, 2, 4)).reshape(4, 1, depth)
    qkv, out, gu, down, qkv_next, out_next, gu_next, down_next = range(8)
    programs0 = (
        ((3, down, 0, 1), (1, gu, 0, 2), (1, gu, 2, 2)),
        ((2, gu, 0, 2),),
        ((2, gu, 2, 2), (3, gu, 0, 2)),
        ((3, gu, 2, 2), (1, qkv_next, 0, 4), (1, out_next, 0, 1)),
        ((2, qkv_next, 0, 4), (2, out_next, 0, 1), (1, down_next, 0, 1), (1, gu_next, 0, 2)),
        ((3, qkv_next, 0, 4), (3, out_next, 0, 1), (2, down_next, 0, 1)),
    )
    programs1 = (
        ((3, down, 0, 1), (2, gu, 0, 2), (1, gu, 2, 2)),
        ((3, gu, 0, 2), (2, gu, 2, 2)),
        (),
        ((3, gu, 2, 2),),
        (),
        (),
    )
    tables = (cosine, sine, lens)
    res = forward_layer(
        programs0, cotangent, 2, conts, hidden, gains[0], gains[2], *tables,
        (g_qkv0, g_out0, g_gu0, g_down0, g_qkv1, g_out1, g_gu1, g_down1),
    )
    weights0, moving1, acts0 = res[:4], res[4:8], res[8:]
    (x1, mid0, lse0, low1, rows0, qkv0, mix0, frows0, gate0, up0, act0, branch) = acts0
    res = forward_layer(programs1, None, 3, conts, x1, gains[1], gains[3], *tables, moving1)
    weights1, acts1 = res[:4], res[4:]
    (x2, mid1, lse1, low2, rows1, qkv1, mix1, frows1, gate1, up1, act1) = acts1

    (low1_back, gmid1, ggf1, dmix1, d_own, d_got, gu_own, gu_other, o_own, o_other) = ffn_backward(
        4, (("g", low1),), branch, True, mid1, gains[3], act1, frows1, gate1, up1, mix1,
        weights1[3], weights1[2], weights1[1],
    )
    sd1 = add_low(d_own, d_got)
    (gu_got, rd1, low2_back, up_1, _, gga1, qkv_own1, qkv_other1) = attn_backward(
        5, (("y", gu_other), ("z", sd1), ("g", low2)), conts,
        gmid1, x1, gains[1], qkv1, dmix1, mix1, lse1, lens, cosine, sine, rows1, weights1[0],
    )
    sgu1 = add_low(gu_own, gu_got)
    (qkv_got1, o_got, rgu1, gmid0, ggf0, dmix0, d_own0, d_got0, gu_own0, gu_other0, o_own0, o_other0) = ffn_backward(
        6, (("y", qkv_other1), ("y", o_other), ("zc", sgu1)), up_1, False, mid0, gains[2], act0, frows0, gate0, up0, mix0,
        weights0[3], weights0[2], weights0[1],
    )
    sqkv1 = add_low(qkv_own1, qkv_got1)
    so1 = add_low(o_own, o_got)
    sd0 = add_low(d_own0, d_got0)
    bgu1 = z_total(sgu1, rgu1, 1)
    (gu_got0, rqkv1, rd0, ro1, tgu1, _, up_low, gga0, qkv_own0, qkv_other0) = attn_backward(
        7, (("y", gu_other0), ("zc", sqkv1), ("z", sd0), ("z", so1), ("t", bgu1)), conts,
        gmid0, hidden, gains[0], qkv0, dmix0, mix0, lse0, lens, cosine, sine, rows0, weights0[0],
    )
    sgu0 = add_low(gu_own0, gu_got0)
    bqkv1 = z_total(sqkv1, rqkv1, 1)
    gain_part = jnp.concatenate([gga0, gga1, ggf0, ggf1, jnp.zeros((4, depth), jnp.float32)], axis=0)
    (gain_sums, osum0, bgu0, bqkv0, tgu0, tqkv0, tqkv1, back) = run_tail(
        8, gain_part, sgu0, o_own0, o_other0, qkv_own0, qkv_other0, bqkv1, up_low
    )
    gain_sums = gain_sums[:4]
    device = lax.axis_index("dp") * lax.axis_size("fsdp") + lax.axis_index("fsdp")
    own_gain = lax.dynamic_slice_in_dim(gain_sums, device * shard, shard, 1)
    (out_x, out_back, grad_q, grad_k, grad_v, grad_o, grad_g, grad_u, grad_d) = end_assembly(
        step, qw, kw,
        (bqkv0, tqkv0, bgu0, tgu0, osum0, sd0, rd0, bqkv1, tqkv1, bgu1, tgu1, so1, ro1, sd1, rd1),
        (low1_back, low2_back), back,
    )
    return (
        out_x, out_back, own_gain[:2], grad_q, grad_k, grad_v, grad_o, own_gain[2:], grad_g, grad_u, grad_d,
    )


def per_device(*arrays):
    tokens, w_query, w_key, w_gate = arrays[0], arrays[2], arrays[3], arrays[7]
    dp_size, z_size = lax.axis_size("dp"), lax.axis_size("fsdp")
    suits = (
        dp_size == 2 * TP
        and z_size == TP
        and w_key.shape[2] // HEAD_DIM == dp_size
        and w_query.shape[2] == 2 * w_key.shape[2]
        and tokens.shape[0] % 128 == 0
        and w_query.shape[1] % 16 == 0
        and w_gate.shape[2] % (TP * dp_size * 128) == 0
    )
    return (fast_device if suits else general_device)(*arrays)


def solution(mesh):
    placed = (
        P(("dp", "fsdp"), None),
        P(None, ("dp", "fsdp")),
        P(None, ("dp", "fsdp"), None),
        P(None, ("dp", "fsdp"), None),
        P(None, ("dp", "fsdp"), None),
        P(None, ("dp", "fsdp"), None),
        P(None, ("dp", "fsdp")),
        P(None, ("dp", "fsdp"), None),
        P(None, ("dp", "fsdp"), None),
        P(None, ("dp", "fsdp"), None),
        P("dp", None),
        P(("dp", "fsdp"), None),
    )
    return jax.shard_map(
        per_device,
        mesh=mesh,
        in_specs=placed,
        out_specs=(
            P(None, ("dp", "fsdp"), None),
            P(("dp", "fsdp"), None),
            P(None, ("dp", "fsdp")),
            P(None, ("dp", "fsdp"), None),
            P(None, ("dp", "fsdp"), None),
            P(None, ("dp", "fsdp"), None),
            P(None, ("dp", "fsdp"), None),
            P(None, ("dp", "fsdp")),
            P(None, ("dp", "fsdp"), None),
            P(None, ("dp", "fsdp"), None),
            P(None, ("dp", "fsdp"), None),
        ),
        check_vma=False,
    )
```

```python
import functools
import math

import jax
import jax.numpy as jnp
from jax import lax
from jax.experimental import pallas as pl
from jax.experimental.pallas import tpu as pltpu
from jax.sharding import PartitionSpec as P

HEAD_DIM = 96


EPSILON = 1e-05
ROPE_BASE = 100000.0
NEGATIVE = -1e30


def layout(lengths_row, group_tok):
    places = jnp.arange(group_tok, dtype=jnp.int32)
    prompt_len = group_tok - jnp.sum(lengths_row)
    starts = prompt_len + jnp.cumsum(lengths_row) - lengths_row
    inside = places[:, None] >= starts[None, :]
    segment = jnp.sum(inside.astype(jnp.int32), axis=1)
    begins = jnp.max(jnp.where(inside, starts[None, :], 0), axis=1)
    position = jnp.where(segment > 0, places - begins + prompt_len, places)
    return (segment, position)


def rotate(values, position, direction):
    row_count = values.shape[0]
    shaped = values.reshape(row_count, -1, HEAD_DIM)
    halfway = HEAD_DIM // 2
    frequency = ROPE_BASE ** (-jnp.arange(halfway, dtype=jnp.float32) * 2.0 / HEAD_DIM)
    angles = position.astype(jnp.float32)[:, None] * frequency[None, :]
    cosine = jnp.cos(angles)[:, None, :]
    sine_part = direction * jnp.sin(angles)[:, None, :]
    first_half = shaped[..., :halfway]
    second_half = shaped[..., halfway:]
    turned = jnp.concatenate(
        [
            first_half * cosine - second_half * sine_part,
            second_half * cosine + first_half * sine_part,
        ],
        axis=-1,
    )
    return turned.reshape(values.shape)


def norm_apply(values, gain_vec):
    inv_rms = lax.rsqrt(jnp.mean(values * values, axis=-1, keepdims=True) + EPSILON)
    return values * inv_rms * gain_vec


def norm_back(values, gain_vec, incoming):
    inv_rms = lax.rsqrt(jnp.mean(values * values, axis=-1, keepdims=True) + EPSILON)
    weighted = incoming * gain_vec
    inner_sum = jnp.mean(weighted * values, axis=-1, keepdims=True)
    grad_values = inv_rms * weighted - values * inv_rms * inv_rms * inv_rms * inner_sum
    grad_gain = jnp.sum(incoming * values * inv_rms, axis=0)
    return (grad_values, grad_gain)


def matmul(left, right):
    return jnp.dot(left, right, preferred_element_type=jnp.float32)


def visibility(seg_rows, row_places, segment, places):
    same_seq = (seg_rows[:, None] == segment[None, :]) & (places[None, :] <= row_places[:, None])
    prompt_seen = (segment[None, :] == 0) & (seg_rows[:, None] > 0)
    return same_seq | prompt_seen


def head_slices(query_b, keys_all, head_index):
    row_count = query_b.shape[0]
    kv_width = keys_all.shape[1] // 2
    sharing = query_b.shape[1] // kv_width
    query_part = lax.dynamic_slice_in_dim(
        query_b, head_index * sharing * HEAD_DIM, sharing * HEAD_DIM, 1
    ).reshape(row_count, sharing, HEAD_DIM)
    key_part = lax.dynamic_slice_in_dim(keys_all, head_index * HEAD_DIM, HEAD_DIM, 1)
    value_part = lax.dynamic_slice_in_dim(keys_all, kv_width + head_index * HEAD_DIM, HEAD_DIM, 1)
    return (query_part, key_part, value_part)


def attend_forward(query_b, keys_all, visible):
    row_count = query_b.shape[0]
    kv_heads = keys_all.shape[1] // 2 // HEAD_DIM
    factor = 1.0 / math.sqrt(HEAD_DIM)

    def per_head(head_index):
        query_part, key_part, value_part = head_slices(query_b, keys_all, head_index)
        scores = (
            jnp.einsum("tgd,kd->gtk", query_part, key_part, preferred_element_type=jnp.float32)
            * factor
        )
        masked = jnp.where(visible[None], scores, NEGATIVE)
        peak_score = jnp.max(masked, axis=-1)
        exponent = jnp.where(visible[None], jnp.exp(masked - peak_score[..., None]), 0.0)
        totals = jnp.sum(exponent, axis=-1)
        probability = (exponent / totals[..., None]).astype(jnp.bfloat16)
        mixed_heads = jnp.einsum(
            "gtk,kd->tgd", probability, value_part, preferred_element_type=jnp.float32
        )
        return (mixed_heads.reshape(row_count, -1), peak_score, totals)

    mixed_heads, peak_score, totals = lax.map(per_head, jnp.arange(kv_heads, dtype=jnp.int32))
    return (jnp.transpose(mixed_heads, (1, 0, 2)).reshape(row_count, -1), peak_score, totals)


def attend_backward(query_b, keys_all, visible, peak_score, totals, grad_mixed):
    row_count = query_b.shape[0]
    kv_width = keys_all.shape[1] // 2
    kv_heads = kv_width // HEAD_DIM
    sharing = query_b.shape[1] // kv_width
    factor = 1.0 / math.sqrt(HEAD_DIM)

    def per_head(pieces):
        head_index, peak_head, total_head = pieces
        query_part, key_part, value_part = head_slices(query_b, keys_all, head_index)
        grad_part = lax.dynamic_slice_in_dim(
            grad_mixed, head_index * sharing * HEAD_DIM, sharing * HEAD_DIM, 1
        ).reshape(row_count, sharing, HEAD_DIM)
        scores = (
            jnp.einsum("tgd,kd->gtk", query_part, key_part, preferred_element_type=jnp.float32)
            * factor
        )
        masked = jnp.where(visible[None], scores, NEGATIVE)
        exponent = jnp.where(visible[None], jnp.exp(masked - peak_head[..., None]), 0.0)
        probability = exponent / total_head[..., None]
        prob_low = probability.astype(jnp.bfloat16)
        grad_probs = jnp.einsum(
            "tgd,kd->gtk", grad_part, value_part, preferred_element_type=jnp.float32
        )
        inner_sum = jnp.sum(probability * grad_probs, axis=-1, keepdims=True)
        grad_scores = (probability * (grad_probs - inner_sum)).astype(jnp.bfloat16)
        grad_query = (
            jnp.einsum("gtk,kd->tgd", grad_scores, key_part, preferred_element_type=jnp.float32)
            * factor
        )
        grad_key = (
            jnp.einsum("gtk,tgd->kd", grad_scores, query_part, preferred_element_type=jnp.float32)
            * factor
        )
        grad_value = jnp.einsum(
            "gtk,tgd->kd", prob_low, grad_part, preferred_element_type=jnp.float32
        )
        return (grad_query.reshape(row_count, -1), grad_key, grad_value)

    grad_query, grad_key, grad_value = lax.map(
        per_head, (jnp.arange(kv_heads, dtype=jnp.int32), peak_score, totals)
    )
    group_rows = keys_all.shape[0]
    key_terms = jnp.concatenate(
        [
            jnp.transpose(grad_key, (1, 0, 2)).reshape(group_rows, -1),
            jnp.transpose(grad_value, (1, 0, 2)).reshape(group_rows, -1),
        ],
        axis=1,
    )
    return (jnp.transpose(grad_query, (1, 0, 2)).reshape(row_count, -1), key_terms)


def fetch_attention(layer_index, gain_attn, w_query, w_key, w_value, w_out):
    return (
        lax.all_gather(gain_attn[layer_index], ("dp", "fsdp"), axis=0, tiled=True),
        lax.all_gather(w_query[layer_index], ("dp", "fsdp"), axis=0, tiled=True),
        lax.all_gather(w_key[layer_index], ("dp", "fsdp"), axis=0, tiled=True),
        lax.all_gather(w_value[layer_index], ("dp", "fsdp"), axis=0, tiled=True),
        lax.all_gather(w_out[layer_index], ("dp", "fsdp"), axis=0, tiled=True),
    )


def fetch_ffn(layer_index, gain_ffn, w_gate, w_up, w_down):
    return (
        lax.all_gather(gain_ffn[layer_index], ("dp", "fsdp"), axis=0, tiled=True),
        lax.all_gather(w_gate[layer_index], ("dp", "fsdp"), axis=0, tiled=True),
        lax.all_gather(w_up[layer_index], ("dp", "fsdp"), axis=0, tiled=True),
        lax.all_gather(w_down[layer_index], ("dp", "fsdp"), axis=0, tiled=True),
    )


def share_keys(stacked):
    return lax.all_gather(stacked, "fsdp", axis=0, tiled=True)


def layer_forward(hidden, attn_weights, ffn_weights, pos_rows, visible):
    gain_a, query_w, key_w, value_w, out_w = attn_weights
    gain_f, gate_w, upper_w, down_w = ffn_weights
    normed = norm_apply(hidden, gain_a.astype(jnp.float32)).astype(jnp.bfloat16)
    query_b = rotate(matmul(normed, query_w), pos_rows, 1.0).astype(jnp.bfloat16)
    key_b = rotate(matmul(normed, key_w), pos_rows, 1.0).astype(jnp.bfloat16)
    value_b = matmul(normed, value_w).astype(jnp.bfloat16)
    stacked = jnp.concatenate([key_b, value_b], axis=1)
    keys_all = share_keys(stacked)
    mixed_heads, peak_score, totals = attend_forward(query_b, keys_all, visible)
    mixed_b = mixed_heads.astype(jnp.bfloat16)
    middle = hidden + matmul(mixed_b, out_w)
    normed_ffn = norm_apply(middle, gain_f.astype(jnp.float32)).astype(jnp.bfloat16)
    gating = matmul(normed_ffn, gate_w)
    upward = matmul(normed_ffn, upper_w)
    activated = (jax.nn.silu(gating) * upward).astype(jnp.bfloat16)
    result = middle + matmul(activated, down_w)
    saved = (
        hidden,
        normed,
        query_b,
        stacked,
        keys_all,
        peak_score,
        totals,
        mixed_b,
        middle,
        normed_ffn,
        gating,
        upward,
        activated,
    )
    return (result, saved)


def layer_backward(upstream, saved, attn_weights, ffn_weights, keys_all, pos_rows, visible):
    (
        hidden,
        normed,
        query_b,
        stacked,
        unused_keys,
        peak_score,
        totals,
        mixed_b,
        middle,
        normed_ffn,
        gating,
        upward,
        activated,
    ) = saved
    gain_a, query_w, key_w, value_w, out_w = attn_weights
    gain_f, gate_w, upper_w, down_w = ffn_weights
    grad_branch = upstream.astype(jnp.bfloat16)
    grad_down_w = matmul(activated.T, grad_branch)
    grad_act = matmul(grad_branch, down_w.T)
    sigmoid_g = jax.nn.sigmoid(gating)
    grad_gate = (grad_act * upward * sigmoid_g * (1.0 + gating * (1.0 - sigmoid_g))).astype(
        jnp.bfloat16
    )
    grad_up = (grad_act * gating * sigmoid_g).astype(jnp.bfloat16)
    grad_gate_w = matmul(normed_ffn.T, grad_gate)
    grad_up_w = matmul(normed_ffn.T, grad_up)
    grad_normed_ffn = matmul(grad_gate, gate_w.T) + matmul(grad_up, upper_w.T)
    grad_middle_part, grad_gain_f = norm_back(middle, gain_f.astype(jnp.float32), grad_normed_ffn)
    ffn_blocks = (
        lax.psum_scatter(
            grad_gain_f.astype(jnp.bfloat16), "dp", scatter_dimension=0, tiled=True
        ).astype(jnp.float32),
        lax.psum_scatter(
            grad_gate_w.astype(jnp.bfloat16), "dp", scatter_dimension=0, tiled=True
        ).astype(jnp.float32),
        lax.psum_scatter(
            grad_up_w.astype(jnp.bfloat16), "dp", scatter_dimension=0, tiled=True
        ).astype(jnp.float32),
        lax.psum_scatter(
            grad_down_w.astype(jnp.bfloat16), "dp", scatter_dimension=0, tiled=True
        ).astype(jnp.float32),
    )
    ffn_grads = (
        lax.psum_scatter(
            ffn_blocks[0].astype(jnp.bfloat16), "fsdp", scatter_dimension=0, tiled=True
        ).astype(jnp.float32),
        lax.psum_scatter(
            ffn_blocks[1].astype(jnp.bfloat16), "fsdp", scatter_dimension=0, tiled=True
        ).astype(jnp.float32),
        lax.psum_scatter(
            ffn_blocks[2].astype(jnp.bfloat16), "fsdp", scatter_dimension=0, tiled=True
        ).astype(jnp.float32),
        lax.psum_scatter(
            ffn_blocks[3].astype(jnp.bfloat16), "fsdp", scatter_dimension=0, tiled=True
        ).astype(jnp.float32),
    )
    grad_middle = upstream + grad_middle_part
    grad_proj = grad_middle.astype(jnp.bfloat16)
    grad_out_w = matmul(mixed_b.T, grad_proj)
    grad_mixed = matmul(grad_proj, out_w.T).astype(jnp.bfloat16)
    grad_query_rot, key_terms = attend_backward(
        query_b, keys_all, visible, peak_score, totals, grad_mixed
    )
    key_grads = lax.psum_scatter(
        key_terms.astype(jnp.bfloat16), "fsdp", scatter_dimension=0, tiled=True
    ).astype(jnp.float32)
    kv_width = key_terms.shape[1] // 2
    grad_query = rotate(grad_query_rot, pos_rows, -1.0).astype(jnp.bfloat16)
    grad_key = rotate(key_grads[:, :kv_width], pos_rows, -1.0).astype(jnp.bfloat16)
    grad_value = key_grads[:, kv_width:].astype(jnp.bfloat16)
    grad_normed = (
        matmul(grad_query, query_w.T) + matmul(grad_key, key_w.T) + matmul(grad_value, value_w.T)
    )
    grad_query_w = matmul(normed.T, grad_query)
    grad_key_w = matmul(normed.T, grad_key)
    grad_value_w = matmul(normed.T, grad_value)
    grad_hidden_part, grad_gain_a = norm_back(hidden, gain_a.astype(jnp.float32), grad_normed)
    attn_blocks = (
        lax.psum_scatter(
            grad_gain_a.astype(jnp.bfloat16), "dp", scatter_dimension=0, tiled=True
        ).astype(jnp.float32),
        lax.psum_scatter(
            grad_query_w.astype(jnp.bfloat16), "dp", scatter_dimension=0, tiled=True
        ).astype(jnp.float32),
        lax.psum_scatter(
            grad_key_w.astype(jnp.bfloat16), "dp", scatter_dimension=0, tiled=True
        ).astype(jnp.float32),
        lax.psum_scatter(
            grad_value_w.astype(jnp.bfloat16), "dp", scatter_dimension=0, tiled=True
        ).astype(jnp.float32),
        lax.psum_scatter(
            grad_out_w.astype(jnp.bfloat16), "dp", scatter_dimension=0, tiled=True
        ).astype(jnp.float32),
    )
    attn_grads = (
        lax.psum_scatter(
            attn_blocks[0].astype(jnp.bfloat16), "fsdp", scatter_dimension=0, tiled=True
        ).astype(jnp.float32),
        lax.psum_scatter(
            attn_blocks[1].astype(jnp.bfloat16), "fsdp", scatter_dimension=0, tiled=True
        ).astype(jnp.float32),
        lax.psum_scatter(
            attn_blocks[2].astype(jnp.bfloat16), "fsdp", scatter_dimension=0, tiled=True
        ).astype(jnp.float32),
        lax.psum_scatter(
            attn_blocks[3].astype(jnp.bfloat16), "fsdp", scatter_dimension=0, tiled=True
        ).astype(jnp.float32),
        lax.psum_scatter(
            attn_blocks[4].astype(jnp.bfloat16), "fsdp", scatter_dimension=0, tiled=True
        ).astype(jnp.float32),
    )
    return (grad_middle + grad_hidden_part, attn_grads, ffn_grads)


def general_device(
    tokens,
    gain_attn,
    w_query,
    w_key,
    w_value,
    w_out,
    gain_ffn,
    w_gate,
    w_up,
    w_down,
    lengths,
    cotangent,
):
    tok_rows = tokens.shape[0]
    group_tok = tok_rows * lax.axis_size("fsdp")
    segment, position = layout(lengths[0], group_tok)
    first_row = lax.axis_index("fsdp") * tok_rows
    row_places = first_row + jnp.arange(tok_rows, dtype=jnp.int32)
    seg_rows = lax.dynamic_slice_in_dim(segment, first_row, tok_rows)
    pos_rows = lax.dynamic_slice_in_dim(position, first_row, tok_rows)
    visible = visibility(seg_rows, row_places, segment, jnp.arange(group_tok, dtype=jnp.int32))
    hidden = tokens.astype(jnp.float32)
    layer_store = []
    results = []
    for layer_index in range(2):
        attn_weights = fetch_attention(layer_index, gain_attn, w_query, w_key, w_value, w_out)
        ffn_weights = fetch_ffn(layer_index, gain_ffn, w_gate, w_up, w_down)
        hidden, saved = layer_forward(hidden, attn_weights, ffn_weights, pos_rows, visible)
        layer_store.append(saved)
        results.append(hidden.astype(jnp.bfloat16))
    upstream = cotangent.astype(jnp.float32)
    attn_list = []
    ffn_list = []
    for layer_index in (1, 0):
        attn_weights = fetch_attention(layer_index, gain_attn, w_query, w_key, w_value, w_out)
        ffn_weights = fetch_ffn(layer_index, gain_ffn, w_gate, w_up, w_down)
        saved = layer_store[layer_index]
        keys_all = share_keys(saved[3])
        upstream, attn_grads, ffn_grads = layer_backward(
            upstream, saved, attn_weights, ffn_weights, keys_all, pos_rows, visible
        )
        attn_list.append(attn_grads)
        ffn_list.append(ffn_grads)
    layer_outputs = jnp.stack(results)
    grad_gain_attn = jnp.stack([attn_list[1][0], attn_list[0][0]])
    grad_w_query = jnp.stack([attn_list[1][1], attn_list[0][1]])
    grad_w_key = jnp.stack([attn_list[1][2], attn_list[0][2]])
    grad_w_value = jnp.stack([attn_list[1][3], attn_list[0][3]])
    grad_w_out = jnp.stack([attn_list[1][4], attn_list[0][4]])
    grad_gain_ffn = jnp.stack([ffn_list[1][0], ffn_list[0][0]])
    grad_w_gate = jnp.stack([ffn_list[1][1], ffn_list[0][1]])
    grad_w_up = jnp.stack([ffn_list[1][2], ffn_list[0][2]])
    grad_w_down = jnp.stack([ffn_list[1][3], ffn_list[0][3]])
    return (
        layer_outputs,
        upstream,
        grad_gain_attn,
        grad_w_query,
        grad_w_key,
        grad_w_value,
        grad_w_out,
        grad_gain_ffn,
        grad_w_gate,
        grad_w_up,
        grad_w_down,
    )


TP = 4


def head_partner(values, halfway):
    width = values.shape[1]
    lane = lax.broadcasted_iota(jnp.int32, values.shape, 1)
    ahead = pltpu.roll(values, width - halfway, 1)
    behind = pltpu.roll(values, halfway, 1)
    return jnp.where(lane % HEAD_DIM < halfway, ahead, behind)


def block_mask(row_seg, col_seg, same_block, block):
    visible = (row_seg == col_seg) | (col_seg == 0)
    if same_block:
        rows = lax.broadcasted_iota(jnp.int32, (block, block), 0)
        cols = lax.broadcasted_iota(jnp.int32, (block, block), 1)
        visible = visible & (cols <= rows)
    return visible


MESH = pl.DeviceIdType.MESH
VMEM_LIMIT = 61 * 2**20
ANYWHERE = pl.BlockSpec(memory_space=pl.ANY)
IN_VMEM = pl.BlockSpec(memory_space=pltpu.VMEM)


class Net:
    def __init__(self, send_sems, recv_sems, local_sems):
        dp, z = lax.axis_index("dp"), lax.axis_index("fsdp")
        self.z = z
        self.q = lax.rem(dp, TP)
        self.y = lax.div(dp, TP)
        self.r = self.y * TP + z
        core = dp + 1 - 2 * lax.rem(dp, 2)
        across = dp + 2 - 4 * lax.rem(lax.div(dp, 2), 2)
        both = core + 2 - 4 * lax.rem(lax.div(dp, 2), 2)
        other = dp + TP - 2 * TP * lax.div(dp, TP)
        self.peer = {
            "core": (core, z),
            "x": (across, z),
            "both": (both, z),
            "y": (other, z),
            "z1": (dp, flip_index(z, 1)),
            "z2": (dp, flip_index(z, 2)),
            "z3": (dp, flip_index(z, 3)),
        }
        x, c = lax.div(self.q, 2), lax.rem(self.q, 2)
        high, low = lax.div(z, 2), lax.rem(z, 2)
        twisted = x + low - 2 * x * low
        self.peer["group"] = (self.y * TP + 2 * twisted + high, 2 * c + x)
        self.peer["home"] = (self.y * TP + 2 * low + high, 2 * c + twisted)
        self.alone = (self.peer["group"][0] == dp) & (self.peer["group"][1] == z)
        self.base = 2 * c + twisted
        self.send_sems, self.recv_sems, self.local_sems = send_sems, recv_sems, local_sems
        self.n_remote = self.n_local = 0
        self.flying = []
        self.leaving = []
        self.inner, self.outer = {}, {}

    def greet(self, names, regroup=None):
        barrier = pltpu.get_barrier_semaphore()
        for name in names:
            pl.semaphore_signal(barrier, inc=1, device_id=self.peer[name], device_id_type=MESH)
        if regroup is None:
            pl.semaphore_wait(barrier, len(names))
            return
        sender = self.peer["home" if regroup == "group" else "group"]

        @pl.when(jnp.logical_not(self.alone))
        def _():
            pl.semaphore_signal(barrier, inc=1, device_id=sender, device_id_type=MESH)
            pl.semaphore_wait(barrier, len(names) + 1)

        @pl.when(self.alone)
        def _():
            pl.semaphore_wait(barrier, len(names))

    def remote(self, src, dst, name):
        n = self.n_remote
        self.n_remote += 1
        copy = pltpu.make_async_remote_copy(
            src_ref=src,
            dst_ref=dst,
            send_sem=self.send_sems.at[n],
            recv_sem=self.recv_sems.at[n],
            device_id=self.peer[name],
            device_id_type=MESH,
        )
        copy.start()
        return copy

    def regroup(self, src, dst, name):
        n, k = self.n_remote, self.n_local
        self.n_remote += 1
        self.n_local += 1
        away = pltpu.make_async_remote_copy(
            src_ref=src,
            dst_ref=dst,
            send_sem=self.send_sems.at[n],
            recv_sem=self.recv_sems.at[n],
            device_id=self.peer[name],
            device_id_type=MESH,
        )
        here = pltpu.make_async_copy(src, dst, self.local_sems.at[k])
        copy = EitherCopy(self.alone, here, away)
        copy.start()
        return copy

    def local(self, src, dst):
        n = self.n_local
        self.n_local += 1
        copy = pltpu.make_async_copy(src, dst, self.local_sems.at[n])
        copy.start()
        return copy

    def keep(self, src, dst):
        self.leaving.append(self.local(src, dst))

    def finish(self):
        for copies in (*self.inner.values(), *self.outer.values(), self.flying, self.leaving):
            for copy in copies:
                copy.wait()
        self.inner, self.outer = {}, {}
        self.flying, self.leaving = [], []

    def arrived(self, ref):
        for pending in (self.inner, self.outer):
            for key in [k for k in pending if k[0] == id(ref)]:
                for copy in pending.pop(key):
                    copy.wait()

    def advance(self, moves):
        for stage, ref, low, count in moves:
            key = (id(ref), low)
            for copy in self.inner.pop(key, []):
                copy.wait()
            part = lambda bits: ref.at[self.y, pl.ds(low, count), flip_index(self.z, bits)]
            if stage == 1:
                sent = ((0, "z2"), (0, "z1"), (0, "y"))
            elif stage == 4:
                sent = ((0, "y"),)
            elif stage == 5:
                sent = ((0, "z2"), (0, "z1"))
            elif stage == 2:
                sent = ((2, "z1"), (1, "y"), (2, "y"))
            else:
                sent = ((3, "y"),)
            for bits, name in sent:
                pending = self.outer if name == "y" else self.inner
                pending.setdefault(key, []).append(self.remote(part(bits), part(bits), name))


class EitherCopy:
    def __init__(self, alone, here, away):
        self.alone, self.here, self.away = alone, here, away

    def start(self):
        pl.when(self.alone)(self.here.start)
        pl.when(jnp.logical_not(self.alone))(self.away.start)

    def wait(self):
        pl.when(self.alone)(self.here.wait)
        pl.when(jnp.logical_not(self.alone))(self.away.wait)


def flip_index(value, bits):
    low = lax.rem(value, 2)
    high = lax.div(value, 2)
    if bits & 1:
        low = 1 - low
    if bits & 2:
        high = 1 - high
    return high * 2 + low


def mixed_index(static, dynamic):
    return flip_index(dynamic, static)


def swap_index(value):
    return lax.rem(value, 2) * 2 + lax.div(value, 2)


def sems(remote, local):
    return [
        pltpu.SemaphoreType.DMA((max(remote, 1),)),
        pltpu.SemaphoreType.DMA((max(remote, 1),)),
        pltpu.SemaphoreType.DMA((max(local, 1),)),
    ]


PEERS = ("core", "x", "both", "y", "z1", "z2", "z3")
RANK_PEERS = (("core", 1), ("x", 2), ("both", 3))


def segments(lengths_ref, conts, group_tok, places):
    one = [lengths_ref[0:1, c : c + 1] for c in range(conts)]
    prompt = group_tok - sum(one)
    begin = prompt
    segment = jnp.zeros(places.shape, jnp.int32)
    begins = jnp.zeros(places.shape, jnp.int32)
    for c in range(conts):
        inside = places >= begin
        segment = segment + inside.astype(jnp.int32)
        begins = jnp.where(inside, jnp.maximum(begins, begin), begins)
        begin = begin + one[c]
    position = jnp.where(segment > 0, places - begins + prompt, places)
    return segment, position


def block_segments(lengths_ref, conts, block, index, row):
    shape = (block, 1) if row else (1, block)
    places = index * block + lax.broadcasted_iota(jnp.int32, shape, 0 if row else 1)
    return segments(lengths_ref, conts, TP * block, places)[0]


def start_kernel(
    conts, qkv_pack, w_gate, w_up, out_own, down_own, gain_tile, tokens, lengths, frequency, spread_cos, spread_sin,
    tok_out, cos_ref, sin_ref, len_out,
    g_qkv0, g_qkv1, g_gu0, g_gu1, g_out0, g_out1, g_down0, g_down1, g_gain,
    tok_buf, len_buf, send_sems, recv_sems, local_sems,
):
    net = Net(send_sems, recv_sems, local_sems)
    net.greet(PEERS, "group")
    bring = [net.regroup(lengths, len_buf, "group"), net.regroup(tokens, tok_buf, "group")]
    y, q, z = net.y, net.q, net.z
    step = w_gate.shape[2] // (2 * TP)

    def qkv_columns(layer, target):
        copies = [
            net.remote(qkv_pack.at[layer, flip_index(q, bits)], target.at[y, q, z], name)
            for name, bits in RANK_PEERS
        ]
        return copies + [net.local(qkv_pack.at[layer, q], target.at[y, q, z])]

    def gu_columns(layer, target):
        copies = []
        for name, bits in RANK_PEERS + ((None, 0),):
            for n, weight in enumerate((w_gate, w_up)):
                for half in range(2):
                    at = pl.multiple_of((half * TP + flip_index(q, bits)) * step, step)
                    src = weight.at[layer, :, pl.ds(at, step)]
                    dst = target.at[y, q, z, :, pl.ds((2 * n + half) * step, step)]
                    copies.append(net.local(src, dst) if name is None else net.remote(src, dst, name))
        return copies

    first = qkv_columns(0, g_qkv0)
    first += [net.remote(gain_tile, g_gain.at[y, q, z], name) for name, _ in RANK_PEERS]
    first.append(net.local(gain_tile, g_gain.at[y, q, z]))
    placed = [
        net.local(out_own.at[0], g_out0.at[y, 0, z]),
        net.local(down_own.at[0], g_down0.at[y, 0, z]),
        net.local(out_own.at[1], g_out1.at[y, 0, z]),
        net.local(down_own.at[1], g_down1.at[y, 0, z]),
    ]
    second = gu_columns(0, g_gu0)
    placed[0].wait()
    net.advance(((1, g_out0, 0, 1),))
    for copy in first:
        copy.wait()
    net.advance(((1, g_qkv0, 0, TP), (1, g_gain, 0, TP)))
    placed[1].wait()
    net.advance(((1, g_down0, 0, 1),))
    second += qkv_columns(1, g_qkv1) + gu_columns(1, g_gu1)
    bring[0].wait()
    block = tok_buf.shape[0]
    len_out[...] = len_buf[...]
    def table(s):
        places = mixed_index(s, net.base) * block + lax.broadcasted_iota(jnp.int32, (block, 1), 0)
        position = segments(len_buf, conts, TP * block, places)[1]
        angles = position.astype(jnp.float32) * frequency[...]
        at = slice(s * block, (s + 1) * block)
        for table_ref, values, lanes in (
            (cos_ref, jnp.cos(angles), spread_cos), (sin_ref, jnp.sin(angles), spread_sin)
        ):
            table_ref[at, :] = jnp.dot(
                values, lanes[...], precision=lax.Precision.HIGHEST, preferred_element_type=jnp.float32
            )

    table(0)
    net.advance(((2, g_out0, 0, 1), (2, g_qkv0, 0, TP), (2, g_gain, 0, TP)))
    second += placed[2:]
    table(1)
    net.advance(((3, g_out0, 0, 1), (3, g_qkv0, 0, TP), (3, g_gain, 0, TP), (2, g_down0, 0, 1)))
    table(2)
    table(3)
    bring[1].wait()
    tok_out[...] = tok_buf[...].astype(jnp.float32)
    for copy in second:
        copy.wait()
    net.finish()


def start_exchange(conts, qkv_pack, w_gate, w_up, out_own, down_own, gain_tile, tokens, lengths, frequency, spread_cos, spread_sin):
    bf, f32 = jnp.bfloat16, jnp.float32
    shape = jax.ShapeDtypeStruct
    block, depth = tokens.shape
    shard, qkv_width = qkv_pack.shape[2:]
    units = w_gate.shape[2] // TP * 2
    outs = [
        shape((block, depth), f32),
        shape((TP * block, spread_cos.shape[1]), f32),
        shape((TP * block, spread_cos.shape[1]), f32),
        shape(lengths.shape, lengths.dtype),
    ]
    for ranks, rows, width in (
        (TP, shard, qkv_width),
        (TP, shard, units),
        (1, shard, depth),
        (1, down_own.shape[1], depth),
    ):
        outs += [shape((2, ranks, TP, rows, width), bf)] * 2
    outs.append(shape((2, TP, TP) + gain_tile.shape, f32))
    return pl.pallas_call(
        functools.partial(start_kernel, conts),
        out_shape=outs,
        in_specs=[IN_VMEM] * 11,
        out_specs=[IN_VMEM] * 4 + [ANYWHERE] * 9,
        scratch_shapes=[
            pltpu.VMEM((block, depth), bf),
            pltpu.VMEM(lengths.shape, lengths.dtype),
        ] + sems(80, 24),
        compiler_params=pltpu.CompilerParams(
            collective_id=1, has_side_effects=True, vmem_limit_bytes=VMEM_LIMIT
        ),
        cost_estimate=pl.CostEstimate(flops=0, bytes_accessed=300 * 2**20, transcendentals=0),
    )(qkv_pack, w_gate, w_up, out_own, down_own, gain_tile, tokens, lengths, frequency, spread_cos, spread_sin)


def attend_rows(net, block):
    return [
        pl.ds(pl.multiple_of(mixed_index(b, net.base) * block, block), block) for b in range(TP)
    ]


def attend_forward_block(net, qkv_ref, len_ref, conts, mixed_ref, lse_ref):
    total, width = qkv_ref.shape
    block = total // TP
    q_heads = width // (2 * HEAD_DIM)
    kv_heads = q_heads // 2
    factor = 1.0 / math.sqrt(HEAD_DIM)
    key_at = q_heads * HEAD_DIM
    value_at = key_at + kv_heads * HEAD_DIM
    places = attend_rows(net, block)
    nt = (((1,), (1,)), ((), ()))
    for i in range(TP):
        row_seg = block_segments(len_ref, conts, block, i, True)
        masks = [
            block_mask(row_seg, block_segments(len_ref, conts, block, j, False), i == j, block)
            for j in range(i + 1)
        ]
        for h in range(q_heads):
            kv = h // 2
            query = qkv_ref[places[i], h * HEAD_DIM : (h + 1) * HEAD_DIM]
            scores = []
            for j in range(i + 1):
                key = qkv_ref[places[j], key_at + kv * HEAD_DIM : key_at + (kv + 1) * HEAD_DIM]
                s = lax.dot_general(query, key, nt, preferred_element_type=jnp.float32) * factor
                scores.append(jnp.where(masks[j], s, NEGATIVE))
            peak = scores[0].max(axis=1, keepdims=True)
            for s in scores[1:]:
                peak = jnp.maximum(peak, s.max(axis=1, keepdims=True))
            total_e = jnp.zeros((block, 1), jnp.float32)
            mixed = jnp.zeros((block, HEAD_DIM), jnp.float32)
            for j in range(i + 1):
                e = jnp.exp(scores[j] - peak)
                total_e = total_e + e.sum(axis=1, keepdims=True)
                value = qkv_ref[places[j], value_at + kv * HEAD_DIM : value_at + (kv + 1) * HEAD_DIM]
                mixed = mixed + jnp.dot(
                    e.astype(jnp.bfloat16), value, preferred_element_type=jnp.float32
                )
            mixed_ref[places[i], h * HEAD_DIM : (h + 1) * HEAD_DIM] = (mixed / total_e).astype(
                jnp.bfloat16
            )
            lse_ref[i, :, h : h + 1] = peak + jnp.log(total_e)


def normalize(values, gain_row):
    scale = lax.rsqrt(jnp.mean(values * values, axis=-1, keepdims=True) + EPSILON)
    return (values * scale * gain_row).astype(jnp.bfloat16)


def spread_begin(net, buf):
    return (net.remote(buf.at[0], buf.at[1], "x"), net.remote(buf.at[0], buf.at[2], "core"))


def spread_each(net, buf, begun, work):
    over_x, over_core = begun
    work(0)
    over_core.wait()
    work(2)
    over_x.wait()
    forward = net.remote(buf.at[1], buf.at[3], "core")
    work(1)
    forward.wait()
    work(3)


def collect(net, part, far_out, far_in, pass_out, pass_in):
    low = lambda v: v.astype(jnp.bfloat16)
    far_out[0] = low(part(3))
    first = net.remote(far_out.at[0], far_in.at[0], "core")
    near = part(1)
    first.wait()
    pass_out[...] = low(near + far_in[0].astype(jnp.float32))
    passed = net.remote(pass_out, pass_in, "x")
    far_out[1] = low(part(2))
    second = net.remote(far_out.at[1], far_in.at[1], "core")
    own = part(0)
    second.wait()
    own = own + far_in[1].astype(jnp.float32)
    passed.wait()
    return own + pass_in[...].astype(jnp.float32)


def forward_kernel(programs, has_cot, conts, n_moving, *refs):
    x_own, gain_a, gain_f, cos_ref, sin_ref, lengths = refs[:6]
    refs = refs[6:]
    if has_cot:
        cot, refs = refs[0], refs[1:]
    refs = refs[n_moving:]
    moving, refs = refs[:n_moving], refs[n_moving:]
    (x_next, middle_ref, lse_ref, x_low, rows_out, qkv_out, mixed_out, ffn_rows_out, gate_out, up_out, act_out) = refs[:11]
    refs = refs[11:]
    if has_cot:
        branch_out, refs, branch = refs[0], refs[1:-1], refs[-1]
    (rows, ffn_rows, w_qkv, w_o, w_gu, w_d, qkv, mixed, gate, up, act,
     far_out, far_in, pass_out, pass_in, send_sems, recv_sems, local_sems) = refs
    net = Net(send_sems, recv_sems, local_sems)
    steps = [[(kind, moving[n], low, count) for kind, n, low, count in step] for step in programs]
    block, depth = x_own.shape
    load_qkv = net.local(moving[0], w_qkv)
    load_o = net.local(moving[1], w_o)
    net.greet(("core", "x", "y", "z1", "z2", "z3"), "group" if has_cot else None)
    net.advance(steps[0])
    rows[0] = normalize(x_own[...], gain_a[...])
    begun = spread_begin(net, rows)
    load_qkv.wait()

    def project(s):
        raw = jnp.dot(
            rows[s], w_qkv[...].reshape(depth, -1), preferred_element_type=jnp.float32
        )
        at = slice(s * block, (s + 1) * block)
        turned = raw * cos_ref[at, :] + head_partner(raw, HEAD_DIM // 2) * sin_ref[at, :]
        qkv[at, :] = turned.astype(jnp.bfloat16)

    spread_each(net, rows, begun, project)
    net.keep(rows, rows_out)
    net.keep(qkv, qkv_out)
    net.advance(steps[1])
    if has_cot:
        bring = net.regroup(cot, branch.at[0], "group")
    attend_forward_block(net, qkv, lengths, conts, mixed, lse_ref)
    net.keep(mixed, mixed_out)
    net.advance(steps[2])
    load_o.wait()

    def out_part(s):
        return jnp.dot(
            mixed[s * block : (s + 1) * block, :],
            w_o[...].reshape(-1, depth),
            preferred_element_type=jnp.float32,
        )

    middle = x_own[...] + collect(
        net, out_part, far_out, far_in.at[0], pass_out, pass_in.at[0]
    )
    middle_ref[...] = middle
    net.advance(steps[3])
    net.arrived(moving[3])
    load_d = net.local(moving[3], w_d)
    ffn_rows[0] = normalize(middle, gain_f[...])
    begun = spread_begin(net, ffn_rows)
    if has_cot:
        bring.wait()
        over_x, over_core = spread_begin(net, branch)
    net.arrived(moving[2])
    load_gu = net.local(moving[2], w_gu)
    net.advance(steps[4])
    load_d.wait()
    load_gu.wait()
    units = act.shape[2]

    def expand(s):
        value = ffn_rows[s]
        gating = jnp.dot(
            value, w_gu[:, :, :, :, :units].reshape(depth, units), preferred_element_type=jnp.float32
        )
        upward = jnp.dot(
            value, w_gu[:, :, :, :, units:].reshape(depth, units), preferred_element_type=jnp.float32
        )
        gate[s] = gating.astype(jnp.bfloat16)
        up[s] = upward.astype(jnp.bfloat16)
        act[s] = (gating * jax.nn.sigmoid(gating) * upward).astype(jnp.bfloat16)

    spread_each(net, ffn_rows, begun, expand)
    if has_cot:
        over_x.wait()
        forward = net.remote(branch.at[1], branch.at[3], "core")
    net.keep(ffn_rows, ffn_rows_out)
    net.keep(gate, gate_out)
    net.keep(up, up_out)
    net.keep(act, act_out)

    def down_part(s):
        return jnp.dot(act[s], w_d[...].reshape(-1, depth), preferred_element_type=jnp.float32)

    result = middle_ref[...] + collect_during(
        net,
        down_part,
        (far_out, far_in.at[1], pass_out, pass_in.at[1]),
        lambda: net.advance(steps[5]),
    )
    if has_cot:
        over_core.wait()
        forward.wait()
        net.keep(branch, branch_out)
    x_next[...] = result
    x_low[...] = result.astype(jnp.bfloat16)
    net.finish()


def forward_layer(programs, cot, cid, conts, x_own, gain_a, gain_f, cosine, sine, lengths, moving):
    bf, f32 = jnp.bfloat16, jnp.float32
    block, depth = x_own.shape
    total, qkv_width = cosine.shape
    units = moving[2].shape[4] // 2
    q_heads = qkv_width // (2 * HEAD_DIM)
    shape = jax.ShapeDtypeStruct
    outs = [shape(m.shape, m.dtype) for m in moving] + [
        shape((block, depth), f32),
        shape((block, depth), f32),
        shape((TP, block, q_heads), f32),
        shape((block, depth), bf),
        shape((TP, block, depth), bf),
        shape((total, qkv_width), bf),
        shape((total, qkv_width // 2), bf),
        shape((TP, block, depth), bf),
        shape((TP, block, units), bf),
        shape((TP, block, units), bf),
        shape((TP, block, units), bf),
    ]
    n = len(moving)
    given = [] if cot is None else [cot]
    c = len(given)
    outs += [shape((TP, block, depth), bf)] * c
    scratch = [
        pltpu.VMEM((TP, block, depth), bf),
        pltpu.VMEM((TP, block, depth), bf),
        pltpu.VMEM(moving[0].shape, bf),
        pltpu.VMEM(moving[1].shape, bf),
        pltpu.VMEM(moving[2].shape, bf),
        pltpu.VMEM(moving[3].shape, bf),
        pltpu.VMEM((total, qkv_width), bf),
        pltpu.VMEM((total, qkv_width // 2), bf),
        pltpu.VMEM((TP, block, units), bf),
        pltpu.VMEM((TP, block, units), bf),
        pltpu.VMEM((TP, block, units), bf),
        pltpu.VMEM((2, block, depth), bf),
        pltpu.VMEM((2, 2, block, depth), bf),
        pltpu.VMEM((block, depth), bf),
        pltpu.VMEM((2, block, depth), bf),
    ] + sems(80, 24) + [pltpu.VMEM((TP, block, depth), bf)] * c
    return pl.pallas_call(
        functools.partial(forward_kernel, programs, bool(c), conts, n),
        out_shape=outs,
        in_specs=[IN_VMEM] * (6 + c) + [ANYWHERE] * n,
        out_specs=[ANYWHERE] * n + [IN_VMEM] * 4 + [ANYWHERE] * (7 + c),
        scratch_shapes=scratch,
        input_output_aliases={6 + c + i: i for i in range(n)},
        compiler_params=pltpu.CompilerParams(
            collective_id=cid, has_side_effects=True, vmem_limit_bytes=VMEM_LIMIT
        ),
        cost_estimate=pl.CostEstimate(
            flops=16 * 10**9, bytes_accessed=400 * 2**20, transcendentals=10**7
        ),
    )(x_own, gain_a, gain_f, cosine, sine, lengths, *given, *moving)


def moved_shape(kind, source):
    shape = source.shape
    if kind in ("y", "whole_y"):
        kept = shape
    elif kind == "g":
        kept = shape
    elif kind == "zc":
        kept = (3, shape[0]) + shape[2:]
    elif kind in ("z", "t"):
        kept = (3,) + shape[1:]
    else:
        kept = (3,) + shape
    return jax.ShapeDtypeStruct(kept, source.dtype)


def begin_move(net, kind, source, target):
    if kind in ("y", "whole_y"):
        return [net.remote(source, target, "y")]
    if kind == "g":
        return [net.regroup(source, target, "home")]
    copies = []
    for name, bits in RANK_PEERS:
        if kind == "z":
            copies.append(
                net.remote(source.at[flip_index(net.z, bits)], target.at[bits - 1], f"z{bits}")
            )
        elif kind == "zc":
            copies.append(
                net.remote(source.at[:, flip_index(net.z, bits)], target.at[bits - 1], f"z{bits}")
            )
        elif kind == "whole_z":
            copies.append(net.remote(source, target.at[bits - 1], f"z{bits}"))
        elif kind == "t":
            copies.append(
                net.remote(source.at[flip_index(net.q, bits)], target.at[bits - 1], name)
            )
        else:
            copies.append(net.remote(source, target.at[bits - 1], name))
    return copies


def begin_moves(net, kinds, sources, targets):
    for kind, source, target in zip(kinds, sources, targets):
        net.flying += begin_move(net, kind, source, target)


def greet_all(net, kinds):
    net.greet(PEERS, "home" if "g" in kinds else None)


def tail_kernel(
    gain_part, sgu_in, o_own_in, o_other, qkv_own_in, qkv_other, bqkv, up_low,
    gain_out, out_sum, b_gu, b_qkv, t_gu, t_qkv, t_qkv1, back,
    sgu, so, s_qkv, qkv_got, o_got, gu_one, gu_pass, gu_two, o_one, o_pass, o_two, q_one, q_pass, q_two,
    gain_t, gain_a, gain_z, gain_b, gain_y, send_sems, recv_sems, local_sems,
):
    net = Net(send_sems, recv_sems, local_sems)
    f32, bf = jnp.float32, jnp.bfloat16
    z, q = net.z, net.q
    z1, z2, z3 = (flip_index(z, bits) for bits in (1, 2, 3))
    loads = [net.local(sgu_in, sgu), net.local(o_own_in, so), net.local(qkv_own_in, s_qkv)]
    net.greet(PEERS, "home")
    over_y = [net.remote(o_other, o_got, "y"), net.remote(qkv_other, qkv_got, "y")]

    def first_hop(source, target, part):
        return [
            net.remote(source.at[part + (z3,)], target.at[(1,) + part], "z1"),
            net.remote(source.at[part + (z1,)], target.at[(0,) + part], "z1"),
        ]

    halves = [(pl.ds(0, 2),), (pl.ds(2, 2),)]
    gu_first = [first_hop(sgu_in, gu_one, part) for part in halves]
    gains = [net.remote(gain_part, gain_t.at[bits - 1], name) for name, bits in RANK_PEERS]
    net.flying += begin_move(net, "t", bqkv, t_qkv1)
    for copy in loads:
        copy.wait()
    over_y[0].wait()
    so[...] = (so[...].astype(f32) + o_got[...].astype(f32)).astype(bf)
    o_first = first_hop(so, o_one, ())
    over_y[1].wait()
    s_qkv[...] = (s_qkv[...].astype(f32) + qkv_got[...].astype(f32)).astype(bf)
    every = (pl.ds(0, TP),)
    q_first = first_hop(s_qkv, q_one, every)
    for copy in gains:
        copy.wait()
    gain_a[...] = gain_part[...] + gain_t[0] + gain_t[1] + gain_t[2]
    gains = [net.remote(gain_a, gain_z.at[bits - 1], f"z{bits}") for bits in (1, 2, 3)]

    def second_hop(own, one, passing, two, part, first):
        first[0].wait()
        passing[part or (Ellipsis,)] = (
            own[part + (z2,)].astype(f32) + one[(1,) + part].astype(f32)
        ).astype(bf)
        at = (lambda ref: ref.at[part]) if part else (lambda ref: ref)
        return net.remote(at(passing), at(two), "z2")

    gu_second = [
        second_hop(sgu, gu_one, gu_pass, gu_two, part, first) for part, first in zip(halves, gu_first)
    ]
    o_second = second_hop(so, o_one, o_pass, o_two, (), o_first)
    q_second = second_hop(s_qkv, q_one, q_pass, q_two, every, q_first)
    net.flying += begin_move(net, "g", up_low, back)
    for copy in gains:
        copy.wait()
    gain_b[...] = gain_a[...] + gain_z[0] + gain_z[1] + gain_z[2]
    gain_over_y = net.remote(gain_b, gain_y, "y")

    def total(own, one, two, part):
        whole = part or (Ellipsis,)
        return (
            own[part + (z,)].astype(f32) + one[(0,) + part].astype(f32) + two[whole].astype(f32)
        )

    for part, first, second in zip(halves, gu_first, gu_second):
        first[1].wait()
        second.wait()
        b_gu[part] = total(sgu, gu_one, gu_two, part).astype(bf)
    net.flying += begin_move(net, "t", b_gu, t_gu)
    o_first[1].wait()
    o_second.wait()
    out_sum[...] = total(so, o_one, o_two, ())
    q_first[1].wait()
    q_second.wait()
    b_qkv[...] = total(s_qkv, q_one, q_two, every).astype(bf)
    net.flying += begin_move(net, "t", b_qkv, t_qkv)
    gain_over_y.wait()
    gain_out[...] = gain_b[...] + gain_y[...]
    net.finish()


def run_tail(cid, gain_part, sgu, so, o_other, qkv_own, qkv_other, bqkv, up_low):
    bf, f32 = jnp.bfloat16, jnp.float32
    shape = jax.ShapeDtypeStruct
    gu_block = (TP,) + sgu.shape[2:]
    o_block = so.shape[1:]
    q_block = (TP,) + qkv_own.shape[2:]
    three = lambda block: (3,) + block[1:]
    return pl.pallas_call(
        tail_kernel,
        out_shape=[
            shape(gain_part.shape, f32),
            shape(o_block, f32),
            shape(gu_block, bf),
            shape(q_block, bf),
            shape(three(gu_block), bf),
            shape(three(q_block), bf),
            shape(three(q_block), bf),
            shape(up_low.shape, bf),
        ],
        in_specs=[IN_VMEM] + [ANYWHERE] * 7,
        out_specs=[IN_VMEM] * 4 + [ANYWHERE] * 4,
        scratch_shapes=[
            pltpu.VMEM(sgu.shape, bf),
            pltpu.VMEM(so.shape, bf),
            pltpu.VMEM(qkv_own.shape, bf),
            pltpu.VMEM(qkv_own.shape, bf),
            pltpu.VMEM(so.shape, bf),
        ]
        + [
            pltpu.VMEM(dims, bf)
            for block in (gu_block, o_block, q_block)
            for dims in ((2,) + block, block, block)
        ]
        + [
            pltpu.VMEM(dims, f32)
            for dims in (
                (3,) + gain_part.shape, gain_part.shape, (3,) + gain_part.shape, gain_part.shape, gain_part.shape
            )
        ]
        + sems(48, 8),
        compiler_params=pltpu.CompilerParams(
            collective_id=cid, has_side_effects=True, vmem_limit_bytes=VMEM_LIMIT
        ),
        cost_estimate=pl.CostEstimate(flops=0, bytes_accessed=200 * 2**20, transcendentals=0),
    )(gain_part, sgu, so, o_other, qkv_own, qkv_other, bqkv, up_low)


def norm_backward(values, gain_row, incoming):
    inv = lax.rsqrt(jnp.mean(values * values, axis=-1, keepdims=True) + EPSILON)
    weighted = incoming * gain_row
    inner = jnp.mean(weighted * values, axis=-1, keepdims=True)
    grad = inv * weighted - values * (inv * inv * inv * inner)
    return grad, jnp.sum(incoming * values * inv, axis=0, keepdims=True)


def collect_during(net, part, bufs, meanwhile):
    far_out, far_in, pass_out, pass_in = bufs
    low = lambda v: v.astype(jnp.bfloat16)
    far_out[0] = low(part(3))
    first = net.remote(far_out.at[0], far_in.at[0], "core")
    near = part(1)
    first.wait()
    pass_out[...] = low(near + far_in[0].astype(jnp.float32))
    passed = net.remote(pass_out, pass_in, "x")
    far_out[1] = low(part(2))
    second = net.remote(far_out.at[1], far_in.at[1], "core")
    own = part(0)
    second.wait()
    own = own + far_in[1].astype(jnp.float32)
    meanwhile()
    passed.wait()
    return own + pass_in[...].astype(jnp.float32)


NT = (((1,), (1,)), ((), ()))
TN = (((0,), (0,)), ((), ()))


def dot_nt(left, right):
    return lax.dot_general(left, right, NT, preferred_element_type=jnp.float32)


def dot_tn(left, right):
    return lax.dot_general(left, right, TN, preferred_element_type=jnp.float32)


def ffn_backward_kernel(kinds, given, *refs):
    n = len(kinds)
    middle, gain, source_in = refs[:3]
    acts, rows_in, gates, ups, mixed_in, wd_in, wgu_in, wo_in = refs[3:11]
    refs = refs[11:]
    sources, targets, refs = refs[:n], refs[n : 2 * n], refs[2 * n :]
    (grad_middle, gain_grad, dmixed_out, d_own, d_got, gu_own, gu_other, o_own, o_other) = refs[:9]
    (branch, proj, act, rows, gate, up, mixed, dmixed, w_d, w_gu, w_o, g_down, g_gu, g_out,
     far_out, far_in, pass_out, pass_in, send_sems, recv_sems, local_sems) = refs[9:]
    net = Net(send_sems, recv_sems, local_sems)
    block, depth = middle.shape
    units = act.shape[2]
    total = TP * block
    loads = {}
    if given:
        loads["branch"] = net.local(source_in, branch)
    for name, src, dst in (
        ("w_d", wd_in, w_d), ("gate", gates, gate), ("up", ups, up), ("act", acts, act),
        ("w_gu", wgu_in, w_gu), ("rows", rows_in, rows), ("w_o", wo_in, w_o), ("mixed", mixed_in, mixed),
    ):
        loads[name] = net.local(src, dst)
    greet_all(net, kinds)
    begin_moves(net, kinds, sources, targets)
    if given:
        loads["branch"].wait()
    else:
        branch[0] = source_in[...].astype(jnp.bfloat16)
        begun = spread_begin(net, branch)
    loads["w_d"].wait()
    loads["gate"].wait()
    loads["up"].wait()

    def through(s):
        grad_act = dot_nt(branch[s], w_d[...].reshape(units, depth))
        gating = gate[s].astype(jnp.float32)
        upward = up[s].astype(jnp.float32)
        sig = jax.nn.sigmoid(gating)
        shared = grad_act * sig
        gate[s] = (shared * upward * (1.0 + gating * (1.0 - sig))).astype(jnp.bfloat16)
        up[s] = (shared * gating).astype(jnp.bfloat16)

    if given:
        for s in (3, 1, 2, 0):
            through(s)
    else:
        spread_each(net, branch, begun, through)
    loads["act"].wait()
    theirs, ours = 1 - net.y, net.y
    drows, urows = g_down.shape[2], g_gu.shape[3]
    dwide, uwide = 2 * drows, 2 * TP * urows

    def down_half(side):
        def tile(m, carry):
            lanes = pl.ds(pl.multiple_of((side * 2 + m) * dwide, dwide), dwide)
            grad = dot_tn(act[:, :, lanes].reshape(total, dwide), branch[...].reshape(total, depth))
            g_down[side, pl.ds(2 * m, 2)] = grad.astype(jnp.bfloat16).reshape(2, drows, depth)
            return carry

        lax.fori_loop(0, 2, tile, 0)

    def gu_half(side):
        def tile(m, carry):
            lanes = pl.ds(pl.multiple_of((side * 2 + m) * uwide, uwide), uwide)
            left = rows[:, :, lanes].reshape(total, uwide)
            for ref, at in ((gate, 0), (up, units)):
                grad = dot_tn(left, ref[...].reshape(total, units)).astype(jnp.bfloat16)
                g_gu[side, pl.ds(2 * m, 2), :, :, at : at + units] = grad.reshape(2, TP, urows, units)
            return carry

        lax.fori_loop(0, 2, tile, 0)

    down_half(theirs)
    net.flying.append(net.remote(g_down.at[theirs], d_got, "y"))
    loads["w_gu"].wait()
    loads["rows"].wait()

    def back(s):
        return dot_nt(gate[s], w_gu[:, :, :, :, :units].reshape(depth, units)) + dot_nt(
            up[s], w_gu[:, :, :, :, units:].reshape(depth, units)
        )

    def meanwhile():
        gu_half(theirs)
        net.keep(g_gu.at[theirs], gu_other)
        gu_half(ours)
        net.keep(g_gu.at[ours], gu_own)
        down_half(ours)
        net.keep(g_down.at[ours], d_own)

    incoming = collect_during(net, back, (far_out, far_in, pass_out, pass_in), meanwhile)
    part, gain_part = norm_backward(middle[...], gain[...], incoming)
    gain_grad[...] = gain_part
    grad_mid = (branch[0].astype(jnp.float32) if given else source_in[...]) + part
    grad_middle[...] = grad_mid
    proj[0] = grad_mid.astype(jnp.bfloat16)
    begun = spread_begin(net, proj)
    loads["w_o"].wait()
    loads["mixed"].wait()

    def mix_back(s):
        dmixed[s * block : (s + 1) * block, :] = dot_nt(
            proj[s], w_o[...].reshape(-1, depth)
        ).astype(jnp.bfloat16)

    spread_each(net, proj, begun, mix_back)
    net.keep(dmixed, dmixed_out)
    grad = dot_tn(mixed[...], proj[...].reshape(total, depth)).astype(jnp.bfloat16)
    g_out[...] = grad.reshape(g_out.shape)
    net.keep(g_out.at[ours], o_own)
    net.keep(g_out.at[theirs], o_other)
    net.finish()


def ffn_backward(cid, moves, source, given, middle, gain, acts, rows, gates, ups, mixed, w_d, w_gu, w_o):
    bf, f32 = jnp.bfloat16, jnp.float32
    shape = jax.ShapeDtypeStruct
    block, depth = middle.shape
    units = gates.shape[2]
    total, mixed_width = mixed.shape
    kinds = tuple(kind for kind, _ in moves)
    sources = [source for _, source in moves]
    n = len(moves)
    drows, urows, orows = w_d.shape[3], w_gu.shape[3], w_o.shape[3]
    outs = [moved_shape(kind, source) for kind, source in moves] + [
        shape((block, depth), f32),
        shape((1, depth), f32),
        shape((total, mixed_width), bf),
        shape((TP, drows, depth), bf),
        shape((TP, drows, depth), bf),
        shape((TP, TP, urows, 2 * units), bf),
        shape((TP, TP, urows, 2 * units), bf),
        shape((TP, orows, depth), bf),
        shape((TP, orows, depth), bf),
    ]
    scratch = [
        pltpu.VMEM((TP, block, depth), bf),
        pltpu.VMEM((TP, block, depth), bf),
        pltpu.VMEM((TP, block, units), bf),
        pltpu.VMEM((TP, block, depth), bf),
        pltpu.VMEM((TP, block, units), bf),
        pltpu.VMEM((TP, block, units), bf),
        pltpu.VMEM((total, mixed_width), bf),
        pltpu.VMEM((total, mixed_width), bf),
        pltpu.VMEM(w_d.shape, bf),
        pltpu.VMEM(w_gu.shape, bf),
        pltpu.VMEM(w_o.shape, bf),
        pltpu.VMEM((2, TP, drows, depth), bf),
        pltpu.VMEM((2, TP, TP, urows, 2 * units), bf),
        pltpu.VMEM((2, TP, orows, depth), bf),
        pltpu.VMEM((2, block, depth), bf),
        pltpu.VMEM((2, block, depth), bf),
        pltpu.VMEM((block, depth), bf),
        pltpu.VMEM((block, depth), bf),
    ] + sems(48, 20)
    operands = [middle, gain, source, acts, rows, gates, ups, mixed, w_d, w_gu, w_o]
    return pl.pallas_call(
        functools.partial(ffn_backward_kernel, kinds, given),
        out_shape=outs,
        in_specs=[IN_VMEM] * 2 + [ANYWHERE if given else IN_VMEM] + [ANYWHERE] * (8 + n),
        out_specs=[ANYWHERE] * n + [IN_VMEM] * 2 + [ANYWHERE] * 7,
        scratch_shapes=scratch,
        compiler_params=pltpu.CompilerParams(
            collective_id=cid, has_side_effects=True, vmem_limit_bytes=VMEM_LIMIT
        ),
        cost_estimate=pl.CostEstimate(
            flops=24 * 10**9, bytes_accessed=200 * 2**20, transcendentals=10**6
        ),
    )(*operands, *sources)


def attend_backward_block(net, qkv_ref, grad_ref, mixed_ref, lse_ref, len_ref, conts, acc_ref):
    total, width = qkv_ref.shape
    block = total // TP
    q_heads = width // (2 * HEAD_DIM)
    kv_heads = q_heads // 2
    factor = 1.0 / math.sqrt(HEAD_DIM)
    key_at = q_heads * HEAD_DIM
    value_at = key_at + kv_heads * HEAD_DIM
    places = attend_rows(net, block)
    acc_ref[:, key_at:] = jnp.zeros((total, width - key_at), jnp.float32)
    for i in range(TP):
        row_seg = block_segments(len_ref, conts, block, i, True)
        masks = [
            block_mask(row_seg, block_segments(len_ref, conts, block, j, False), i == j, block)
            for j in range(i + 1)
        ]
        for h in range(q_heads):
            kv = h // 2
            lanes = slice(h * HEAD_DIM, (h + 1) * HEAD_DIM)
            query = qkv_ref[places[i], lanes]
            grad = grad_ref[places[i], lanes]
            lse = lse_ref[i, :, h : h + 1]
            inner = jnp.sum(
                grad.astype(jnp.float32) * mixed_ref[places[i], lanes].astype(jnp.float32),
                axis=1,
                keepdims=True,
            )
            grad_query = jnp.zeros((block, HEAD_DIM), jnp.float32)
            key_lanes = slice(key_at + kv * HEAD_DIM, key_at + (kv + 1) * HEAD_DIM)
            value_lanes = slice(value_at + kv * HEAD_DIM, value_at + (kv + 1) * HEAD_DIM)
            for j in range(i + 1):
                key = qkv_ref[places[j], key_lanes]
                value = qkv_ref[places[j], value_lanes]
                s = dot_nt(query, key) * factor
                prob = jnp.where(masks[j], jnp.exp(s - lse), 0.0)
                grad_prob = dot_nt(grad, value)
                grad_score = (prob * (grad_prob - inner)).astype(jnp.bfloat16)
                grad_query = grad_query + jnp.dot(
                    grad_score, key, preferred_element_type=jnp.float32
                )
                acc_ref[places[j], key_lanes] += dot_tn(grad_score, query) * factor
                acc_ref[places[j], value_lanes] += dot_tn(prob.astype(jnp.bfloat16), grad)
            acc_ref[places[i], lanes] = grad_query * factor


def attn_backward_kernel(kinds, conts, *refs):
    n = len(kinds)
    (grad_middle, hidden, gain, qkv, dmixed, mixed, lse, lengths, cos_ref, sin_ref) = refs[:10]
    rows_in, w_in = refs[10:12]
    sources, targets, refs = refs[12 : 12 + n], refs[12 + n : 12 + 2 * n], refs[12 + 2 * n :]
    upstream, up_low, gain_grad, qkv_own, qkv_other = refs[:5]
    (acc, dqkv, rows, w_qkv, g_qkv, far_out, far_in, pass_out, pass_in,
     send_sems, recv_sems, local_sems) = refs[5:]
    net = Net(send_sems, recv_sems, local_sems)
    block, depth = hidden.shape
    total = TP * block
    load_rows = net.local(rows_in, rows)
    load_w = net.local(w_in, w_qkv)
    greet_all(net, kinds)
    begin_moves(net, kinds, sources, targets)
    attend_backward_block(net, qkv, dmixed, mixed, lse, lengths, conts, acc)
    for s in range(TP):
        at = slice(s * block, (s + 1) * block)
        value = acc[at, :]
        turned = value * cos_ref[at, :] - head_partner(value, HEAD_DIM // 2) * sin_ref[at, :]
        dqkv[at, :] = turned.astype(jnp.bfloat16)
    load_w.wait()
    load_rows.wait()
    urows = g_qkv.shape[2]
    wide = 2 * TP * urows

    def back(s):
        return dot_nt(dqkv[s * block : (s + 1) * block, :], w_qkv[...].reshape(depth, -1))

    def meanwhile():
        def tile(m, carry):
            lanes = pl.ds(pl.multiple_of(m * wide, wide), wide)
            grad = dot_tn(rows[:, :, lanes].reshape(total, wide), dqkv[...])
            g_qkv[pl.ds(2 * m, 2)] = grad.astype(jnp.bfloat16).reshape(2, TP, urows, -1)
            return carry

        lax.fori_loop(0, TP, tile, 0)
        net.keep(g_qkv.at[pl.ds(net.y * TP, TP)], qkv_own)
        net.keep(g_qkv.at[pl.ds((1 - net.y) * TP, TP)], qkv_other)

    incoming = collect_during(net, back, (far_out, far_in, pass_out, pass_in), meanwhile)
    part, gain_part = norm_backward(hidden[...], gain[...], incoming)
    gain_grad[...] = gain_part
    result = grad_middle[...] + part
    upstream[...] = result
    up_low[...] = result.astype(jnp.bfloat16)
    net.finish()


def attn_backward(
    cid, moves, conts, grad_middle, hidden, gain, qkv, dmixed, mixed, lse, lengths, cosine, sine, rows, w_qkv
):
    bf, f32 = jnp.bfloat16, jnp.float32
    shape = jax.ShapeDtypeStruct
    block, depth = hidden.shape
    total, width = qkv.shape
    kinds = tuple(kind for kind, _ in moves)
    sources = [source for _, source in moves]
    n = len(moves)
    urows = w_qkv.shape[3]
    outs = [moved_shape(kind, source) for kind, source in moves] + [
        shape((block, depth), f32),
        shape((block, depth), bf),
        shape((1, depth), f32),
        shape((TP, TP, urows, width), bf),
        shape((TP, TP, urows, width), bf),
    ]
    scratch = [
        pltpu.VMEM((total, width), f32),
        pltpu.VMEM((total, width), bf),
        pltpu.VMEM((TP, block, depth), bf),
        pltpu.VMEM(w_qkv.shape, bf),
        pltpu.VMEM((2 * TP, TP, urows, width), bf),
        pltpu.VMEM((2, block, depth), bf),
        pltpu.VMEM((2, block, depth), bf),
        pltpu.VMEM((block, depth), bf),
        pltpu.VMEM((block, depth), bf),
    ] + sems(48, 8)
    return pl.pallas_call(
        functools.partial(attn_backward_kernel, kinds, conts),
        out_shape=outs,
        in_specs=[IN_VMEM] * 10 + [ANYWHERE] * (2 + n),
        out_specs=[ANYWHERE] * n + [IN_VMEM] * 3 + [ANYWHERE] * 2,
        scratch_shapes=scratch,
        compiler_params=pltpu.CompilerParams(
            collective_id=cid, has_side_effects=True, vmem_limit_bytes=VMEM_LIMIT
        ),
        cost_estimate=pl.CostEstimate(
            flops=16 * 10**9, bytes_accessed=200 * 2**20, transcendentals=10**7
        ),
    )(grad_middle, hidden, gain, qkv, dmixed, mixed, lse, lengths, cosine, sine, rows, w_qkv, *sources)


def add_low(own, got):
    return (own.astype(jnp.float32) + got.astype(jnp.float32)).astype(jnp.bfloat16)


def z_total(summed, got, axis):
    own = lax.dynamic_index_in_dim(summed, lax.axis_index("fsdp"), axis, keepdims=False)
    return (own.astype(jnp.float32) + jnp.sum(got.astype(jnp.float32), axis=0)).astype(jnp.bfloat16)


def end_kernel(step, qw, kw, *refs):
    layers, refs = (refs[:7], refs[7:15]), refs[15:]
    x_outs, back, refs = refs[:2], refs[2], refs[3:]
    out_x, out_back, out_q, out_k, out_v, out_o, out_g, out_u, out_d = refs
    q = lax.rem(lax.axis_index("dp"), TP)
    z = lax.axis_index("fsdp")
    low, high = lax.rem(q, 2) == 1, lax.div(q, 2) == 1

    def columns(blocks, got):
        pieces = [blocks[q]] + [got[k] for k in range(3)]
        a = [jnp.where(low, pieces[i ^ 1], pieces[i]) for i in range(4)]
        return [jnp.where(high, a[i ^ 2], a[i]).astype(jnp.float32) for i in range(4)]

    def lay(target, layer, pieces, at, width):
        half = width // 2
        for n, piece in enumerate(pieces):
            for side in range(2):
                to = (side * TP + n) * half
                target[layer, :, to : to + half] = piece[:, at + side * half : at + (side + 1) * half]

    for layer in range(2):
        bqkv, tqkv, bgu, tgu = layers[layer][:4]
        pieces = columns(bqkv, tqkv)
        lay(out_q, layer, pieces, 0, qw)
        lay(out_k, layer, pieces, qw, kw)
        lay(out_v, layer, pieces, qw + kw, kw)
        pieces = columns(bgu, tgu)
        lay(out_g, layer, pieces, 0, 2 * step)
        lay(out_u, layer, pieces, 2 * step, 2 * step)
        sums = [(*layers[layer][-2:], out_d)]
        if layer == 0:
            out_o[0] = layers[0][4][...]
        else:
            sums.append((*layers[1][4:6], out_o))
        for summed, got, target in sums:
            value = summed[z].astype(jnp.float32)
            for k in range(3):
                value = value + got[k].astype(jnp.float32)
            target[layer] = value
        out_x[layer] = x_outs[layer][...]
    out_back[...] = back[...].astype(jnp.float32)


def end_assembly(step, qw, kw, pieces, x_outs, back):
    f32 = jnp.float32
    shape = jax.ShapeDtypeStruct
    block, depth = back.shape
    rows = pieces[0].shape[1]
    drows = pieces[5].shape[1]
    outs = [
        shape((2, block, depth), jnp.bfloat16),
        shape((block, depth), f32),
        shape((2, rows, TP * qw), f32),
        shape((2, rows, TP * kw), f32),
        shape((2, rows, TP * kw), f32),
        shape((2, rows, depth), f32),
        shape((2, rows, TP * 2 * step), f32),
        shape((2, rows, TP * 2 * step), f32),
        shape((2, drows, depth), f32),
    ]
    return pl.pallas_call(
        functools.partial(end_kernel, step, qw, kw),
        out_shape=outs,
        in_specs=[IN_VMEM] * 18,
        out_specs=[IN_VMEM] * 9,
        compiler_params=pltpu.CompilerParams(vmem_limit_bytes=VMEM_LIMIT),
    )(*pieces, *x_outs, back)


def column_pack(weights):
    parts = []
    for weight in weights:
        layers, rows, width = weight.shape
        view = weight.reshape(layers, rows, 2, TP, width // (2 * TP))
        parts.append(view.transpose(0, 3, 1, 2, 4).reshape(layers, TP, rows, width // TP))
    return jnp.concatenate(parts, axis=3)


def fast_device(
    tokens, gain_attn, w_query, w_key, w_value, w_out, gain_ffn, w_gate, w_up, w_down, lengths, cotangent
):
    depth = tokens.shape[1]
    shard = w_query.shape[1]
    conts = lengths.shape[1]
    halfway = HEAD_DIM // 2
    qw, kw = w_query.shape[2] // TP, w_key.shape[2] // TP
    step = w_gate.shape[2] // (2 * TP)
    frequency = ROPE_BASE ** (-jnp.arange(halfway, dtype=jnp.float32) * 2.0 / HEAD_DIM)
    lane = jnp.arange(128)[:, None]
    column = jnp.arange(qw + 2 * kw)[None]
    turned = column < qw + kw
    frequency = jnp.pad(frequency, (0, 128 - halfway))[None]
    picks = (lane == jnp.where(turned, column % halfway, halfway)).astype(jnp.float32)
    signed = picks * jnp.where(turned, jnp.where(column % HEAD_DIM < halfway, -1.0, 1.0), 0.0)
    gain_tile = jnp.pad(
        jnp.concatenate([gain_attn, gain_ffn], axis=0).astype(jnp.float32), ((0, 4), (0, 128 - shard))
    )
    len_tile = jnp.pad(lengths, ((0, 7), (0, 128 - conts)))
    (hidden, cosine, sine, lens, g_qkv0, g_qkv1, g_gu0, g_gu1, g_out0, g_out1, g_down0, g_down1, g_gain) = (
        start_exchange(
            conts, column_pack((w_query, w_key, w_value)), w_gate, w_up, w_out, w_down, gain_tile,
            tokens, len_tile, frequency, picks, signed,
        )
    )
    gains = jnp.transpose(g_gain[..., :4, :shard], (3, 0, 1, 2, 4)).reshape(4, 1, depth)
    qkv, out, gu, down, qkv_next, out_next, gu_next, down_next = range(8)
    programs0 = (
        ((3, down, 0, 1), (1, gu, 0, 2), (1, gu, 2, 2)),
        ((2, gu, 0, 2),),
        ((2, gu, 2, 2), (3, gu, 0, 2)),
        ((3, gu, 2, 2), (1, qkv_next, 0, 4), (1, out_next, 0, 1)),
        ((2, qkv_next, 0, 4), (2, out_next, 0, 1), (1, down_next, 0, 1), (1, gu_next, 0, 2)),
        ((3, qkv_next, 0, 4), (3, out_next, 0, 1), (2, down_next, 0, 1)),
    )
    programs1 = (
        ((3, down, 0, 1), (2, gu, 0, 2), (1, gu, 2, 2)),
        ((3, gu, 0, 2), (2, gu, 2, 2)),
        (),
        ((3, gu, 2, 2),),
        (),
        (),
    )
    tables = (cosine, sine, lens)
    res = forward_layer(
        programs0, cotangent, 2, conts, hidden, gains[0], gains[2], *tables,
        (g_qkv0, g_out0, g_gu0, g_down0, g_qkv1, g_out1, g_gu1, g_down1),
    )
    weights0, moving1, acts0 = res[:4], res[4:8], res[8:]
    (x1, mid0, lse0, low1, rows0, qkv0, mix0, frows0, gate0, up0, act0, branch) = acts0
    res = forward_layer(programs1, None, 3, conts, x1, gains[1], gains[3], *tables, moving1)
    weights1, acts1 = res[:4], res[4:]
    (x2, mid1, lse1, low2, rows1, qkv1, mix1, frows1, gate1, up1, act1) = acts1

    (low1_back, gmid1, ggf1, dmix1, d_own, d_got, gu_own, gu_other, o_own, o_other) = ffn_backward(
        4, (("g", low1),), branch, True, mid1, gains[3], act1, frows1, gate1, up1, mix1,
        weights1[3], weights1[2], weights1[1],
    )
    sd1 = add_low(d_own, d_got)
    (gu_got, rd1, low2_back, up_1, _, gga1, qkv_own1, qkv_other1) = attn_backward(
        5, (("y", gu_other), ("z", sd1), ("g", low2)), conts,
        gmid1, x1, gains[1], qkv1, dmix1, mix1, lse1, lens, cosine, sine, rows1, weights1[0],
    )
    sgu1 = add_low(gu_own, gu_got)
    (qkv_got1, o_got, rgu1, gmid0, ggf0, dmix0, d_own0, d_got0, gu_own0, gu_other0, o_own0, o_other0) = ffn_backward(
        6, (("y", qkv_other1), ("y", o_other), ("zc", sgu1)), up_1, False, mid0, gains[2], act0, frows0, gate0, up0, mix0,
        weights0[3], weights0[2], weights0[1],
    )
    sqkv1 = add_low(qkv_own1, qkv_got1)
    so1 = add_low(o_own, o_got)
    sd0 = add_low(d_own0, d_got0)
    bgu1 = z_total(sgu1, rgu1, 1)
    (gu_got0, rqkv1, rd0, ro1, tgu1, _, up_low, gga0, qkv_own0, qkv_other0) = attn_backward(
        7, (("y", gu_other0), ("zc", sqkv1), ("z", sd0), ("z", so1), ("t", bgu1)), conts,
        gmid0, hidden, gains[0], qkv0, dmix0, mix0, lse0, lens, cosine, sine, rows0, weights0[0],
    )
    sgu0 = add_low(gu_own0, gu_got0)
    bqkv1 = z_total(sqkv1, rqkv1, 1)
    gain_part = jnp.concatenate([gga0, gga1, ggf0, ggf1, jnp.zeros((4, depth), jnp.float32)], axis=0)
    (gain_sums, osum0, bgu0, bqkv0, tgu0, tqkv0, tqkv1, back) = run_tail(
        8, gain_part, sgu0, o_own0, o_other0, qkv_own0, qkv_other0, bqkv1, up_low
    )
    gain_sums = gain_sums[:4]
    device = lax.axis_index("dp") * lax.axis_size("fsdp") + lax.axis_index("fsdp")
    own_gain = lax.dynamic_slice_in_dim(gain_sums, device * shard, shard, 1)
    (out_x, out_back, grad_q, grad_k, grad_v, grad_o, grad_g, grad_u, grad_d) = end_assembly(
        step, qw, kw,
        (bqkv0, tqkv0, bgu0, tgu0, osum0, sd0, rd0, bqkv1, tqkv1, bgu1, tgu1, so1, ro1, sd1, rd1),
        (low1_back, low2_back), back,
    )
    return (
        out_x, out_back, own_gain[:2], grad_q, grad_k, grad_v, grad_o, own_gain[2:], grad_g, grad_u, grad_d,
    )


def per_device(*arrays):
    tokens, w_query, w_key, w_gate = arrays[0], arrays[2], arrays[3], arrays[7]
    dp_size, z_size = lax.axis_size("dp"), lax.axis_size("fsdp")
    suits = (
        dp_size == 2 * TP
        and z_size == TP
        and w_key.shape[2] // HEAD_DIM == dp_size
        and w_query.shape[2] == 2 * w_key.shape[2]
        and tokens.shape[0] % 128 == 0
        and w_query.shape[1] % 16 == 0
        and w_gate.shape[2] % (TP * dp_size * 128) == 0
    )
    return (fast_device if suits else general_device)(*arrays)


def solution(mesh):
    placed = (
        P(("dp", "fsdp"), None),
        P(None, ("dp", "fsdp")),
        P(None, ("dp", "fsdp"), None),
        P(None, ("dp", "fsdp"), None),
        P(None, ("dp", "fsdp"), None),
        P(None, ("dp", "fsdp"), None),
        P(None, ("dp", "fsdp")),
        P(None, ("dp", "fsdp"), None),
        P(None, ("dp", "fsdp"), None),
        P(None, ("dp", "fsdp"), None),
        P("dp", None),
        P(("dp", "fsdp"), None),
    )
    return jax.shard_map(
        per_device,
        mesh=mesh,
        in_specs=placed,
        out_specs=(
            P(None, ("dp", "fsdp"), None),
            P(("dp", "fsdp"), None),
            P(None, ("dp", "fsdp")),
            P(None, ("dp", "fsdp"), None),
            P(None, ("dp", "fsdp"), None),
            P(None, ("dp", "fsdp"), None),
            P(None, ("dp", "fsdp"), None),
            P(None, ("dp", "fsdp")),
            P(None, ("dp", "fsdp"), None),
            P(None, ("dp", "fsdp"), None),
            P(None, ("dp", "fsdp"), None),
        ),
        check_vma=False,
    )
```
